32 devices in a mesh: dp: 8 (over y, x, core), blk: 4 (over z).
Axes of the slice: x: 2, y: 2, z: 4, core: 2. Of those that a mesh axis runs over, the one named last changes fastest.
Arguments:
- bytes_in: bfloat16 [131072, 512], P(('dp', 'blk')), may hold values from -16 to 16
- flags: int32 [131072], P(('dp', 'blk')), may hold values from 0 to 1, as said below
- lengths: int32 [8, 4], P('dp'), may hold values from 1024 to 13312, as said below
- cotangent: float32 [16384, 512], P(('dp', 'blk')), may hold values from -6 to 6
- w_query: bfloat16 [512, 512], replicated, may hold values from -0.25 to 0.25
- w_key: bfloat16 [512, 512], replicated, may hold values from -0.25 to 0.25
- w_value: bfloat16 [512, 512], replicated, may hold values from -0.25 to 0.25
- w_out: bfloat16 [512, 512], replicated, may hold values from -2 to 2
- w_up: bfloat16 [512, 2048], replicated, may hold values from -0.25 to 0.25
- w_down: bfloat16 [2048, 512], replicated, may hold values from -0.125 to 0.125
- gain_attn: float32 [512], replicated, may hold values from 0.5 to 1.5
- gain_ffn: float32 [512], replicated, may hold values from 0.5 to 1.5
Outputs:
- output: float32 [16384, 512], P(('dp', 'blk'))
- grad_bytes: float32 [131072, 512], P(('dp', 'blk'))
- grad_w_query: float32 [512, 512], replicated
- grad_w_key: float32 [512, 512], replicated
- grad_w_value: float32 [512, 512], replicated
- grad_w_out: float32 [512, 512], replicated
- grad_w_up: float32 [512, 2048], replicated
- grad_w_down: float32 [2048, 512], replicated
- grad_gain_attn: float32 [512], replicated
- grad_gain_ffn: float32 [512], replicated
The draws below stay inside these ranges and needn't reach their ends.
Inputs may be any that keep to these rules, and one draw needn't show every extreme that they name: `flags`: each aligned cell of 8 bytes holds at most one 1; the first cell of every block of 4096 bytes holds one; the first byte of every sequence is a 1; in each group some block of 4096 bytes holds exactly 512 ones. The lengths of a group add up to 16384; one of them is 13312, the others 1024.
All inputs are finite; a program needn't handle non-finite values.
Results may differ from the reference program's by a relative error of at most 0.015.
Values may be sent and summed in bfloat16 or wider, within the bound.
A program may use at most 320 MiB of HBM per device.

```python
import jax
import jax.numpy as jnp
from jax import lax

D = 512
HEADS = 8
HEAD_DIM = 64
FF = 2048
BYTES_DEV = 4096
CELL = 8
SHORT_LEN = 1024
SHORTS = 3
SEQS = 4
SEG_DEV = 512
GROUP_BYTES = 16384
SEGMENTS = 2048
N_DP = 8
N_BLK = 4


def group_plan(key):
    before = jax.random.randint(key, (N_DP,), 0, SHORTS + 1)
    seq_ids = jnp.arange(SEQS, dtype=jnp.int32)
    long_len = N_BLK * BYTES_DEV - SHORTS * SHORT_LEN
    return jnp.where(seq_ids[None, :] == before[:, None], long_len, SHORT_LEN).astype(jnp.int32)


def draw_lengths(key, part):
    seq_sizes = group_plan(key)
    return seq_sizes


def draw_flags(key, part):
    seq_sizes = group_plan(key)
    key = jax.random.fold_in(key, 7)
    key_one, key_two, key_three = jax.random.split(key, 3)
    cells_dev = BYTES_DEV // CELL
    cell_total = N_BLK * cells_dev
    starts = jnp.cumsum(seq_sizes, axis=1) - seq_sizes
    cell_ids = jnp.arange(cell_total, dtype=jnp.int32)
    opening = jnp.any(cell_ids[None, :, None] * CELL == starts[:, None, :], axis=2)
    chance = jax.random.randint(key_one, (N_DP, cell_total), 0, 4) < 3
    full_dev = jax.random.randint(key_two, (N_DP,), 0, N_BLK)
    offset_in = jax.random.randint(key_three, (N_DP, cell_total), 0, CELL)
    has_mark = chance | (cell_ids[None, :] % cells_dev == 0) | ((cell_ids // cells_dev)[None, :] == full_dev[:, None]) | opening
    offset_in = jnp.where(opening, 0, offset_in)
    byte_ids = jnp.arange(N_BLK * BYTES_DEV, dtype=jnp.int32)
    cell_of = byte_ids // CELL
    mark_bits = has_mark[:, cell_of] & ((byte_ids % CELL)[None, :] == offset_in[:, cell_of])
    return mark_bits.astype(jnp.int32).reshape(-1)


def block_scale(own_key, shape, shards, least, top_value):
    def one(dim, blocks):
        steps = jax.random.uniform(jax.random.fold_in(jax.random.fold_in(own_key, 6), dim), (blocks,), jnp.float32, least / len(shards), top_value / len(shards))
        return jnp.repeat(jnp.exp(steps), shape[dim] // blocks).reshape((-1,) + (1,) * (len(shape) - dim - 1))

    loudness = one(*shards[0])
    for cut in shards[1:]:
        loudness = loudness * one(*cut)
    return loudness


def normal_values(key, dims, scale, reach, pieces=(), kind=jnp.bfloat16):
    values = jax.random.normal(key, dims, jnp.float32) * scale
    if len(pieces) > 0:
        values = block_scale(key, dims, pieces, -0.22, 0.18) * values
    return jnp.clip(values, min=-reach, max=reach).astype(kind)


def setup_inputs(seed: int = 0) -> dict:
    streams_of = jax.random.split(jax.random.key(seed), 13)
    bytes_in = normal_values(streams_of[0], (N_DP * GROUP_BYTES, D), 3.0, 16.0, ((0, 32),))
    flags = draw_flags(jax.random.fold_in(streams_of[12], 71), 0)
    lengths = draw_lengths(jax.random.fold_in(streams_of[12], 71), 0)
    cotangent = normal_values(streams_of[3], (N_DP * SEGMENTS, D), 1.0, 6.0, ((0, 32),), jnp.float32)
    w_query = normal_values(streams_of[4], (D, D), D ** -0.5, 0.25)
    w_key = normal_values(streams_of[5], (D, D), D ** -0.5, 0.25)
    w_value = normal_values(streams_of[6], (D, D), D ** -0.5, 0.25)
    w_out = normal_values(streams_of[7], (D, D), (D // 64) ** -0.5, 2.0)
    w_up = normal_values(streams_of[8], (D, FF), D ** -0.5, 0.25)
    w_down = normal_values(streams_of[9], (FF, D), FF ** -0.5, 0.125)
    gain_attn = jnp.clip(1.0 + 0.1 * jax.random.normal(streams_of[10], (D,), jnp.float32), 0.5, 1.5)
    gain_ffn = jnp.clip(1.0 + 0.1 * jax.random.normal(streams_of[11], (D,), jnp.float32), 0.5, 1.5)
    return {"bytes_in": bytes_in, "flags": flags, "lengths": lengths, "cotangent": cotangent, "w_query": w_query, "w_key": w_key, "w_value": w_value, "w_out": w_out, "w_up": w_up, "w_down": w_down, "gain_attn": gain_attn, "gain_ffn": gain_ffn}


@jax.custom_vjp
def low(v):
    return lax.optimization_barrier(v.astype(jnp.bfloat16)).astype(jnp.float32)

@jax.custom_vjp
def low_back(v):
    return v

def low_keep(v):
    return (low(v), None)

def low_pass(kept, grad):
    return (grad,)

def back_keep(v):
    return (v, None)

def back_low(kept, grad):
    return (low(grad),)
low.defvjp(low_keep, low_pass)
low_back.defvjp(back_keep, back_low)
EPSILON = 1e-05
ROTARY_BASE = 10000.0
NEGATIVE = -1e+30
PRECISE = lax.Precision.HIGHEST

def layer_norm(values, gain):
    center = values - lax.optimization_barrier(jnp.mean(values, axis=-1, keepdims=True))
    spread = lax.optimization_barrier(jnp.mean(center * center, axis=-1, keepdims=True))
    return center * lax.rsqrt(spread + EPSILON) * gain

def rotate(vectors, positions):
    half_dim = vectors.shape[-1] // 2
    freqs = ROTARY_BASE ** (-2.0 * jnp.arange(half_dim, dtype=jnp.float32) / vectors.shape[-1])
    angles = positions.astype(jnp.float32)[:, None] * freqs[None, :]
    cosine = jnp.cos(angles)[:, None, :]
    sine = jnp.sin(angles)[:, None, :]
    first_half = vectors[..., :half_dim]
    second_half = vectors[..., half_dim:]
    return jnp.concatenate([first_half * cosine - second_half * sine, second_half * cosine + first_half * sine], axis=-1)

def slot_layout(marks, seq_sizes):
    grid = marks.reshape(N_BLK, BYTES_DEV)
    running = jnp.cumsum(grid, axis=1).astype(jnp.int32)
    slot_of = running - 1
    counts = running[:, -1]
    previous = jnp.concatenate([jnp.zeros((1,), jnp.int32), counts[:-1]]).astype(jnp.int32)
    block_ids = jnp.arange(N_BLK, dtype=jnp.int32)[:, None]
    owner = jnp.where(slot_of >= 0, block_ids * SEG_DEV + slot_of, (block_ids - 1) * SEG_DEV + previous[:, None] - 1)
    offsets = (jnp.cumsum(counts) - counts).astype(jnp.int32)
    slot_ids = jnp.arange(N_BLK * SEG_DEV, dtype=jnp.int32)
    owner_dev = slot_ids // SEG_DEV
    within = slot_ids % SEG_DEV
    positions = (offsets[owner_dev] + jnp.minimum(within, counts[owner_dev] - 1)).astype(jnp.int32)
    live = within < counts[owner_dev]
    starts = (jnp.cumsum(seq_sizes) - seq_sizes).astype(jnp.int32)
    byte_ids = jnp.arange(N_BLK * BYTES_DEV, dtype=jnp.int32)
    seq_first = lax.optimization_barrier(jnp.sum(marks[None, :] * (byte_ids[None, :] < starts[:, None]).astype(jnp.int32), axis=1)).astype(jnp.int32)
    firsts = lax.optimization_barrier(jnp.max(jnp.where(seq_first[None, :] <= positions[:, None], seq_first[None, :], 0), axis=1)).astype(jnp.int32)
    return (owner.reshape(-1).astype(jnp.int32), positions, live, firsts)

def group_forward(raw, params, owner, seg_tally, positions, live, firsts):
    w_query, w_key, w_value, w_out, w_up, w_down, gain_attn, gain_ffn = params
    slots = N_BLK * SEG_DEV
    scale = HEAD_DIM ** (-0.5)
    seg_sums = jax.ops.segment_sum(raw, owner, num_segments=slots)
    pooled = low_back(seg_sums) / jnp.maximum(seg_tally, 1.0)[:, None]
    n1 = low(layer_norm(pooled, gain_attn))
    query_rot = low(rotate(low_back(jnp.dot(n1, w_query, precision=PRECISE)).reshape(slots, HEADS, HEAD_DIM), positions))
    key_rot = low(rotate(low_back(jnp.dot(n1, w_key, precision=PRECISE)).reshape(slots, HEADS, HEAD_DIM), positions))
    value_low = low(low_back(jnp.dot(n1, w_value, precision=PRECISE))).reshape(slots, HEADS, HEAD_DIM)
    block_rows = min(512, slots)

    def one_block(inputs):
        query_block, pos_block, first_block = inputs
        scores = low_back(jnp.einsum('qhe,khe->hqk', query_block, key_rot, precision=PRECISE) * scale)
        allowed = (positions[None, :] <= pos_block[:, None]) & (positions[None, :] >= first_block[:, None]) & live[None, :]
        scores = jnp.where(allowed[None], scores, NEGATIVE)
        prob_low = low(jax.nn.softmax(scores, axis=-1))
        return jnp.einsum('hqk,khe->qhe', prob_low, value_low, precision=PRECISE)
    blocks_out = lax.map(jax.checkpoint(one_block), (query_rot.reshape(slots // block_rows, block_rows, HEADS, HEAD_DIM), positions.reshape(-1, block_rows), firsts.reshape(-1, block_rows)))
    attended = low(blocks_out.reshape(slots, D))
    middle = pooled + low_back(jnp.dot(attended, w_out, precision=PRECISE))
    n2 = low(layer_norm(middle, gain_ffn))
    act_low = low(jax.nn.gelu(low_back(jnp.dot(n2, w_up, precision=PRECISE)), approximate=False))
    result = middle + low_back(jnp.dot(act_low, w_down, precision=PRECISE))
    return result * live.astype(jnp.float32)[:, None]

def reference(bytes_in, flags, lengths, cotangent, w_query, w_key, w_value, w_out, w_up, w_down, gain_attn, gain_ffn):
    params = (w_query.astype(jnp.float32), w_key.astype(jnp.float32), w_value.astype(jnp.float32), w_out.astype(jnp.float32), w_up.astype(jnp.float32), w_down.astype(jnp.float32), gain_attn, gain_ffn)
    group_bytes = N_BLK * BYTES_DEV
    slots = N_BLK * SEG_DEV

    def one_group(totals, items):
        raw, marks, seq_sizes, seed_grad = items
        owner, positions, live, firsts = slot_layout(marks, seq_sizes)
        seg_tally = jax.ops.segment_sum(jnp.ones(owner.shape, jnp.float32), owner, num_segments=slots)

        def forward(raw_f, param_f):
            return group_forward(raw_f, param_f, owner, seg_tally, positions, live, firsts)
        result, pullback = jax.vjp(forward, raw.astype(jnp.float32), params)
        grad_raw, grad_params = pullback(seed_grad)
        totals = jax.tree.map(lambda left, right: left + right, totals, grad_params)
        return (totals, (result, grad_raw))
    start = jax.tree.map(jnp.zeros_like, params)
    totals, (results, grad_raw) = lax.scan(one_group, start, (bytes_in.reshape(N_DP, group_bytes, D), flags.reshape(N_DP, group_bytes), lengths, cotangent.reshape(N_DP, slots, D)))
    return (results.reshape(-1, D), grad_raw.reshape(-1, D), totals[0], totals[1], totals[2], totals[3], totals[4], totals[5], totals[6], totals[7])
```

```python
import functools
import math

import jax
import jax.numpy as jnp
import numpy as np
from jax import lax
from jax.experimental import pallas as pl
from jax.experimental.pallas import tpu as pltpu
from jax.sharding import PartitionSpec as P

HEADS = 8
HEAD_DIM = 64
EPSILON = 1e-05
ROTARY_BASE = 10000.0
NEGATIVE = -1e30
LOG2E = math.log2(math.e)

MESH = pl.DeviceIdType.MESH
F32 = jnp.float32
BF16 = jnp.bfloat16
NN = (((1,), (0,)), ((), ()))
NT = (((1,), (1,)), ((), ()))
TN = (((0,), (0,)), ((), ()))


def mm(a, b, dims):
    return lax.dot_general(a, b, dims, preferred_element_type=F32)


def iota(shape, dim):
    return lax.broadcasted_iota(jnp.int32, shape, dim)


class Copy:
    def __init__(self, src, dst, send_sem, recv_sem, device, cond=None):
        self.parts = (src, dst, send_sem, recv_sem)
        self.device = device
        self.cond = cond

    def _do(self, act):
        def run():
            src, dst, send_sem, recv_sem = self.parts
            act(
                pltpu.make_async_remote_copy(
                    src_ref=src,
                    dst_ref=dst,
                    send_sem=send_sem,
                    recv_sem=recv_sem,
                    device_id=self.device,
                    device_id_type=MESH,
                )
            )

        if self.cond is None:
            run()
        else:
            pl.when(self.cond)(run)

    def start(self):
        self._do(lambda d: d.start())

    def wait_send(self):
        self._do(lambda d: d.wait_send())

    def wait_recv(self):
        self._do(lambda d: d.wait_recv())


CHUNKS = ((0, 4), (4, 9), (9, 12))
SEMS_AR = 22


def layer_kernel(
    bytes_hbm,
    flags_ref,
    lengths_ref,
    cot_hbm,
    wq_hbm,
    wk_hbm,
    wv_hbm,
    wo_hbm,
    wup_hbm,
    wdn_hbm,
    gains_ref,
    freq_ref,
    out_ref,
    gs_ref,
    came_ref,
    slots_ref,
    wgrad_hbm,
    ggain_ref,
    bytes_v,
    weights,
    wup,
    wdn,
    meta,
    tail,
    slot_sc,
    p_own,
    relay,
    p_all,
    n1,
    k_t,
    v_t,
    q_t,
    tab_c,
    tab_s,
    pos,
    gcol,
    cot_own,
    cot_w,
    o_acc,
    m_sc,
    l_sc,
    att,
    gb,
    hat2,
    d_o,
    d_sc,
    gmid,
    dk,
    dv,
    dq,
    gwqkv,
    big,
    wg,
    r1,
    r2,
    r3,
    r4,
    ppart,
    rc,
    rz,
    gfin,
    out_s,
    out_r,
    rdiv,
    last_s,
    last_r,
    gain_acc,
    gain_s,
    gain_r,
    ss,
    rs,
    ls,
):
    cot_v, acc = hat2, big.at[0]
    dp = lax.axis_index("dp")
    z = lax.axis_index("blk")
    feat = 512
    half = 256
    nblk = 4
    c = lax.rem(dp, 2)
    x = lax.rem(lax.div(dp, 2), 2)
    y = lax.div(dp, 4)
    sib = (dp + 1 - 2 * c, z)
    xnb = (dp + 2 - 4 * x, z)
    ynb = (dp + 4 - 8 * y, z)
    g = lax.div(z, 2)
    zl = lax.rem(z, 2)
    w = 2 * zl + c
    zo = 4 * g + 1 - z
    near = 1 + g
    is_near = z == near
    own_worker = g == c

    def dev(core, zz):
        return (dp - c + core, zz)

    counter = {"s": 0, "r": 0, "l": 0}

    def ids(kind, n):
        first = counter[kind]
        counter[kind] = first + n
        return first

    sends = []

    def go(copy):
        copy.start()
        sends.append(copy)

    l_bytes = ids("l", 8)
    rows_chunk = bytes_v.shape[1]
    loads_bytes = [
        pltpu.make_async_copy(
            bytes_hbm.at[pl.ds(i * rows_chunk, rows_chunk)], bytes_v.at[i], ls.at[l_bytes + i]
        )
        for i in range(8)
    ]
    for d in loads_bytes:
        d.start()
    l_cot = ids("l", 1)
    load_cot = pltpu.make_async_copy(cot_hbm, cot_v, ls.at[l_cot])
    load_cot.start()
    l_w = ids("l", 4)
    loads_w = [
        pltpu.make_async_copy(src, weights.at[i], ls.at[l_w + i])
        for i, src in enumerate((wq_hbm, wk_hbm, wv_hbm, wo_hbm))
    ]
    for d in loads_w:
        d.start()
    l_f = ids("l", 8)
    loads_f = []
    for j in range(4):
        loads_f.append(
            pltpu.make_async_copy(
                wup_hbm.at[:, pl.ds(j * feat, feat)], wup.at[j], ls.at[l_f + 2 * j]
            )
        )
        loads_f.append(
            pltpu.make_async_copy(
                wdn_hbm.at[pl.ds(j * feat, feat)], wdn.at[j], ls.at[l_f + 2 * j + 1]
            )
        )
    for d in loads_f:
        d.start()

    barrier = pltpu.get_barrier_semaphore()
    me_line = c * nblk + z
    line = []
    for k in range(1, 8):
        t = lax.rem(me_line + k, 8)
        line.append((lax.div(t, nblk), lax.rem(t, nblk)))
    for core, zz in line:
        pl.semaphore_signal(barrier, inc=1, device_id=dev(core, zz), device_id_type=MESH)
    for d in (xnb, ynb):
        pl.semaphore_signal(barrier, inc=1, device_id=d, device_id_type=MESH)
    pl.semaphore_wait(barrier, 9)

    meta[c, z, 0:32, :] = flags_ref[...]
    meta[c, z, 32:40, :] = lengths_ref[...]
    s_meta, r_meta = ids("s", 7), ids("r", 8)
    for k, (core, zz) in enumerate(line):
        go(
            Copy(
                meta.at[c, z],
                meta.at[c, z],
                ss.at[s_meta + k],
                rs.at[r_meta + me_line],
                dev(core, zz),
            )
        )
    s_tail, r_tail = ids("s", 1), ids("r", 1)
    copy_tail = Copy(
        bytes_hbm.at[pl.ds(0, 16)],
        tail,
        ss.at[s_tail],
        rs.at[r_tail],
        (dp, lax.rem(z + nblk - 1, nblk)),
        z > 0,
    )
    go(copy_tail)

    @pl.when(z == nblk - 1)
    def _():
        tail[...] = jnp.zeros_like(tail)

    upper = (iota((128, 128), 0) <= iota((128, 128), 1)).astype(F32).astype(BF16)
    ones_sq = jnp.ones((128, 128), BF16)
    below = (iota((32, 32), 1) < iota((32, 32), 0)).astype(F32).astype(BF16)
    own_flags = flags_ref[...].astype(F32)
    flags_low = own_flags.astype(BF16)
    within = mm(flags_low, upper, NN)
    row_sums = mm(flags_low, ones_sq, NN)
    row_base = mm(below, row_sums.astype(BF16), NN)
    slot_of = within + row_base - 1.0
    for k in range(8):
        slot_sc[k] = slot_of[4 * k : 4 * k + 4, :]
    slots_ref[...] = slot_of
    cnt = jnp.sum(own_flags)

    acc[...] = jnp.zeros_like(acc)
    rdiv[...] = jnp.zeros_like(rdiv)
    slot_iota = iota((feat, 128), 0).astype(F32)
    ones_rows = jnp.ones((16, feat), BF16)

    def pool(k, carry):
        pltpu.make_async_copy(
            bytes_hbm.at[pl.ds(0, rows_chunk)], bytes_v.at[k], ls.at[l_bytes + k]
        ).wait()
        rows = slot_sc[k]
        member = jnp.concatenate(
            [
                (slot_iota == rows[r : r + 1, :]).astype(F32).astype(BF16)
                for r in range(4)
            ],
            axis=1,
        )
        acc[...] += mm(member, bytes_v[k], NN)
        rdiv[...] += mm(ones_rows, member, NT)
        return carry

    lax.fori_loop(0, 8, pool, 0)

    for i in range(2):
        row = jnp.broadcast_to(gains_ref[i : i + 1, :], (128, feat))
        col = row.T
        gcol[i] = jnp.concatenate([col, col], axis=1)

    for core, zz in line:
        Copy(
            meta.at[core, zz],
            meta.at[core, zz],
            ss.at[0],
            rs.at[r_meta + core * nblk + zz],
            sib,
        ).wait_recv()
    Copy(tail, tail, ss.at[0], rs.at[r_tail], sib, z < nblk - 1).wait_recv()
    zn = jnp.minimum(z + 1, nblk - 1)
    next_flags = meta[c, zn, 0:16, :].astype(F32).astype(BF16)
    next_within = mm(next_flags, upper, NN)
    has_next = (z < nblk - 1).astype(F32)
    lead = jnp.where(next_within[0:1, :] < 0.5, 1.0, 0.0) * has_next
    is_last16 = iota((feat, 16), 0).astype(F32) == cnt - 1.0
    member_tail = jnp.where(is_last16, lead[:, 0:16], 0.0).astype(BF16)
    sums = acc[...] + mm(member_tail, tail[...], NN)
    lane_row = iota((1, feat), 1).astype(F32)
    tally = rdiv[0:1, :] + jnp.where(lane_row == cnt - 1.0, jnp.sum(lead), 0.0)
    inverse_tally = 1.0 / jnp.maximum(tally, 1.0)
    rdiv[0:1, :] = inverse_tally
    live_row = jnp.where(lane_row < cnt, 1.0, 0.0)
    rdiv[1:2, :] = live_row
    pooled_t = (sums.T * inverse_tally).astype(BF16)
    p_own[0] = pooled_t[:, 0:half]
    p_own[1] = pooled_t[:, half:]

    s_p, r_p, r_relay = ids("s", 9), ids("r", 8), ids("r", 1)
    near_c = 1 + c

    def p_copy(src, hb, slot, device, cond=None):
        return Copy(src, p_all.at[hb], ss.at[s_p + slot], rs.at[r_p + hb], device, cond)

    other_worker = jnp.logical_not(own_worker)
    go(p_copy(p_own.at[c], 2 * z + c, 0, dev(c, zo), own_worker))
    go(p_copy(p_own.at[1 - c], 2 * z + 1 - c, 1, sib, own_worker))
    go(p_copy(p_own.at[c], 2 * z + c, 2, sib, own_worker))
    go(
        Copy(p_own.at[1 - c], relay, ss.at[s_p + 1], rs.at[r_relay], sib, other_worker)
    )
    go(p_copy(p_own.at[c], 2 * z + c, 2, dev(c, near_c), other_worker))

    @pl.when(own_worker)
    def _():
        p_all[2 * z] = p_own[0]
        p_all[2 * z + 1] = p_own[1]

    Copy(relay, relay, ss.at[0], rs.at[r_relay], sib, own_worker).wait_recv()
    go(p_copy(relay, 2 * z + c, 3, dev(c, 2 - c), own_worker))

    def p_wait(hb, cond=None):
        Copy(p_all.at[hb], p_all.at[hb], ss.at[0], rs.at[r_p + hb], sib, cond).wait_recv()

    p_wait(2 * z + c, other_worker)
    go(p_copy(p_all.at[2 * z + c], 2 * z + c, 0, dev(c, zo), other_worker))
    p_wait(2 * z + 1 - c, other_worker)

    load_cot.wait()
    cot_t = (cot_v[...].T * live_row).astype(BF16)
    cot_own[0] = cot_t[:, 0:half]
    cot_own[1] = cot_t[:, half:]
    s_cot, r_cot = ids("s", 2), ids("r", 2)
    early = z < 2
    slot_to = jnp.where(early, 0, 1)
    chip_to = 2 * c + jnp.where(early, z, 3 - z)
    for i in range(2):
        core_to = jnp.where(early, i, 1 - i)
        here = jnp.logical_and(core_to == c, chip_to == z)
        go(
            Copy(
                cot_own.at[i],
                cot_w.at[slot_to],
                ss.at[s_cot + i],
                rs.at[r_cot + slot_to],
                dev(core_to, chip_to),
                jnp.logical_not(here),
            )
        )

        @pl.when(here)
        def _():
            cot_w[slot_to] = cot_own[i]

    lo_here = jnp.logical_and(g == c, zl == z)
    hi_here = jnp.logical_and(g == c, 3 - zl == z)

    counts = []
    for b in range(nblk):
        counts.append(jnp.sum(meta[g, b, 0:32, :].astype(F32)))
    offsets = [jnp.float32(0.0)]
    for b in range(nblk):
        offsets.append(offsets[-1] + counts[b])
    lens = meta[g, z, 32:40, :].astype(F32)
    first_row = iota((8, 128), 0) == 0
    lane8 = iota((8, 128), 1)
    byte_at = (iota((32, 128), 0) * 128 + iota((32, 128), 1)).astype(F32)
    seq_first = [jnp.float32(0.0)]
    for s in range(1, 4):
        start = jnp.sum(jnp.where(jnp.logical_and(first_row, lane8 < s), lens, 0.0))
        prior = jnp.zeros((32, 128), F32)
        for b in range(nblk):
            prior = prior + jnp.where(
                byte_at + float(b * 4096) < start, meta[g, b, 0:32, :].astype(F32), 0.0
            )
        seq_first.append(jnp.sum(prior))

    freq = jnp.concatenate([freq_ref[...], freq_ref[...]], axis=1)
    lane_half = iota((1, half), 1).astype(F32)
    for hb in range(8):
        b = hb // 2
        j = lane_half + float((hb % 2) * half)
        p = offsets[b] + jnp.minimum(j, counts[b] - 1.0)
        first = jnp.zeros_like(p)
        for s in range(1, 4):
            first = jnp.maximum(first, jnp.where(p >= seq_first[s], seq_first[s], 0.0))
        pos[hb, 0:1, :] = p
        pos[hb, 1:2, :] = first
        angle = freq * p
        tab_c[hb] = jnp.cos(angle)
        tab_s[hb] = jnp.sin(angle)

    def pick(values, b):
        total = jnp.float32(0.0)
        for i, v in enumerate(values):
            total = total + jnp.where(b == i, v, 0.0)
        return total

    gain_col = gcol[0]

    def norm_parts(values):
        mean = jnp.mean(values, axis=0, keepdims=True)
        center = values - mean
        inverse = lax.rsqrt(jnp.mean(center * center, axis=0, keepdims=True) + EPSILON)
        return center * inverse, inverse

    def turned(values, hb, direction):
        cos = tab_c[hb]
        sin = tab_s[hb] * direction
        parts = []
        for h in range(HEADS):
            a = values[64 * h : 64 * h + 32, :]
            b = values[64 * h + 32 : 64 * h + 64, :]
            parts.append(a * cos - b * sin)
            parts.append(b * cos + a * sin)
        return jnp.concatenate(parts, axis=0).astype(BF16)

    for d in loads_w:
        d.wait()

    def keys_values(hb):
        unit, _ = norm_parts(p_all[hb].astype(F32))
        normed = (unit * gcol[0]).astype(BF16)
        n1[hb] = normed
        k_t[hb] = turned(mm(weights[1], normed, TN), hb, 1.0)
        v_t[hb] = mm(weights[2], normed, TN).astype(BF16)

    def both_halves(block):
        def one(i, carry):
            keys_values(2 * block + i)
            return carry

        lax.fori_loop(0, 2, one, 0)

    both_halves(z)
    for n, block in enumerate((zo, 2 - g, 3 - 3 * g)):
        p_wait(2 * block + c)
        if n > 0:
            go(p_copy(p_all.at[2 * block + c], 2 * block + c, 6 + n, dev(c, zo), is_near))
        go(p_copy(p_all.at[2 * block + c], 2 * block + c, 4 + n, sib))
        p_wait(2 * block + 1 - c)
        both_halves(block)

    hq_of = (w, 7 - w)

    def hq_at(slot):
        return jnp.where(slot == 0, w, 7 - w)

    for slot in range(2):
        q_t[slot] = turned(mm(weights[0], n1[hq_of[slot]], TN), hq_of[slot], 1.0)
    score_scale = HEAD_DIM ** (-0.5) * LOG2E

    def bias_of(hq, kb):
        b = lax.div(kb, 2)
        j = (iota((half, half), 0) + lax.rem(kb, 2) * half).astype(F32)
        kpos = j + pick(offsets[:nblk], b)
        alive = j < pick(counts, b)
        qpos = pos[hq, 0:1, :]
        qfirst = pos[hq, 1:2, :]
        allowed = jnp.logical_and(alive, jnp.logical_and(kpos <= qpos, kpos >= qfirst))
        return jnp.where(allowed, 0.0, NEGATIVE)

    o_acc[...] = jnp.zeros_like(o_acc)
    l_sc[...] = jnp.zeros_like(l_sc)
    m_sc[...] = jnp.full(m_sc.shape, NEGATIVE, F32)

    def forward_step(t, carry):
        low_half = t <= w
        slot = jnp.where(low_half, 0, 1)
        kb = jnp.where(low_half, t, t - w - 1)
        hq = hq_at(slot)
        bias = bias_of(hq, kb)
        for h in range(HEADS):
            part = slice(64 * h, 64 * h + 64)
            s = mm(k_t[kb, part, :], q_t[slot, part, :], TN) * score_scale + bias
            old = m_sc[slot, h : h + 1, :]
            new = jnp.maximum(old, jnp.max(s, axis=0, keepdims=True))
            prob = jnp.exp2(s - new)
            shrink = jnp.exp2(old - new)
            l_sc[slot, h : h + 1, :] = l_sc[slot, h : h + 1, :] * shrink + jnp.sum(
                prob, axis=0, keepdims=True
            )
            m_sc[slot, h : h + 1, :] = new
            o_acc[slot, part, :] = o_acc[slot, part, :] * shrink + mm(
                v_t[kb, part, :], prob.astype(BF16), NN
            )
        return carry

    lax.fori_loop(0, 9, forward_step, 0)

    for slot in range(2):
        total = l_sc[slot]
        for h in range(HEADS):
            part = slice(64 * h, 64 * h + 64)
            o_acc[slot, part, :] = o_acc[slot, part, :] * (1.0 / total[h : h + 1, :])
        att[:, slot * half : (slot + 1) * half] = o_acc[slot].astype(BF16)
        m_sc[slot] = m_sc[slot] + jnp.log2(total)

    own_pooled = jnp.concatenate([p_all[hq_of[0]], p_all[hq_of[1]]], axis=1).astype(F32)
    middle = own_pooled + mm(weights[3], att[...], TN)
    unit2, inverse2 = norm_parts(middle)
    hat2[...] = unit2
    gain_col2 = jnp.concatenate([gcol[1], gcol[1]], axis=1)
    n2 = (unit2 * gain_col2).astype(BF16)
    big[0] = middle
    big[1] = jnp.zeros((feat, feat), F32)
    Copy(cot_w.at[0], cot_w.at[0], ss.at[0], rs.at[r_cot], sib, jnp.logical_not(lo_here)).wait_recv()
    Copy(cot_w.at[1], cot_w.at[1], ss.at[0], rs.at[r_cot + 1], sib, jnp.logical_not(hi_here)).wait_recv()
    gb[...] = jnp.concatenate([cot_w[0], cot_w[1]], axis=1)
    n2_ref = d_o
    n2_ref[...] = n2

    base1 = c * 256
    keep2x, give2x = base1 + x * 128, base1 + (1 - x) * 128
    keep2y, give2y = base1 + y * 128, base1 + (1 - y) * 128
    keep3x, give3x = keep2x + y * 64, keep2x + (1 - y) * 64
    keep3y, give3y = keep2y + x * 64, keep2y + (1 - x) * 64
    lanes_x, lanes_y = pl.ds(0, 256), pl.ds(256, 256)

    def rows_of(first, n):
        return pl.ds(pl.multiple_of(first, 16), n)

    class Reduce:
        def __init__(self, chunk):
            self.b0, self.b1 = CHUNKS[chunk]
            self.nb = self.b1 - self.b0
            self.s0, self.r0 = ids("s", SEMS_AR), ids("r", SEMS_AR)
            self.blocks = pl.ds(self.b0, self.nb)
            self.phases = {}

        def _w(self, first, n, lanes):
            return wg.at[self.blocks, rows_of(first, n), lanes]

        def _list(self, phase):
            every = pl.ds(0, 512)
            b, s0, r0 = self.blocks, self.s0, self.r0

            def copy(i, src, dst, device):
                return Copy(src, dst, ss.at[s0 + i], rs.at[r0 + i], device)

            if phase == 1:
                return [copy(0, self._w((1 - c) * 256, 256, every), r1.at[b], sib)]
            if phase == 2:
                return [
                    copy(1, self._w(give2x, 128, lanes_x), r2.at[b, :, lanes_x], xnb),
                    copy(2, self._w(give2y, 128, lanes_y), r2.at[b, :, lanes_y], ynb),
                ]
            if phase == 3:
                return [
                    copy(3, self._w(give3x, 64, lanes_x), r3.at[b, :, lanes_x], ynb),
                    copy(4, self._w(give3y, 64, lanes_y), r3.at[b, :, lanes_y], xnb),
                ]
            if phase == 4:
                out = []
                for k in range(1, 4):
                    zt = lax.rem(z + k, nblk)
                    out.append(
                        copy(
                            3 + 2 * k,
                            self._w(keep3x + 16 * zt, 16, lanes_x),
                            r4.at[k - 1, b, :, lanes_x],
                            (dp, zt),
                        )
                    )
                    out.append(
                        copy(
                            4 + 2 * k,
                            self._w(keep3y + 16 * zt, 16, lanes_y),
                            r4.at[k - 1, b, :, lanes_y],
                            (dp, zt),
                        )
                    )
                return out
            if phase == 5:
                out = []
                for k in range(1, 4):
                    zt = lax.rem(z + k, nblk)
                    for i, (keep, lanes) in enumerate(((keep3x, lanes_x), (keep3y, lanes_y))):
                        mine = self._f(keep + 16 * z, 16, lanes)
                        out.append(copy(9 + 2 * k + i, mine, mine, (dp, zt)))
                return out
            if phase == 6:
                mine_x, mine_y = self._f(keep3x, 64, lanes_x), self._f(keep3y, 64, lanes_y)
                return [copy(17, mine_x, mine_x, ynb), copy(18, mine_y, mine_y, xnb)]
            if phase == 7:
                mine_x, mine_y = self._f(keep2x, 128, lanes_x), self._f(keep2y, 128, lanes_y)
                return [copy(19, mine_x, mine_x, xnb), copy(20, mine_y, mine_y, ynb)]
            return [copy(21, r1.at[b], self._out(base1), sib)]

        def _f(self, first, n, lanes):
            return r1.at[self.blocks, rows_of(first - base1, n), lanes]

        def _out(self, first):
            return wgrad_hbm.at[self.blocks, rows_of(first, 256), pl.ds(0, 512)]

        def start(self, phase):
            for one in self._list(phase):
                one.start()

        def finish(self, phase):
            if phase == 8:
                other = self._out((1 - c) * 256)
                Copy(other, other, ss.at[0], rs.at[self.r0 + 21], sib).wait_recv()
                return
            for one in self._list(phase):
                one.wait_recv()
            if phase > 4:
                return

            def add(i, carry):
                b = self.b0 + i
                if phase == 1:
                    here = (b, rows_of(base1, 256), slice(None))
                    wg[here] = wg[here] + r1[b]
                if phase == 2:
                    for keep, lo in ((keep2x, 0), (keep2y, 256)):
                        here = (b, rows_of(keep, 128), slice(lo, lo + 256))
                        wg[here] = wg[here] + r2[b, :, lo : lo + 256]
                if phase == 3:
                    for keep, lo in ((keep3x, 0), (keep3y, 256)):
                        here = (b, rows_of(keep, 64), slice(lo, lo + 256))
                        wg[here] = wg[here] + r3[b, :, lo : lo + 256]
                if phase == 4:
                    for keep, lo in ((keep3x, 0), (keep3y, 256)):
                        here = (b, rows_of(keep + 16 * z, 16), slice(lo, lo + 256))
                        total = wg[here].astype(F32)
                        for k in range(3):
                            total = total + r4[k, b, :, lo : lo + 256].astype(F32)
                        r1[b, rows_of(keep - base1 + 16 * z, 16), lo : lo + 256] = total.astype(BF16)
                return carry

            lax.fori_loop(0, self.nb, add, 0)

        def step(self, phase):
            self.finish(phase)
            if phase < 8:
                self.start(phase + 1)
            if phase == 7:
                self.store().start()

        def store(self):
            return pltpu.make_async_copy(r1.at[self.blocks], self._out(base1), ls.at[self.store_sem])

        def wait_sends(self):
            for phase in range(1, 9):
                for one in self._list(phase):
                    one.wait_send()

    red = [Reduce(i) for i in range(3)]
    for one in red:
        one.store_sem = ids("l", 1)

    for d in loads_f:
        d.wait()

    def ffn_chunk(j, carry):
        up = mm(wup[j], n2_ref[...], TN)
        size = jnp.abs(up) * (0.5**0.5)
        t = 1.0 / (1.0 + 0.3275911 * size)
        poly = t * (
            0.254829592
            + t * (-0.284496736 + t * (1.421413741 + t * (-1.453152027 + t * 1.061405429)))
        )
        decay = jnp.exp(-0.5 * up * up)
        far = 0.5 * poly * decay
        phi = jnp.where(up < 0.0, far, 1.0 - far)
        slope = phi + up * decay * (1.0 / math.sqrt(2.0 * math.pi))
        act = (up * phi).astype(BF16)
        wg[2 * j] = mm(act, gb[...], NT).astype(BF16)
        big[0] += mm(wdn[j], act, TN)
        grad_up = (mm(wdn[j], gb[...], NN) * slope).astype(BF16)
        wg[2 * j + 1] = mm(n2_ref[...], grad_up, NT).astype(BF16)
        big[1] += mm(wup[j], grad_up, NN)

        @pl.when(j == 1)
        def _():
            red[0].start(1)

        return carry

    lax.fori_loop(0, 4, ffn_chunk, 0)
    red[0].step(1)

    s_out, r_out = ids("s", 2), ids("r", 2)
    res = big[0].astype(BF16)
    owners = ((zl, c, lo_here), (3 - zl, 1 - c, hi_here))
    for slot, (chip, i, here) in enumerate(owners):
        out_s[slot] = res[:, slot * half : (slot + 1) * half]
        go(
            Copy(
                out_s.at[slot],
                out_r.at[i],
                ss.at[s_out + slot],
                rs.at[r_out + i],
                dev(g, chip),
                jnp.logical_not(here),
            )
        )

        @pl.when(here)
        def _():
            out_r[i] = out_s[slot]

    grad_n2 = big[1]
    unit2 = hat2[...]
    product = grad_n2 * unit2

    def lane_fold(values):
        total = values[:, 0:128]
        for k in range(1, values.shape[1] // 128):
            total = total + values[:, 128 * k : 128 * (k + 1)]
        return total

    gain_acc[1] = lane_fold(product)
    e = grad_n2 * gain_col2
    grad_mid = gb[...].astype(F32) + inverse2 * (
        e
        - jnp.mean(e, axis=0, keepdims=True)
        - unit2 * jnp.mean(e * unit2, axis=0, keepdims=True)
    )
    gmid[0] = grad_mid[:, 0:half]
    gmid[1] = grad_mid[:, half:]
    branch = grad_mid.astype(BF16)
    wg[8] = mm(att[...], branch, NT).astype(BF16)
    red[1].start(1)
    grad_att = mm(weights[3], branch, NN)
    d_o[...] = grad_att.astype(BF16)
    for slot in range(2):
        lanes = slice(slot * half, (slot + 1) * half)
        both = d_o[:, lanes].astype(F32) * o_acc[slot]
        for h in range(HEADS):
            d_sc[slot, h : h + 1, :] = jnp.sum(
                both[64 * h : 64 * h + 64, :], axis=0, keepdims=True
            )

    dq[...] = jnp.zeros_like(dq)
    gwqkv[...] = jnp.zeros_like(gwqkv)
    gain_acc[0] = jnp.zeros((feat, 128), F32)
    s_rc, r_rc = ids("s", 4), ids("r", 4)
    s_rz, r_rz = ids("s", 4), ids("r", 4)
    s_fin, r_fin = ids("s", 4), ids("r", 2)

    def backward_step(slot, kb):
        hq = hq_at(slot)
        bias = bias_of(hq, kb)
        lanes = pl.ds(pl.multiple_of(slot * half, half), half)
        for h in range(HEADS):
            part = slice(64 * h, 64 * h + 64)
            key = k_t[kb, part, :]
            query = q_t[slot, part, :]
            grad_o = d_o[part, lanes]
            s = mm(key, query, TN) * score_scale + bias
            prob = jnp.exp2(s - m_sc[slot, h : h + 1, :])
            grad_prob = mm(v_t[kb, part, :], grad_o, TN)
            grad_s = (prob * (grad_prob - d_sc[slot, h : h + 1, :])).astype(BF16)
            dv[part, :] += mm(grad_o, prob.astype(BF16), NT)
            dk[part, :] += mm(query, grad_s, NT)
            dq[slot, part, :] += mm(key, grad_s, NN)

    att_scale = HEAD_DIM ** (-0.5)

    def rc_copy(kb):
        zb = lax.div(kb, 2)
        return Copy(
            ppart.at[kb],
            rc.at[zb],
            ss.at[s_rc + zb],
            rs.at[r_rc + zb],
            sib,
            lax.rem(kb, 2) != c,
        )

    def is_final(zb):
        return jnp.where(lax.div(zb, 2) == g, z == zb, is_near)

    def rz_copy(zb):
        return Copy(
            ppart.at[2 * zb + c],
            rz.at[zb],
            ss.at[s_rz + zb],
            rs.at[r_rz + zb],
            dev(c, zo),
            jnp.logical_not(is_final(zb)),
        )

    def fin_copy(zb):
        here = jnp.logical_and(zb == z, g == c)
        return Copy(
            ppart.at[2 * zb + c],
            gfin.at[c],
            ss.at[s_fin + zb],
            rs.at[r_fin + c],
            dev(g, zb),
            jnp.logical_and(is_final(zb), jnp.logical_not(here)),
        )

    def combine(zb):
        kb = 2 * zb + c
        Copy(rc.at[zb], rc.at[zb], ss.at[0], rs.at[r_rc + zb], sib).wait_recv()
        ppart[kb] = ppart[kb] + rc[zb]
        rz_copy(zb).start()

    def deliver(zb):
        kb = 2 * zb + c
        final = is_final(zb)
        Copy(rz.at[zb], rz.at[zb], ss.at[0], rs.at[r_rz + zb], sib, final).wait_recv()

        @pl.when(final)
        def _():
            ppart[kb] = ppart[kb] + rz[zb]

        @pl.when(jnp.logical_and(zb == z, g == c))
        def _():
            gfin[c] = ppart[kb]

        fin_copy(zb).start()

    schedule = {
        0: [(0, 2), (1, 1)],
        1: [(0, 3)],
        2: [(1, 2)],
        3: [(0, 4), (1, 3)],
        4: [(0, 5)],
        5: [(0, 6), (1, 4)],
        6: [],
        7: [(0, 7), (1, 5)],
    }

    def key_block(kb, carry):
        @pl.when(kb <= 7 - w)
        def _():
            dk[...] = jnp.zeros_like(dk)
            dv[...] = jnp.zeros_like(dv)

            def one(i, carry):
                slot = 1 - i
                backward_step(slot, kb)
                return carry

            lax.fori_loop(0, jnp.where(kb <= w, 2, 1), one, 0)
            grad_key = turned(dk[...] * att_scale, kb, -1.0)
            grad_value = dv[...].astype(BF16)
            normed = n1[kb]
            gwqkv[1] += mm(normed, grad_key, NT)
            gwqkv[2] += mm(normed, grad_value, NT)
            big[0, :, 0:half] = mm(weights[1], grad_key, NN) + mm(weights[2], grad_value, NN)

            @pl.when(jnp.logical_or(kb == w, kb == 7 - w))
            def _():
                slot = jnp.where(kb == w, 0, 1)
                grad_query = turned(dq[slot] * att_scale, kb, -1.0)
                gwqkv[0] += mm(normed, grad_query, NT)
                big[0, :, 0:half] += mm(weights[0], grad_query, NN)

            grad_n1 = big[0, :, 0:half]
            unit, inverse = norm_parts(p_all[kb].astype(F32))
            gain_acc[0] += lane_fold(grad_n1 * unit)
            e = grad_n1 * gcol[0]
            big[0, :, 0:half] = inverse * (
                e
                - jnp.mean(e, axis=0, keepdims=True)
                - unit * jnp.mean(e * unit, axis=0, keepdims=True)
            )

            @pl.when(jnp.logical_or(kb == w, kb == 7 - w))
            def _():
                slot = jnp.where(kb == w, 0, 1)
                big[0, :, 0:half] += gmid[slot]

            ppart[kb] = big[0, :, 0:half].astype(BF16)

        @pl.when(kb > 7 - w)
        def _():
            ppart[kb] = jnp.zeros(ppart.shape[1:], BF16)

        rc_copy(kb).start()

        @pl.when(lax.rem(kb, 2) == 1)
        def _():
            combine(lax.div(kb, 2))

        @pl.when(jnp.logical_and(lax.rem(kb, 2) == 1, kb > 1))
        def _():
            deliver(lax.div(kb, 2) - 1)

        for i, todo in schedule.items():
            if todo:

                @pl.when(kb == i)
                def _():
                    for chunk, phase in todo:
                        red[chunk].step(phase)

        return carry

    lax.fori_loop(0, 8, key_block, 0)

    for i in range(3):
        wg[9 + i] = gwqkv[i].astype(BF16)
    red[2].start(1)
    for i in range(2):
        gain_s[0, i : i + 1, :] = jnp.sum(gain_acc[i].T, axis=0, keepdims=True)
    gain_s[0, 2:8, :] = jnp.zeros((6, feat), F32)
    s_gain, r_gain = ids("s", 6), ids("r", 6)

    def gain_list(phase):
        if phase < 4:
            device = (sib, xnb, ynb)[phase - 1]
            k = phase - 1
            return [
                Copy(gain_s.at[k], gain_r.at[k], ss.at[s_gain + k], rs.at[r_gain + k], device)
            ]
        return [
            Copy(
                gain_s.at[3],
                gain_r.at[2 + k],
                ss.at[s_gain + 2 + k],
                rs.at[r_gain + 2 + k],
                (dp, lax.rem(z + k, nblk)),
            )
            for k in range(1, 4)
        ]

    def gain_finish(phase):
        for one in gain_list(phase):
            one.wait_recv()
        if phase < 4:
            gain_s[phase] = gain_s[phase - 1] + gain_r[phase - 1]
            for one in gain_list(phase + 1):
                one.start()
        else:
            total = jnp.zeros((8, feat), F32)
            for zz in range(nblk):
                k = lax.rem(z - zz + nblk, nblk)
                part = gain_s[3]
                for i in range(1, 4):
                    part = jnp.where(k == i, gain_r[2 + i], part)
                total = total + part
            ggain_ref[...] = total

    gain_list(1)[0].start()
    deliver(3)
    red[0].step(8)
    red[1].step(6)
    red[2].step(1)
    gain_finish(1)

    for i in range(2):
        mine = out_from_self(i, c, z)
        Copy(
            out_r.at[i], out_r.at[i], ss.at[0], rs.at[r_out + i], sib, jnp.logical_not(mine)
        ).wait_recv()
        live = rdiv[1:2, i * half : (i + 1) * half]
        out_ref[i * half : (i + 1) * half, :] = (out_r[i].astype(F32) * live).T

    red[1].step(7)
    red[2].step(2)
    gain_finish(2)

    for i in range(2):
        mine = jnp.logical_and(own_worker, c == i)
        Copy(
            gfin.at[i], gfin.at[i], ss.at[0], rs.at[r_fin + i], sib, jnp.logical_not(mine)
        ).wait_recv()
        grad_sums = gfin[i].astype(F32) * rdiv[0:1, i * half : (i + 1) * half]
        gs_ref[i * half : (i + 1) * half, :] = grad_sums.T.astype(BF16)

    is_last = jnp.where(iota((16, feat), 1).astype(F32) == cnt - 1.0, 1.0, 0.0).astype(BF16)
    last_s[...] = mm(is_last, gs_ref[...], NN).astype(BF16)
    s_last, r_last = ids("s", 1), ids("r", 1)
    copy_last = Copy(
        last_s,
        last_r,
        ss.at[s_last],
        rs.at[r_last],
        (dp, lax.rem(z + 1, nblk)),
        z < nblk - 1,
    )
    go(copy_last)

    red[2].step(3)
    gain_finish(3)
    red[1].step(8)
    red[2].step(4)
    gain_finish(4)
    Copy(last_r, last_r, ss.at[0], rs.at[r_last], sib, z > 0).wait_recv()

    @pl.when(z == 0)
    def _():
        last_r[...] = jnp.zeros_like(last_r)

    came_ref[...] = last_r[...]
    for phase in range(5, 9):
        red[2].step(phase)

    for one in sends:
        one.wait_send()

    def close_key(kb, carry):
        rc_copy(kb).wait_send()
        return carry

    lax.fori_loop(0, 8, close_key, 0)

    def close_block(zb, carry):
        rz_copy(zb).wait_send()
        fin_copy(zb).wait_send()
        return carry

    lax.fori_loop(0, 4, close_block, 0)
    for phase in range(1, 5):
        for one in gain_list(phase):
            one.wait_send()
    for one in red:
        one.wait_sends()
        one.store().wait()


def out_from_self(i, c, z):
    chip = 2 * c + jnp.where(z < 2, z, 3 - z)
    core = jnp.where(z < 2, i, 1 - i)
    return jnp.logical_and(core == c, chip == z)


def expand_kernel(
    slots_ref, gs_ref, came_ref, dn_ref, up0, up1, up2, up3, wo_ref, wq_ref, wk_ref, wv_ref,
    bytes_out, dn_out, up_out, wo_out, wq_out, wk_out, wv_out,
):
    rows = slots_ref[0]
    slot_iota = iota((512, 128), 0).astype(F32)
    member = jnp.concatenate(
        [(slot_iota == rows[r : r + 1, :]).astype(F32).astype(BF16) for r in range(4)], axis=1
    )
    first = iota((16, 128), 0) == 0
    lead = jnp.concatenate(
        [
            jnp.where(jnp.logical_and(first, rows[r : r + 1, :] < -0.5), 1.0, 0.0).astype(BF16)
            for r in range(4)
        ],
        axis=1,
    )
    bytes_out[...] = mm(member, gs_ref[...], TN) + mm(lead, came_ref[...], TN)
    dn_out[...] = dn_ref[0].astype(F32)
    for j, up in enumerate((up0, up1, up2, up3)):
        up_out[:, 512 * j : 512 * (j + 1)] = up[0].astype(F32)
    for src, dst in ((wo_ref, wo_out), (wq_ref, wq_out), (wk_ref, wk_out), (wv_ref, wv_out)):
        dst[...] = src[0].astype(F32)


def fast_local(
    bytes_in, flags, lengths, cotangent, w_query, w_key, w_value, w_out, w_up, w_down, gain_attn, gain_ffn
):
    meta_flags = flags.reshape(32, 128)
    meta_lengths = jnp.pad(lengths, ((0, 7), (0, 124)))
    gains = jnp.stack([gain_attn, gain_ffn])
    freqs = ROTARY_BASE ** (-2.0 * jnp.arange(32, dtype=jnp.float32) / 64)
    freq = jnp.broadcast_to(freqs[:, None], (32, 128))
    vm = pl.BlockSpec(memory_space=pltpu.VMEM)
    hbm = pl.BlockSpec(memory_space=pl.ANY)
    hb = lambda n: pltpu.VMEM((n, 512, 256), BF16)
    hbf = lambda n: pltpu.VMEM((n, 512, 256), F32)
    sq = lambda n, t: pltpu.VMEM((n, 512, 512), t)
    scratch = dict(
        bytes_v=sq(8, BF16),
        weights=sq(4, BF16),
        wup=sq(4, BF16),
        wdn=sq(4, BF16),
        meta=pltpu.VMEM((2, 4, 40, 128), jnp.int32),
        tail=pltpu.VMEM((16, 512), BF16),
        slot_sc=pltpu.VMEM((8, 4, 128), F32),
        p_own=hb(2),
        relay=pltpu.VMEM((512, 256), BF16),
        p_all=hb(8),
        n1=hb(8),
        k_t=hb(8),
        v_t=hb(8),
        q_t=hb(2),
        tab_c=pltpu.VMEM((8, 32, 256), F32),
        tab_s=pltpu.VMEM((8, 32, 256), F32),
        pos=pltpu.VMEM((8, 8, 256), F32),
        gcol=hbf(2),
        cot_own=hb(2),
        cot_w=hb(2),
        o_acc=hbf(2),
        m_sc=pltpu.VMEM((2, 8, 256), F32),
        l_sc=pltpu.VMEM((2, 8, 256), F32),
        att=pltpu.VMEM((512, 512), BF16),
        gb=pltpu.VMEM((512, 512), BF16),
        hat2=pltpu.VMEM((512, 512), F32),
        d_o=pltpu.VMEM((512, 512), BF16),
        d_sc=pltpu.VMEM((2, 8, 256), F32),
        gmid=hbf(2),
        dk=pltpu.VMEM((512, 256), F32),
        dv=pltpu.VMEM((512, 256), F32),
        dq=hbf(2),
        gwqkv=sq(3, F32),
        big=sq(2, F32),
        wg=sq(12, BF16),
        r1=pltpu.VMEM((12, 256, 512), BF16),
        r2=pltpu.VMEM((12, 128, 512), BF16),
        r3=pltpu.VMEM((12, 64, 512), BF16),
        r4=pltpu.VMEM((3, 12, 16, 512), BF16),
        ppart=hb(8),
        rc=hb(4),
        rz=hb(4),
        gfin=hb(2),
        out_s=hb(2),
        out_r=hb(2),
        rdiv=pltpu.VMEM((16, 512), F32),
        last_s=pltpu.VMEM((16, 512), BF16),
        last_r=pltpu.VMEM((16, 512), BF16),
        gain_acc=pltpu.VMEM((2, 512, 128), F32),
        gain_s=pltpu.VMEM((4, 8, 512), F32),
        gain_r=pltpu.VMEM((6, 8, 512), F32),
        ss=pltpu.SemaphoreType.DMA((128,)),
        rs=pltpu.SemaphoreType.DMA((128,)),
        ls=pltpu.SemaphoreType.DMA((32,)),
    )
    out, gs, came, slots, wgrad, ggain = pl.pallas_call(
        layer_kernel,
        out_shape=(
            jax.ShapeDtypeStruct((512, 512), F32),
            jax.ShapeDtypeStruct((512, 512), BF16),
            jax.ShapeDtypeStruct((16, 512), BF16),
            jax.ShapeDtypeStruct((32, 128), F32),
            jax.ShapeDtypeStruct((12, 512, 512), BF16),
            jax.ShapeDtypeStruct((8, 512), F32),
        ),
        in_specs=[hbm, vm, vm, hbm, hbm, hbm, hbm, hbm, hbm, hbm, vm, vm],
        out_specs=(vm, vm, vm, vm, hbm, vm),
        scratch_shapes=list(scratch.values()),
        compiler_params=pltpu.CompilerParams(
            collective_id=0, has_side_effects=True, vmem_limit_bytes=60 * 2**20
        ),
        name="layer",
    )(
        bytes_in, meta_flags, meta_lengths, cotangent, w_query, w_key, w_value, w_out, w_up, w_down,
        gains, freq,
    )
    block = lambda rows, cols, index: pl.BlockSpec((1, rows, cols), index)
    ups = [block(64, 512, functools.partial(lambda j, i: (2 * j + 1, i, 0), j)) for j in range(4)]
    rest = [block(64, 512, functools.partial(lambda j, i: (j, i, 0), j)) for j in range(8, 12)]
    whole = lambda shape: pl.BlockSpec(shape, lambda i: (0, 0))
    flat = lambda rows, cols: pl.BlockSpec((rows, cols), lambda i: (i, 0))
    grad_bytes, dn, up, wo, wq, wk, wv = pl.pallas_call(
        expand_kernel,
        grid=(8,),
        out_shape=(
            jax.ShapeDtypeStruct((4096, 512), F32),
            jax.ShapeDtypeStruct((2048, 512), F32),
            jax.ShapeDtypeStruct((512, 2048), F32),
        )
        + (jax.ShapeDtypeStruct((512, 512), F32),) * 4,
        in_specs=[
            block(4, 128, lambda i: (i, 0, 0)),
            whole((512, 512)),
            whole((16, 512)),
            block(256, 512, lambda i: (2 * lax.div(i, 2), lax.rem(i, 2), 0)),
        ]
        + ups
        + rest,
        out_specs=(flat(512, 512), flat(256, 512), flat(64, 2048)) + (flat(64, 512),) * 4,
        compiler_params=pltpu.CompilerParams(vmem_limit_bytes=40 * 2**20),
        name="expand",
    )(slots.reshape(8, 4, 128), gs, came, wgrad, wgrad, wgrad, wgrad, wgrad, wgrad, wgrad, wgrad, wgrad)
    return out, grad_bytes, wq, wk, wv, wo, up, dn, ggain[0], ggain[1]


def passed_along(block, axis, distance):
    devices = range(lax.axis_size(axis))
    route = [((i - distance) % len(devices), i) for i in devices]
    return lax.ppermute(block, axis, route)


def from_behind(value, axis, by):
    count = lax.axis_size(axis)
    pairs = [(i, i + by) for i in range(count) if 0 <= i + by < count]
    return lax.ppermute(value, axis, pairs)


def rotate(vectors, positions, direction):
    half_dim = vectors.shape[-1] // 2
    freqs = ROTARY_BASE ** (-2.0 * jnp.arange(half_dim, dtype=jnp.float32) / vectors.shape[-1])
    angles = positions.astype(jnp.float32)[:, None] * freqs[None, :]
    cosine = jnp.cos(angles)[:, None, :]
    sine = direction * jnp.sin(angles)[:, None, :]
    first_half = vectors[..., :half_dim]
    second_half = vectors[..., half_dim:]
    return jnp.concatenate(
        [first_half * cosine - second_half * sine, second_half * cosine + first_half * sine],
        axis=-1,
    )


def layer_norm_parts(values, gain):
    center = values - jnp.mean(values, axis=-1, keepdims=True)
    spread = jnp.mean(center * center, axis=-1, keepdims=True)
    inverse = lax.rsqrt(spread + EPSILON)
    normed = center * inverse
    return (normed * gain, normed, inverse)


def layer_norm_back(grad_in, normed, inverse, gain):
    scaled = grad_in * gain
    grad_values = inverse * (
        scaled
        - jnp.mean(scaled, axis=-1, keepdims=True)
        - normed * jnp.mean(scaled * normed, axis=-1, keepdims=True)
    )
    grad_gain = jnp.sum(grad_in * normed, axis=0)
    return (grad_values, grad_gain)


def pass_grads(grad_key, grad_value):
    return (
        passed_along(grad_key.astype(jnp.bfloat16), "blk", 1).astype(grad_key.dtype),
        passed_along(grad_value.astype(jnp.bfloat16), "blk", 1).astype(grad_value.dtype),
    )


def local(
    bytes_in,
    flags,
    lengths,
    cotangent,
    w_query,
    w_key,
    w_value,
    w_out,
    w_up,
    w_down,
    gain_attn,
    gain_ffn,
):
    blocks = lax.axis_size("blk")
    own_index = lax.axis_index("blk")
    seg_rows = cotangent.shape[0]
    byte_rows = bytes_in.shape[0]
    features = bytes_in.shape[1]
    scale = HEAD_DIM ** (-0.5)
    running = jnp.cumsum(flags)
    slot_of = running - 1
    seg_count = running[-1]
    slot_ids = jnp.arange(seg_rows, dtype=jnp.int32)
    member = (slot_of[None, :] == slot_ids[:, None]).astype(jnp.bfloat16)
    seg_sums = jnp.dot(member, bytes_in, preferred_element_type=jnp.float32)
    seg_tally = jnp.sum(member, axis=1, dtype=jnp.float32)
    leading = slot_of < 0
    tail_sum = jnp.dot(
        leading.astype(jnp.bfloat16)[None, :], bytes_in, preferred_element_type=jnp.float32
    )
    tail_count = jnp.sum(leading.astype(jnp.float32), keepdims=True)
    got_sum, got_count = from_behind((tail_sum, tail_count), "blk", -1)
    last_slot = slot_ids == seg_count - 1
    seg_sums = seg_sums + jnp.where(last_slot[:, None], got_sum, 0.0)
    seg_tally = seg_tally + jnp.where(last_slot, got_count[0], 0.0)
    divisor = jnp.maximum(seg_tally, 1.0)
    pooled = seg_sums / divisor[:, None]
    starts = jnp.cumsum(lengths[0]) - lengths[0]
    byte_at = own_index * byte_rows + jnp.arange(byte_rows, dtype=jnp.int32)
    prior_flags = jnp.sum(
        flags[None, :] * (byte_at[None, :] < starts[:, None]).astype(jnp.int32), axis=1
    )
    all_counts, all_prior = (
        lax.all_gather(seg_count[None], "blk", axis=0, tiled=True),
        lax.all_gather(prior_flags[None, :], "blk", axis=0, tiled=True),
    )
    offsets = jnp.cumsum(all_counts) - all_counts
    seq_first = jnp.sum(all_prior, axis=0)
    dev_ids = jnp.arange(blocks, dtype=jnp.int32)

    def layout(first_row, row_count):
        row_index = first_row + jnp.arange(row_count, dtype=jnp.int32)
        owner_dev = row_index // seg_rows
        within = row_index % seg_rows
        dev_pick = owner_dev[:, None] == dev_ids[None, :]
        dev_base = jnp.sum(jnp.where(dev_pick, offsets[None, :], 0), axis=1)
        dev_have = jnp.sum(jnp.where(dev_pick, all_counts[None, :], 0), axis=1)
        return (dev_base + jnp.minimum(within, dev_have - 1), within < dev_have)

    query_pos, query_live = layout(own_index * seg_rows, seg_rows)
    query_first = jnp.max(
        jnp.where(seq_first[None, :] <= query_pos[:, None], seq_first[None, :], 0), axis=1
    )

    def visible(first_row, row_count):
        key_pos, key_live = layout(first_row, row_count)
        return (
            (key_pos[None, :] <= query_pos[:, None])
            & (key_pos[None, :] >= query_first[:, None])
            & key_live[None, :]
        )

    normed_attn, unit_attn, scale_attn = layer_norm_parts(pooled, gain_attn)
    n_one = normed_attn.astype(jnp.bfloat16)
    query_pre = jnp.dot(n_one, w_query, preferred_element_type=jnp.float32)
    query_rot = rotate(query_pre.reshape(seg_rows, HEADS, HEAD_DIM), query_pos, 1.0).astype(
        jnp.bfloat16
    )
    key_pre = jnp.dot(n_one, w_key, preferred_element_type=jnp.float32)
    key_rot = (
        rotate(key_pre.reshape(seg_rows, HEADS, HEAD_DIM), query_pos, 1.0)
        .reshape(seg_rows, features)
        .astype(jnp.bfloat16)
    )
    value_low = jnp.dot(n_one, w_value, preferred_element_type=jnp.float32).astype(jnp.bfloat16)
    start_state = (
        jnp.full((HEADS, seg_rows), NEGATIVE, jnp.float32),
        jnp.zeros((HEADS, seg_rows), jnp.float32),
        jnp.zeros((seg_rows, HEADS, HEAD_DIM), jnp.float32),
    )
    key_piece = lax.all_gather(key_rot, "blk", axis=0, tiled=True)
    value_piece = lax.all_gather(value_low, "blk", axis=0, tiled=True)
    row_count = key_piece.shape[0]
    allowed = visible(jnp.int32(0), row_count)

    def absorb_update(running_state):
        row_max, row_sum, weighted = running_state
        scores = (
            jnp.einsum(
                "qhe,khe->hqk",
                query_rot,
                key_piece.reshape(row_count, HEADS, HEAD_DIM),
                preferred_element_type=jnp.float32,
            )
            * scale
        )
        scores = jnp.where(allowed[None], scores, NEGATIVE)
        new_max = jnp.maximum(row_max, jnp.max(scores, axis=-1))
        weights = jnp.where(allowed[None], jnp.exp(scores - new_max[:, :, None]), 0.0)
        shrink = jnp.exp(row_max - new_max)
        row_sum = jnp.sum(weights, axis=-1)
        weighted = weighted * shrink.T[:, :, None] + jnp.einsum(
            "hqk,khe->qhe",
            weights.astype(jnp.bfloat16),
            value_piece.reshape(row_count, HEADS, HEAD_DIM),
            preferred_element_type=jnp.float32,
        )
        return (new_max, row_sum, weighted)

    row_max, row_sum, weighted = lax.cond(
        jnp.any(allowed), absorb_update, lambda unchanged: unchanged, start_state
    )
    log_total = row_max + jnp.log(row_sum)
    attended_full = weighted / row_sum.T[:, :, None]
    attended = attended_full.reshape(seg_rows, features).astype(jnp.bfloat16)
    middle = pooled + jnp.dot(attended, w_out, preferred_element_type=jnp.float32)
    normed_ffn, unit_ffn, scale_ffn = layer_norm_parts(middle, gain_ffn)
    n_two = normed_ffn.astype(jnp.bfloat16)
    up_proj = jnp.dot(n_two, w_up, preferred_element_type=jnp.float32)
    act_full, gelu_back = jax.vjp(lambda inner: jax.nn.gelu(inner, approximate=False), up_proj)
    act_low = act_full.astype(jnp.bfloat16)
    result = middle + jnp.dot(act_low, w_down, preferred_element_type=jnp.float32)
    live_rows = query_live.astype(jnp.float32)[:, None]
    output = result * live_rows
    grad_out = cotangent * live_rows
    grad_branch = grad_out.astype(jnp.bfloat16)
    grad_w_down = jnp.einsum("sf,sd->fd", act_low, grad_branch, preferred_element_type=jnp.float32)
    grad_act = jnp.einsum("sd,fd->sf", grad_branch, w_down, preferred_element_type=jnp.float32)
    grad_up = gelu_back(grad_act)[0].astype(jnp.bfloat16)
    grad_w_up = jnp.einsum("sd,sf->df", n_two, grad_up, preferred_element_type=jnp.float32)
    grad_n_two = jnp.einsum("sf,df->sd", grad_up, w_up, preferred_element_type=jnp.float32)
    grad_mid_norm, grad_gain_ffn = layer_norm_back(grad_n_two, unit_ffn, scale_ffn, gain_ffn)
    grad_middle = grad_out + grad_mid_norm
    grad_attn_branch = grad_middle.astype(jnp.bfloat16)
    grad_w_out = jnp.einsum(
        "sd,se->de", attended, grad_attn_branch, preferred_element_type=jnp.float32
    )
    grad_attended = jnp.einsum(
        "se,de->sd", grad_attn_branch, w_out, preferred_element_type=jnp.float32
    ).astype(jnp.bfloat16)
    grad_att_three = grad_attended.reshape(seg_rows, HEADS, HEAD_DIM)
    row_dot = jnp.sum(grad_att_three.astype(jnp.float32) * attended_full, axis=-1).T

    def block_grads(key_piece, value_piece, source, grad_parts):
        allowed = visible(source * seg_rows, seg_rows)

        def block_update(grad_parts):
            grad_key, grad_value, grad_query = grad_parts
            key_three = key_piece.reshape(seg_rows, HEADS, HEAD_DIM)
            value_three = value_piece.reshape(seg_rows, HEADS, HEAD_DIM)
            scores = (
                jnp.einsum("qhe,khe->hqk", query_rot, key_three, preferred_element_type=jnp.float32)
                * scale
            )
            prob_full = jnp.where(allowed[None], jnp.exp(scores - log_total[:, :, None]), 0.0)
            grad_value = grad_value + jnp.einsum(
                "hqk,qhe->khe",
                prob_full.astype(jnp.bfloat16),
                grad_att_three,
                preferred_element_type=jnp.float32,
            ).reshape(seg_rows, features)
            grad_prob = jnp.einsum(
                "qhe,khe->hqk", grad_att_three, value_three, preferred_element_type=jnp.float32
            )
            grad_scores = (prob_full * (grad_prob - row_dot[:, :, None])).astype(jnp.bfloat16)
            grad_query = (
                grad_query
                + jnp.einsum(
                    "hqk,khe->qhe", grad_scores, key_three, preferred_element_type=jnp.float32
                )
                * scale
            )
            grad_key = grad_key + (
                jnp.einsum(
                    "hqk,qhe->khe", grad_scores, query_rot, preferred_element_type=jnp.float32
                )
                * scale
            ).reshape(seg_rows, features)
            return (grad_key, grad_value, grad_query)

        return lax.cond(jnp.any(allowed), block_update, lambda unchanged: unchanged, grad_parts)

    zero_rows = jnp.zeros((seg_rows, features), jnp.float32)
    zero_query = jnp.zeros((seg_rows, HEADS, HEAD_DIM), jnp.float32)

    def visit(visit_no, loop_state):
        key_piece, value_piece, grad_key, grad_value, grad_query = loop_state
        source = (own_index - visit_no) % blocks
        grad_key, grad_value, grad_query = block_grads(
            key_piece, value_piece, source, (grad_key, grad_value, grad_query)
        )
        key_piece, value_piece = from_behind((key_piece, value_piece), "blk", 1)
        grad_key, grad_value = pass_grads(grad_key, grad_value)
        return (key_piece, value_piece, grad_key, grad_value, grad_query)

    loop_out = lax.fori_loop(
        0, blocks, visit, (key_rot, value_low, zero_rows, zero_rows, zero_query)
    )
    grad_key_sum, grad_value_sum, grad_query_rot = (loop_out[2], loop_out[3], loop_out[4])
    grad_query = (
        rotate(grad_query_rot, query_pos, -1.0).reshape(seg_rows, features).astype(jnp.bfloat16)
    )
    grad_key = (
        rotate(grad_key_sum.reshape(seg_rows, HEADS, HEAD_DIM), query_pos, -1.0)
        .reshape(seg_rows, features)
        .astype(jnp.bfloat16)
    )
    grad_value_low = grad_value_sum.astype(jnp.bfloat16)
    grad_w_query = jnp.einsum("sd,se->de", n_one, grad_query, preferred_element_type=jnp.float32)
    grad_w_key = jnp.einsum("sd,se->de", n_one, grad_key, preferred_element_type=jnp.float32)
    grad_w_value = jnp.einsum(
        "sd,se->de", n_one, grad_value_low, preferred_element_type=jnp.float32
    )
    grad_n_one = jnp.einsum("se,de->sd", grad_query, w_query, preferred_element_type=jnp.float32)
    grad_n_one = grad_n_one + jnp.einsum(
        "se,de->sd", grad_key, w_key, preferred_element_type=jnp.float32
    )
    grad_n_one = grad_n_one + jnp.einsum(
        "se,de->sd", grad_value_low, w_value, preferred_element_type=jnp.float32
    )
    grad_pool_norm, grad_gain_attn = layer_norm_back(grad_n_one, unit_attn, scale_attn, gain_attn)
    grad_pooled = grad_middle + grad_pool_norm
    grad_sums = (grad_pooled / divisor[:, None]).astype(jnp.bfloat16)
    last_grad = jnp.dot(
        last_slot.astype(jnp.bfloat16)[None, :], grad_sums, preferred_element_type=jnp.float32
    ).astype(jnp.bfloat16)
    came_grad = from_behind(last_grad, "blk", 1)
    spread_rows = jnp.take(grad_sums, jnp.maximum(slot_of, 0), axis=0)
    grad_bytes = jnp.where(leading[:, None], came_grad, spread_rows).astype(jnp.float32)
    (
        grad_w_query,
        grad_w_key,
        grad_w_value,
        grad_w_out,
        grad_w_up,
        grad_w_down,
        grad_gain_attn,
        grad_gain_ffn,
    ) = lax.psum(
        (
            grad_w_query,
            grad_w_key,
            grad_w_value,
            grad_w_out,
            grad_w_up,
            grad_w_down,
            grad_gain_attn,
            grad_gain_ffn,
        ),
        ("dp", "blk"),
    )
    return (
        output,
        grad_bytes,
        grad_w_query,
        grad_w_key,
        grad_w_value,
        grad_w_out,
        grad_w_up,
        grad_w_down,
        grad_gain_attn,
        grad_gain_ffn,
    )


def solution(mesh):
    fits = mesh.shape["blk"] == 4 and mesh.shape["dp"] == 8
    return jax.shard_map(
        fast_local if fits else local,
        mesh=mesh,
        in_specs=(
            P(("dp", "blk"), None),
            P(("dp", "blk")),
            P("dp", None),
            P(("dp", "blk"), None),
            P(),
            P(),
            P(),
            P(),
            P(),
            P(),
            P(),
            P(),
        ),
        out_specs=(
            P(("dp", "blk"), None),
            P(("dp", "blk"), None),
            P(),
            P(),
            P(),
            P(),
            P(),
            P(),
            P(),
            P(),
        ),
        check_vma=False,
    )
```

```python
import functools
import math

import jax
import jax.numpy as jnp
import numpy as np
from jax import lax
from jax.experimental import pallas as pl
from jax.experimental.pallas import tpu as pltpu
from jax.sharding import PartitionSpec as P

HEADS = 8
HEAD_DIM = 64
EPSILON = 1e-05
ROTARY_BASE = 10000.0
NEGATIVE = -1e30
LOG2E = math.log2(math.e)

MESH = pl.DeviceIdType.MESH
F32 = jnp.float32
BF16 = jnp.bfloat16
NN = (((1,), (0,)), ((), ()))
NT = (((1,), (1,)), ((), ()))
TN = (((0,), (0,)), ((), ()))


def mm(a, b, dims):
    return lax.dot_general(a, b, dims, preferred_element_type=F32)


def iota(shape, dim):
    return lax.broadcasted_iota(jnp.int32, shape, dim)


class Copy:
    def __init__(self, src, dst, send_sem, recv_sem, device, cond=None):
        self.parts = (src, dst, send_sem, recv_sem)
        self.device = device
        self.cond = cond

    def _do(self, act):
        def run():
            src, dst, send_sem, recv_sem = self.parts
            act(
                pltpu.make_async_remote_copy(
                    src_ref=src,
                    dst_ref=dst,
                    send_sem=send_sem,
                    recv_sem=recv_sem,
                    device_id=self.device,
                    device_id_type=MESH,
                )
            )

        if self.cond is None:
            run()
        else:
            pl.when(self.cond)(run)

    def start(self):
        self._do(lambda d: d.start())

    def wait_send(self):
        self._do(lambda d: d.wait_send())

    def wait_recv(self):
        self._do(lambda d: d.wait_recv())


CHUNKS = ((0, 4), (4, 9), (9, 12))
SEMS_AR = 22


def layer_kernel(
    bytes_hbm,
    flags_ref,
    lengths_ref,
    cot_hbm,
    wq_hbm,
    wk_hbm,
    wv_hbm,
    wo_hbm,
    wup_hbm,
    wdn_hbm,
    gain_attn_ref,
    gain_ffn_ref,
    freq_ref,
    out_ref,
    gs_ref,
    came_ref,
    slots_ref,
    wgrad_hbm,
    ggain_ref,
    bytes_v,
    weights,
    wup,
    wdn,
    meta,
    tail,
    slot_sc,
    p_own,
    relay,
    p_all,
    n1,
    k_t,
    v_t,
    q_t,
    tab_c,
    tab_s,
    pos,
    gcol,
    cot_own,
    cot_w,
    o_acc,
    m_sc,
    l_sc,
    att,
    gb,
    hat2,
    d_o,
    d_sc,
    gmid,
    dk,
    dv,
    dq,
    gwqkv,
    big,
    wg,
    r1,
    r2,
    r3,
    r4,
    ppart,
    rc,
    rz,
    gfin,
    out_s,
    out_r,
    rdiv,
    last_s,
    last_r,
    gain_acc,
    gain_s,
    gain_r,
    ss,
    rs,
    ls,
):
    cot_v, acc = hat2, big.at[0]
    dp = lax.axis_index("dp")
    z = lax.axis_index("blk")
    feat = 512
    half = 256
    nblk = 4
    c = lax.rem(dp, 2)
    x = lax.rem(lax.div(dp, 2), 2)
    y = lax.div(dp, 4)
    sib = (dp + 1 - 2 * c, z)
    xnb = (dp + 2 - 4 * x, z)
    ynb = (dp + 4 - 8 * y, z)
    g = lax.div(z, 2)
    zl = lax.rem(z, 2)
    w = 2 * zl + c
    zo = 4 * g + 1 - z
    near = 1 + g
    is_near = z == near
    own_worker = g == c

    def dev(core, zz):
        return (dp - c + core, zz)

    counter = {"s": 0, "r": 0, "l": 0}

    def ids(kind, n):
        first = counter[kind]
        counter[kind] = first + n
        return first

    sends = []

    def go(copy):
        copy.start()
        sends.append(copy)

    l_bytes = ids("l", 8)
    rows_chunk = bytes_v.shape[1]
    loads_bytes = [
        pltpu.make_async_copy(
            bytes_hbm.at[pl.ds(i * rows_chunk, rows_chunk)], bytes_v.at[i], ls.at[l_bytes + i]
        )
        for i in range(8)
    ]
    for d in loads_bytes:
        d.start()
    l_cot = ids("l", 1)
    load_cot = pltpu.make_async_copy(cot_hbm, cot_v, ls.at[l_cot])
    load_cot.start()
    l_w = ids("l", 4)
    loads_w = [
        pltpu.make_async_copy(src, weights.at[i], ls.at[l_w + i])
        for i, src in enumerate((wq_hbm, wk_hbm, wv_hbm, wo_hbm))
    ]
    for d in loads_w:
        d.start()
    l_f = ids("l", 8)
    loads_f = []
    for j in range(4):
        loads_f.append(
            pltpu.make_async_copy(
                wup_hbm.at[:, pl.ds(j * feat, feat)], wup.at[j], ls.at[l_f + 2 * j]
            )
        )
        loads_f.append(
            pltpu.make_async_copy(
                wdn_hbm.at[pl.ds(j * feat, feat)], wdn.at[j], ls.at[l_f + 2 * j + 1]
            )
        )
    for d in loads_f:
        d.start()

    barrier = pltpu.get_barrier_semaphore()
    me_line = c * nblk + z
    line = []
    for k in range(1, 8):
        t = lax.rem(me_line + k, 8)
        line.append((lax.div(t, nblk), lax.rem(t, nblk)))
    for core, zz in line:
        pl.semaphore_signal(barrier, inc=1, device_id=dev(core, zz), device_id_type=MESH)
    for d in (xnb, ynb):
        pl.semaphore_signal(barrier, inc=1, device_id=d, device_id_type=MESH)
    pl.semaphore_wait(barrier, 9)

    meta[c, z, 0:32, :] = flags_ref[...]
    meta[c, z, 32:40, :] = jnp.zeros((8, 128), jnp.int32)
    meta[c, z, 32:33, 0:4] = lengths_ref[...]
    s_meta, r_meta = ids("s", 7), ids("r", 8)
    for k, (core, zz) in enumerate(line):
        go(
            Copy(
                meta.at[c, z],
                meta.at[c, z],
                ss.at[s_meta + k],
                rs.at[r_meta + me_line],
                dev(core, zz),
            )
        )
    s_tail, r_tail = ids("s", 1), ids("r", 1)
    copy_tail = Copy(
        bytes_hbm.at[pl.ds(0, 16)],
        tail,
        ss.at[s_tail],
        rs.at[r_tail],
        (dp, lax.rem(z + nblk - 1, nblk)),
        z > 0,
    )
    go(copy_tail)

    @pl.when(z == nblk - 1)
    def _():
        tail[...] = jnp.zeros_like(tail)

    upper = (iota((128, 128), 0) <= iota((128, 128), 1)).astype(F32).astype(BF16)
    ones_sq = jnp.ones((128, 128), BF16)
    below = (iota((32, 32), 1) < iota((32, 32), 0)).astype(F32).astype(BF16)
    own_flags = flags_ref[...].astype(F32)
    flags_low = own_flags.astype(BF16)
    within = mm(flags_low, upper, NN)
    row_sums = mm(flags_low, ones_sq, NN)
    row_base = mm(below, row_sums.astype(BF16), NN)
    slot_of = within + row_base - 1.0
    for k in range(8):
        slot_sc[k] = slot_of[4 * k : 4 * k + 4, :]
    slots_ref[...] = slot_of
    cnt = jnp.sum(own_flags)

    acc[...] = jnp.zeros_like(acc)
    rdiv[...] = jnp.zeros_like(rdiv)
    slot_iota = iota((feat, 128), 0).astype(F32)
    ones_rows = jnp.ones((16, feat), BF16)

    def pool(k, carry):
        pltpu.make_async_copy(
            bytes_hbm.at[pl.ds(0, rows_chunk)], bytes_v.at[k], ls.at[l_bytes + k]
        ).wait()
        rows = slot_sc[k]
        member = jnp.concatenate(
            [
                (slot_iota == rows[r : r + 1, :]).astype(F32).astype(BF16)
                for r in range(4)
            ],
            axis=1,
        )
        acc[...] += mm(member, bytes_v[k], NN)
        rdiv[...] += mm(ones_rows, member, NT)
        return carry

    lax.fori_loop(0, 8, pool, 0)

    for i, gain in enumerate((gain_attn_ref, gain_ffn_ref)):
        row = jnp.broadcast_to(gain[...], (128, feat))
        col = row.T
        gcol[i] = jnp.concatenate([col, col], axis=1)

    for core, zz in line:
        Copy(
            meta.at[core, zz],
            meta.at[core, zz],
            ss.at[0],
            rs.at[r_meta + core * nblk + zz],
            sib,
        ).wait_recv()
    Copy(tail, tail, ss.at[0], rs.at[r_tail], sib, z < nblk - 1).wait_recv()
    zn = jnp.minimum(z + 1, nblk - 1)
    next_flags = meta[c, zn, 0:16, :].astype(F32).astype(BF16)
    next_within = mm(next_flags, upper, NN)
    has_next = (z < nblk - 1).astype(F32)
    lead = jnp.where(next_within[0:1, :] < 0.5, 1.0, 0.0) * has_next
    is_last16 = iota((feat, 16), 0).astype(F32) == cnt - 1.0
    member_tail = jnp.where(is_last16, lead[:, 0:16], 0.0).astype(BF16)
    sums = acc[...] + mm(member_tail, tail[...], NN)
    lane_row = iota((1, feat), 1).astype(F32)
    tally = rdiv[0:1, :] + jnp.where(lane_row == cnt - 1.0, jnp.sum(lead), 0.0)
    inverse_tally = 1.0 / jnp.maximum(tally, 1.0)
    rdiv[0:1, :] = inverse_tally
    live_row = jnp.where(lane_row < cnt, 1.0, 0.0)
    rdiv[1:2, :] = live_row
    pooled_t = (sums.T * inverse_tally).astype(BF16)
    p_own[0] = pooled_t[:, 0:half]
    p_own[1] = pooled_t[:, half:]

    s_p, r_p, r_relay = ids("s", 9), ids("r", 8), ids("r", 1)
    near_c = 1 + c

    def p_copy(src, hb, slot, device, cond=None):
        return Copy(src, p_all.at[hb], ss.at[s_p + slot], rs.at[r_p + hb], device, cond)

    other_worker = jnp.logical_not(own_worker)
    go(p_copy(p_own.at[c], 2 * z + c, 0, dev(c, zo), own_worker))
    go(p_copy(p_own.at[1 - c], 2 * z + 1 - c, 1, sib, own_worker))
    go(p_copy(p_own.at[c], 2 * z + c, 2, sib, own_worker))
    go(
        Copy(p_own.at[1 - c], relay, ss.at[s_p + 1], rs.at[r_relay], sib, other_worker)
    )
    go(p_copy(p_own.at[c], 2 * z + c, 2, dev(c, near_c), other_worker))

    @pl.when(own_worker)
    def _():
        p_all[2 * z] = p_own[0]
        p_all[2 * z + 1] = p_own[1]

    Copy(relay, relay, ss.at[0], rs.at[r_relay], sib, own_worker).wait_recv()
    go(p_copy(relay, 2 * z + c, 3, dev(c, 2 - c), own_worker))

    def p_wait(hb, cond=None):
        Copy(p_all.at[hb], p_all.at[hb], ss.at[0], rs.at[r_p + hb], sib, cond).wait_recv()

    p_wait(2 * z + c, other_worker)
    go(p_copy(p_all.at[2 * z + c], 2 * z + c, 0, dev(c, zo), other_worker))
    p_wait(2 * z + 1 - c, other_worker)

    load_cot.wait()
    cot_t = (cot_v[...].T * live_row).astype(BF16)
    cot_own[0] = cot_t[:, 0:half]
    cot_own[1] = cot_t[:, half:]
    s_cot, r_cot = ids("s", 2), ids("r", 2)
    early = z < 2
    slot_to = jnp.where(early, 0, 1)
    chip_to = 2 * c + jnp.where(early, z, 3 - z)
    for i in range(2):
        core_to = jnp.where(early, i, 1 - i)
        here = jnp.logical_and(core_to == c, chip_to == z)
        go(
            Copy(
                cot_own.at[i],
                cot_w.at[slot_to],
                ss.at[s_cot + i],
                rs.at[r_cot + slot_to],
                dev(core_to, chip_to),
                jnp.logical_not(here),
            )
        )

        @pl.when(here)
        def _():
            cot_w[slot_to] = cot_own[i]

    lo_here = jnp.logical_and(g == c, zl == z)
    hi_here = jnp.logical_and(g == c, 3 - zl == z)

    counts = []
    for b in range(nblk):
        counts.append(jnp.sum(meta[g, b, 0:32, :].astype(F32)))
    offsets = [jnp.float32(0.0)]
    for b in range(nblk):
        offsets.append(offsets[-1] + counts[b])
    lens = meta[g, z, 32:40, :].astype(F32)
    first_row = iota((8, 128), 0) == 0
    lane8 = iota((8, 128), 1)
    byte_at = (iota((32, 128), 0) * 128 + iota((32, 128), 1)).astype(F32)
    seq_first = [jnp.float32(0.0)]
    for s in range(1, 4):
        start = jnp.sum(jnp.where(jnp.logical_and(first_row, lane8 < s), lens, 0.0))
        prior = jnp.zeros((32, 128), F32)
        for b in range(nblk):
            prior = prior + jnp.where(
                byte_at + float(b * 4096) < start, meta[g, b, 0:32, :].astype(F32), 0.0
            )
        seq_first.append(jnp.sum(prior))

    freq = jnp.concatenate([freq_ref[...], freq_ref[...]], axis=1)
    lane_half = iota((1, half), 1).astype(F32)
    for hb in range(8):
        b = hb // 2
        j = lane_half + float((hb % 2) * half)
        p = offsets[b] + jnp.minimum(j, counts[b] - 1.0)
        first = jnp.zeros_like(p)
        for s in range(1, 4):
            first = jnp.maximum(first, jnp.where(p >= seq_first[s], seq_first[s], 0.0))
        pos[hb, 0:1, :] = p
        pos[hb, 1:2, :] = first
        angle = freq * p
        tab_c[hb] = jnp.cos(angle)
        tab_s[hb] = jnp.sin(angle)

    def pick(values, b):
        total = jnp.float32(0.0)
        for i, v in enumerate(values):
            total = total + jnp.where(b == i, v, 0.0)
        return total

    gain_col = gcol[0]

    def norm_parts(values):
        mean = jnp.mean(values, axis=0, keepdims=True)
        center = values - mean
        inverse = lax.rsqrt(jnp.mean(center * center, axis=0, keepdims=True) + EPSILON)
        return center * inverse, inverse

    def turned(values, hb, direction):
        cos = tab_c[hb]
        sin = tab_s[hb] * direction
        parts = []
        for h in range(HEADS):
            a = values[64 * h : 64 * h + 32, :]
            b = values[64 * h + 32 : 64 * h + 64, :]
            parts.append(a * cos - b * sin)
            parts.append(b * cos + a * sin)
        return jnp.concatenate(parts, axis=0).astype(BF16)

    for d in loads_w:
        d.wait()

    def keys_values(hb):
        unit, _ = norm_parts(p_all[hb].astype(F32))
        normed = (unit * gcol[0]).astype(BF16)
        n1[hb] = normed
        k_t[hb] = turned(mm(weights[1], normed, TN), hb, 1.0)
        v_t[hb] = mm(weights[2], normed, TN).astype(BF16)

    def both_halves(block):
        def one(i, carry):
            keys_values(2 * block + i)
            return carry

        lax.fori_loop(0, 2, one, 0)

    both_halves(z)
    for n, block in enumerate((zo, 2 - g, 3 - 3 * g)):
        p_wait(2 * block + c)
        if n > 0:
            go(p_copy(p_all.at[2 * block + c], 2 * block + c, 6 + n, dev(c, zo), is_near))
        go(p_copy(p_all.at[2 * block + c], 2 * block + c, 4 + n, sib))
        p_wait(2 * block + 1 - c)
        both_halves(block)

    hq_of = (w, 7 - w)

    def hq_at(slot):
        return jnp.where(slot == 0, w, 7 - w)

    for slot in range(2):
        q_t[slot] = turned(mm(weights[0], n1[hq_of[slot]], TN), hq_of[slot], 1.0)
    score_scale = HEAD_DIM ** (-0.5) * LOG2E

    def bias_of(hq, kb):
        b = lax.div(kb, 2)
        j = (iota((half, half), 0) + lax.rem(kb, 2) * half).astype(F32)
        kpos = j + pick(offsets[:nblk], b)
        alive = j < pick(counts, b)
        qpos = pos[hq, 0:1, :]
        qfirst = pos[hq, 1:2, :]
        allowed = jnp.logical_and(alive, jnp.logical_and(kpos <= qpos, kpos >= qfirst))
        return jnp.where(allowed, 0.0, NEGATIVE)

    o_acc[...] = jnp.zeros_like(o_acc)
    l_sc[...] = jnp.zeros_like(l_sc)
    m_sc[...] = jnp.full(m_sc.shape, NEGATIVE, F32)

    def s_at(h):
        return gwqkv.at[h // 4, pl.ds(half * ((h // 2) % 2), half), pl.ds(half * (h % 2), half)]

    o_new = big.at[1, :, pl.ds(0, half)]

    def forward_step(t, carry):
        low_half = t <= w
        slot = jnp.where(low_half, 0, 1)
        kb = jnp.where(low_half, t, t - w - 1)
        hq = hq_at(slot)
        bias = bias_of(hq, kb)
        old = m_sc[slot]
        old_sum = l_sc[slot]
        for h in range(HEADS):
            part = slice(64 * h, 64 * h + 64)
            s_at(h)[...] = mm(k_t[kb, part, :], q_t[slot, part, :], TN)
        tops, sums = [], []
        for h in range(HEADS):
            part = slice(64 * h, 64 * h + 64)
            s = s_at(h)[...] * score_scale + bias
            top = jnp.maximum(old[h : h + 1, :], jnp.max(s, axis=0, keepdims=True))
            prob = jnp.exp2(s - top)
            tops.append(top)
            sums.append(jnp.sum(prob, axis=0, keepdims=True))
            o_new[part, :] = mm(v_t[kb, part, :], prob.astype(BF16), NN)
        new = jnp.concatenate(tops, axis=0)
        shrink = jnp.exp2(old - new)
        m_sc[slot] = new
        l_sc[slot] = old_sum * shrink + jnp.concatenate(sums, axis=0)
        for h in range(HEADS):
            part = slice(64 * h, 64 * h + 64)
            o_acc[slot, part, :] = o_acc[slot, part, :] * shrink[h : h + 1, :] + o_new[part, :]
        return carry

    lax.fori_loop(0, 9, forward_step, 0)

    for slot in range(2):
        total = l_sc[slot]
        for h in range(HEADS):
            part = slice(64 * h, 64 * h + 64)
            o_acc[slot, part, :] = o_acc[slot, part, :] * (1.0 / total[h : h + 1, :])
        att[:, slot * half : (slot + 1) * half] = o_acc[slot].astype(BF16)
        m_sc[slot] = m_sc[slot] + jnp.log2(total)

    own_pooled = jnp.concatenate([p_all[hq_of[0]], p_all[hq_of[1]]], axis=1).astype(F32)
    middle = own_pooled + mm(weights[3], att[...], TN)
    unit2, inverse2 = norm_parts(middle)
    hat2[...] = unit2
    gain_col2 = jnp.concatenate([gcol[1], gcol[1]], axis=1)
    n2 = (unit2 * gain_col2).astype(BF16)
    big[0] = middle
    big[1] = jnp.zeros((feat, feat), F32)
    Copy(cot_w.at[0], cot_w.at[0], ss.at[0], rs.at[r_cot], sib, jnp.logical_not(lo_here)).wait_recv()
    Copy(cot_w.at[1], cot_w.at[1], ss.at[0], rs.at[r_cot + 1], sib, jnp.logical_not(hi_here)).wait_recv()
    gb[...] = jnp.concatenate([cot_w[0], cot_w[1]], axis=1)
    n2_ref = d_o
    n2_ref[...] = n2

    base1 = c * 256
    keep2x, give2x = base1 + x * 128, base1 + (1 - x) * 128
    keep2y, give2y = base1 + y * 128, base1 + (1 - y) * 128
    keep3x, give3x = keep2x + y * 64, keep2x + (1 - y) * 64
    keep3y, give3y = keep2y + x * 64, keep2y + (1 - x) * 64
    lanes_x, lanes_y = pl.ds(0, 256), pl.ds(256, 256)

    def rows_of(first, n):
        return pl.ds(pl.multiple_of(first, 16), n)

    class Reduce:
        def __init__(self, chunk):
            self.b0, self.b1 = CHUNKS[chunk]
            self.nb = self.b1 - self.b0
            self.s0, self.r0 = ids("s", SEMS_AR), ids("r", SEMS_AR)
            self.blocks = pl.ds(self.b0, self.nb)
            self.phases = {}

        def _w(self, first, n, lanes):
            return wg.at[self.blocks, rows_of(first, n), lanes]

        def _list(self, phase):
            every = pl.ds(0, 512)
            b, s0, r0 = self.blocks, self.s0, self.r0

            def copy(i, src, dst, device):
                return Copy(src, dst, ss.at[s0 + i], rs.at[r0 + i], device)

            if phase == 1:
                return [copy(0, self._w((1 - c) * 256, 256, every), r1.at[b], sib)]
            if phase == 2:
                return [
                    copy(1, self._w(give2x, 128, lanes_x), r2.at[b, :, lanes_x], xnb),
                    copy(2, self._w(give2y, 128, lanes_y), r2.at[b, :, lanes_y], ynb),
                ]
            if phase == 3:
                return [
                    copy(3, self._w(give3x, 64, lanes_x), r3.at[b, :, lanes_x], ynb),
                    copy(4, self._w(give3y, 64, lanes_y), r3.at[b, :, lanes_y], xnb),
                ]
            if phase == 4:
                out = []
                for k in range(1, 4):
                    zt = lax.rem(z + k, nblk)
                    out.append(
                        copy(
                            3 + 2 * k,
                            self._w(keep3x + 16 * zt, 16, lanes_x),
                            r4.at[k - 1, b, :, lanes_x],
                            (dp, zt),
                        )
                    )
                    out.append(
                        copy(
                            4 + 2 * k,
                            self._w(keep3y + 16 * zt, 16, lanes_y),
                            r4.at[k - 1, b, :, lanes_y],
                            (dp, zt),
                        )
                    )
                return out
            if phase == 5:
                out = []
                for k in range(1, 4):
                    zt = lax.rem(z + k, nblk)
                    for i, (keep, lanes) in enumerate(((keep3x, lanes_x), (keep3y, lanes_y))):
                        mine = self._f(keep + 16 * z, 16, lanes)
                        out.append(copy(9 + 2 * k + i, mine, mine, (dp, zt)))
                return out
            if phase == 6:
                mine_x, mine_y = self._f(keep3x, 64, lanes_x), self._f(keep3y, 64, lanes_y)
                return [copy(17, mine_x, mine_x, ynb), copy(18, mine_y, mine_y, xnb)]
            if phase == 7:
                mine_x, mine_y = self._f(keep2x, 128, lanes_x), self._f(keep2y, 128, lanes_y)
                return [copy(19, mine_x, mine_x, xnb), copy(20, mine_y, mine_y, ynb)]
            return [copy(21, r1.at[b], self._out(base1), sib)]

        def _f(self, first, n, lanes):
            return r1.at[self.blocks, rows_of(first - base1, n), lanes]

        def _out(self, first):
            return wgrad_hbm.at[self.blocks, rows_of(first, 256), pl.ds(0, 512)]

        def start(self, phase):
            for one in self._list(phase):
                one.start()

        def finish(self, phase):
            if phase == 8:
                other = self._out((1 - c) * 256)
                Copy(other, other, ss.at[0], rs.at[self.r0 + 21], sib).wait_recv()
                return
            for one in self._list(phase):
                one.wait_recv()
            if phase > 4:
                return

            def add(i, carry):
                b = self.b0 + i
                if phase == 1:
                    here = (b, rows_of(base1, 256), slice(None))
                    wg[here] = wg[here] + r1[b]
                if phase == 2:
                    for keep, lo in ((keep2x, 0), (keep2y, 256)):
                        here = (b, rows_of(keep, 128), slice(lo, lo + 256))
                        wg[here] = wg[here] + r2[b, :, lo : lo + 256]
                if phase == 3:
                    for keep, lo in ((keep3x, 0), (keep3y, 256)):
                        here = (b, rows_of(keep, 64), slice(lo, lo + 256))
                        wg[here] = wg[here] + r3[b, :, lo : lo + 256]
                if phase == 4:
                    for keep, lo in ((keep3x, 0), (keep3y, 256)):
                        here = (b, rows_of(keep + 16 * z, 16), slice(lo, lo + 256))
                        total = wg[here].astype(F32)
                        for k in range(3):
                            total = total + r4[k, b, :, lo : lo + 256].astype(F32)
                        r1[b, rows_of(keep - base1 + 16 * z, 16), lo : lo + 256] = total.astype(BF16)
                return carry

            lax.fori_loop(0, self.nb, add, 0)

        def step(self, phase):
            self.finish(phase)
            if phase < 8:
                self.start(phase + 1)
            if phase == 7:
                self.store().start()

        def store(self):
            return pltpu.make_async_copy(r1.at[self.blocks], self._out(base1), ls.at[self.store_sem])

        def wait_sends(self):
            for phase in range(1, 9):
                for one in self._list(phase):
                    one.wait_send()

    red = [Reduce(i) for i in range(3)]
    for one in red:
        one.store_sem = ids("l", 1)

    for d in loads_f:
        d.wait()

    def ffn_chunk(j, carry):
        up = mm(wup[j], n2_ref[...], TN)
        size = jnp.abs(up) * (0.5**0.5)
        t = 1.0 / (1.0 + 0.3275911 * size)
        poly = t * (
            0.254829592
            + t * (-0.284496736 + t * (1.421413741 + t * (-1.453152027 + t * 1.061405429)))
        )
        decay = jnp.exp(-0.5 * up * up)
        far = 0.5 * poly * decay
        phi = jnp.where(up < 0.0, far, 1.0 - far)
        slope = phi + up * decay * (1.0 / math.sqrt(2.0 * math.pi))
        act = (up * phi).astype(BF16)
        wg[2 * j] = mm(act, gb[...], NT).astype(BF16)
        big[0] += mm(wdn[j], act, TN)
        grad_up = (mm(wdn[j], gb[...], NN) * slope).astype(BF16)
        wg[2 * j + 1] = mm(n2_ref[...], grad_up, NT).astype(BF16)
        big[1] += mm(wup[j], grad_up, NN)

        @pl.when(j == 1)
        def _():
            red[0].start(1)

        return carry

    lax.fori_loop(0, 4, ffn_chunk, 0)
    red[0].step(1)

    s_out, r_out = ids("s", 2), ids("r", 2)
    res = big[0].astype(BF16)
    owners = ((zl, c, lo_here), (3 - zl, 1 - c, hi_here))
    for slot, (chip, i, here) in enumerate(owners):
        out_s[slot] = res[:, slot * half : (slot + 1) * half]
        go(
            Copy(
                out_s.at[slot],
                out_r.at[i],
                ss.at[s_out + slot],
                rs.at[r_out + i],
                dev(g, chip),
                jnp.logical_not(here),
            )
        )

        @pl.when(here)
        def _():
            out_r[i] = out_s[slot]

    grad_n2 = big[1]
    unit2 = hat2[...]
    product = grad_n2 * unit2

    def lane_fold(values):
        total = values[:, 0:128]
        for k in range(1, values.shape[1] // 128):
            total = total + values[:, 128 * k : 128 * (k + 1)]
        return total

    gain_acc[1] = lane_fold(product)
    e = grad_n2 * gain_col2
    grad_mid = gb[...].astype(F32) + inverse2 * (
        e
        - jnp.mean(e, axis=0, keepdims=True)
        - unit2 * jnp.mean(e * unit2, axis=0, keepdims=True)
    )
    gmid[0] = grad_mid[:, 0:half]
    gmid[1] = grad_mid[:, half:]
    branch = grad_mid.astype(BF16)
    wg[8] = mm(att[...], branch, NT).astype(BF16)
    red[1].start(1)
    grad_att = mm(weights[3], branch, NN)
    d_o[...] = grad_att.astype(BF16)
    for slot in range(2):
        lanes = slice(slot * half, (slot + 1) * half)
        both = d_o[:, lanes].astype(F32) * o_acc[slot]
        for h in range(HEADS):
            d_sc[slot, h : h + 1, :] = jnp.sum(
                both[64 * h : 64 * h + 64, :], axis=0, keepdims=True
            )

    dq[...] = jnp.zeros_like(dq)
    gwqkv[...] = jnp.zeros_like(gwqkv)
    gain_acc[0] = jnp.zeros((feat, 128), F32)
    s_rc, r_rc = ids("s", 4), ids("r", 4)
    s_rz, r_rz = ids("s", 4), ids("r", 4)
    s_fin, r_fin = ids("s", 4), ids("r", 2)

    def sd_at(which, h):
        return big.at[which, pl.ds(half * ((h // 2) % 2), half), pl.ds(half * (h % 2), half)]

    def backward_step(slot, kb):
        hq = hq_at(slot)
        bias = bias_of(hq, kb)
        lanes = pl.ds(pl.multiple_of(slot * half, half), half)
        lse = m_sc[slot]
        dots = d_sc[slot]
        for first in (0, 4):
            for h in range(first, first + 4):
                part = slice(64 * h, 64 * h + 64)
                grad_o = d_o[part, lanes]
                sd_at(0, h)[...] = mm(k_t[kb, part, :], q_t[slot, part, :], TN)
                sd_at(1, h)[...] = mm(v_t[kb, part, :], grad_o, TN)
            for h in range(first, first + 4):
                part = slice(64 * h, 64 * h + 64)
                prob = jnp.exp2(sd_at(0, h)[...] * score_scale + bias - lse[h : h + 1, :])
                grad_s = (prob * (sd_at(1, h)[...] - dots[h : h + 1, :])).astype(BF16)
                dv[part, :] += mm(d_o[part, lanes], prob.astype(BF16), NT)
                dk[part, :] += mm(q_t[slot, part, :], grad_s, NT)
                dq[slot, part, :] += mm(k_t[kb, part, :], grad_s, NN)

    att_scale = HEAD_DIM ** (-0.5)

    def rc_copy(kb):
        zb = lax.div(kb, 2)
        return Copy(
            ppart.at[kb],
            rc.at[zb],
            ss.at[s_rc + zb],
            rs.at[r_rc + zb],
            sib,
            lax.rem(kb, 2) != c,
        )

    def is_final(zb):
        return jnp.where(lax.div(zb, 2) == g, z == zb, is_near)

    def rz_copy(zb):
        return Copy(
            ppart.at[2 * zb + c],
            rz.at[zb],
            ss.at[s_rz + zb],
            rs.at[r_rz + zb],
            dev(c, zo),
            jnp.logical_not(is_final(zb)),
        )

    def fin_copy(zb):
        here = jnp.logical_and(zb == z, g == c)
        return Copy(
            ppart.at[2 * zb + c],
            gfin.at[c],
            ss.at[s_fin + zb],
            rs.at[r_fin + c],
            dev(g, zb),
            jnp.logical_and(is_final(zb), jnp.logical_not(here)),
        )

    def combine(zb):
        kb = 2 * zb + c
        Copy(rc.at[zb], rc.at[zb], ss.at[0], rs.at[r_rc + zb], sib).wait_recv()
        ppart[kb] = ppart[kb] + rc[zb]
        rz_copy(zb).start()

    def deliver(zb):
        kb = 2 * zb + c
        final = is_final(zb)
        Copy(rz.at[zb], rz.at[zb], ss.at[0], rs.at[r_rz + zb], sib, final).wait_recv()

        @pl.when(final)
        def _():
            ppart[kb] = ppart[kb] + rz[zb]

        @pl.when(jnp.logical_and(zb == z, g == c))
        def _():
            gfin[c] = ppart[kb]

        fin_copy(zb).start()

    def ticks(at, schedule):
        for i, todo in schedule.items():

            @pl.when(at == i)
            def _():
                for chunk, phase in todo:
                    red[chunk].step(phase)

    def key_block(kb, carry):
        @pl.when(kb <= 7 - w)
        def _():
            dk[...] = jnp.zeros_like(dk)
            dv[...] = jnp.zeros_like(dv)

            def one(i, carry):
                backward_step(1 - i, kb)
                return carry

            lax.fori_loop(0, jnp.where(kb <= w, 2, 1), one, 0)
            grad_key = turned(dk[...] * att_scale, kb, -1.0)
            grad_value = dv[...].astype(BF16)
            normed = n1[kb]
            k_t[kb] = grad_key
            v_t[kb] = grad_value
            gwqkv[1] += mm(normed, grad_key, NT)
            gwqkv[2] += mm(normed, grad_value, NT)

            @pl.when(jnp.logical_or(kb == w, kb == 7 - w))
            def _():
                slot = jnp.where(kb == w, 0, 1)
                grad_query = turned(dq[slot] * att_scale, kb, -1.0)
                q_t[slot] = grad_query
                gwqkv[0] += mm(normed, grad_query, NT)

        ticks(
            kb,
            {
                0: [(1, 1)],
                1: [(0, 2)],
                2: [(0, 3)],
                3: [(1, 2)],
                4: [(0, 4)],
                5: [(1, 3)],
                6: [(0, 5)],
                7: [(0, 6)],
            },
        )
        return carry

    lax.fori_loop(0, 8, key_block, 0)
    for i in range(3):
        wg[9 + i] = gwqkv[i].astype(BF16)
    red[2].start(1)

    def block_at(j):
        return jnp.where(g == 0, 3 - j, j)

    def row_block(i, carry):
        j = lax.div(i, 2)
        kb = 2 * block_at(j) + lax.rem(i, 2)

        @pl.when(kb <= 7 - w)
        def _():
            big[0, :, 0:half] = mm(weights[1], k_t[kb], NN) + mm(weights[2], v_t[kb], NN)
            own = jnp.logical_or(kb == w, kb == 7 - w)
            slot = jnp.where(kb == w, 0, 1)

            @pl.when(own)
            def _():
                big[0, :, 0:half] += mm(weights[0], q_t[slot], NN)

            grad_n1 = big[0, :, 0:half]
            unit, inverse = norm_parts(p_all[kb].astype(F32))
            gain_acc[0] += lane_fold(grad_n1 * unit)
            e = grad_n1 * gcol[0]
            total = inverse * (
                e
                - jnp.mean(e, axis=0, keepdims=True)
                - unit * jnp.mean(e * unit, axis=0, keepdims=True)
            )
            ppart[kb] = (total + jnp.where(own, 1.0, 0.0) * gmid[slot]).astype(BF16)

        @pl.when(kb > 7 - w)
        def _():
            ppart[kb] = jnp.zeros(ppart.shape[1:], BF16)

        rc_copy(kb).start()

        @pl.when(lax.rem(i, 2) == 1)
        def _():
            combine(block_at(j))

        @pl.when(jnp.logical_and(lax.rem(i, 2) == 1, i > 1))
        def _():
            deliver(block_at(j - 1))

        ticks(
            i,
            {
                0: [(2, 1)],
                1: [(1, 4)],
                2: [(0, 7)],
                3: [(2, 2)],
                4: [(1, 5)],
                5: [(0, 8)],
                6: [(2, 3)],
                7: [(1, 6)],
            },
        )
        return carry

    lax.fori_loop(0, 8, row_block, 0)

    for i in range(2):
        gain_s[0, i : i + 1, :] = jnp.sum(gain_acc[i].T, axis=0, keepdims=True)
    gain_s[0, 2:8, :] = jnp.zeros((6, feat), F32)
    s_gain, r_gain = ids("s", 6), ids("r", 6)

    def gain_list(phase):
        if phase < 4:
            device = (sib, xnb, ynb)[phase - 1]
            k = phase - 1
            return [
                Copy(gain_s.at[k], gain_r.at[k], ss.at[s_gain + k], rs.at[r_gain + k], device)
            ]
        return [
            Copy(
                gain_s.at[3],
                gain_r.at[2 + k],
                ss.at[s_gain + 2 + k],
                rs.at[r_gain + 2 + k],
                (dp, lax.rem(z + k, nblk)),
            )
            for k in range(1, 4)
        ]

    def gain_finish(phase):
        for one in gain_list(phase):
            one.wait_recv()
        if phase < 4:
            gain_s[phase] = gain_s[phase - 1] + gain_r[phase - 1]
            for one in gain_list(phase + 1):
                one.start()
        else:
            total = jnp.zeros((8, feat), F32)
            for zz in range(nblk):
                k = lax.rem(z - zz + nblk, nblk)
                part = gain_s[3]
                for i in range(1, 4):
                    part = jnp.where(k == i, gain_r[2 + i], part)
                total = total + part
            ggain_ref[...] = total

    gain_list(1)[0].start()
    red[2].step(4)
    deliver(block_at(3))
    gain_finish(1)
    red[1].step(7)

    for i in range(2):
        mine = out_from_self(i, c, z)
        Copy(
            out_r.at[i], out_r.at[i], ss.at[0], rs.at[r_out + i], sib, jnp.logical_not(mine)
        ).wait_recv()
        live = rdiv[1:2, i * half : (i + 1) * half]
        out_ref[i * half : (i + 1) * half, :] = (out_r[i].astype(F32) * live).T.astype(BF16)

    gain_finish(2)
    red[2].step(5)

    for i in range(2):
        mine = jnp.logical_and(own_worker, c == i)
        Copy(
            gfin.at[i], gfin.at[i], ss.at[0], rs.at[r_fin + i], sib, jnp.logical_not(mine)
        ).wait_recv()
        grad_sums = gfin[i].astype(F32) * rdiv[0:1, i * half : (i + 1) * half]
        gs_ref[i * half : (i + 1) * half, :] = grad_sums.T.astype(BF16)

    is_last = jnp.where(iota((16, feat), 1).astype(F32) == cnt - 1.0, 1.0, 0.0).astype(BF16)
    last_s[...] = mm(is_last, gs_ref[...], NN).astype(BF16)
    s_last, r_last = ids("s", 1), ids("r", 1)
    copy_last = Copy(
        last_s,
        last_r,
        ss.at[s_last],
        rs.at[r_last],
        (dp, lax.rem(z + 1, nblk)),
        z < nblk - 1,
    )
    go(copy_last)

    red[1].step(8)
    gain_finish(3)
    red[2].step(6)
    gain_finish(4)
    Copy(last_r, last_r, ss.at[0], rs.at[r_last], sib, z > 0).wait_recv()

    @pl.when(z == 0)
    def _():
        last_r[...] = jnp.zeros_like(last_r)

    came_ref[...] = last_r[...]
    for phase in range(7, 9):
        red[2].step(phase)

    for one in sends:
        one.wait_send()

    def close_key(kb, carry):
        rc_copy(kb).wait_send()
        return carry

    lax.fori_loop(0, 8, close_key, 0)

    def close_block(zb, carry):
        rz_copy(zb).wait_send()
        fin_copy(zb).wait_send()
        return carry

    lax.fori_loop(0, 4, close_block, 0)
    for phase in range(1, 5):
        for one in gain_list(phase):
            one.wait_send()
    for one in red:
        one.wait_sends()
        one.store().wait()


def out_from_self(i, c, z):
    chip = 2 * c + jnp.where(z < 2, z, 3 - z)
    core = jnp.where(z < 2, i, 1 - i)
    return jnp.logical_and(core == c, chip == z)


def expand_kernel(
    slots_ref, gs_ref, came_ref, out_ref, ggain_ref, dn_ref, up0, up1, up2, up3, wo_ref, wq_ref, wk_ref, wv_ref,
    bytes_out, out_out, ga_out, gf_out, dn_out, up_out, wo_out, wq_out, wk_out, wv_out,
):
    rows = slots_ref[0]
    slot_iota = iota((512, 128), 0).astype(F32)
    member = jnp.concatenate(
        [(slot_iota == rows[r : r + 1, :]).astype(F32).astype(BF16) for r in range(4)], axis=1
    )
    first = iota((16, 128), 0) == 0
    lead = jnp.concatenate(
        [
            jnp.where(jnp.logical_and(first, rows[r : r + 1, :] < -0.5), 1.0, 0.0).astype(BF16)
            for r in range(4)
        ],
        axis=1,
    )
    bytes_out[...] = mm(member, gs_ref[...], TN) + mm(lead, came_ref[...], TN)
    out_out[...] = out_ref[...].astype(F32)
    ga_out[...] = ggain_ref[0:1, :]
    gf_out[...] = ggain_ref[1:2, :]
    dn_out[...] = dn_ref[0].astype(F32)
    for j, up in enumerate((up0, up1, up2, up3)):
        up_out[:, 512 * j : 512 * (j + 1)] = up[0].astype(F32)
    for src, dst in ((wo_ref, wo_out), (wq_ref, wq_out), (wk_ref, wk_out), (wv_ref, wv_out)):
        dst[...] = src[0].astype(F32)


def fast_local(
    bytes_in, flags, lengths, cotangent, w_query, w_key, w_value, w_out, w_up, w_down, gain_attn, gain_ffn
):
    meta_flags = flags.reshape(32, 128)
    freqs = np.float32(ROTARY_BASE) ** (-2.0 * np.arange(32, dtype=np.float32) / np.float32(64))
    freq = np.ascontiguousarray(np.broadcast_to(freqs.astype(np.float32)[:, None], (32, 128)))
    vm = pl.BlockSpec(memory_space=pltpu.VMEM)
    hbm = pl.BlockSpec(memory_space=pl.ANY)
    hb = lambda n: pltpu.VMEM((n, 512, 256), BF16)
    hbf = lambda n: pltpu.VMEM((n, 512, 256), F32)
    sq = lambda n, t: pltpu.VMEM((n, 512, 512), t)
    scratch = dict(
        bytes_v=sq(8, BF16),
        weights=sq(4, BF16),
        wup=sq(4, BF16),
        wdn=sq(4, BF16),
        meta=pltpu.VMEM((2, 4, 40, 128), jnp.int32),
        tail=pltpu.VMEM((16, 512), BF16),
        slot_sc=pltpu.VMEM((8, 4, 128), F32),
        p_own=hb(2),
        relay=pltpu.VMEM((512, 256), BF16),
        p_all=hb(8),
        n1=hb(8),
        k_t=hb(8),
        v_t=hb(8),
        q_t=hb(2),
        tab_c=pltpu.VMEM((8, 32, 256), F32),
        tab_s=pltpu.VMEM((8, 32, 256), F32),
        pos=pltpu.VMEM((8, 8, 256), F32),
        gcol=hbf(2),
        cot_own=hb(2),
        cot_w=hb(2),
        o_acc=hbf(2),
        m_sc=pltpu.VMEM((2, 8, 256), F32),
        l_sc=pltpu.VMEM((2, 8, 256), F32),
        att=pltpu.VMEM((512, 512), BF16),
        gb=pltpu.VMEM((512, 512), BF16),
        hat2=pltpu.VMEM((512, 512), F32),
        d_o=pltpu.VMEM((512, 512), BF16),
        d_sc=pltpu.VMEM((2, 8, 256), F32),
        gmid=hbf(2),
        dk=pltpu.VMEM((512, 256), F32),
        dv=pltpu.VMEM((512, 256), F32),
        dq=hbf(2),
        gwqkv=sq(3, F32),
        big=sq(2, F32),
        wg=sq(12, BF16),
        r1=pltpu.VMEM((12, 256, 512), BF16),
        r2=pltpu.VMEM((12, 128, 512), BF16),
        r3=pltpu.VMEM((12, 64, 512), BF16),
        r4=pltpu.VMEM((3, 12, 16, 512), BF16),
        ppart=hb(8),
        rc=hb(4),
        rz=hb(4),
        gfin=hb(2),
        out_s=hb(2),
        out_r=hb(2),
        rdiv=pltpu.VMEM((16, 512), F32),
        last_s=pltpu.VMEM((16, 512), BF16),
        last_r=pltpu.VMEM((16, 512), BF16),
        gain_acc=pltpu.VMEM((2, 512, 128), F32),
        gain_s=pltpu.VMEM((4, 8, 512), F32),
        gain_r=pltpu.VMEM((6, 8, 512), F32),
        ss=pltpu.SemaphoreType.DMA((128,)),
        rs=pltpu.SemaphoreType.DMA((128,)),
        ls=pltpu.SemaphoreType.DMA((32,)),
    )
    out, gs, came, slots, wgrad, ggain = pl.pallas_call(
        layer_kernel,
        out_shape=(
            jax.ShapeDtypeStruct((512, 512), BF16),
            jax.ShapeDtypeStruct((512, 512), BF16),
            jax.ShapeDtypeStruct((16, 512), BF16),
            jax.ShapeDtypeStruct((32, 128), F32),
            jax.ShapeDtypeStruct((12, 512, 512), BF16),
            jax.ShapeDtypeStruct((8, 512), F32),
        ),
        in_specs=[hbm, vm, vm, hbm, hbm, hbm, hbm, hbm, hbm, hbm, vm, vm, vm],
        out_specs=(vm, vm, vm, vm, hbm, vm),
        scratch_shapes=list(scratch.values()),
        compiler_params=pltpu.CompilerParams(
            collective_id=0, has_side_effects=True, vmem_limit_bytes=60 * 2**20
        ),
        name="layer",
    )(
        bytes_in, meta_flags, lengths, cotangent, w_query, w_key, w_value, w_out, w_up, w_down,
        gain_attn.reshape(1, 512), gain_ffn.reshape(1, 512), freq,
    )
    block = lambda rows, cols, index: pl.BlockSpec((1, rows, cols), index)
    ups = [block(64, 512, functools.partial(lambda j, i: (2 * j + 1, i, 0), j)) for j in range(4)]
    rest = [block(64, 512, functools.partial(lambda j, i: (j, i, 0), j)) for j in range(8, 12)]
    whole = lambda shape: pl.BlockSpec(shape, lambda i: (0, 0))
    flat = lambda rows, cols: pl.BlockSpec((rows, cols), lambda i: (i, 0))
    grad_bytes, out, g_attn, g_ffn, dn, up, wo, wq, wk, wv = pl.pallas_call(
        expand_kernel,
        grid=(8,),
        out_shape=(
            jax.ShapeDtypeStruct((4096, 512), F32),
            jax.ShapeDtypeStruct((512, 512), F32),
            jax.ShapeDtypeStruct((1, 512), F32),
            jax.ShapeDtypeStruct((1, 512), F32),
            jax.ShapeDtypeStruct((2048, 512), F32),
            jax.ShapeDtypeStruct((512, 2048), F32),
        )
        + (jax.ShapeDtypeStruct((512, 512), F32),) * 4,
        in_specs=[
            block(4, 128, lambda i: (i, 0, 0)),
            whole((512, 512)),
            whole((16, 512)),
            flat(64, 512),
            whole((8, 512)),
            block(256, 512, lambda i: (2 * lax.div(i, 2), lax.rem(i, 2), 0)),
        ]
        + ups
        + rest,
        out_specs=(flat(512, 512), flat(64, 512), whole((1, 512)), whole((1, 512)), flat(256, 512), flat(64, 2048)) + (flat(64, 512),) * 4,
        compiler_params=pltpu.CompilerParams(vmem_limit_bytes=60 * 2**20),
        name="expand",
    )(slots.reshape(8, 4, 128), gs, came, out, ggain, wgrad, wgrad, wgrad, wgrad, wgrad, wgrad, wgrad, wgrad, wgrad)
    return out, grad_bytes, wq, wk, wv, wo, up, dn, g_attn.reshape(512), g_ffn.reshape(512)


def passed_along(block, axis, distance):
    devices = range(lax.axis_size(axis))
    route = [((i - distance) % len(devices), i) for i in devices]
    return lax.ppermute(block, axis, route)


def from_behind(value, axis, by):
    count = lax.axis_size(axis)
    pairs = [(i, i + by) for i in range(count) if 0 <= i + by < count]
    return lax.ppermute(value, axis, pairs)


def rotate(vectors, positions, direction):
    half_dim = vectors.shape[-1] // 2
    freqs = ROTARY_BASE ** (-2.0 * jnp.arange(half_dim, dtype=jnp.float32) / vectors.shape[-1])
    angles = positions.astype(jnp.float32)[:, None] * freqs[None, :]
    cosine = jnp.cos(angles)[:, None, :]
    sine = direction * jnp.sin(angles)[:, None, :]
    first_half = vectors[..., :half_dim]
    second_half = vectors[..., half_dim:]
    return jnp.concatenate(
        [first_half * cosine - second_half * sine, second_half * cosine + first_half * sine],
        axis=-1,
    )


def layer_norm_parts(values, gain):
    center = values - jnp.mean(values, axis=-1, keepdims=True)
    spread = jnp.mean(center * center, axis=-1, keepdims=True)
    inverse = lax.rsqrt(spread + EPSILON)
    normed = center * inverse
    return (normed * gain, normed, inverse)


def layer_norm_back(grad_in, normed, inverse, gain):
    scaled = grad_in * gain
    grad_values = inverse * (
        scaled
        - jnp.mean(scaled, axis=-1, keepdims=True)
        - normed * jnp.mean(scaled * normed, axis=-1, keepdims=True)
    )
    grad_gain = jnp.sum(grad_in * normed, axis=0)
    return (grad_values, grad_gain)


def pass_grads(grad_key, grad_value):
    return (
        passed_along(grad_key.astype(jnp.bfloat16), "blk", 1).astype(grad_key.dtype),
        passed_along(grad_value.astype(jnp.bfloat16), "blk", 1).astype(grad_value.dtype),
    )


def local(
    bytes_in,
    flags,
    lengths,
    cotangent,
    w_query,
    w_key,
    w_value,
    w_out,
    w_up,
    w_down,
    gain_attn,
    gain_ffn,
):
    blocks = lax.axis_size("blk")
    own_index = lax.axis_index("blk")
    seg_rows = cotangent.shape[0]
    byte_rows = bytes_in.shape[0]
    features = bytes_in.shape[1]
    scale = HEAD_DIM ** (-0.5)
    running = jnp.cumsum(flags)
    slot_of = running - 1
    seg_count = running[-1]
    slot_ids = jnp.arange(seg_rows, dtype=jnp.int32)
    member = (slot_of[None, :] == slot_ids[:, None]).astype(jnp.bfloat16)
    seg_sums = jnp.dot(member, bytes_in, preferred_element_type=jnp.float32)
    seg_tally = jnp.sum(member, axis=1, dtype=jnp.float32)
    leading = slot_of < 0
    tail_sum = jnp.dot(
        leading.astype(jnp.bfloat16)[None, :], bytes_in, preferred_element_type=jnp.float32
    )
    tail_count = jnp.sum(leading.astype(jnp.float32), keepdims=True)
    got_sum, got_count = from_behind((tail_sum, tail_count), "blk", -1)
    last_slot = slot_ids == seg_count - 1
    seg_sums = seg_sums + jnp.where(last_slot[:, None], got_sum, 0.0)
    seg_tally = seg_tally + jnp.where(last_slot, got_count[0], 0.0)
    divisor = jnp.maximum(seg_tally, 1.0)
    pooled = seg_sums / divisor[:, None]
    starts = jnp.cumsum(lengths[0]) - lengths[0]
    byte_at = own_index * byte_rows + jnp.arange(byte_rows, dtype=jnp.int32)
    prior_flags = jnp.sum(
        flags[None, :] * (byte_at[None, :] < starts[:, None]).astype(jnp.int32), axis=1
    )
    all_counts, all_prior = (
        lax.all_gather(seg_count[None], "blk", axis=0, tiled=True),
        lax.all_gather(prior_flags[None, :], "blk", axis=0, tiled=True),
    )
    offsets = jnp.cumsum(all_counts) - all_counts
    seq_first = jnp.sum(all_prior, axis=0)
    dev_ids = jnp.arange(blocks, dtype=jnp.int32)

    def layout(first_row, row_count):
        row_index = first_row + jnp.arange(row_count, dtype=jnp.int32)
        owner_dev = row_index // seg_rows
        within = row_index % seg_rows
        dev_pick = owner_dev[:, None] == dev_ids[None, :]
        dev_base = jnp.sum(jnp.where(dev_pick, offsets[None, :], 0), axis=1)
        dev_have = jnp.sum(jnp.where(dev_pick, all_counts[None, :], 0), axis=1)
        return (dev_base + jnp.minimum(within, dev_have - 1), within < dev_have)

    query_pos, query_live = layout(own_index * seg_rows, seg_rows)
    query_first = jnp.max(
        jnp.where(seq_first[None, :] <= query_pos[:, None], seq_first[None, :], 0), axis=1
    )

    def visible(first_row, row_count):
        key_pos, key_live = layout(first_row, row_count)
        return (
            (key_pos[None, :] <= query_pos[:, None])
            & (key_pos[None, :] >= query_first[:, None])
            & key_live[None, :]
        )

    normed_attn, unit_attn, scale_attn = layer_norm_parts(pooled, gain_attn)
    n_one = normed_attn.astype(jnp.bfloat16)
    query_pre = jnp.dot(n_one, w_query, preferred_element_type=jnp.float32)
    query_rot = rotate(query_pre.reshape(seg_rows, HEADS, HEAD_DIM), query_pos, 1.0).astype(
        jnp.bfloat16
    )
    key_pre = jnp.dot(n_one, w_key, preferred_element_type=jnp.float32)
    key_rot = (
        rotate(key_pre.reshape(seg_rows, HEADS, HEAD_DIM), query_pos, 1.0)
        .reshape(seg_rows, features)
        .astype(jnp.bfloat16)
    )
    value_low = jnp.dot(n_one, w_value, preferred_element_type=jnp.float32).astype(jnp.bfloat16)
    start_state = (
        jnp.full((HEADS, seg_rows), NEGATIVE, jnp.float32),
        jnp.zeros((HEADS, seg_rows), jnp.float32),
        jnp.zeros((seg_rows, HEADS, HEAD_DIM), jnp.float32),
    )
    key_piece = lax.all_gather(key_rot, "blk", axis=0, tiled=True)
    value_piece = lax.all_gather(value_low, "blk", axis=0, tiled=True)
    row_count = key_piece.shape[0]
    allowed = visible(jnp.int32(0), row_count)

    def absorb_update(running_state):
        row_max, row_sum, weighted = running_state
        scores = (
            jnp.einsum(
                "qhe,khe->hqk",
                query_rot,
                key_piece.reshape(row_count, HEADS, HEAD_DIM),
                preferred_element_type=jnp.float32,
            )
            * scale
        )
        scores = jnp.where(allowed[None], scores, NEGATIVE)
        new_max = jnp.maximum(row_max, jnp.max(scores, axis=-1))
        weights = jnp.where(allowed[None], jnp.exp(scores - new_max[:, :, None]), 0.0)
        shrink = jnp.exp(row_max - new_max)
        row_sum = jnp.sum(weights, axis=-1)
        weighted = weighted * shrink.T[:, :, None] + jnp.einsum(
            "hqk,khe->qhe",
            weights.astype(jnp.bfloat16),
            value_piece.reshape(row_count, HEADS, HEAD_DIM),
            preferred_element_type=jnp.float32,
        )
        return (new_max, row_sum, weighted)

    row_max, row_sum, weighted = lax.cond(
        jnp.any(allowed), absorb_update, lambda unchanged: unchanged, start_state
    )
    log_total = row_max + jnp.log(row_sum)
    attended_full = weighted / row_sum.T[:, :, None]
    attended = attended_full.reshape(seg_rows, features).astype(jnp.bfloat16)
    middle = pooled + jnp.dot(attended, w_out, preferred_element_type=jnp.float32)
    normed_ffn, unit_ffn, scale_ffn = layer_norm_parts(middle, gain_ffn)
    n_two = normed_ffn.astype(jnp.bfloat16)
    up_proj = jnp.dot(n_two, w_up, preferred_element_type=jnp.float32)
    act_full, gelu_back = jax.vjp(lambda inner: jax.nn.gelu(inner, approximate=False), up_proj)
    act_low = act_full.astype(jnp.bfloat16)
    result = middle + jnp.dot(act_low, w_down, preferred_element_type=jnp.float32)
    live_rows = query_live.astype(jnp.float32)[:, None]
    output = result * live_rows
    grad_out = cotangent * live_rows
    grad_branch = grad_out.astype(jnp.bfloat16)
    grad_w_down = jnp.einsum("sf,sd->fd", act_low, grad_branch, preferred_element_type=jnp.float32)
    grad_act = jnp.einsum("sd,fd->sf", grad_branch, w_down, preferred_element_type=jnp.float32)
    grad_up = gelu_back(grad_act)[0].astype(jnp.bfloat16)
    grad_w_up = jnp.einsum("sd,sf->df", n_two, grad_up, preferred_element_type=jnp.float32)
    grad_n_two = jnp.einsum("sf,df->sd", grad_up, w_up, preferred_element_type=jnp.float32)
    grad_mid_norm, grad_gain_ffn = layer_norm_back(grad_n_two, unit_ffn, scale_ffn, gain_ffn)
    grad_middle = grad_out + grad_mid_norm
    grad_attn_branch = grad_middle.astype(jnp.bfloat16)
    grad_w_out = jnp.einsum(
        "sd,se->de", attended, grad_attn_branch, preferred_element_type=jnp.float32
    )
    grad_attended = jnp.einsum(
        "se,de->sd", grad_attn_branch, w_out, preferred_element_type=jnp.float32
    ).astype(jnp.bfloat16)
    grad_att_three = grad_attended.reshape(seg_rows, HEADS, HEAD_DIM)
    row_dot = jnp.sum(grad_att_three.astype(jnp.float32) * attended_full, axis=-1).T

    def block_grads(key_piece, value_piece, source, grad_parts):
        allowed = visible(source * seg_rows, seg_rows)

        def block_update(grad_parts):
            grad_key, grad_value, grad_query = grad_parts
            key_three = key_piece.reshape(seg_rows, HEADS, HEAD_DIM)
            value_three = value_piece.reshape(seg_rows, HEADS, HEAD_DIM)
            scores = (
                jnp.einsum("qhe,khe->hqk", query_rot, key_three, preferred_element_type=jnp.float32)
                * scale
            )
            prob_full = jnp.where(allowed[None], jnp.exp(scores - log_total[:, :, None]), 0.0)
            grad_value = grad_value + jnp.einsum(
                "hqk,qhe->khe",
                prob_full.astype(jnp.bfloat16),
                grad_att_three,
                preferred_element_type=jnp.float32,
            ).reshape(seg_rows, features)
            grad_prob = jnp.einsum(
                "qhe,khe->hqk", grad_att_three, value_three, preferred_element_type=jnp.float32
            )
            grad_scores = (prob_full * (grad_prob - row_dot[:, :, None])).astype(jnp.bfloat16)
            grad_query = (
                grad_query
                + jnp.einsum(
                    "hqk,khe->qhe", grad_scores, key_three, preferred_element_type=jnp.float32
                )
                * scale
            )
            grad_key = grad_key + (
                jnp.einsum(
                    "hqk,qhe->khe", grad_scores, query_rot, preferred_element_type=jnp.float32
                )
                * scale
            ).reshape(seg_rows, features)
            return (grad_key, grad_value, grad_query)

        return lax.cond(jnp.any(allowed), block_update, lambda unchanged: unchanged, grad_parts)

    zero_rows = jnp.zeros((seg_rows, features), jnp.float32)
    zero_query = jnp.zeros((seg_rows, HEADS, HEAD_DIM), jnp.float32)

    def visit(visit_no, loop_state):
        key_piece, value_piece, grad_key, grad_value, grad_query = loop_state
        source = (own_index - visit_no) % blocks
        grad_key, grad_value, grad_query = block_grads(
            key_piece, value_piece, source, (grad_key, grad_value, grad_query)
        )
        key_piece, value_piece = from_behind((key_piece, value_piece), "blk", 1)
        grad_key, grad_value = pass_grads(grad_key, grad_value)
        return (key_piece, value_piece, grad_key, grad_value, grad_query)

    loop_out = lax.fori_loop(
        0, blocks, visit, (key_rot, value_low, zero_rows, zero_rows, zero_query)
    )
    grad_key_sum, grad_value_sum, grad_query_rot = (loop_out[2], loop_out[3], loop_out[4])
    grad_query = (
        rotate(grad_query_rot, query_pos, -1.0).reshape(seg_rows, features).astype(jnp.bfloat16)
    )
    grad_key = (
        rotate(grad_key_sum.reshape(seg_rows, HEADS, HEAD_DIM), query_pos, -1.0)
        .reshape(seg_rows, features)
        .astype(jnp.bfloat16)
    )
    grad_value_low = grad_value_sum.astype(jnp.bfloat16)
    grad_w_query = jnp.einsum("sd,se->de", n_one, grad_query, preferred_element_type=jnp.float32)
    grad_w_key = jnp.einsum("sd,se->de", n_one, grad_key, preferred_element_type=jnp.float32)
    grad_w_value = jnp.einsum(
        "sd,se->de", n_one, grad_value_low, preferred_element_type=jnp.float32
    )
    grad_n_one = jnp.einsum("se,de->sd", grad_query, w_query, preferred_element_type=jnp.float32)
    grad_n_one = grad_n_one + jnp.einsum(
        "se,de->sd", grad_key, w_key, preferred_element_type=jnp.float32
    )
    grad_n_one = grad_n_one + jnp.einsum(
        "se,de->sd", grad_value_low, w_value, preferred_element_type=jnp.float32
    )
    grad_pool_norm, grad_gain_attn = layer_norm_back(grad_n_one, unit_attn, scale_attn, gain_attn)
    grad_pooled = grad_middle + grad_pool_norm
    grad_sums = (grad_pooled / divisor[:, None]).astype(jnp.bfloat16)
    last_grad = jnp.dot(
        last_slot.astype(jnp.bfloat16)[None, :], grad_sums, preferred_element_type=jnp.float32
    ).astype(jnp.bfloat16)
    came_grad = from_behind(last_grad, "blk", 1)
    spread_rows = jnp.take(grad_sums, jnp.maximum(slot_of, 0), axis=0)
    grad_bytes = jnp.where(leading[:, None], came_grad, spread_rows).astype(jnp.float32)
    (
        grad_w_query,
        grad_w_key,
        grad_w_value,
        grad_w_out,
        grad_w_up,
        grad_w_down,
        grad_gain_attn,
        grad_gain_ffn,
    ) = lax.psum(
        (
            grad_w_query,
            grad_w_key,
            grad_w_value,
            grad_w_out,
            grad_w_up,
            grad_w_down,
            grad_gain_attn,
            grad_gain_ffn,
        ),
        ("dp", "blk"),
    )
    return (
        output,
        grad_bytes,
        grad_w_query,
        grad_w_key,
        grad_w_value,
        grad_w_out,
        grad_w_up,
        grad_w_down,
        grad_gain_attn,
        grad_gain_ffn,
    )


def solution(mesh):
    fits = mesh.shape["blk"] == 4 and mesh.shape["dp"] == 8
    return jax.shard_map(
        fast_local if fits else local,
        mesh=mesh,
        in_specs=(
            P(("dp", "blk"), None),
            P(("dp", "blk")),
            P("dp", None),
            P(("dp", "blk"), None),
            P(),
            P(),
            P(),
            P(),
            P(),
            P(),
            P(),
            P(),
        ),
        out_specs=(
            P(("dp", "blk"), None),
            P(("dp", "blk"), None),
            P(),
            P(),
            P(),
            P(),
            P(),
            P(),
            P(),
            P(),
        ),
        check_vma=False,
    )
```

```python
import functools
import math

import jax
import jax.numpy as jnp
import numpy as np
from jax import lax
from jax.experimental import pallas as pl
from jax.experimental.pallas import tpu as pltpu
from jax.sharding import PartitionSpec as P

HEADS = 8
HEAD_DIM = 64
EPSILON = 1e-05
ROTARY_BASE = 10000.0
NEGATIVE = -1e30
LOG2E = math.log2(math.e)

MESH = pl.DeviceIdType.MESH
F32 = jnp.float32
BF16 = jnp.bfloat16
NN = (((1,), (0,)), ((), ()))
NT = (((1,), (1,)), ((), ()))
TN = (((0,), (0,)), ((), ()))


def mm(a, b, dims):
    return lax.dot_general(a, b, dims, preferred_element_type=F32)


def iota(shape, dim):
    return lax.broadcasted_iota(jnp.int32, shape, dim)


class Copy:
    def __init__(self, src, dst, send_sem, recv_sem, device, cond=None):
        self.parts = (src, dst, send_sem, recv_sem)
        self.device = device
        self.cond = cond

    def _do(self, act):
        def run():
            src, dst, send_sem, recv_sem = self.parts
            act(
                pltpu.make_async_remote_copy(
                    src_ref=src,
                    dst_ref=dst,
                    send_sem=send_sem,
                    recv_sem=recv_sem,
                    device_id=self.device,
                    device_id_type=MESH,
                )
            )

        if self.cond is None:
            run()
        else:
            pl.when(self.cond)(run)

    def start(self):
        self._do(lambda d: d.start())

    def wait_send(self):
        self._do(lambda d: d.wait_send())

    def wait_recv(self):
        self._do(lambda d: d.wait_recv())


CHUNKS = ((0, 4), (4, 9), (9, 12))
SEMS_AR = 22


def layer_kernel(
    bytes_hbm,
    flags_ref,
    lengths_ref,
    cot_hbm,
    wq_hbm,
    wk_hbm,
    wv_hbm,
    wo_hbm,
    wup_hbm,
    wdn_hbm,
    gain_attn_ref,
    gain_ffn_ref,
    freq_ref,
    out_ref,
    gs_ref,
    came_ref,
    slots_ref,
    wgrad_hbm,
    ggain_ref,
    bytes_v,
    weights,
    wup,
    wdn,
    meta,
    tail,
    p_own,
    relay,
    p_all,
    n1,
    k_t,
    v_t,
    q_t,
    tab_c,
    tab_s,
    pos,
    gcol,
    cot_own,
    cot_w,
    o_acc,
    m_sc,
    l_sc,
    att,
    gb,
    hat2,
    d_o,
    d_sc,
    gmid,
    dk,
    dv,
    dq,
    gwqkv,
    big,
    wg,
    r1,
    r2,
    r3,
    r4,
    ppart,
    rc,
    rz,
    gfin,
    out_s,
    out_r,
    rdiv,
    last_s,
    last_r,
    gain_acc,
    gain_s,
    gain_r,
    ss,
    rs,
    ls,
):
    cot_v, acc = hat2, big.at[0]
    dp = lax.axis_index("dp")
    z = lax.axis_index("blk")
    feat = 512
    half = 256
    nblk = 4
    c = lax.rem(dp, 2)
    x = lax.rem(lax.div(dp, 2), 2)
    y = lax.div(dp, 4)
    sib = (dp + 1 - 2 * c, z)
    xnb = (dp + 2 - 4 * x, z)
    ynb = (dp + 4 - 8 * y, z)
    g = lax.div(z, 2)
    zl = lax.rem(z, 2)
    w = 2 * (1 - zl) + c
    zo = 4 * g + 1 - z
    near = 1 + g
    is_near = z == near
    own_worker = g == c

    def dev(core, zz):
        return (dp - c + core, zz)

    counter = {"s": 0, "r": 0, "l": 0}

    def ids(kind, n):
        first = counter[kind]
        counter[kind] = first + n
        return first

    sends = []

    def go(copy):
        copy.start()
        sends.append(copy)

    l_bytes = ids("l", 8)
    rows_chunk = bytes_v.shape[1]
    l_cot = ids("l", 1)
    load_cot = pltpu.make_async_copy(cot_hbm, cot_v, ls.at[l_cot])
    load_cot.start()
    loads_bytes = [
        pltpu.make_async_copy(
            bytes_hbm.at[pl.ds(i * rows_chunk, rows_chunk)], bytes_v.at[i], ls.at[l_bytes + i]
        )
        for i in range(8)
    ]
    for d in loads_bytes:
        d.start()
    l_w = ids("l", 4)
    loads_w = [
        pltpu.make_async_copy(src, weights.at[i], ls.at[l_w + i])
        for i, src in enumerate((wq_hbm, wk_hbm, wv_hbm, wo_hbm))
    ]
    l_f = ids("l", 8)
    loads_f = []
    for j in range(4):
        loads_f.append(
            pltpu.make_async_copy(
                wup_hbm.at[:, pl.ds(j * feat, feat)], wup.at[j], ls.at[l_f + 2 * j]
            )
        )
        loads_f.append(
            pltpu.make_async_copy(
                wdn_hbm.at[pl.ds(j * feat, feat)], wdn.at[j], ls.at[l_f + 2 * j + 1]
            )
        )

    barrier = pltpu.get_barrier_semaphore()
    me_line = c * nblk + z
    line = []
    for k in range(1, 8):
        t = lax.rem(me_line + k, 8)
        line.append((lax.div(t, nblk), lax.rem(t, nblk)))
    for core, zz in line:
        pl.semaphore_signal(barrier, inc=1, device_id=dev(core, zz), device_id_type=MESH)
    for d in (xnb, ynb):
        pl.semaphore_signal(barrier, inc=1, device_id=d, device_id_type=MESH)
    pl.semaphore_wait(barrier, 9)

    meta[c, z, 0:32, :] = flags_ref[...]
    meta[c, z, 32:40, :] = jnp.zeros((8, 128), jnp.int32)
    meta[c, z, 32:33, 0:4] = lengths_ref[...]
    s_meta, r_meta = ids("s", 7), ids("r", 8)
    for k, (core, zz) in enumerate(line):
        go(
            Copy(
                meta.at[c, z],
                meta.at[c, z],
                ss.at[s_meta + k],
                rs.at[r_meta + me_line],
                dev(core, zz),
            )
        )
    s_tail, r_tail = ids("s", 1), ids("r", 1)
    copy_tail = Copy(
        bytes_hbm.at[pl.ds(0, 16)],
        tail,
        ss.at[s_tail],
        rs.at[r_tail],
        (dp, lax.rem(z + nblk - 1, nblk)),
        z > 0,
    )
    go(copy_tail)

    @pl.when(z == nblk - 1)
    def _():
        tail[...] = jnp.zeros_like(tail)

    cnt = jnp.sum(flags_ref[...].astype(F32))
    lane_row = iota((1, feat), 1).astype(F32)
    live_row = jnp.where(lane_row < cnt, 1.0, 0.0)
    for d in loads_w:
        d.start()
    for d in loads_f:
        d.start()

    upper = (iota((128, 128), 0) <= iota((128, 128), 1)).astype(F32).astype(BF16)
    ones_sq = jnp.ones((128, 128), BF16)
    below = (iota((32, 32), 1) < iota((32, 32), 0)).astype(F32).astype(BF16)
    own_flags = flags_ref[...].astype(F32)
    flags_low = own_flags.astype(BF16)
    within = mm(flags_low, upper, NN)
    row_sums = mm(flags_low, ones_sq, NN)
    row_base = mm(below, row_sums.astype(BF16), NN)
    slot_of = within + row_base - 1.0
    slots_ref[...] = slot_of

    acc[...] = jnp.zeros_like(acc)
    rdiv[...] = jnp.zeros_like(rdiv)
    slot_iota = iota((feat, 128), 0).astype(F32)
    ones_rows = jnp.ones((16, feat), BF16)

    cells = rows_chunk // 8
    for k in range(8):
        loads_bytes[k].wait()
        reach = cells * (k + 1)
        member = jnp.concatenate(
            [
                (slot_iota[0:reach] == slot_of[r : r + 1, :]).astype(F32).astype(BF16)
                for r in range(4 * k, 4 * k + 4)
            ],
            axis=1,
        )
        acc[0:reach, :] += mm(member, bytes_v[k], NN)
        rdiv[:, 0:feat] += mm(
            ones_rows,
            jnp.concatenate([member, jnp.zeros((feat - reach, rows_chunk), BF16)], axis=0)
            if reach < feat
            else member,
            NT,
        )

    for i, gain in enumerate((gain_attn_ref, gain_ffn_ref)):
        row = jnp.broadcast_to(gain[...], (128, feat))
        col = row.T
        gcol[i] = jnp.concatenate([col, col], axis=1)

    for core, zz in line:
        Copy(
            meta.at[core, zz],
            meta.at[core, zz],
            ss.at[0],
            rs.at[r_meta + core * nblk + zz],
            sib,
        ).wait_recv()
    Copy(tail, tail, ss.at[0], rs.at[r_tail], sib, z < nblk - 1).wait_recv()
    zn = jnp.minimum(z + 1, nblk - 1)
    next_flags = meta[c, zn, 0:16, :].astype(F32).astype(BF16)
    next_within = mm(next_flags, upper, NN)
    has_next = (z < nblk - 1).astype(F32)
    lead = jnp.where(next_within[0:1, :] < 0.5, 1.0, 0.0) * has_next
    is_last16 = iota((feat, 16), 0).astype(F32) == cnt - 1.0
    member_tail = jnp.where(is_last16, lead[:, 0:16], 0.0).astype(BF16)
    sums = acc[...] + mm(member_tail, tail[...], NN)
    tally = rdiv[0:1, :] + jnp.where(lane_row == cnt - 1.0, jnp.sum(lead), 0.0)
    inverse_tally = 1.0 / jnp.maximum(tally, 1.0)
    rdiv[0:1, :] = inverse_tally
    rdiv[1:2, :] = live_row
    pooled_t = (sums.T * inverse_tally).astype(BF16)
    p_own[0] = pooled_t[:, 0:half]
    p_own[1] = pooled_t[:, half:]

    s_p, r_p, r_relay = ids("s", 22), ids("r", 16), ids("r", 1)
    near_c = 1 + c
    pieces = (pl.ds(0, half), pl.ds(half, half))

    def p_piece(src, hb, piece, slot, device, cond=None):
        at = pieces[piece]
        return Copy(
            src.at[at],
            p_all.at[hb, at],
            ss.at[s_p + slot],
            rs.at[r_p + 2 * hb + piece],
            device,
            cond,
        )

    def p_whole(src, hb, slot, device, cond=None):
        return Copy(src, p_all.at[hb], ss.at[s_p + slot], rs.at[r_p + 2 * hb], device, cond)

    other_worker = jnp.logical_not(own_worker)
    to_pair = z != nblk - 1
    inner = jnp.logical_or(z == 1, z == 2)

    outer = jnp.logical_not(inner)

    def outside_copies(cond):
        own_out = jnp.logical_and(other_worker, cond)
        relayed = jnp.logical_and(own_worker, cond)
        return [
            p_piece(p_own.at[c], 2 * z + c, i, 4 + i, dev(c, near_c), own_out) for i in range(2)
        ] + [p_piece(relay, 2 * z + c, i, 4 + i, dev(c, 2 - c), relayed) for i in range(2)]

    outside_late = outside_copies(outer)

    go(Copy(p_own.at[1 - c], relay, ss.at[s_p + 3], rs.at[r_relay], sib, other_worker))
    for i in range(2):
        own_pair = jnp.logical_and(own_worker, to_pair)
        go(p_piece(p_own.at[c], 2 * z + c, i, i, dev(c, zo), own_pair))
    go(p_whole(p_own.at[1 - c], 2 * z + 1 - c, 3, sib, own_worker))
    go(p_whole(p_own.at[c], 2 * z + c, 2, sib, own_worker))

    @pl.when(own_worker)
    def _():
        p_all[2 * z] = p_own[0]
        p_all[2 * z + 1] = p_own[1]

    def p_wait(hb, cond=None):
        Copy(p_all.at[hb], p_all.at[hb], ss.at[0], rs.at[r_p + 2 * hb], sib, cond).wait_recv()

    Copy(relay, relay, ss.at[0], rs.at[r_relay], sib, own_worker).wait_recv()
    for one in outside_copies(inner):
        go(one)
    p_wait(2 * z + c, other_worker)
    for i in range(2):
        passed = jnp.logical_and(other_worker, to_pair)
        go(p_piece(p_all.at[2 * z + c], 2 * z + c, i, i, dev(c, zo), passed))
    p_wait(2 * z + 1 - c, other_worker)

    load_cot.wait()
    cot_t = (cot_v[...].T * live_row).astype(BF16)
    cot_own[0] = cot_t[:, 0:half]
    cot_own[1] = cot_t[:, half:]
    lo_here = False
    hi_here = jnp.logical_and(g == c, z >= 2)

    counts = []
    for b in range(nblk):
        counts.append(jnp.sum(meta[g, b, 0:32, :].astype(F32)))
    offsets = [jnp.float32(0.0)]
    for b in range(nblk):
        offsets.append(offsets[-1] + counts[b])
    lens = meta[g, z, 32:40, :].astype(F32)
    first_row = iota((8, 128), 0) == 0
    lane8 = iota((8, 128), 1)
    byte_at = (iota((32, 128), 0) * 128 + iota((32, 128), 1)).astype(F32)
    seq_first = [jnp.float32(0.0)]
    for s in range(1, 4):
        start = jnp.sum(jnp.where(jnp.logical_and(first_row, lane8 < s), lens, 0.0))
        prior = jnp.zeros((32, 128), F32)
        for b in range(nblk):
            prior = prior + jnp.where(
                byte_at + float(b * 4096) < start, meta[g, b, 0:32, :].astype(F32), 0.0
            )
        seq_first.append(jnp.sum(prior))

    freq = jnp.concatenate([freq_ref[...], freq_ref[...]], axis=1)
    lane_half = iota((1, half), 1).astype(F32)
    for hb in range(8):
        b = hb // 2
        j = lane_half + float((hb % 2) * half)
        p = offsets[b] + jnp.minimum(j, counts[b] - 1.0)
        first = jnp.zeros_like(p)
        for s in range(1, 4):
            first = jnp.maximum(first, jnp.where(p >= seq_first[s], seq_first[s], 0.0))
        pos[hb, 0:1, :] = p
        pos[hb, 1:2, :] = first
        angle = freq * p
        tab_c[hb] = jnp.cos(angle)
        tab_s[hb] = jnp.sin(angle)

    def pick(values, b):
        total = jnp.float32(0.0)
        for i, v in enumerate(values):
            total = total + jnp.where(b == i, v, 0.0)
        return total

    gain_col = gcol[0]

    def norm_parts(values):
        mean = jnp.mean(values, axis=0, keepdims=True)
        center = values - mean
        inverse = lax.rsqrt(jnp.mean(center * center, axis=0, keepdims=True) + EPSILON)
        return center * inverse, inverse

    def turned(values, hb, direction):
        cos = tab_c[hb]
        sin = tab_s[hb] * direction
        parts = []
        for h in range(HEADS):
            a = values[64 * h : 64 * h + 32, :]
            b = values[64 * h + 32 : 64 * h + 64, :]
            parts.append(a * cos - b * sin)
            parts.append(b * cos + a * sin)
        return jnp.concatenate(parts, axis=0).astype(BF16)

    for d in loads_w:
        d.wait()

    def keys_values(hb):
        unit, _ = norm_parts(p_all[hb].astype(F32))
        normed = (unit * gcol[0]).astype(BF16)
        n1[hb] = normed
        k_t[hb] = turned(mm(weights[1], normed, TN), hb, 1.0)
        v_t[hb] = mm(weights[2], normed, TN).astype(BF16)

    s_cot, r_cot = ids("s", 2), ids("r", 2)
    early = z < 2
    slot_to = jnp.where(early, 0, 1)
    chip_to = 2 * c + 1 - jnp.where(early, z, 3 - z)

    def cot_copy(i):
        core_to = jnp.where(early, i, 1 - i)
        here = jnp.logical_and(core_to == c, chip_to == z)
        return here, Copy(
            cot_own.at[i],
            cot_w.at[slot_to],
            ss.at[s_cot + i],
            rs.at[r_cot + slot_to],
            dev(core_to, chip_to),
            jnp.logical_not(here),
        )

    def send_cot():
        for i in range(2):
            here, copy = cot_copy(i)
            copy.start()

            @pl.when(here)
            def _():
                cot_w[slot_to] = cot_own[i]

    hq_of = (w, 7 - w)
    first_far, second_far = 2 - g, 3 - 3 * g
    score_scale = HEAD_DIM ** (-0.5) * LOG2E

    def hq_at(slot):
        return jnp.where(slot == 0, w, 7 - w)

    def bias_of(hq, kb):
        b = lax.div(kb, 2)
        j = (iota((half, half), 0) + lax.rem(kb, 2) * half).astype(F32)
        kpos = j + pick(offsets[:nblk], b)
        alive = j < pick(counts, b)
        qpos = pos[hq, 0:1, :]
        qfirst = pos[hq, 1:2, :]
        allowed = jnp.logical_and(alive, jnp.logical_and(kpos <= qpos, kpos >= qfirst))
        return jnp.where(allowed, 0.0, NEGATIVE)

    o_acc[...] = jnp.zeros_like(o_acc)
    l_sc[...] = jnp.zeros_like(l_sc)
    m_sc[...] = jnp.full(m_sc.shape, NEGATIVE, F32)

    def s_at(h):
        return gwqkv.at[h // 4, pl.ds(half * ((h // 2) % 2), half), pl.ds(half * (h % 2), half)]

    o_new = big.at[1, :, pl.ds(0, half)]

    def forward_step(slot, kb):
        hq = hq_at(slot)
        bias = bias_of(hq, kb)
        old = m_sc[slot]
        old_sum = l_sc[slot]
        for h in range(HEADS):
            part = slice(64 * h, 64 * h + 64)
            s_at(h)[...] = mm(k_t[kb, part, :], q_t[slot, part, :], TN)
        tops, sums = [], []
        for h in range(HEADS):
            part = slice(64 * h, 64 * h + 64)
            s = s_at(h)[...] * score_scale + bias
            top = jnp.maximum(old[h : h + 1, :], jnp.max(s, axis=0, keepdims=True))
            prob = jnp.exp2(s - top)
            tops.append(top)
            sums.append(jnp.sum(prob, axis=0, keepdims=True))
            o_new[part, :] = mm(v_t[kb, part, :], prob.astype(BF16), NN)
        new = jnp.concatenate(tops, axis=0)
        shrink = jnp.exp2(old - new)
        m_sc[slot] = new
        l_sc[slot] = old_sum * shrink + jnp.concatenate(sums, axis=0)
        for h in range(HEADS):
            part = slice(64 * h, 64 * h + 64)
            o_acc[slot, part, :] = o_acc[slot, part, :] * shrink[h : h + 1, :] + o_new[part, :]

    def block_nth(n):
        swapped = jnp.where(n < 2, 1 - n, n)
        return jnp.where(z == 0, n, jnp.where(z == 1, swapped, z - n))

    def pass_on(block, slot, cond, onward=None):
        hb = 2 * block + c

        @pl.when(cond)
        def _():
            for i in range(2):
                there = p_all.at[hb, pieces[i]]
                Copy(there, there, ss.at[0], rs.at[r_p + 2 * hb + i], sib).wait_recv()
                if onward is not None:
                    p_piece(p_all.at[hb], hb, i, slot + 2 + i, dev(c, zo), onward).start()
                p_piece(p_all.at[hb], hb, i, slot + i, sib).start()

    def pass_on_sent():
        for block, slot, cond, onward in passes:
            hb = 2 * block + c

            @pl.when(cond)
            def _(hb=hb, slot=slot, onward=onward):
                for i in range(2):
                    if onward is not None:
                        p_piece(p_all.at[hb], hb, i, slot + 2 + i, dev(c, zo), onward).wait_send()
                    p_piece(p_all.at[hb], hb, i, slot + i, sib).wait_send()

    second_near = z == 2
    passes = (
        (zo, 6, z != 2),
        (first_far, 8, is_near, is_near),
        (first_far, 12, jnp.logical_not(is_near)),
        (second_far, 14, second_near, second_near),
        (second_far, 18, zl == 1),
    )
    passes = tuple(p if len(p) == 4 else p + (None,) for p in passes)

    def arrival(n, carry):
        block = block_nth(n)

        @pl.when(n == 1)
        def _():
            for one in outside_late:
                one.start()
            pass_on(*passes[0])
            pass_on(*passes[1])

        @pl.when(n == 2)
        def _():
            pass_on(*passes[2])
            pass_on(*passes[3])

        @pl.when(n == 3)
        def _():
            pass_on(*passes[4])
            send_cot()

        @pl.when(jnp.logical_and(n > 0, n < 3 + zl))
        def _():
            for i in range(2):
                there = p_all.at[2 * block + 1 - c, pieces[i]]
                Copy(
                    there, there, ss.at[0], rs.at[r_p + 2 * (2 * block + 1 - c) + i], sib
                ).wait_recv()

        @pl.when(n < 3 + zl)
        def _():
            def one(i, carry):
                keys_values(2 * block + i)
                return carry

            lax.fori_loop(0, 2, one, 0)

            def query(slot, carry):
                hq = hq_at(slot)

                @pl.when(lax.div(hq, 2) == block)
                def _():
                    q_t[slot] = turned(mm(weights[0], n1[hq], TN), hq, 1.0)

                return carry

            lax.fori_loop(0, 2, query, 0)

            def pair(i, carry):
                slot, kb = lax.div(i, 8), lax.rem(i, 8)
                hq = hq_at(slot)
                q_block, k_block = lax.div(hq, 2), lax.div(kb, 2)

                def came_by(b, m):
                    found = block_nth(0) == b
                    for k in range(1, 4):
                        found = jnp.logical_or(
                            found, jnp.logical_and(block_nth(k) == b, k <= m)
                        )
                    return found

                new_query = jnp.logical_and(q_block == block, came_by(k_block, n))
                new_keys = jnp.logical_and(k_block == block, came_by(q_block, n))
                new = jnp.logical_or(new_query, new_keys)

                @pl.when(jnp.logical_and(kb <= hq, new))
                def _():
                    forward_step(slot, kb)

                return carry

            lax.fori_loop(0, 16, pair, 0)

        return carry

    lax.fori_loop(0, 4, arrival, 0)

    for slot in range(2):
        total = l_sc[slot]
        for h in range(HEADS):
            part = slice(64 * h, 64 * h + 64)
            o_acc[slot, part, :] = o_acc[slot, part, :] * (1.0 / total[h : h + 1, :])
        att[:, slot * half : (slot + 1) * half] = o_acc[slot].astype(BF16)
        m_sc[slot] = m_sc[slot] + jnp.log2(total)

    own_pooled = jnp.concatenate([p_all[hq_of[0]], p_all[hq_of[1]]], axis=1).astype(F32)
    middle = own_pooled + mm(weights[3], att[...], TN)
    unit2, inverse2 = norm_parts(middle)
    hat2[...] = unit2
    gain_col2 = jnp.concatenate([gcol[1], gcol[1]], axis=1)
    n2 = (unit2 * gain_col2).astype(BF16)
    big[0] = middle
    big[1] = jnp.zeros((feat, feat), F32)
    n2_ref = d_o
    n2_ref[...] = n2

    base1 = c * 256
    keep2x, give2x = base1 + x * 128, base1 + (1 - x) * 128
    keep2y, give2y = base1 + y * 128, base1 + (1 - y) * 128
    keep3x, give3x = keep2x + y * 64, keep2x + (1 - y) * 64
    keep3y, give3y = keep2y + x * 64, keep2y + (1 - x) * 64
    lanes_x, lanes_y = pl.ds(0, 256), pl.ds(256, 256)

    def rows_of(first, n):
        return pl.ds(pl.multiple_of(first, 16), n)

    class Reduce:
        def __init__(self, chunk):
            self.b0, self.b1 = CHUNKS[chunk]
            self.nb = self.b1 - self.b0
            self.s0, self.r0 = ids("s", SEMS_AR), ids("r", SEMS_AR)
            self.blocks = pl.ds(self.b0, self.nb)
            self.phases = {}

        def _w(self, first, n, lanes):
            return wg.at[self.blocks, rows_of(first, n), lanes]

        def _list(self, phase):
            every = pl.ds(0, 512)
            b, s0, r0 = self.blocks, self.s0, self.r0

            def copy(i, src, dst, device):
                return Copy(src, dst, ss.at[s0 + i], rs.at[r0 + i], device)

            if phase == 1:
                return [copy(0, self._w((1 - c) * 256, 256, every), r1.at[b], sib)]
            if phase == 2:
                return [
                    copy(1, self._w(give2x, 128, lanes_x), r2.at[b, :, lanes_x], xnb),
                    copy(2, self._w(give2y, 128, lanes_y), r2.at[b, :, lanes_y], ynb),
                ]
            if phase == 3:
                return [
                    copy(3, self._w(give3x, 64, lanes_x), r3.at[b, :, lanes_x], ynb),
                    copy(4, self._w(give3y, 64, lanes_y), r3.at[b, :, lanes_y], xnb),
                ]
            if phase == 4:
                out = []
                for k in range(1, 4):
                    zt = lax.rem(z + k, nblk)
                    out.append(
                        copy(
                            3 + 2 * k,
                            self._w(keep3x + 16 * zt, 16, lanes_x),
                            r4.at[k - 1, b, :, lanes_x],
                            (dp, zt),
                        )
                    )
                    out.append(
                        copy(
                            4 + 2 * k,
                            self._w(keep3y + 16 * zt, 16, lanes_y),
                            r4.at[k - 1, b, :, lanes_y],
                            (dp, zt),
                        )
                    )
                return out
            if phase == 5:
                out = []
                for k in range(1, 4):
                    zt = lax.rem(z + k, nblk)
                    for i, (keep, lanes) in enumerate(((keep3x, lanes_x), (keep3y, lanes_y))):
                        mine = self._f(keep + 16 * z, 16, lanes)
                        out.append(copy(9 + 2 * k + i, mine, mine, (dp, zt)))
                return out
            if phase == 6:
                mine_x, mine_y = self._f(keep3x, 64, lanes_x), self._f(keep3y, 64, lanes_y)
                return [copy(17, mine_x, mine_x, ynb), copy(18, mine_y, mine_y, xnb)]
            if phase == 7:
                mine_x, mine_y = self._f(keep2x, 128, lanes_x), self._f(keep2y, 128, lanes_y)
                return [copy(19, mine_x, mine_x, xnb), copy(20, mine_y, mine_y, ynb)]
            return [copy(21, r1.at[b], self._out(base1), sib)]

        def _f(self, first, n, lanes):
            return r1.at[self.blocks, rows_of(first - base1, n), lanes]

        def _out(self, first):
            return wgrad_hbm.at[self.blocks, rows_of(first, 256), pl.ds(0, 512)]

        def start(self, phase):
            for one in self._list(phase):
                one.start()

        def finish(self, phase):
            if phase == 8:
                other = self._out((1 - c) * 256)
                Copy(other, other, ss.at[0], rs.at[self.r0 + 21], sib).wait_recv()
                return
            for one in self._list(phase):
                one.wait_recv()
            if phase > 4:
                return

            def add(i, carry):
                b = self.b0 + i
                if phase == 1:
                    here = (b, rows_of(base1, 256), slice(None))
                    wg[here] = wg[here] + r1[b]
                if phase == 2:
                    for keep, lo in ((keep2x, 0), (keep2y, 256)):
                        here = (b, rows_of(keep, 128), slice(lo, lo + 256))
                        wg[here] = wg[here] + r2[b, :, lo : lo + 256]
                if phase == 3:
                    for keep, lo in ((keep3x, 0), (keep3y, 256)):
                        here = (b, rows_of(keep, 64), slice(lo, lo + 256))
                        wg[here] = wg[here] + r3[b, :, lo : lo + 256]
                if phase == 4:
                    for keep, lo in ((keep3x, 0), (keep3y, 256)):
                        here = (b, rows_of(keep + 16 * z, 16), slice(lo, lo + 256))
                        total = wg[here].astype(F32)
                        for k in range(3):
                            total = total + r4[k, b, :, lo : lo + 256].astype(F32)
                        r1[b, rows_of(keep - base1 + 16 * z, 16), lo : lo + 256] = total.astype(BF16)
                return carry

            lax.fori_loop(0, self.nb, add, 0)

        def step(self, phase):
            self.finish(phase)
            if phase < 8:
                self.start(phase + 1)
            if phase == 7:
                self.store().start()

        def store(self):
            return pltpu.make_async_copy(r1.at[self.blocks], self._out(base1), ls.at[self.store_sem])

        def wait_sends(self):
            for phase in range(1, 9):
                for one in self._list(phase):
                    one.wait_send()

    red = [Reduce(i) for i in range(3)]
    for one in red:
        one.store_sem = ids("l", 1)

    for d in loads_f:
        d.wait()

    def ffn_forward(j, carry):
        up = mm(wup[j], n2_ref[...], TN)
        size = jnp.abs(up) * (0.5**0.5)
        t = 1.0 / (1.0 + 0.3275911 * size)
        poly = t * (
            0.254829592
            + t * (-0.284496736 + t * (1.421413741 + t * (-1.453152027 + t * 1.061405429)))
        )
        decay = jnp.exp(-0.5 * up * up)
        far = 0.5 * poly * decay
        phi = jnp.where(up < 0.0, far, 1.0 - far)
        slope = phi + up * decay * (1.0 / math.sqrt(2.0 * math.pi))
        act = (up * phi).astype(BF16)
        bytes_v[j] = act
        bytes_v[4 + j] = slope.astype(BF16)
        big[0] += mm(wdn[j], act, TN)
        return carry

    lax.fori_loop(0, 4, ffn_forward, 0)

    Copy(cot_w.at[0], cot_w.at[0], ss.at[0], rs.at[r_cot], sib).wait_recv()
    Copy(cot_w.at[1], cot_w.at[1], ss.at[0], rs.at[r_cot + 1], sib, jnp.logical_not(hi_here)).wait_recv()
    gb[...] = jnp.concatenate([cot_w[0], cot_w[1]], axis=1)

    def ffn_backward(j, carry):
        wg[2 * j] = mm(bytes_v[j], gb[...], NT).astype(BF16)
        grad_up = (mm(wdn[j], gb[...], NN) * bytes_v[4 + j].astype(F32)).astype(BF16)
        wg[2 * j + 1] = mm(n2_ref[...], grad_up, NT).astype(BF16)
        big[1] += mm(wup[j], grad_up, NN)

        @pl.when(j == 1)
        def _():
            red[0].start(1)

        return carry

    lax.fori_loop(0, 4, ffn_backward, 0)
    red[0].step(1)

    s_out, r_out = ids("s", 2), ids("r", 2)
    res = big[0].astype(BF16)
    owners = ((1 - zl, c, lo_here), (2 + zl, 1 - c, hi_here))
    for slot, (chip, i, here) in enumerate(owners):
        out_s[slot] = res[:, slot * half : (slot + 1) * half]
        go(
            Copy(
                out_s.at[slot],
                out_r.at[i],
                ss.at[s_out + slot],
                rs.at[r_out + i],
                dev(g, chip),
                None if here is False else jnp.logical_not(here),
            )
        )
        if here is not False:

            @pl.when(here)
            def _():
                out_r[i] = out_s[slot]

    grad_n2 = big[1]
    unit2 = hat2[...]
    product = grad_n2 * unit2

    def lane_fold(values):
        total = values[:, 0:128]
        for k in range(1, values.shape[1] // 128):
            total = total + values[:, 128 * k : 128 * (k + 1)]
        return total

    gain_acc[1] = lane_fold(product)
    e = grad_n2 * gain_col2
    grad_mid = gb[...].astype(F32) + inverse2 * (
        e
        - jnp.mean(e, axis=0, keepdims=True)
        - unit2 * jnp.mean(e * unit2, axis=0, keepdims=True)
    )
    gmid[0] = grad_mid[:, 0:half]
    gmid[1] = grad_mid[:, half:]
    branch = grad_mid.astype(BF16)
    wg[8] = mm(att[...], branch, NT).astype(BF16)
    red[1].start(1)
    grad_att = mm(weights[3], branch, NN)
    d_o[...] = grad_att.astype(BF16)
    for slot in range(2):
        lanes = slice(slot * half, (slot + 1) * half)
        both = d_o[:, lanes].astype(F32) * o_acc[slot]
        for h in range(HEADS):
            d_sc[slot, h : h + 1, :] = jnp.sum(
                both[64 * h : 64 * h + 64, :], axis=0, keepdims=True
            )

    dq[...] = jnp.zeros_like(dq)
    gwqkv[...] = jnp.zeros_like(gwqkv)
    gain_acc[0] = jnp.zeros((feat, 128), F32)
    s_rc, r_rc = ids("s", 4), ids("r", 4)
    s_rz, r_rz = ids("s", 4), ids("r", 4)
    s_fin, r_fin = ids("s", 4), ids("r", 2)

    def sd_at(which, h):
        return big.at[which, pl.ds(half * ((h // 2) % 2), half), pl.ds(half * (h % 2), half)]

    def backward_step(slot, kb):
        hq = hq_at(slot)
        bias = bias_of(hq, kb)
        lanes = pl.ds(pl.multiple_of(slot * half, half), half)
        lse = m_sc[slot]
        dots = d_sc[slot]
        for first in (0, 4):
            for h in range(first, first + 4):
                part = slice(64 * h, 64 * h + 64)
                grad_o = d_o[part, lanes]
                sd_at(0, h)[...] = mm(k_t[kb, part, :], q_t[slot, part, :], TN)
                sd_at(1, h)[...] = mm(v_t[kb, part, :], grad_o, TN)
            for h in range(first, first + 4):
                part = slice(64 * h, 64 * h + 64)
                prob = jnp.exp2(sd_at(0, h)[...] * score_scale + bias - lse[h : h + 1, :])
                grad_s = (prob * (sd_at(1, h)[...] - dots[h : h + 1, :])).astype(BF16)
                dv[part, :] += mm(d_o[part, lanes], prob.astype(BF16), NT)
                dk[part, :] += mm(q_t[slot, part, :], grad_s, NT)
                dq[slot, part, :] += mm(k_t[kb, part, :], grad_s, NN)

    att_scale = HEAD_DIM ** (-0.5)

    def rc_copy(kb):
        zb = lax.div(kb, 2)
        return Copy(
            ppart.at[kb],
            rc.at[zb],
            ss.at[s_rc + zb],
            rs.at[r_rc + zb],
            sib,
            lax.rem(kb, 2) != c,
        )

    def is_final(zb):
        return jnp.where(lax.div(zb, 2) == g, z == zb, is_near)

    def rz_copy(zb):
        return Copy(
            ppart.at[2 * zb + c],
            rz.at[zb],
            ss.at[s_rz + zb],
            rs.at[r_rz + zb],
            dev(c, zo),
            jnp.logical_and(jnp.logical_not(is_final(zb)), zb < nblk - 1),
        )

    def fin_copy(zb):
        here = jnp.logical_and(zb == z, g == c)
        return Copy(
            ppart.at[2 * zb + c],
            gfin.at[c],
            ss.at[s_fin + zb],
            rs.at[r_fin + c],
            dev(g, zb),
            jnp.logical_and(is_final(zb), jnp.logical_not(here)),
        )

    def combine(zb):
        kb = 2 * zb + c
        Copy(rc.at[zb], rc.at[zb], ss.at[0], rs.at[r_rc + zb], sib).wait_recv()
        ppart[kb] = ppart[kb] + rc[zb]
        rz_copy(zb).start()

    def deliver(zb):
        kb = 2 * zb + c
        final = jnp.logical_and(is_final(zb), zb < nblk - 1)
        Copy(rz.at[zb], rz.at[zb], ss.at[0], rs.at[r_rz + zb], sib, final).wait_recv()

        @pl.when(final)
        def _():
            ppart[kb] = ppart[kb] + rz[zb]

        @pl.when(jnp.logical_and(zb == z, g == c))
        def _():
            gfin[c] = ppart[kb]

        fin_copy(zb).start()

    def ticks(at, schedule):
        for i, todo in schedule.items():

            @pl.when(at == i)
            def _():
                for chunk, phase in todo:
                    red[chunk].step(phase)

    def key_block(kb, carry):
        @pl.when(kb <= 7 - w)
        def _():
            dk[...] = jnp.zeros_like(dk)
            dv[...] = jnp.zeros_like(dv)

            def one(i, carry):
                backward_step(1 - i, kb)
                return carry

            lax.fori_loop(0, jnp.where(kb <= w, 2, 1), one, 0)
            grad_key = turned(dk[...] * att_scale, kb, -1.0)
            grad_value = dv[...].astype(BF16)
            normed = n1[kb]
            k_t[kb] = grad_key
            v_t[kb] = grad_value
            gwqkv[1] += mm(normed, grad_key, NT)
            gwqkv[2] += mm(normed, grad_value, NT)

            @pl.when(jnp.logical_or(kb == w, kb == 7 - w))
            def _():
                slot = jnp.where(kb == w, 0, 1)
                grad_query = turned(dq[slot] * att_scale, kb, -1.0)
                q_t[slot] = grad_query
                gwqkv[0] += mm(normed, grad_query, NT)

        ticks(
            kb,
            {
                0: [(1, 1)],
                1: [(0, 2)],
                2: [(0, 3)],
                3: [(1, 2)],
                4: [(0, 4)],
                5: [(1, 3)],
                6: [(0, 5)],
                7: [(0, 6)],
            },
        )
        return carry

    lax.fori_loop(0, 8, key_block, 0)
    for i in range(3):
        wg[9 + i] = gwqkv[i].astype(BF16)
    red[2].start(1)

    def block_at(j):
        return jnp.where(g == 0, 3 - j, j)

    def row_block(i, carry):
        j = lax.div(i, 2)
        kb = 2 * block_at(j) + lax.rem(i, 2)

        @pl.when(kb <= 7 - w)
        def _():
            big[0, :, 0:half] = mm(weights[1], k_t[kb], NN) + mm(weights[2], v_t[kb], NN)
            own = jnp.logical_or(kb == w, kb == 7 - w)
            slot = jnp.where(kb == w, 0, 1)

            @pl.when(own)
            def _():
                big[0, :, 0:half] += mm(weights[0], q_t[slot], NN)

            grad_n1 = big[0, :, 0:half]
            unit, inverse = norm_parts(p_all[kb].astype(F32))
            gain_acc[0] += lane_fold(grad_n1 * unit)
            e = grad_n1 * gcol[0]
            total = inverse * (
                e
                - jnp.mean(e, axis=0, keepdims=True)
                - unit * jnp.mean(e * unit, axis=0, keepdims=True)
            )
            ppart[kb] = (total + jnp.where(own, 1.0, 0.0) * gmid[slot]).astype(BF16)

        @pl.when(kb > 7 - w)
        def _():
            ppart[kb] = jnp.zeros(ppart.shape[1:], BF16)

        rc_copy(kb).start()

        @pl.when(lax.rem(i, 2) == 1)
        def _():
            combine(block_at(j))

        @pl.when(jnp.logical_and(lax.rem(i, 2) == 1, i > 1))
        def _():
            deliver(block_at(j - 1))

        ticks(
            i,
            {
                0: [(2, 1)],
                1: [(1, 4)],
                2: [(0, 7)],
                3: [(2, 2)],
                4: [(1, 5)],
                5: [(0, 8)],
                6: [(2, 3)],
                7: [(1, 6)],
            },
        )
        return carry

    lax.fori_loop(0, 8, row_block, 0)

    for i in range(2):
        gain_s[0, i : i + 1, :] = jnp.sum(gain_acc[i].T, axis=0, keepdims=True)
    gain_s[0, 2:8, :] = jnp.zeros((6, feat), F32)
    s_gain, r_gain = ids("s", 6), ids("r", 6)

    def gain_list(phase):
        if phase < 4:
            device = (sib, xnb, ynb)[phase - 1]
            k = phase - 1
            return [
                Copy(gain_s.at[k], gain_r.at[k], ss.at[s_gain + k], rs.at[r_gain + k], device)
            ]
        return [
            Copy(
                gain_s.at[3],
                gain_r.at[2 + k],
                ss.at[s_gain + 2 + k],
                rs.at[r_gain + 2 + k],
                (dp, lax.rem(z + k, nblk)),
            )
            for k in range(1, 4)
        ]

    def gain_finish(phase):
        for one in gain_list(phase):
            one.wait_recv()
        if phase < 4:
            gain_s[phase] = gain_s[phase - 1] + gain_r[phase - 1]
            for one in gain_list(phase + 1):
                one.start()
        else:
            total = jnp.zeros((8, feat), F32)
            for zz in range(nblk):
                k = lax.rem(z - zz + nblk, nblk)
                part = gain_s[3]
                for i in range(1, 4):
                    part = jnp.where(k == i, gain_r[2 + i], part)
                total = total + part
            ggain_ref[...] = total

    gain_list(1)[0].start()
    red[2].step(4)
    deliver(block_at(3))
    gain_finish(1)
    red[1].step(7)

    for i in range(2):
        mine = out_from_self(i, c, z)
        Copy(
            out_r.at[i], out_r.at[i], ss.at[0], rs.at[r_out + i], sib, jnp.logical_not(mine)
        ).wait_recv()
        live = rdiv[1:2, i * half : (i + 1) * half]
        out_ref[i * half : (i + 1) * half, :] = (out_r[i].astype(F32) * live).T.astype(BF16)

    gain_finish(2)
    red[2].step(5)

    for i in range(2):
        mine = jnp.logical_and(own_worker, c == i)
        Copy(
            gfin.at[i], gfin.at[i], ss.at[0], rs.at[r_fin + i], sib, jnp.logical_not(mine)
        ).wait_recv()
        grad_sums = gfin[i].astype(F32) * rdiv[0:1, i * half : (i + 1) * half]
        gs_ref[i * half : (i + 1) * half, :] = grad_sums.T.astype(BF16)

    is_last = jnp.where(iota((16, feat), 1).astype(F32) == cnt - 1.0, 1.0, 0.0).astype(BF16)
    last_s[...] = mm(is_last, gs_ref[...], NN).astype(BF16)
    s_last, r_last = ids("s", 1), ids("r", 1)
    copy_last = Copy(
        last_s,
        last_r,
        ss.at[s_last],
        rs.at[r_last],
        (dp, lax.rem(z + 1, nblk)),
        z < nblk - 1,
    )
    go(copy_last)

    red[1].step(8)
    gain_finish(3)
    red[2].step(6)
    gain_finish(4)
    Copy(last_r, last_r, ss.at[0], rs.at[r_last], sib, z > 0).wait_recv()

    @pl.when(z == 0)
    def _():
        last_r[...] = jnp.zeros_like(last_r)

    came_ref[...] = last_r[...]
    for phase in range(7, 9):
        red[2].step(phase)

    for one in sends:
        one.wait_send()
    pass_on_sent()
    for one in outside_late:
        one.wait_send()
    for i in range(2):
        cot_copy(i)[1].wait_send()

    def close_key(kb, carry):
        rc_copy(kb).wait_send()
        return carry

    lax.fori_loop(0, 8, close_key, 0)

    def close_block(zb, carry):
        rz_copy(zb).wait_send()
        fin_copy(zb).wait_send()
        return carry

    lax.fori_loop(0, 4, close_block, 0)
    for phase in range(1, 5):
        for one in gain_list(phase):
            one.wait_send()
    for one in red:
        one.wait_sends()
        one.store().wait()


def out_from_self(i, c, z):
    chip = 2 * c + 1 - jnp.where(z < 2, z, 3 - z)
    core = jnp.where(z < 2, i, 1 - i)
    return jnp.logical_and(core == c, chip == z)


def expand_kernel(
    slots_ref, gs_ref, came_ref, out_ref, ggain_ref, dn_ref, up0, up1, up2, up3, wo_ref, wq_ref, wk_ref, wv_ref,
    bytes_out, out_out, ga_out, gf_out, dn_out, up_out, wo_out, wq_out, wk_out, wv_out,
):
    rows = slots_ref[0]
    slot_iota = iota((512, 128), 0).astype(F32)
    member = jnp.concatenate(
        [(slot_iota == rows[r : r + 1, :]).astype(F32).astype(BF16) for r in range(4)], axis=1
    )
    first = iota((16, 128), 0) == 0
    lead = jnp.concatenate(
        [
            jnp.where(jnp.logical_and(first, rows[r : r + 1, :] < -0.5), 1.0, 0.0).astype(BF16)
            for r in range(4)
        ],
        axis=1,
    )
    bytes_out[...] = mm(member, gs_ref[...], TN) + mm(lead, came_ref[...], TN)
    out_out[...] = out_ref[...].astype(F32)
    ga_out[...] = ggain_ref[0:1, :]
    gf_out[...] = ggain_ref[1:2, :]
    dn_out[...] = dn_ref[0].astype(F32)
    for j, up in enumerate((up0, up1, up2, up3)):
        up_out[:, 512 * j : 512 * (j + 1)] = up[0].astype(F32)
    for src, dst in ((wo_ref, wo_out), (wq_ref, wq_out), (wk_ref, wk_out), (wv_ref, wv_out)):
        dst[...] = src[0].astype(F32)


def fast_local(
    bytes_in, flags, lengths, cotangent, w_query, w_key, w_value, w_out, w_up, w_down, gain_attn, gain_ffn
):
    meta_flags = flags.reshape(32, 128)
    freqs = np.float32(ROTARY_BASE) ** (-2.0 * np.arange(32, dtype=np.float32) / np.float32(64))
    freq = np.ascontiguousarray(np.broadcast_to(freqs.astype(np.float32)[:, None], (32, 128)))
    vm = pl.BlockSpec(memory_space=pltpu.VMEM)
    hbm = pl.BlockSpec(memory_space=pl.ANY)
    hb = lambda n: pltpu.VMEM((n, 512, 256), BF16)
    hbf = lambda n: pltpu.VMEM((n, 512, 256), F32)
    sq = lambda n, t: pltpu.VMEM((n, 512, 512), t)
    scratch = dict(
        bytes_v=sq(8, BF16),
        weights=sq(4, BF16),
        wup=sq(4, BF16),
        wdn=sq(4, BF16),
        meta=pltpu.VMEM((2, 4, 40, 128), jnp.int32),
        tail=pltpu.VMEM((16, 512), BF16),
        p_own=hb(2),
        relay=pltpu.VMEM((512, 256), BF16),
        p_all=hb(8),
        n1=hb(8),
        k_t=hb(8),
        v_t=hb(8),
        q_t=hb(2),
        tab_c=pltpu.VMEM((8, 32, 256), F32),
        tab_s=pltpu.VMEM((8, 32, 256), F32),
        pos=pltpu.VMEM((8, 8, 256), F32),
        gcol=hbf(2),
        cot_own=hb(2),
        cot_w=hb(2),
        o_acc=hbf(2),
        m_sc=pltpu.VMEM((2, 8, 256), F32),
        l_sc=pltpu.VMEM((2, 8, 256), F32),
        att=pltpu.VMEM((512, 512), BF16),
        gb=pltpu.VMEM((512, 512), BF16),
        hat2=pltpu.VMEM((512, 512), F32),
        d_o=pltpu.VMEM((512, 512), BF16),
        d_sc=pltpu.VMEM((2, 8, 256), F32),
        gmid=hbf(2),
        dk=pltpu.VMEM((512, 256), F32),
        dv=pltpu.VMEM((512, 256), F32),
        dq=hbf(2),
        gwqkv=sq(3, F32),
        big=sq(2, F32),
        wg=sq(12, BF16),
        r1=pltpu.VMEM((12, 256, 512), BF16),
        r2=pltpu.VMEM((12, 128, 512), BF16),
        r3=pltpu.VMEM((12, 64, 512), BF16),
        r4=pltpu.VMEM((3, 12, 16, 512), BF16),
        ppart=hb(8),
        rc=hb(4),
        rz=hb(4),
        gfin=hb(2),
        out_s=hb(2),
        out_r=hb(2),
        rdiv=pltpu.VMEM((16, 512), F32),
        last_s=pltpu.VMEM((16, 512), BF16),
        last_r=pltpu.VMEM((16, 512), BF16),
        gain_acc=pltpu.VMEM((2, 512, 128), F32),
        gain_s=pltpu.VMEM((4, 8, 512), F32),
        gain_r=pltpu.VMEM((6, 8, 512), F32),
        ss=pltpu.SemaphoreType.DMA((160,)),
        rs=pltpu.SemaphoreType.DMA((160,)),
        ls=pltpu.SemaphoreType.DMA((32,)),
    )
    out, gs, came, slots, wgrad, ggain = pl.pallas_call(
        layer_kernel,
        out_shape=(
            jax.ShapeDtypeStruct((512, 512), BF16),
            jax.ShapeDtypeStruct((512, 512), BF16),
            jax.ShapeDtypeStruct((16, 512), BF16),
            jax.ShapeDtypeStruct((32, 128), F32),
            jax.ShapeDtypeStruct((12, 512, 512), BF16),
            jax.ShapeDtypeStruct((8, 512), F32),
        ),
        in_specs=[hbm, vm, vm, hbm, hbm, hbm, hbm, hbm, hbm, hbm, vm, vm, vm],
        out_specs=(vm, vm, vm, vm, hbm, vm),
        scratch_shapes=list(scratch.values()),
        compiler_params=pltpu.CompilerParams(
            collective_id=0, has_side_effects=True, vmem_limit_bytes=60 * 2**20
        ),
        name="layer",
    )(
        bytes_in, meta_flags, lengths, cotangent, w_query, w_key, w_value, w_out, w_up, w_down,
        gain_attn.reshape(1, 512), gain_ffn.reshape(1, 512), freq,
    )
    block = lambda rows, cols, index: pl.BlockSpec((1, rows, cols), index)
    ups = [block(64, 512, functools.partial(lambda j, i: (2 * j + 1, i, 0), j)) for j in range(4)]
    rest = [block(64, 512, functools.partial(lambda j, i: (j, i, 0), j)) for j in range(8, 12)]
    whole = lambda shape: pl.BlockSpec(shape, lambda i: (0, 0))
    flat = lambda rows, cols: pl.BlockSpec((rows, cols), lambda i: (i, 0))
    grad_bytes, out, g_attn, g_ffn, dn, up, wo, wq, wk, wv = pl.pallas_call(
        expand_kernel,
        grid=(8,),
        out_shape=(
            jax.ShapeDtypeStruct((4096, 512), F32),
            jax.ShapeDtypeStruct((512, 512), F32),
            jax.ShapeDtypeStruct((1, 512), F32),
            jax.ShapeDtypeStruct((1, 512), F32),
            jax.ShapeDtypeStruct((2048, 512), F32),
            jax.ShapeDtypeStruct((512, 2048), F32),
        )
        + (jax.ShapeDtypeStruct((512, 512), F32),) * 4,
        in_specs=[
            block(4, 128, lambda i: (i, 0, 0)),
            whole((512, 512)),
            whole((16, 512)),
            flat(64, 512),
            whole((8, 512)),
            block(256, 512, lambda i: (2 * lax.div(i, 2), lax.rem(i, 2), 0)),
        ]
        + ups
        + rest,
        out_specs=(flat(512, 512), flat(64, 512), whole((1, 512)), whole((1, 512)), flat(256, 512), flat(64, 2048)) + (flat(64, 512),) * 4,
        compiler_params=pltpu.CompilerParams(vmem_limit_bytes=60 * 2**20),
        name="expand",
    )(slots.reshape(8, 4, 128), gs, came, out, ggain, wgrad, wgrad, wgrad, wgrad, wgrad, wgrad, wgrad, wgrad, wgrad)
    return out, grad_bytes, wq, wk, wv, wo, up, dn, g_attn.reshape(512), g_ffn.reshape(512)


def passed_along(block, axis, distance):
    devices = range(lax.axis_size(axis))
    route = [((i - distance) % len(devices), i) for i in devices]
    return lax.ppermute(block, axis, route)


def from_behind(value, axis, by):
    count = lax.axis_size(axis)
    pairs = [(i, i + by) for i in range(count) if 0 <= i + by < count]
    return lax.ppermute(value, axis, pairs)


def rotate(vectors, positions, direction):
    half_dim = vectors.shape[-1] // 2
    freqs = ROTARY_BASE ** (-2.0 * jnp.arange(half_dim, dtype=jnp.float32) / vectors.shape[-1])
    angles = positions.astype(jnp.float32)[:, None] * freqs[None, :]
    cosine = jnp.cos(angles)[:, None, :]
    sine = direction * jnp.sin(angles)[:, None, :]
    first_half = vectors[..., :half_dim]
    second_half = vectors[..., half_dim:]
    return jnp.concatenate(
        [first_half * cosine - second_half * sine, second_half * cosine + first_half * sine],
        axis=-1,
    )


def layer_norm_parts(values, gain):
    center = values - jnp.mean(values, axis=-1, keepdims=True)
    spread = jnp.mean(center * center, axis=-1, keepdims=True)
    inverse = lax.rsqrt(spread + EPSILON)
    normed = center * inverse
    return (normed * gain, normed, inverse)


def layer_norm_back(grad_in, normed, inverse, gain):
    scaled = grad_in * gain
    grad_values = inverse * (
        scaled
        - jnp.mean(scaled, axis=-1, keepdims=True)
        - normed * jnp.mean(scaled * normed, axis=-1, keepdims=True)
    )
    grad_gain = jnp.sum(grad_in * normed, axis=0)
    return (grad_values, grad_gain)


def pass_grads(grad_key, grad_value):
    return (
        passed_along(grad_key.astype(jnp.bfloat16), "blk", 1).astype(grad_key.dtype),
        passed_along(grad_value.astype(jnp.bfloat16), "blk", 1).astype(grad_value.dtype),
    )


def local(
    bytes_in,
    flags,
    lengths,
    cotangent,
    w_query,
    w_key,
    w_value,
    w_out,
    w_up,
    w_down,
    gain_attn,
    gain_ffn,
):
    blocks = lax.axis_size("blk")
    own_index = lax.axis_index("blk")
    seg_rows = cotangent.shape[0]
    byte_rows = bytes_in.shape[0]
    features = bytes_in.shape[1]
    scale = HEAD_DIM ** (-0.5)
    running = jnp.cumsum(flags)
    slot_of = running - 1
    seg_count = running[-1]
    slot_ids = jnp.arange(seg_rows, dtype=jnp.int32)
    member = (slot_of[None, :] == slot_ids[:, None]).astype(jnp.bfloat16)
    seg_sums = jnp.dot(member, bytes_in, preferred_element_type=jnp.float32)
    seg_tally = jnp.sum(member, axis=1, dtype=jnp.float32)
    leading = slot_of < 0
    tail_sum = jnp.dot(
        leading.astype(jnp.bfloat16)[None, :], bytes_in, preferred_element_type=jnp.float32
    )
    tail_count = jnp.sum(leading.astype(jnp.float32), keepdims=True)
    got_sum, got_count = from_behind((tail_sum, tail_count), "blk", -1)
    last_slot = slot_ids == seg_count - 1
    seg_sums = seg_sums + jnp.where(last_slot[:, None], got_sum, 0.0)
    seg_tally = seg_tally + jnp.where(last_slot, got_count[0], 0.0)
    divisor = jnp.maximum(seg_tally, 1.0)
    pooled = seg_sums / divisor[:, None]
    starts = jnp.cumsum(lengths[0]) - lengths[0]
    byte_at = own_index * byte_rows + jnp.arange(byte_rows, dtype=jnp.int32)
    prior_flags = jnp.sum(
        flags[None, :] * (byte_at[None, :] < starts[:, None]).astype(jnp.int32), axis=1
    )
    all_counts, all_prior = (
        lax.all_gather(seg_count[None], "blk", axis=0, tiled=True),
        lax.all_gather(prior_flags[None, :], "blk", axis=0, tiled=True),
    )
    offsets = jnp.cumsum(all_counts) - all_counts
    seq_first = jnp.sum(all_prior, axis=0)
    dev_ids = jnp.arange(blocks, dtype=jnp.int32)

    def layout(first_row, row_count):
        row_index = first_row + jnp.arange(row_count, dtype=jnp.int32)
        owner_dev = row_index // seg_rows
        within = row_index % seg_rows
        dev_pick = owner_dev[:, None] == dev_ids[None, :]
        dev_base = jnp.sum(jnp.where(dev_pick, offsets[None, :], 0), axis=1)
        dev_have = jnp.sum(jnp.where(dev_pick, all_counts[None, :], 0), axis=1)
        return (dev_base + jnp.minimum(within, dev_have - 1), within < dev_have)

    query_pos, query_live = layout(own_index * seg_rows, seg_rows)
    query_first = jnp.max(
        jnp.where(seq_first[None, :] <= query_pos[:, None], seq_first[None, :], 0), axis=1
    )

    def visible(first_row, row_count):
        key_pos, key_live = layout(first_row, row_count)
        return (
            (key_pos[None, :] <= query_pos[:, None])
            & (key_pos[None, :] >= query_first[:, None])
            & key_live[None, :]
        )

    normed_attn, unit_attn, scale_attn = layer_norm_parts(pooled, gain_attn)
    n_one = normed_attn.astype(jnp.bfloat16)
    query_pre = jnp.dot(n_one, w_query, preferred_element_type=jnp.float32)
    query_rot = rotate(query_pre.reshape(seg_rows, HEADS, HEAD_DIM), query_pos, 1.0).astype(
        jnp.bfloat16
    )
    key_pre = jnp.dot(n_one, w_key, preferred_element_type=jnp.float32)
    key_rot = (
        rotate(key_pre.reshape(seg_rows, HEADS, HEAD_DIM), query_pos, 1.0)
        .reshape(seg_rows, features)
        .astype(jnp.bfloat16)
    )
    value_low = jnp.dot(n_one, w_value, preferred_element_type=jnp.float32).astype(jnp.bfloat16)
    start_state = (
        jnp.full((HEADS, seg_rows), NEGATIVE, jnp.float32),
        jnp.zeros((HEADS, seg_rows), jnp.float32),
        jnp.zeros((seg_rows, HEADS, HEAD_DIM), jnp.float32),
    )
    key_piece = lax.all_gather(key_rot, "blk", axis=0, tiled=True)
    value_piece = lax.all_gather(value_low, "blk", axis=0, tiled=True)
    row_count = key_piece.shape[0]
    allowed = visible(jnp.int32(0), row_count)

    def absorb_update(running_state):
        row_max, row_sum, weighted = running_state
        scores = (
            jnp.einsum(
                "qhe,khe->hqk",
                query_rot,
                key_piece.reshape(row_count, HEADS, HEAD_DIM),
                preferred_element_type=jnp.float32,
            )
            * scale
        )
        scores = jnp.where(allowed[None], scores, NEGATIVE)
        new_max = jnp.maximum(row_max, jnp.max(scores, axis=-1))
        weights = jnp.where(allowed[None], jnp.exp(scores - new_max[:, :, None]), 0.0)
        shrink = jnp.exp(row_max - new_max)
        row_sum = jnp.sum(weights, axis=-1)
        weighted = weighted * shrink.T[:, :, None] + jnp.einsum(
            "hqk,khe->qhe",
            weights.astype(jnp.bfloat16),
            value_piece.reshape(row_count, HEADS, HEAD_DIM),
            preferred_element_type=jnp.float32,
        )
        return (new_max, row_sum, weighted)

    row_max, row_sum, weighted = lax.cond(
        jnp.any(allowed), absorb_update, lambda unchanged: unchanged, start_state
    )
    log_total = row_max + jnp.log(row_sum)
    attended_full = weighted / row_sum.T[:, :, None]
    attended = attended_full.reshape(seg_rows, features).astype(jnp.bfloat16)
    middle = pooled + jnp.dot(attended, w_out, preferred_element_type=jnp.float32)
    normed_ffn, unit_ffn, scale_ffn = layer_norm_parts(middle, gain_ffn)
    n_two = normed_ffn.astype(jnp.bfloat16)
    up_proj = jnp.dot(n_two, w_up, preferred_element_type=jnp.float32)
    act_full, gelu_back = jax.vjp(lambda inner: jax.nn.gelu(inner, approximate=False), up_proj)
    act_low = act_full.astype(jnp.bfloat16)
    result = middle + jnp.dot(act_low, w_down, preferred_element_type=jnp.float32)
    live_rows = query_live.astype(jnp.float32)[:, None]
    output = result * live_rows
    grad_out = cotangent * live_rows
    grad_branch = grad_out.astype(jnp.bfloat16)
    grad_w_down = jnp.einsum("sf,sd->fd", act_low, grad_branch, preferred_element_type=jnp.float32)
    grad_act = jnp.einsum("sd,fd->sf", grad_branch, w_down, preferred_element_type=jnp.float32)
    grad_up = gelu_back(grad_act)[0].astype(jnp.bfloat16)
    grad_w_up = jnp.einsum("sd,sf->df", n_two, grad_up, preferred_element_type=jnp.float32)
    grad_n_two = jnp.einsum("sf,df->sd", grad_up, w_up, preferred_element_type=jnp.float32)
    grad_mid_norm, grad_gain_ffn = layer_norm_back(grad_n_two, unit_ffn, scale_ffn, gain_ffn)
    grad_middle = grad_out + grad_mid_norm
    grad_attn_branch = grad_middle.astype(jnp.bfloat16)
    grad_w_out = jnp.einsum(
        "sd,se->de", attended, grad_attn_branch, preferred_element_type=jnp.float32
    )
    grad_attended = jnp.einsum(
        "se,de->sd", grad_attn_branch, w_out, preferred_element_type=jnp.float32
    ).astype(jnp.bfloat16)
    grad_att_three = grad_attended.reshape(seg_rows, HEADS, HEAD_DIM)
    row_dot = jnp.sum(grad_att_three.astype(jnp.float32) * attended_full, axis=-1).T

    def block_grads(key_piece, value_piece, source, grad_parts):
        allowed = visible(source * seg_rows, seg_rows)

        def block_update(grad_parts):
            grad_key, grad_value, grad_query = grad_parts
            key_three = key_piece.reshape(seg_rows, HEADS, HEAD_DIM)
            value_three = value_piece.reshape(seg_rows, HEADS, HEAD_DIM)
            scores = (
                jnp.einsum("qhe,khe->hqk", query_rot, key_three, preferred_element_type=jnp.float32)
                * scale
            )
            prob_full = jnp.where(allowed[None], jnp.exp(scores - log_total[:, :, None]), 0.0)
            grad_value = grad_value + jnp.einsum(
                "hqk,qhe->khe",
                prob_full.astype(jnp.bfloat16),
                grad_att_three,
                preferred_element_type=jnp.float32,
            ).reshape(seg_rows, features)
            grad_prob = jnp.einsum(
                "qhe,khe->hqk", grad_att_three, value_three, preferred_element_type=jnp.float32
            )
            grad_scores = (prob_full * (grad_prob - row_dot[:, :, None])).astype(jnp.bfloat16)
            grad_query = (
                grad_query
                + jnp.einsum(
                    "hqk,khe->qhe", grad_scores, key_three, preferred_element_type=jnp.float32
                )
                * scale
            )
            grad_key = grad_key + (
                jnp.einsum(
                    "hqk,qhe->khe", grad_scores, query_rot, preferred_element_type=jnp.float32
                )
                * scale
            ).reshape(seg_rows, features)
            return (grad_key, grad_value, grad_query)

        return lax.cond(jnp.any(allowed), block_update, lambda unchanged: unchanged, grad_parts)

    zero_rows = jnp.zeros((seg_rows, features), jnp.float32)
    zero_query = jnp.zeros((seg_rows, HEADS, HEAD_DIM), jnp.float32)

    def visit(visit_no, loop_state):
        key_piece, value_piece, grad_key, grad_value, grad_query = loop_state
        source = (own_index - visit_no) % blocks
        grad_key, grad_value, grad_query = block_grads(
            key_piece, value_piece, source, (grad_key, grad_value, grad_query)
        )
        key_piece, value_piece = from_behind((key_piece, value_piece), "blk", 1)
        grad_key, grad_value = pass_grads(grad_key, grad_value)
        return (key_piece, value_piece, grad_key, grad_value, grad_query)

    loop_out = lax.fori_loop(
        0, blocks, visit, (key_rot, value_low, zero_rows, zero_rows, zero_query)
    )
    grad_key_sum, grad_value_sum, grad_query_rot = (loop_out[2], loop_out[3], loop_out[4])
    grad_query = (
        rotate(grad_query_rot, query_pos, -1.0).reshape(seg_rows, features).astype(jnp.bfloat16)
    )
    grad_key = (
        rotate(grad_key_sum.reshape(seg_rows, HEADS, HEAD_DIM), query_pos, -1.0)
        .reshape(seg_rows, features)
        .astype(jnp.bfloat16)
    )
    grad_value_low = grad_value_sum.astype(jnp.bfloat16)
    grad_w_query = jnp.einsum("sd,se->de", n_one, grad_query, preferred_element_type=jnp.float32)
    grad_w_key = jnp.einsum("sd,se->de", n_one, grad_key, preferred_element_type=jnp.float32)
    grad_w_value = jnp.einsum(
        "sd,se->de", n_one, grad_value_low, preferred_element_type=jnp.float32
    )
    grad_n_one = jnp.einsum("se,de->sd", grad_query, w_query, preferred_element_type=jnp.float32)
    grad_n_one = grad_n_one + jnp.einsum(
        "se,de->sd", grad_key, w_key, preferred_element_type=jnp.float32
    )
    grad_n_one = grad_n_one + jnp.einsum(
        "se,de->sd", grad_value_low, w_value, preferred_element_type=jnp.float32
    )
    grad_pool_norm, grad_gain_attn = layer_norm_back(grad_n_one, unit_attn, scale_attn, gain_attn)
    grad_pooled = grad_middle + grad_pool_norm
    grad_sums = (grad_pooled / divisor[:, None]).astype(jnp.bfloat16)
    last_grad = jnp.dot(
        last_slot.astype(jnp.bfloat16)[None, :], grad_sums, preferred_element_type=jnp.float32
    ).astype(jnp.bfloat16)
    came_grad = from_behind(last_grad, "blk", 1)
    spread_rows = jnp.take(grad_sums, jnp.maximum(slot_of, 0), axis=0)
    grad_bytes = jnp.where(leading[:, None], came_grad, spread_rows).astype(jnp.float32)
    (
        grad_w_query,
        grad_w_key,
        grad_w_value,
        grad_w_out,
        grad_w_up,
        grad_w_down,
        grad_gain_attn,
        grad_gain_ffn,
    ) = lax.psum(
        (
            grad_w_query,
            grad_w_key,
            grad_w_value,
            grad_w_out,
            grad_w_up,
            grad_w_down,
            grad_gain_attn,
            grad_gain_ffn,
        ),
        ("dp", "blk"),
    )
    return (
        output,
        grad_bytes,
        grad_w_query,
        grad_w_key,
        grad_w_value,
        grad_w_out,
        grad_w_up,
        grad_w_down,
        grad_gain_attn,
        grad_gain_ffn,
    )


def solution(mesh):
    fits = mesh.shape["blk"] == 4 and mesh.shape["dp"] == 8
    return jax.shard_map(
        fast_local if fits else local,
        mesh=mesh,
        in_specs=(
            P(("dp", "blk"), None),
            P(("dp", "blk")),
            P("dp", None),
            P(("dp", "blk"), None),
            P(),
            P(),
            P(),
            P(),
            P(),
            P(),
            P(),
            P(),
        ),
        out_specs=(
            P(("dp", "blk"), None),
            P(("dp", "blk"), None),
            P(),
            P(),
            P(),
            P(),
            P(),
            P(),
            P(),
            P(),
        ),
        check_vma=False,
    )
```

```python
import functools
import math

import jax
import jax.numpy as jnp
import numpy as np
from jax import lax
from jax.experimental import pallas as pl
from jax.experimental.pallas import tpu as pltpu
from jax.sharding import PartitionSpec as P

HEADS = 8
HEAD_DIM = 64
EPSILON = 1e-05
ROTARY_BASE = 10000.0
NEGATIVE = -1e30
LOG2E = math.log2(math.e)

MESH = pl.DeviceIdType.MESH
F32 = jnp.float32
BF16 = jnp.bfloat16
NN = (((1,), (0,)), ((), ()))
NT = (((1,), (1,)), ((), ()))
TN = (((0,), (0,)), ((), ()))


def mm(a, b, dims):
    return lax.dot_general(a, b, dims, preferred_element_type=F32)


def iota(shape, dim):
    return lax.broadcasted_iota(jnp.int32, shape, dim)


class Copy:
    def __init__(self, src, dst, send_sem, recv_sem, device, cond=None):
        self.parts = (src, dst, send_sem, recv_sem)
        self.device = device
        self.cond = cond

    def _do(self, act):
        def run():
            src, dst, send_sem, recv_sem = self.parts
            act(
                pltpu.make_async_remote_copy(
                    src_ref=src,
                    dst_ref=dst,
                    send_sem=send_sem,
                    recv_sem=recv_sem,
                    device_id=self.device,
                    device_id_type=MESH,
                )
            )

        if self.cond is None:
            run()
        else:
            pl.when(self.cond)(run)

    def start(self):
        self._do(lambda d: d.start())

    def wait_send(self):
        self._do(lambda d: d.wait_send())

    def wait_recv(self):
        self._do(lambda d: d.wait_recv())


CHUNKS = (
    (0, 2, "F0"),
    (2, 4, "F1"),
    (4, 6, "F2"),
    (6, 9, "post"),
    (9, 10, "W"),
    (10, 12, "W"),
)
SEMS_AR = 18
EARLY = 4
SCHEDULE = {
    "F2": ((0, 1), (1, 1)),
    "F3": ((2, 1),),
    "K0": ((3, 1),),
    "K1": ((0, 2), (1, 2)),
    "K2": ((2, 2),),
    "K3": ((0, 3), (1, 3)),
    "K4": ((2, 3), (3, 2)),
    "K5": ((0, 4), (1, 4), (3, 3)),
    "K6": ((2, 4),),
    "K7": ((0, 5), (1, 5), (2, 5), (3, 4), "deliver0"),
    "R6": ((4, 1), (5, 1)),
    "end": ("gain0", (0, 6), "deliver1", "out", (1, 6), "gain1", (2, 6), "deliver3", (3, 5), (4, 2), "gain2", (5, 2), (4, 3), (0, 7), "gain3", (1, 7), (2, 7), (4, 4), (5, 3), "gain4", (0, 8), "deliver2", (3, 6), (1, 8), (5, 4), (2, 8), (4, 5), (3, 7), "sums", (4, 6), (5, 5), (0, 9), "came", (0, 10), (4, 7), (5, 6), (1, 9), (3, 8), (2, 9), (4, 8), (1, 10), (5, 7), (2, 10), (4, 9), (5, 8), (4, 10), (3, 9), (3, 10), (5, 9), (5, 10)),
}


def layer_kernel(
    bytes_hbm,
    flags_ref,
    lengths_ref,
    cot_hbm,
    wq_hbm,
    wk_hbm,
    wv_hbm,
    wo_hbm,
    wup_hbm,
    wdn_hbm,
    gain_attn_ref,
    gain_ffn_ref,
    freq_ref,
    out_ref,
    gs_ref,
    came_ref,
    slots_ref,
    wgrad_hbm,
    ggain_ref,
    bytes_v,
    weights,
    wup,
    wdn,
    meta,
    tail,
    p_own,
    relay,
    p_all,
    n1,
    k_t,
    v_t,
    q_t,
    tab_c,
    tab_s,
    pos,
    gcol,
    cot_own,
    cot_w,
    o_acc,
    m_sc,
    l_sc,
    att,
    gb,
    hat2,
    d_o,
    d_sc,
    gmid,
    dk,
    dv,
    dq,
    gwqkv,
    big,
    wg,
    r1,
    r2,
    r3,
    r4,
    r5,
    ppart,
    rc,
    rz,
    gfin,
    out_s,
    out_r,
    rdiv,
    last_s,
    last_r,
    gain_acc,
    gain_s,
    gain_r,
    ss,
    rs,
    ls,
):
    cot_v, acc = hat2, big.at[0]
    dp = lax.axis_index("dp")
    z = lax.axis_index("blk")
    feat = 512
    half = 256
    nblk = 4
    c = lax.rem(dp, 2)
    x = lax.rem(lax.div(dp, 2), 2)
    y = lax.div(dp, 4)
    sib = (dp + 1 - 2 * c, z)
    xnb = (dp + 2 - 4 * x, z)
    ynb = (dp + 4 - 8 * y, z)
    g = lax.div(z, 2)
    zl = lax.rem(z, 2)
    w = 2 * (1 - zl) + c
    zo = 4 * g + 1 - z
    near = 1 + g
    is_near = z == near
    own_worker = g == c

    def dev(core, zz):
        return (dp - c + core, zz)

    counter = {"s": 0, "r": 0, "l": 0}

    def ids(kind, n):
        first = counter[kind]
        counter[kind] = first + n
        return first

    sends = []

    def go(copy):
        copy.start()
        sends.append(copy)

    l_bytes = ids("l", 8)
    rows_chunk = bytes_v.shape[1]
    l_cot = ids("l", 1)
    load_cot = pltpu.make_async_copy(cot_hbm, cot_v, ls.at[l_cot])
    load_cot.start()
    loads_bytes = [
        pltpu.make_async_copy(
            bytes_hbm.at[pl.ds(i * rows_chunk, rows_chunk)], bytes_v.at[i], ls.at[l_bytes + i]
        )
        for i in range(8)
    ]
    for d in loads_bytes:
        d.start()
    l_w = ids("l", 4)
    loads_w = [
        pltpu.make_async_copy(src, weights.at[i], ls.at[l_w + i])
        for i, src in enumerate((wq_hbm, wk_hbm, wv_hbm, wo_hbm))
    ]
    l_f = ids("l", 8)
    loads_f = []
    for j in range(4):
        loads_f.append(
            pltpu.make_async_copy(
                wup_hbm.at[:, pl.ds(j * feat, feat)], wup.at[j], ls.at[l_f + 2 * j]
            )
        )
        loads_f.append(
            pltpu.make_async_copy(
                wdn_hbm.at[pl.ds(j * feat, feat)], wdn.at[j], ls.at[l_f + 2 * j + 1]
            )
        )

    barrier = pltpu.get_barrier_semaphore()
    me_line = c * nblk + z
    line = []
    for k in range(1, 8):
        t = lax.rem(me_line + k, 8)
        line.append((lax.div(t, nblk), lax.rem(t, nblk)))
    for core, zz in line:
        pl.semaphore_signal(barrier, inc=1, device_id=dev(core, zz), device_id_type=MESH)
    for d in (xnb, ynb):
        pl.semaphore_signal(barrier, inc=1, device_id=d, device_id_type=MESH)
    pl.semaphore_wait(barrier, 9)

    meta[c, z, 0:32, :] = flags_ref[...]
    meta[c, z, 32:40, :] = jnp.zeros((8, 128), jnp.int32)
    meta[c, z, 32:33, 0:4] = lengths_ref[...]
    s_meta, r_meta = ids("s", 7), ids("r", 8)
    for k, (core, zz) in enumerate(line):
        go(
            Copy(
                meta.at[c, z],
                meta.at[c, z],
                ss.at[s_meta + k],
                rs.at[r_meta + me_line],
                dev(core, zz),
            )
        )
    s_tail, r_tail = ids("s", 1), ids("r", 1)
    copy_tail = Copy(
        bytes_hbm.at[pl.ds(0, 16)],
        tail,
        ss.at[s_tail],
        rs.at[r_tail],
        (dp, lax.rem(z + nblk - 1, nblk)),
        z > 0,
    )
    go(copy_tail)

    @pl.when(z == nblk - 1)
    def _():
        tail[...] = jnp.zeros_like(tail)

    cnt = jnp.sum(flags_ref[...].astype(F32))
    lane_row = iota((1, feat), 1).astype(F32)
    live_row = jnp.where(lane_row < cnt, 1.0, 0.0)
    for d in loads_w:
        d.start()
    for d in loads_f:
        d.start()

    upper = (iota((128, 128), 0) <= iota((128, 128), 1)).astype(F32).astype(BF16)
    ones_sq = jnp.ones((128, 128), BF16)
    below = (iota((32, 32), 1) < iota((32, 32), 0)).astype(F32).astype(BF16)
    own_flags = flags_ref[...].astype(F32)
    flags_low = own_flags.astype(BF16)
    within = mm(flags_low, upper, NN)
    row_sums = mm(flags_low, ones_sq, NN)
    row_base = mm(below, row_sums.astype(BF16), NN)
    slot_of = within + row_base - 1.0
    slots_ref[...] = slot_of

    acc[...] = jnp.zeros_like(acc)
    rdiv[...] = jnp.zeros_like(rdiv)
    slot_iota = iota((feat, 128), 0).astype(F32)
    ones_rows = jnp.ones((16, feat), BF16)

    cells = rows_chunk // 8
    for k in range(8):
        loads_bytes[k].wait()
        reach = cells * (k + 1)
        member = jnp.concatenate(
            [
                (slot_iota[0:reach] == slot_of[r : r + 1, :]).astype(F32).astype(BF16)
                for r in range(4 * k, 4 * k + 4)
            ],
            axis=1,
        )
        acc[0:reach, :] += mm(member, bytes_v[k], NN)
        rdiv[:, 0:feat] += mm(
            ones_rows,
            jnp.concatenate([member, jnp.zeros((feat - reach, rows_chunk), BF16)], axis=0)
            if reach < feat
            else member,
            NT,
        )

    for i, gain in enumerate((gain_attn_ref, gain_ffn_ref)):
        row = jnp.broadcast_to(gain[...], (128, feat))
        col = row.T
        gcol[i] = jnp.concatenate([col, col], axis=1)

    for core, zz in line:
        Copy(
            meta.at[core, zz],
            meta.at[core, zz],
            ss.at[0],
            rs.at[r_meta + core * nblk + zz],
            sib,
        ).wait_recv()
    Copy(tail, tail, ss.at[0], rs.at[r_tail], sib, z < nblk - 1).wait_recv()
    zn = jnp.minimum(z + 1, nblk - 1)
    next_flags = meta[c, zn, 0:16, :].astype(F32).astype(BF16)
    next_within = mm(next_flags, upper, NN)
    has_next = (z < nblk - 1).astype(F32)
    lead = jnp.where(next_within[0:1, :] < 0.5, 1.0, 0.0) * has_next
    is_last16 = iota((feat, 16), 0).astype(F32) == cnt - 1.0
    member_tail = jnp.where(is_last16, lead[:, 0:16], 0.0).astype(BF16)
    sums = acc[...] + mm(member_tail, tail[...], NN)
    tally = rdiv[0:1, :] + jnp.where(lane_row == cnt - 1.0, jnp.sum(lead), 0.0)
    inverse_tally = 1.0 / jnp.maximum(tally, 1.0)
    rdiv[0:1, :] = inverse_tally
    rdiv[1:2, :] = live_row
    pooled_t = (sums.T * inverse_tally).astype(BF16)
    p_own[0] = pooled_t[:, 0:half]
    p_own[1] = pooled_t[:, half:]

    s_p, r_p, r_relay = ids("s", 22), ids("r", 16), ids("r", 1)
    near_c = 1 + c
    pieces = (pl.ds(0, half), pl.ds(half, half))

    def p_piece(src, hb, piece, slot, device, cond=None):
        at = pieces[piece]
        return Copy(
            src.at[at],
            p_all.at[hb, at],
            ss.at[s_p + slot],
            rs.at[r_p + 2 * hb + piece],
            device,
            cond,
        )

    def p_whole(src, hb, slot, device, cond=None):
        return Copy(src, p_all.at[hb], ss.at[s_p + slot], rs.at[r_p + 2 * hb], device, cond)

    other_worker = jnp.logical_not(own_worker)
    to_pair = z != nblk - 1
    inner = jnp.logical_or(z == 1, z == 2)

    outer = jnp.logical_not(inner)

    def outside_copies(cond):
        own_out = jnp.logical_and(other_worker, cond)
        relayed = jnp.logical_and(own_worker, cond)
        return [
            p_piece(p_own.at[c], 2 * z + c, i, 4 + i, dev(c, near_c), own_out) for i in range(2)
        ] + [p_piece(relay, 2 * z + c, i, 4 + i, dev(c, 2 - c), relayed) for i in range(2)]

    outside_late = outside_copies(outer)

    go(Copy(p_own.at[1 - c], relay, ss.at[s_p + 3], rs.at[r_relay], sib, other_worker))
    for i in range(2):
        own_pair = jnp.logical_and(own_worker, to_pair)
        go(p_piece(p_own.at[c], 2 * z + c, i, i, dev(c, zo), own_pair))
    go(p_whole(p_own.at[1 - c], 2 * z + 1 - c, 3, sib, own_worker))
    go(p_whole(p_own.at[c], 2 * z + c, 2, sib, own_worker))

    @pl.when(own_worker)
    def _():
        p_all[2 * z] = p_own[0]
        p_all[2 * z + 1] = p_own[1]

    def p_wait(hb, cond=None):
        Copy(p_all.at[hb], p_all.at[hb], ss.at[0], rs.at[r_p + 2 * hb], sib, cond).wait_recv()

    Copy(relay, relay, ss.at[0], rs.at[r_relay], sib, own_worker).wait_recv()
    for one in outside_copies(inner):
        go(one)
    p_wait(2 * z + c, other_worker)
    for i in range(2):
        passed = jnp.logical_and(other_worker, to_pair)
        go(p_piece(p_all.at[2 * z + c], 2 * z + c, i, i, dev(c, zo), passed))
    p_wait(2 * z + 1 - c, other_worker)

    load_cot.wait()
    cot_t = (cot_v[...].T * live_row).astype(BF16)
    cot_own[0] = cot_t[:, 0:half]
    cot_own[1] = cot_t[:, half:]
    lo_here = False
    hi_here = jnp.logical_and(g == c, z >= 2)

    counts = []
    for b in range(nblk):
        counts.append(jnp.sum(meta[g, b, 0:32, :].astype(F32)))
    offsets = [jnp.float32(0.0)]
    for b in range(nblk):
        offsets.append(offsets[-1] + counts[b])
    lens = meta[g, z, 32:40, :].astype(F32)
    first_row = iota((8, 128), 0) == 0
    lane8 = iota((8, 128), 1)
    byte_at = (iota((32, 128), 0) * 128 + iota((32, 128), 1)).astype(F32)
    seq_first = [jnp.float32(0.0)]
    for s in range(1, 4):
        start = jnp.sum(jnp.where(jnp.logical_and(first_row, lane8 < s), lens, 0.0))
        prior = jnp.zeros((32, 128), F32)
        for b in range(nblk):
            prior = prior + jnp.where(
                byte_at + float(b * 4096) < start, meta[g, b, 0:32, :].astype(F32), 0.0
            )
        seq_first.append(jnp.sum(prior))

    freq = jnp.concatenate([freq_ref[...], freq_ref[...]], axis=1)
    lane_half = iota((1, half), 1).astype(F32)
    for hb in range(8):
        b = hb // 2
        j = lane_half + float((hb % 2) * half)
        p = offsets[b] + jnp.minimum(j, counts[b] - 1.0)
        first = jnp.zeros_like(p)
        for s in range(1, 4):
            first = jnp.maximum(first, jnp.where(p >= seq_first[s], seq_first[s], 0.0))
        pos[hb, 0:1, :] = p
        pos[hb, 1:2, :] = first
        angle = freq * p
        tab_c[hb] = jnp.cos(angle)
        tab_s[hb] = jnp.sin(angle)

    def pick(values, b):
        total = jnp.float32(0.0)
        for i, v in enumerate(values):
            total = total + jnp.where(b == i, v, 0.0)
        return total

    gain_col = gcol[0]

    def norm_parts(values):
        mean = jnp.mean(values, axis=0, keepdims=True)
        center = values - mean
        inverse = lax.rsqrt(jnp.mean(center * center, axis=0, keepdims=True) + EPSILON)
        return center * inverse, inverse

    def turned(values, hb, direction):
        cos = tab_c[hb]
        sin = tab_s[hb] * direction
        parts = []
        for h in range(HEADS):
            a = values[64 * h : 64 * h + 32, :]
            b = values[64 * h + 32 : 64 * h + 64, :]
            parts.append(a * cos - b * sin)
            parts.append(b * cos + a * sin)
        return jnp.concatenate(parts, axis=0).astype(BF16)

    for d in loads_w:
        d.wait()

    def keys_values(hb):
        unit, _ = norm_parts(p_all[hb].astype(F32))
        normed = (unit * gcol[0]).astype(BF16)
        n1[hb] = normed
        k_t[hb] = turned(mm(weights[1], normed, TN), hb, 1.0)
        v_t[hb] = mm(weights[2], normed, TN).astype(BF16)

    s_cot, r_cot = ids("s", 2), ids("r", 2)
    early = z < 2
    slot_to = jnp.where(early, 0, 1)
    chip_to = 2 * c + 1 - jnp.where(early, z, 3 - z)

    def cot_copy(i):
        core_to = jnp.where(early, i, 1 - i)
        here = jnp.logical_and(core_to == c, chip_to == z)
        return here, Copy(
            cot_own.at[i],
            cot_w.at[slot_to],
            ss.at[s_cot + i],
            rs.at[r_cot + slot_to],
            dev(core_to, chip_to),
            jnp.logical_not(here),
        )

    def send_cot():
        for i in range(2):
            here, copy = cot_copy(i)
            copy.start()

            @pl.when(here)
            def _():
                cot_w[slot_to] = cot_own[i]

    hq_of = (w, 7 - w)
    first_far, second_far = 2 - g, 3 - 3 * g
    score_scale = HEAD_DIM ** (-0.5) * LOG2E

    def hq_at(slot):
        return jnp.where(slot == 0, w, 7 - w)

    def bias_of(hq, kb):
        b = lax.div(kb, 2)
        j = (iota((half, half), 0) + lax.rem(kb, 2) * half).astype(F32)
        kpos = j + pick(offsets[:nblk], b)
        alive = j < pick(counts, b)
        qpos = pos[hq, 0:1, :]
        qfirst = pos[hq, 1:2, :]
        allowed = jnp.logical_and(alive, jnp.logical_and(kpos <= qpos, kpos >= qfirst))
        return jnp.where(allowed, 0.0, NEGATIVE)

    o_acc[...] = jnp.zeros_like(o_acc)
    l_sc[...] = jnp.zeros_like(l_sc)
    m_sc[...] = jnp.full(m_sc.shape, NEGATIVE, F32)

    def s_at(h):
        return gwqkv.at[h // 4, pl.ds(half * ((h // 2) % 2), half), pl.ds(half * (h % 2), half)]

    o_new = big.at[1, :, pl.ds(0, half)]

    def forward_step(slot, kb):
        hq = hq_at(slot)
        bias = bias_of(hq, kb)
        old = m_sc[slot]
        old_sum = l_sc[slot]
        for h in range(HEADS):
            part = slice(64 * h, 64 * h + 64)
            s_at(h)[...] = mm(k_t[kb, part, :], q_t[slot, part, :], TN)
        tops, sums = [], []
        for h in range(HEADS):
            part = slice(64 * h, 64 * h + 64)
            s = s_at(h)[...] * score_scale + bias
            top = jnp.maximum(old[h : h + 1, :], jnp.max(s, axis=0, keepdims=True))
            prob = jnp.exp2(s - top)
            tops.append(top)
            sums.append(jnp.sum(prob, axis=0, keepdims=True))
            o_new[part, :] = mm(v_t[kb, part, :], prob.astype(BF16), NN)
        new = jnp.concatenate(tops, axis=0)
        shrink = jnp.exp2(old - new)
        m_sc[slot] = new
        l_sc[slot] = old_sum * shrink + jnp.concatenate(sums, axis=0)
        for h in range(HEADS):
            part = slice(64 * h, 64 * h + 64)
            o_acc[slot, part, :] = o_acc[slot, part, :] * shrink[h : h + 1, :] + o_new[part, :]

    def block_nth(n):
        swapped = jnp.where(n < 2, 1 - n, n)
        return jnp.where(z == 0, n, jnp.where(z == 1, swapped, z - n))

    def pass_on(block, slot, cond, onward=None):
        hb = 2 * block + c

        @pl.when(cond)
        def _():
            for i in range(2):
                there = p_all.at[hb, pieces[i]]
                Copy(there, there, ss.at[0], rs.at[r_p + 2 * hb + i], sib).wait_recv()
                if onward is not None:
                    p_piece(p_all.at[hb], hb, i, slot + 2 + i, dev(c, zo), onward).start()
                p_piece(p_all.at[hb], hb, i, slot + i, sib).start()

    def pass_on_sent():
        for block, slot, cond, onward in passes:
            hb = 2 * block + c

            @pl.when(cond)
            def _(hb=hb, slot=slot, onward=onward):
                for i in range(2):
                    if onward is not None:
                        p_piece(p_all.at[hb], hb, i, slot + 2 + i, dev(c, zo), onward).wait_send()
                    p_piece(p_all.at[hb], hb, i, slot + i, sib).wait_send()

    second_near = z == 2
    passes = (
        (zo, 6, z != 2),
        (first_far, 8, is_near, is_near),
        (first_far, 12, jnp.logical_not(is_near)),
        (second_far, 14, second_near, second_near),
        (second_far, 18, zl == 1),
    )
    passes = tuple(p if len(p) == 4 else p + (None,) for p in passes)

    def arrival(n, carry):
        block = block_nth(n)

        @pl.when(n == 1)
        def _():
            for one in outside_late:
                one.start()
            pass_on(*passes[0])
            pass_on(*passes[1])

        @pl.when(n == 2)
        def _():
            pass_on(*passes[2])
            pass_on(*passes[3])

        @pl.when(n == 3)
        def _():
            pass_on(*passes[4])
            send_cot()

        @pl.when(jnp.logical_and(n > 0, n < 3 + zl))
        def _():
            for i in range(2):
                there = p_all.at[2 * block + 1 - c, pieces[i]]
                Copy(
                    there, there, ss.at[0], rs.at[r_p + 2 * (2 * block + 1 - c) + i], sib
                ).wait_recv()

        @pl.when(n < 3 + zl)
        def _():
            def one(i, carry):
                keys_values(2 * block + i)
                return carry

            lax.fori_loop(0, 2, one, 0)

            def query(slot, carry):
                hq = hq_at(slot)

                @pl.when(lax.div(hq, 2) == block)
                def _():
                    q_t[slot] = turned(mm(weights[0], n1[hq], TN), hq, 1.0)

                return carry

            lax.fori_loop(0, 2, query, 0)

            def pair(i, carry):
                slot, kb = lax.div(i, 8), lax.rem(i, 8)
                hq = hq_at(slot)
                q_block, k_block = lax.div(hq, 2), lax.div(kb, 2)

                def came_by(b, m):
                    found = block_nth(0) == b
                    for k in range(1, 4):
                        found = jnp.logical_or(
                            found, jnp.logical_and(block_nth(k) == b, k <= m)
                        )
                    return found

                new_query = jnp.logical_and(q_block == block, came_by(k_block, n))
                new_keys = jnp.logical_and(k_block == block, came_by(q_block, n))
                new = jnp.logical_or(new_query, new_keys)

                @pl.when(jnp.logical_and(kb <= hq, new))
                def _():
                    forward_step(slot, kb)

                return carry

            lax.fori_loop(0, 16, pair, 0)

        return carry

    lax.fori_loop(0, 4, arrival, 0)

    for slot in range(2):
        total = l_sc[slot]
        for h in range(HEADS):
            part = slice(64 * h, 64 * h + 64)
            o_acc[slot, part, :] = o_acc[slot, part, :] * (1.0 / total[h : h + 1, :])
        att[:, slot * half : (slot + 1) * half] = o_acc[slot].astype(BF16)
        m_sc[slot] = m_sc[slot] + jnp.log2(total)

    own_pooled = jnp.concatenate([p_all[hq_of[0]], p_all[hq_of[1]]], axis=1).astype(F32)
    middle = own_pooled + mm(weights[3], att[...], TN)
    unit2, inverse2 = norm_parts(middle)
    hat2[...] = unit2
    gain_col2 = jnp.concatenate([gcol[1], gcol[1]], axis=1)
    n2 = (unit2 * gain_col2).astype(BF16)
    big[0] = middle
    big[1] = jnp.zeros((feat, feat), F32)
    n2_ref = d_o
    n2_ref[...] = n2

    base1 = c * 256
    keep2x, give2x = base1 + x * 128, base1 + (1 - x) * 128
    keep2y, give2y = base1 + y * 128, base1 + (1 - y) * 128
    keep3x, give3x = keep2x + y * 64, keep2x + (1 - y) * 64
    keep3y, give3y = keep2y + x * 64, keep2y + (1 - x) * 64
    keep4x, give4x = keep3x + 32 * zl, keep3x + 32 * (1 - zl)
    keep4y, give4y = keep3y + 32 * zl, keep3y + 32 * (1 - zl)
    keep5x, give5x = keep4x + 16 * g, keep4x + 16 * (1 - g)
    keep5y, give5y = keep4y + 16 * g, keep4y + 16 * (1 - g)
    znb, zfar = (dp, z + 1 - 2 * zl), (dp, lax.rem(z + 2, nblk))
    lanes_x, lanes_y = pl.ds(0, 256), pl.ds(256, 256)

    def rows_of(first, n):
        return pl.ds(pl.multiple_of(first, 16), n)

    class Reduce:
        def __init__(self, chunk):
            self.b0, self.b1 = CHUNKS[chunk][:2]
            self.nb = self.b1 - self.b0
            self.s0, self.r0 = ids("s", SEMS_AR), ids("r", SEMS_AR)
            self.blocks = pl.ds(self.b0, self.nb)
            self.phases = {}

        def _w(self, first, n, lanes):
            return wg.at[self.blocks, rows_of(first, n), lanes]

        def _list(self, phase):
            every = pl.ds(0, 512)
            b, s0, r0 = self.blocks, self.s0, self.r0

            def copy(i, src, dst, device):
                return Copy(src, dst, ss.at[s0 + i], rs.at[r0 + i], device)

            if phase == 1:
                return [copy(0, self._w((1 - c) * 256, 256, every), r1.at[b], sib)]
            if phase == 2:
                return [
                    copy(1, self._w(give2x, 128, lanes_x), r2.at[b, :, lanes_x], xnb),
                    copy(2, self._w(give2y, 128, lanes_y), r2.at[b, :, lanes_y], ynb),
                ]
            if phase == 3:
                return [
                    copy(3, self._w(give3x, 64, lanes_x), r3.at[b, :, lanes_x], ynb),
                    copy(4, self._w(give3y, 64, lanes_y), r3.at[b, :, lanes_y], xnb),
                ]
            if phase == 4:
                return [
                    copy(5, self._w(give4x, 32, lanes_x), r4.at[b, :, lanes_x], znb),
                    copy(6, self._w(give4y, 32, lanes_y), r4.at[b, :, lanes_y], znb),
                ]
            if phase == 5:
                return [
                    copy(7, self._w(give5x, 16, lanes_x), r5.at[b, :, lanes_x], zfar),
                    copy(8, self._w(give5y, 16, lanes_y), r5.at[b, :, lanes_y], zfar),
                ]
            if phase < 10:
                keep_x, keep_y, n, to_x, to_y = (
                    (keep5x, keep5y, 16, zfar, zfar),
                    (keep4x, keep4y, 32, znb, znb),
                    (keep3x, keep3y, 64, ynb, xnb),
                    (keep2x, keep2y, 128, xnb, ynb),
                )[phase - 6]
                mine_x, mine_y = self._f(keep_x, n, lanes_x), self._f(keep_y, n, lanes_y)
                first = 2 * phase - 3
                return [copy(first, mine_x, mine_x, to_x), copy(first + 1, mine_y, mine_y, to_y)]
            return [copy(17, r1.at[b], self._out(base1), sib)]

        def _f(self, first, n, lanes):
            return r1.at[self.blocks, rows_of(first - base1, n), lanes]

        def _out(self, first):
            return wgrad_hbm.at[self.blocks, rows_of(first, 256), pl.ds(0, 512)]

        def start(self, phase):
            for one in self._list(phase):
                one.start()

        def finish(self, phase):
            if phase == 10:
                other = self._out((1 - c) * 256)
                Copy(other, other, ss.at[0], rs.at[self.r0 + 17], sib).wait_recv()
                return
            for one in self._list(phase):
                one.wait_recv()
            if phase > 5:
                return

            def add(i, carry):
                b = self.b0 + i
                if phase == 1:
                    here = (b, rows_of(base1, 256), slice(None))
                    wg[here] = wg[here] + r1[b]
                if phase == 2:
                    for keep, lo in ((keep2x, 0), (keep2y, 256)):
                        here = (b, rows_of(keep, 128), slice(lo, lo + 256))
                        wg[here] = wg[here] + r2[b, :, lo : lo + 256]
                if phase == 3:
                    for keep, lo in ((keep3x, 0), (keep3y, 256)):
                        here = (b, rows_of(keep, 64), slice(lo, lo + 256))
                        wg[here] = wg[here] + r3[b, :, lo : lo + 256]
                if phase == 4:
                    for keep, lo in ((keep4x, 0), (keep4y, 256)):
                        here = (b, rows_of(keep, 32), slice(lo, lo + 256))
                        wg[here] = wg[here] + r4[b, :, lo : lo + 256]
                if phase == 5:
                    for keep, lo in ((keep5x, 0), (keep5y, 256)):
                        total = wg[b, rows_of(keep, 16), lo : lo + 256] + r5[b, :, lo : lo + 256]
                        r1[b, rows_of(keep - base1, 16), lo : lo + 256] = total
                return carry

            lax.fori_loop(0, self.nb, add, 0)

        def step(self, phase):
            self.finish(phase)
            if phase < 10:
                self.begin(phase + 1)

        def begin(self, phase):
            self.start(phase)
            if phase == 10:
                self.store().start()

        def store(self):
            return pltpu.make_async_copy(r1.at[self.blocks], self._out(base1), ls.at[self.store_sem])

        def wait_sends(self):
            for phase in range(1, 11):
                for one in self._list(phase):
                    one.wait_send()

    red = [Reduce(i) for i in range(len(CHUNKS))]
    for one in red:
        one.store_sem = ids("l", 1)

    for d in loads_f:
        d.wait()

    def do(item):
        if not isinstance(item, str):
            if item[0] == "f":
                red[item[1]].finish(item[2])
            elif item[0] == "s":
                red[item[1]].begin(item[2])
            else:
                red[item[0]].step(item[1])
        elif item == "gain0":
            gains_start()
        elif item.startswith("gain"):
            gain_finish(int(item[4:]))
        elif item.startswith("deliver"):
            deliver(int(item[7:]))
        else:
            {"out": finish_output, "sums": finish_sums, "came": finish_came}[item]()

    def run_after(name, index=None):
        if index is None:
            for (_, _, when), one in zip(CHUNKS, red):
                if when == name:
                    one.start(1)
            for item in SCHEDULE.get(name, ()):
                do(item)
            return
        for i in range(9):
            full = name + str(i)
            if full in SCHEDULE or any(when == full for _, _, when in CHUNKS):

                @pl.when(index == i)
                def _():
                    run_after(full)

    def ffn_forward(j, carry):
        up = mm(wup[j], n2_ref[...], TN)
        size = jnp.abs(up) * (0.5**0.5)
        t = 1.0 / (1.0 + 0.3275911 * size)
        poly = t * (
            0.254829592
            + t * (-0.284496736 + t * (1.421413741 + t * (-1.453152027 + t * 1.061405429)))
        )
        decay = jnp.exp(-0.5 * up * up)
        far = 0.5 * poly * decay
        phi = jnp.where(up < 0.0, far, 1.0 - far)
        slope = phi + up * decay * (1.0 / math.sqrt(2.0 * math.pi))
        act = (up * phi).astype(BF16)
        bytes_v[j] = act
        bytes_v[4 + j] = slope.astype(BF16)
        big[0] += mm(wdn[j], act, TN)
        return carry

    lax.fori_loop(0, 4, ffn_forward, 0)

    Copy(cot_w.at[0], cot_w.at[0], ss.at[0], rs.at[r_cot], sib).wait_recv()
    Copy(cot_w.at[1], cot_w.at[1], ss.at[0], rs.at[r_cot + 1], sib, jnp.logical_not(hi_here)).wait_recv()
    gb[...] = jnp.concatenate([cot_w[0], cot_w[1]], axis=1)

    def ffn_backward(j, carry):
        wg[2 * j] = mm(bytes_v[j], gb[...], NT).astype(BF16)
        grad_up = (mm(wdn[j], gb[...], NN) * bytes_v[4 + j].astype(F32)).astype(BF16)
        wg[2 * j + 1] = mm(n2_ref[...], grad_up, NT).astype(BF16)
        big[1] += mm(wup[j], grad_up, NN)
        run_after("F", j)
        return carry

    lax.fori_loop(0, 4, ffn_backward, 0)

    s_out, r_out = ids("s", 2), ids("r", 2)
    res = big[0].astype(BF16)
    owners = ((1 - zl, c, lo_here), (2 + zl, 1 - c, hi_here))
    for slot, (chip, i, here) in enumerate(owners):
        out_s[slot] = res[:, slot * half : (slot + 1) * half]
        go(
            Copy(
                out_s.at[slot],
                out_r.at[i],
                ss.at[s_out + slot],
                rs.at[r_out + i],
                dev(g, chip),
                None if here is False else jnp.logical_not(here),
            )
        )
        if here is not False:

            @pl.when(here)
            def _():
                out_r[i] = out_s[slot]

    grad_n2 = big[1]
    unit2 = hat2[...]
    product = grad_n2 * unit2

    def lane_fold(values):
        total = values[:, 0:128]
        for k in range(1, values.shape[1] // 128):
            total = total + values[:, 128 * k : 128 * (k + 1)]
        return total

    gain_acc[1] = lane_fold(product)
    e = grad_n2 * gain_col2
    grad_mid = gb[...].astype(F32) + inverse2 * (
        e
        - jnp.mean(e, axis=0, keepdims=True)
        - unit2 * jnp.mean(e * unit2, axis=0, keepdims=True)
    )
    gmid[0] = grad_mid[:, 0:half]
    gmid[1] = grad_mid[:, half:]
    branch = grad_mid.astype(BF16)
    wg[8] = mm(att[...], branch, NT).astype(BF16)
    run_after("post")
    grad_att = mm(weights[3], branch, NN)
    d_o[...] = grad_att.astype(BF16)
    for slot in range(2):
        lanes = slice(slot * half, (slot + 1) * half)
        both = d_o[:, lanes].astype(F32) * o_acc[slot]
        for h in range(HEADS):
            d_sc[slot, h : h + 1, :] = jnp.sum(
                both[64 * h : 64 * h + 64, :], axis=0, keepdims=True
            )

    dq[...] = jnp.zeros_like(dq)
    gwqkv[...] = jnp.zeros_like(gwqkv)
    gain_acc[0] = jnp.zeros((feat, 128), F32)
    s_rc, r_rc = ids("s", 4), ids("r", 4)
    s_rz, r_rz = ids("s", 4), ids("r", 4)
    s_fin, r_fin = ids("s", 4), ids("r", 2)

    def sd_at(which, h):
        return big.at[which, pl.ds(half * ((h // 2) % 2), half), pl.ds(half * (h % 2), half)]

    def backward_step(slot, kb):
        hq = hq_at(slot)
        bias = bias_of(hq, kb)
        lanes = pl.ds(pl.multiple_of(slot * half, half), half)
        lse = m_sc[slot]
        dots = d_sc[slot]
        for first in (0, 4):
            for h in range(first, first + 4):
                part = slice(64 * h, 64 * h + 64)
                grad_o = d_o[part, lanes]
                sd_at(0, h)[...] = mm(k_t[kb, part, :], q_t[slot, part, :], TN)
                sd_at(1, h)[...] = mm(v_t[kb, part, :], grad_o, TN)
            for h in range(first, first + 4):
                part = slice(64 * h, 64 * h + 64)
                prob = jnp.exp2(sd_at(0, h)[...] * score_scale + bias - lse[h : h + 1, :])
                grad_s = (prob * (sd_at(1, h)[...] - dots[h : h + 1, :])).astype(BF16)
                dv[part, :] += mm(d_o[part, lanes], prob.astype(BF16), NT)
                dk[part, :] += mm(q_t[slot, part, :], grad_s, NT)
                dq[slot, part, :] += mm(k_t[kb, part, :], grad_s, NN)

    att_scale = HEAD_DIM ** (-0.5)

    def rc_copy(kb):
        zb = lax.div(kb, 2)
        return Copy(
            ppart.at[kb],
            rc.at[zb],
            ss.at[s_rc + zb],
            rs.at[r_rc + zb],
            sib,
            lax.rem(kb, 2) != c,
        )

    def is_final(zb):
        return jnp.where(lax.div(zb, 2) == g, z == zb, is_near)

    def rz_copy(zb):
        return Copy(
            ppart.at[2 * zb + c],
            rz.at[zb],
            ss.at[s_rz + zb],
            rs.at[r_rz + zb],
            dev(c, zo),
            jnp.logical_and(jnp.logical_not(is_final(zb)), zb < nblk - 1),
        )

    def fin_copy(zb):
        here = jnp.logical_and(zb == z, g == c)
        return Copy(
            ppart.at[2 * zb + c],
            gfin.at[c],
            ss.at[s_fin + zb],
            rs.at[r_fin + c],
            dev(g, zb),
            jnp.logical_and(is_final(zb), jnp.logical_not(here)),
        )

    def combine(zb):
        kb = 2 * zb + c
        Copy(rc.at[zb], rc.at[zb], ss.at[0], rs.at[r_rc + zb], sib).wait_recv()
        ppart[kb] = ppart[kb] + rc[zb]
        rz_copy(zb).start()

    def deliver(zb):
        kb = 2 * zb + c
        final = jnp.logical_and(is_final(zb), zb < nblk - 1)
        Copy(rz.at[zb], rz.at[zb], ss.at[0], rs.at[r_rz + zb], sib, final).wait_recv()

        @pl.when(final)
        def _():
            ppart[kb] = ppart[kb] + rz[zb]

        @pl.when(jnp.logical_and(zb == z, g == c))
        def _():
            gfin[c] = ppart[kb]

        fin_copy(zb).start()

    s_gain, r_gain = ids("s", 6), ids("r", 6)

    def gain_list(phase):
        if phase < 4:
            device = (sib, xnb, ynb)[phase - 1]
            k = phase - 1
            return [
                Copy(gain_s.at[k], gain_r.at[k], ss.at[s_gain + k], rs.at[r_gain + k], device)
            ]
        return [
            Copy(
                gain_s.at[3],
                gain_r.at[2 + k],
                ss.at[s_gain + 2 + k],
                rs.at[r_gain + 2 + k],
                (dp, lax.rem(z + k, nblk)),
            )
            for k in range(1, 4)
        ]

    def gain_finish(phase):
        for one in gain_list(phase):
            one.wait_recv()
        if phase < 4:
            gain_s[phase] = gain_s[phase - 1] + gain_r[phase - 1]
            for one in gain_list(phase + 1):
                one.start()
        else:
            total = jnp.zeros((8, feat), F32)
            for zz in range(nblk):
                k = lax.rem(z - zz + nblk, nblk)
                part = gain_s[3]
                for i in range(1, 4):
                    part = jnp.where(k == i, gain_r[2 + i], part)
                total = total + part
            ggain_ref[...] = total

    def gains_start():
        for i in range(2):
            gain_s[0, i : i + 1, :] = jnp.sum(gain_acc[i].T, axis=0, keepdims=True)
        gain_s[0, 2:8, :] = jnp.zeros((6, feat), F32)
        gain_list(1)[0].start()

    s_last, r_last = ids("s", 1), ids("r", 1)
    copy_last = Copy(
        last_s,
        last_r,
        ss.at[s_last],
        rs.at[r_last],
        (dp, lax.rem(z + 1, nblk)),
        z < nblk - 1,
    )

    def finish_output():
        for i in range(2):
            mine = out_from_self(i, c, z)
            Copy(
                out_r.at[i], out_r.at[i], ss.at[0], rs.at[r_out + i], sib, jnp.logical_not(mine)
            ).wait_recv()
            live = rdiv[1:2, i * half : (i + 1) * half]
            out_ref[i * half : (i + 1) * half, :] = (out_r[i].astype(F32) * live).T.astype(BF16)

    def finish_sums():
        for i in range(2):
            mine = jnp.logical_and(own_worker, c == i)
            Copy(
                gfin.at[i], gfin.at[i], ss.at[0], rs.at[r_fin + i], sib, jnp.logical_not(mine)
            ).wait_recv()
            grad_sums = gfin[i].astype(F32) * rdiv[0:1, i * half : (i + 1) * half]
            gs_ref[i * half : (i + 1) * half, :] = grad_sums.T.astype(BF16)

        is_last = jnp.where(iota((16, feat), 1).astype(F32) == cnt - 1.0, 1.0, 0.0).astype(BF16)
        last_s[...] = mm(is_last, gs_ref[...], NN).astype(BF16)
        copy_last.start()

    def finish_came():
        Copy(last_r, last_r, ss.at[0], rs.at[r_last], sib, z > 0).wait_recv()

        @pl.when(z == 0)
        def _():
            last_r[...] = jnp.zeros_like(last_r)

        came_ref[...] = last_r[...]

    def key_step(t, carry):
        both = t < 2 * w + 2
        kb = jnp.where(both, lax.div(t, 2), t - w - 1)
        slot = jnp.where(both, 1 - lax.rem(t, 2), 1)
        first = jnp.logical_or(jnp.logical_not(both), lax.rem(t, 2) == 0)
        last = jnp.logical_or(jnp.logical_not(both), lax.rem(t, 2) == 1)

        @pl.when(first)
        def _():
            dk[...] = jnp.zeros_like(dk)
            dv[...] = jnp.zeros_like(dv)

        backward_step(slot, kb)

        @pl.when(last)
        def _():
            grad_key = turned(dk[...] * att_scale, kb, -1.0)
            grad_value = dv[...].astype(BF16)
            normed = n1[kb]
            k_t[kb] = grad_key
            v_t[kb] = grad_value
            gwqkv[1] += mm(normed, grad_key, NT)
            gwqkv[2] += mm(normed, grad_value, NT)

            @pl.when(jnp.logical_or(kb == w, kb == 7 - w))
            def _():
                slot = jnp.where(kb == w, 0, 1)
                grad_query = turned(dq[slot] * att_scale, kb, -1.0)
                q_t[slot] = grad_query
                gwqkv[0] += mm(normed, grad_query, NT)


        @pl.when(jnp.logical_and(lax.rem(t, 2) == 1, t < 2 * EARLY))
        def _():
            row_block(lax.div(t, 2))

        run_after("K", t)
        return carry

    def row_block(kb):
        @pl.when(kb <= 7 - w)
        def _():
            big[0, :, 0:half] = mm(weights[1], k_t[kb], NN) + mm(weights[2], v_t[kb], NN)
            own = jnp.logical_or(kb == w, kb == 7 - w)
            slot = jnp.where(kb == w, 0, 1)

            @pl.when(own)
            def _():
                big[0, :, 0:half] += mm(weights[0], q_t[slot], NN)

            grad_n1 = big[0, :, 0:half]
            unit, inverse = norm_parts(p_all[kb].astype(F32))
            gain_acc[0] += lane_fold(grad_n1 * unit)
            e = grad_n1 * gcol[0]
            total = inverse * (
                e
                - jnp.mean(e, axis=0, keepdims=True)
                - unit * jnp.mean(e * unit, axis=0, keepdims=True)
            )
            ppart[kb] = (total + jnp.where(own, 1.0, 0.0) * gmid[slot]).astype(BF16)

        @pl.when(kb > 7 - w)
        def _():
            ppart[kb] = jnp.zeros(ppart.shape[1:], BF16)

        rc_copy(kb).start()

        @pl.when(lax.rem(kb, 2) == 1)
        def _():
            combine(lax.div(kb, 2))

    def late_row_block(kb, carry):
        row_block(kb)
        run_after("R", kb)
        return carry

    lax.fori_loop(0, 9, key_step, 0)
    for i in range(3):
        wg[9 + i] = gwqkv[i].astype(BF16)
    run_after("W")
    lax.fori_loop(EARLY, 8, late_row_block, 0)

    run_after("end")

    for one in sends:
        one.wait_send()
    pass_on_sent()
    copy_last.wait_send()
    for one in outside_late:
        one.wait_send()
    for i in range(2):
        cot_copy(i)[1].wait_send()

    def close_key(kb, carry):
        rc_copy(kb).wait_send()
        return carry

    lax.fori_loop(0, 8, close_key, 0)

    def close_block(zb, carry):
        rz_copy(zb).wait_send()
        fin_copy(zb).wait_send()
        return carry

    lax.fori_loop(0, 4, close_block, 0)
    for phase in range(1, 5):
        for one in gain_list(phase):
            one.wait_send()
    for one in red:
        one.wait_sends()
        one.store().wait()


def out_from_self(i, c, z):
    chip = 2 * c + 1 - jnp.where(z < 2, z, 3 - z)
    core = jnp.where(z < 2, i, 1 - i)
    return jnp.logical_and(core == c, chip == z)


def expand_kernel(
    slots_ref, gs_ref, came_ref, out_ref, ggain_ref, dn_ref, up0, up1, up2, up3, wo_ref, wq_ref, wk_ref, wv_ref,
    bytes_out, out_out, ga_out, gf_out, dn_out, up_out, wo_out, wq_out, wk_out, wv_out,
):
    rows = slots_ref[0]
    slot_iota = iota((512, 128), 0).astype(F32)
    member = jnp.concatenate(
        [(slot_iota == rows[r : r + 1, :]).astype(F32).astype(BF16) for r in range(4)], axis=1
    )
    first = iota((16, 128), 0) == 0
    lead = jnp.concatenate(
        [
            jnp.where(jnp.logical_and(first, rows[r : r + 1, :] < -0.5), 1.0, 0.0).astype(BF16)
            for r in range(4)
        ],
        axis=1,
    )
    bytes_out[...] = mm(member, gs_ref[...], TN) + mm(lead, came_ref[...], TN)
    out_out[...] = out_ref[...].astype(F32)
    ga_out[...] = ggain_ref[0:1, :]
    gf_out[...] = ggain_ref[1:2, :]
    dn_out[...] = dn_ref[0].astype(F32)
    for j, up in enumerate((up0, up1, up2, up3)):
        up_out[:, 512 * j : 512 * (j + 1)] = up[0].astype(F32)
    for src, dst in ((wo_ref, wo_out), (wq_ref, wq_out), (wk_ref, wk_out), (wv_ref, wv_out)):
        dst[...] = src[0].astype(F32)


def fast_local(
    bytes_in, flags, lengths, cotangent, w_query, w_key, w_value, w_out, w_up, w_down, gain_attn, gain_ffn
):
    meta_flags = flags.reshape(32, 128)
    freqs = np.float32(ROTARY_BASE) ** (-2.0 * np.arange(32, dtype=np.float32) / np.float32(64))
    freq = np.ascontiguousarray(np.broadcast_to(freqs.astype(np.float32)[:, None], (32, 128)))
    vm = pl.BlockSpec(memory_space=pltpu.VMEM)
    hbm = pl.BlockSpec(memory_space=pl.ANY)
    hb = lambda n: pltpu.VMEM((n, 512, 256), BF16)
    hbf = lambda n: pltpu.VMEM((n, 512, 256), F32)
    sq = lambda n, t: pltpu.VMEM((n, 512, 512), t)
    scratch = dict(
        bytes_v=sq(8, BF16),
        weights=sq(4, BF16),
        wup=sq(4, BF16),
        wdn=sq(4, BF16),
        meta=pltpu.VMEM((2, 4, 40, 128), jnp.int32),
        tail=pltpu.VMEM((16, 512), BF16),
        p_own=hb(2),
        relay=pltpu.VMEM((512, 256), BF16),
        p_all=hb(8),
        n1=hb(8),
        k_t=hb(8),
        v_t=hb(8),
        q_t=hb(2),
        tab_c=pltpu.VMEM((8, 32, 256), F32),
        tab_s=pltpu.VMEM((8, 32, 256), F32),
        pos=pltpu.VMEM((8, 8, 256), F32),
        gcol=hbf(2),
        cot_own=hb(2),
        cot_w=hb(2),
        o_acc=hbf(2),
        m_sc=pltpu.VMEM((2, 8, 256), F32),
        l_sc=pltpu.VMEM((2, 8, 256), F32),
        att=pltpu.VMEM((512, 512), BF16),
        gb=pltpu.VMEM((512, 512), BF16),
        hat2=pltpu.VMEM((512, 512), F32),
        d_o=pltpu.VMEM((512, 512), BF16),
        d_sc=pltpu.VMEM((2, 8, 256), F32),
        gmid=hbf(2),
        dk=pltpu.VMEM((512, 256), F32),
        dv=pltpu.VMEM((512, 256), F32),
        dq=hbf(2),
        gwqkv=sq(3, F32),
        big=sq(2, F32),
        wg=sq(12, BF16),
        r1=pltpu.VMEM((12, 256, 512), BF16),
        r2=pltpu.VMEM((12, 128, 512), BF16),
        r3=pltpu.VMEM((12, 64, 512), BF16),
        r4=pltpu.VMEM((12, 32, 512), BF16),
        r5=pltpu.VMEM((12, 16, 512), BF16),
        ppart=hb(8),
        rc=hb(4),
        rz=hb(4),
        gfin=hb(2),
        out_s=hb(2),
        out_r=hb(2),
        rdiv=pltpu.VMEM((16, 512), F32),
        last_s=pltpu.VMEM((16, 512), BF16),
        last_r=pltpu.VMEM((16, 512), BF16),
        gain_acc=pltpu.VMEM((2, 512, 128), F32),
        gain_s=pltpu.VMEM((4, 8, 512), F32),
        gain_r=pltpu.VMEM((6, 8, 512), F32),
        ss=pltpu.SemaphoreType.DMA((224,)),
        rs=pltpu.SemaphoreType.DMA((224,)),
        ls=pltpu.SemaphoreType.DMA((32,)),
    )
    out, gs, came, slots, wgrad, ggain = pl.pallas_call(
        layer_kernel,
        out_shape=(
            jax.ShapeDtypeStruct((512, 512), BF16),
            jax.ShapeDtypeStruct((512, 512), BF16),
            jax.ShapeDtypeStruct((16, 512), BF16),
            jax.ShapeDtypeStruct((32, 128), F32),
            jax.ShapeDtypeStruct((12, 512, 512), BF16),
            jax.ShapeDtypeStruct((8, 512), F32),
        ),
        in_specs=[hbm, vm, vm, hbm, hbm, hbm, hbm, hbm, hbm, hbm, vm, vm, vm],
        out_specs=(vm, vm, vm, vm, hbm, vm),
        scratch_shapes=list(scratch.values()),
        compiler_params=pltpu.CompilerParams(
            collective_id=0, has_side_effects=True, vmem_limit_bytes=60 * 2**20
        ),
        name="layer",
    )(
        bytes_in, meta_flags, lengths, cotangent, w_query, w_key, w_value, w_out, w_up, w_down,
        gain_attn.reshape(1, 512), gain_ffn.reshape(1, 512), freq,
    )
    block = lambda rows, cols, index: pl.BlockSpec((1, rows, cols), index)
    ups = [block(64, 512, functools.partial(lambda j, i: (2 * j + 1, i, 0), j)) for j in range(4)]
    rest = [block(64, 512, functools.partial(lambda j, i: (j, i, 0), j)) for j in range(8, 12)]
    whole = lambda shape: pl.BlockSpec(shape, lambda i: (0, 0))
    flat = lambda rows, cols: pl.BlockSpec((rows, cols), lambda i: (i, 0))
    grad_bytes, out, g_attn, g_ffn, dn, up, wo, wq, wk, wv = pl.pallas_call(
        expand_kernel,
        grid=(8,),
        out_shape=(
            jax.ShapeDtypeStruct((4096, 512), F32),
            jax.ShapeDtypeStruct((512, 512), F32),
            jax.ShapeDtypeStruct((1, 512), F32),
            jax.ShapeDtypeStruct((1, 512), F32),
            jax.ShapeDtypeStruct((2048, 512), F32),
            jax.ShapeDtypeStruct((512, 2048), F32),
        )
        + (jax.ShapeDtypeStruct((512, 512), F32),) * 4,
        in_specs=[
            block(4, 128, lambda i: (i, 0, 0)),
            whole((512, 512)),
            whole((16, 512)),
            flat(64, 512),
            whole((8, 512)),
            block(256, 512, lambda i: (2 * lax.div(i, 2), lax.rem(i, 2), 0)),
        ]
        + ups
        + rest,
        out_specs=(flat(512, 512), flat(64, 512), whole((1, 512)), whole((1, 512)), flat(256, 512), flat(64, 2048)) + (flat(64, 512),) * 4,
        compiler_params=pltpu.CompilerParams(vmem_limit_bytes=60 * 2**20),
        name="expand",
    )(slots.reshape(8, 4, 128), gs, came, out, ggain, wgrad, wgrad, wgrad, wgrad, wgrad, wgrad, wgrad, wgrad, wgrad)
    return out, grad_bytes, wq, wk, wv, wo, up, dn, g_attn.reshape(512), g_ffn.reshape(512)


def passed_along(block, axis, distance):
    devices = range(lax.axis_size(axis))
    route = [((i - distance) % len(devices), i) for i in devices]
    return lax.ppermute(block, axis, route)


def from_behind(value, axis, by):
    count = lax.axis_size(axis)
    pairs = [(i, i + by) for i in range(count) if 0 <= i + by < count]
    return lax.ppermute(value, axis, pairs)


def rotate(vectors, positions, direction):
    half_dim = vectors.shape[-1] // 2
    freqs = ROTARY_BASE ** (-2.0 * jnp.arange(half_dim, dtype=jnp.float32) / vectors.shape[-1])
    angles = positions.astype(jnp.float32)[:, None] * freqs[None, :]
    cosine = jnp.cos(angles)[:, None, :]
    sine = direction * jnp.sin(angles)[:, None, :]
    first_half = vectors[..., :half_dim]
    second_half = vectors[..., half_dim:]
    return jnp.concatenate(
        [first_half * cosine - second_half * sine, second_half * cosine + first_half * sine],
        axis=-1,
    )


def layer_norm_parts(values, gain):
    center = values - jnp.mean(values, axis=-1, keepdims=True)
    spread = jnp.mean(center * center, axis=-1, keepdims=True)
    inverse = lax.rsqrt(spread + EPSILON)
    normed = center * inverse
    return (normed * gain, normed, inverse)


def layer_norm_back(grad_in, normed, inverse, gain):
    scaled = grad_in * gain
    grad_values = inverse * (
        scaled
        - jnp.mean(scaled, axis=-1, keepdims=True)
        - normed * jnp.mean(scaled * normed, axis=-1, keepdims=True)
    )
    grad_gain = jnp.sum(grad_in * normed, axis=0)
    return (grad_values, grad_gain)


def pass_grads(grad_key, grad_value):
    return (
        passed_along(grad_key.astype(jnp.bfloat16), "blk", 1).astype(grad_key.dtype),
        passed_along(grad_value.astype(jnp.bfloat16), "blk", 1).astype(grad_value.dtype),
    )


def local(
    bytes_in,
    flags,
    lengths,
    cotangent,
    w_query,
    w_key,
    w_value,
    w_out,
    w_up,
    w_down,
    gain_attn,
    gain_ffn,
):
    blocks = lax.axis_size("blk")
    own_index = lax.axis_index("blk")
    seg_rows = cotangent.shape[0]
    byte_rows = bytes_in.shape[0]
    features = bytes_in.shape[1]
    scale = HEAD_DIM ** (-0.5)
    running = jnp.cumsum(flags)
    slot_of = running - 1
    seg_count = running[-1]
    slot_ids = jnp.arange(seg_rows, dtype=jnp.int32)
    member = (slot_of[None, :] == slot_ids[:, None]).astype(jnp.bfloat16)
    seg_sums = jnp.dot(member, bytes_in, preferred_element_type=jnp.float32)
    seg_tally = jnp.sum(member, axis=1, dtype=jnp.float32)
    leading = slot_of < 0
    tail_sum = jnp.dot(
        leading.astype(jnp.bfloat16)[None, :], bytes_in, preferred_element_type=jnp.float32
    )
    tail_count = jnp.sum(leading.astype(jnp.float32), keepdims=True)
    got_sum, got_count = from_behind((tail_sum, tail_count), "blk", -1)
    last_slot = slot_ids == seg_count - 1
    seg_sums = seg_sums + jnp.where(last_slot[:, None], got_sum, 0.0)
    seg_tally = seg_tally + jnp.where(last_slot, got_count[0], 0.0)
    divisor = jnp.maximum(seg_tally, 1.0)
    pooled = seg_sums / divisor[:, None]
    starts = jnp.cumsum(lengths[0]) - lengths[0]
    byte_at = own_index * byte_rows + jnp.arange(byte_rows, dtype=jnp.int32)
    prior_flags = jnp.sum(
        flags[None, :] * (byte_at[None, :] < starts[:, None]).astype(jnp.int32), axis=1
    )
    all_counts, all_prior = (
        lax.all_gather(seg_count[None], "blk", axis=0, tiled=True),
        lax.all_gather(prior_flags[None, :], "blk", axis=0, tiled=True),
    )
    offsets = jnp.cumsum(all_counts) - all_counts
    seq_first = jnp.sum(all_prior, axis=0)
    dev_ids = jnp.arange(blocks, dtype=jnp.int32)

    def layout(first_row, row_count):
        row_index = first_row + jnp.arange(row_count, dtype=jnp.int32)
        owner_dev = row_index // seg_rows
        within = row_index % seg_rows
        dev_pick = owner_dev[:, None] == dev_ids[None, :]
        dev_base = jnp.sum(jnp.where(dev_pick, offsets[None, :], 0), axis=1)
        dev_have = jnp.sum(jnp.where(dev_pick, all_counts[None, :], 0), axis=1)
        return (dev_base + jnp.minimum(within, dev_have - 1), within < dev_have)

    query_pos, query_live = layout(own_index * seg_rows, seg_rows)
    query_first = jnp.max(
        jnp.where(seq_first[None, :] <= query_pos[:, None], seq_first[None, :], 0), axis=1
    )

    def visible(first_row, row_count):
        key_pos, key_live = layout(first_row, row_count)
        return (
            (key_pos[None, :] <= query_pos[:, None])
            & (key_pos[None, :] >= query_first[:, None])
            & key_live[None, :]
        )

    normed_attn, unit_attn, scale_attn = layer_norm_parts(pooled, gain_attn)
    n_one = normed_attn.astype(jnp.bfloat16)
    query_pre = jnp.dot(n_one, w_query, preferred_element_type=jnp.float32)
    query_rot = rotate(query_pre.reshape(seg_rows, HEADS, HEAD_DIM), query_pos, 1.0).astype(
        jnp.bfloat16
    )
    key_pre = jnp.dot(n_one, w_key, preferred_element_type=jnp.float32)
    key_rot = (
        rotate(key_pre.reshape(seg_rows, HEADS, HEAD_DIM), query_pos, 1.0)
        .reshape(seg_rows, features)
        .astype(jnp.bfloat16)
    )
    value_low = jnp.dot(n_one, w_value, preferred_element_type=jnp.float32).astype(jnp.bfloat16)
    start_state = (
        jnp.full((HEADS, seg_rows), NEGATIVE, jnp.float32),
        jnp.zeros((HEADS, seg_rows), jnp.float32),
        jnp.zeros((seg_rows, HEADS, HEAD_DIM), jnp.float32),
    )
    key_piece = lax.all_gather(key_rot, "blk", axis=0, tiled=True)
    value_piece = lax.all_gather(value_low, "blk", axis=0, tiled=True)
    row_count = key_piece.shape[0]
    allowed = visible(jnp.int32(0), row_count)

    def absorb_update(running_state):
        row_max, row_sum, weighted = running_state
        scores = (
            jnp.einsum(
                "qhe,khe->hqk",
                query_rot,
                key_piece.reshape(row_count, HEADS, HEAD_DIM),
                preferred_element_type=jnp.float32,
            )
            * scale
        )
        scores = jnp.where(allowed[None], scores, NEGATIVE)
        new_max = jnp.maximum(row_max, jnp.max(scores, axis=-1))
        weights = jnp.where(allowed[None], jnp.exp(scores - new_max[:, :, None]), 0.0)
        shrink = jnp.exp(row_max - new_max)
        row_sum = jnp.sum(weights, axis=-1)
        weighted = weighted * shrink.T[:, :, None] + jnp.einsum(
            "hqk,khe->qhe",
            weights.astype(jnp.bfloat16),
            value_piece.reshape(row_count, HEADS, HEAD_DIM),
            preferred_element_type=jnp.float32,
        )
        return (new_max, row_sum, weighted)

    row_max, row_sum, weighted = lax.cond(
        jnp.any(allowed), absorb_update, lambda unchanged: unchanged, start_state
    )
    log_total = row_max + jnp.log(row_sum)
    attended_full = weighted / row_sum.T[:, :, None]
    attended = attended_full.reshape(seg_rows, features).astype(jnp.bfloat16)
    middle = pooled + jnp.dot(attended, w_out, preferred_element_type=jnp.float32)
    normed_ffn, unit_ffn, scale_ffn = layer_norm_parts(middle, gain_ffn)
    n_two = normed_ffn.astype(jnp.bfloat16)
    up_proj = jnp.dot(n_two, w_up, preferred_element_type=jnp.float32)
    act_full, gelu_back = jax.vjp(lambda inner: jax.nn.gelu(inner, approximate=False), up_proj)
    act_low = act_full.astype(jnp.bfloat16)
    result = middle + jnp.dot(act_low, w_down, preferred_element_type=jnp.float32)
    live_rows = query_live.astype(jnp.float32)[:, None]
    output = result * live_rows
    grad_out = cotangent * live_rows
    grad_branch = grad_out.astype(jnp.bfloat16)
    grad_w_down = jnp.einsum("sf,sd->fd", act_low, grad_branch, preferred_element_type=jnp.float32)
    grad_act = jnp.einsum("sd,fd->sf", grad_branch, w_down, preferred_element_type=jnp.float32)
    grad_up = gelu_back(grad_act)[0].astype(jnp.bfloat16)
    grad_w_up = jnp.einsum("sd,sf->df", n_two, grad_up, preferred_element_type=jnp.float32)
    grad_n_two = jnp.einsum("sf,df->sd", grad_up, w_up, preferred_element_type=jnp.float32)
    grad_mid_norm, grad_gain_ffn = layer_norm_back(grad_n_two, unit_ffn, scale_ffn, gain_ffn)
    grad_middle = grad_out + grad_mid_norm
    grad_attn_branch = grad_middle.astype(jnp.bfloat16)
    grad_w_out = jnp.einsum(
        "sd,se->de", attended, grad_attn_branch, preferred_element_type=jnp.float32
    )
    grad_attended = jnp.einsum(
        "se,de->sd", grad_attn_branch, w_out, preferred_element_type=jnp.float32
    ).astype(jnp.bfloat16)
    grad_att_three = grad_attended.reshape(seg_rows, HEADS, HEAD_DIM)
    row_dot = jnp.sum(grad_att_three.astype(jnp.float32) * attended_full, axis=-1).T

    def block_grads(key_piece, value_piece, source, grad_parts):
        allowed = visible(source * seg_rows, seg_rows)

        def block_update(grad_parts):
            grad_key, grad_value, grad_query = grad_parts
            key_three = key_piece.reshape(seg_rows, HEADS, HEAD_DIM)
            value_three = value_piece.reshape(seg_rows, HEADS, HEAD_DIM)
            scores = (
                jnp.einsum("qhe,khe->hqk", query_rot, key_three, preferred_element_type=jnp.float32)
                * scale
            )
            prob_full = jnp.where(allowed[None], jnp.exp(scores - log_total[:, :, None]), 0.0)
            grad_value = grad_value + jnp.einsum(
                "hqk,qhe->khe",
                prob_full.astype(jnp.bfloat16),
                grad_att_three,
                preferred_element_type=jnp.float32,
            ).reshape(seg_rows, features)
            grad_prob = jnp.einsum(
                "qhe,khe->hqk", grad_att_three, value_three, preferred_element_type=jnp.float32
            )
            grad_scores = (prob_full * (grad_prob - row_dot[:, :, None])).astype(jnp.bfloat16)
            grad_query = (
                grad_query
                + jnp.einsum(
                    "hqk,khe->qhe", grad_scores, key_three, preferred_element_type=jnp.float32
                )
                * scale
            )
            grad_key = grad_key + (
                jnp.einsum(
                    "hqk,qhe->khe", grad_scores, query_rot, preferred_element_type=jnp.float32
                )
                * scale
            ).reshape(seg_rows, features)
            return (grad_key, grad_value, grad_query)

        return lax.cond(jnp.any(allowed), block_update, lambda unchanged: unchanged, grad_parts)

    zero_rows = jnp.zeros((seg_rows, features), jnp.float32)
    zero_query = jnp.zeros((seg_rows, HEADS, HEAD_DIM), jnp.float32)

    def visit(visit_no, loop_state):
        key_piece, value_piece, grad_key, grad_value, grad_query = loop_state
        source = (own_index - visit_no) % blocks
        grad_key, grad_value, grad_query = block_grads(
            key_piece, value_piece, source, (grad_key, grad_value, grad_query)
        )
        key_piece, value_piece = from_behind((key_piece, value_piece), "blk", 1)
        grad_key, grad_value = pass_grads(grad_key, grad_value)
        return (key_piece, value_piece, grad_key, grad_value, grad_query)

    loop_out = lax.fori_loop(
        0, blocks, visit, (key_rot, value_low, zero_rows, zero_rows, zero_query)
    )
    grad_key_sum, grad_value_sum, grad_query_rot = (loop_out[2], loop_out[3], loop_out[4])
    grad_query = (
        rotate(grad_query_rot, query_pos, -1.0).reshape(seg_rows, features).astype(jnp.bfloat16)
    )
    grad_key = (
        rotate(grad_key_sum.reshape(seg_rows, HEADS, HEAD_DIM), query_pos, -1.0)
        .reshape(seg_rows, features)
        .astype(jnp.bfloat16)
    )
    grad_value_low = grad_value_sum.astype(jnp.bfloat16)
    grad_w_query = jnp.einsum("sd,se->de", n_one, grad_query, preferred_element_type=jnp.float32)
    grad_w_key = jnp.einsum("sd,se->de", n_one, grad_key, preferred_element_type=jnp.float32)
    grad_w_value = jnp.einsum(
        "sd,se->de", n_one, grad_value_low, preferred_element_type=jnp.float32
    )
    grad_n_one = jnp.einsum("se,de->sd", grad_query, w_query, preferred_element_type=jnp.float32)
    grad_n_one = grad_n_one + jnp.einsum(
        "se,de->sd", grad_key, w_key, preferred_element_type=jnp.float32
    )
    grad_n_one = grad_n_one + jnp.einsum(
        "se,de->sd", grad_value_low, w_value, preferred_element_type=jnp.float32
    )
    grad_pool_norm, grad_gain_attn = layer_norm_back(grad_n_one, unit_attn, scale_attn, gain_attn)
    grad_pooled = grad_middle + grad_pool_norm
    grad_sums = (grad_pooled / divisor[:, None]).astype(jnp.bfloat16)
    last_grad = jnp.dot(
        last_slot.astype(jnp.bfloat16)[None, :], grad_sums, preferred_element_type=jnp.float32
    ).astype(jnp.bfloat16)
    came_grad = from_behind(last_grad, "blk", 1)
    spread_rows = jnp.take(grad_sums, jnp.maximum(slot_of, 0), axis=0)
    grad_bytes = jnp.where(leading[:, None], came_grad, spread_rows).astype(jnp.float32)
    (
        grad_w_query,
        grad_w_key,
        grad_w_value,
        grad_w_out,
        grad_w_up,
        grad_w_down,
        grad_gain_attn,
        grad_gain_ffn,
    ) = lax.psum(
        (
            grad_w_query,
            grad_w_key,
            grad_w_value,
            grad_w_out,
            grad_w_up,
            grad_w_down,
            grad_gain_attn,
            grad_gain_ffn,
        ),
        ("dp", "blk"),
    )
    return (
        output,
        grad_bytes,
        grad_w_query,
        grad_w_key,
        grad_w_value,
        grad_w_out,
        grad_w_up,
        grad_w_down,
        grad_gain_attn,
        grad_gain_ffn,
    )


def solution(mesh):
    fits = mesh.shape["blk"] == 4 and mesh.shape["dp"] == 8
    return jax.shard_map(
        fast_local if fits else local,
        mesh=mesh,
        in_specs=(
            P(("dp", "blk"), None),
            P(("dp", "blk")),
            P("dp", None),
            P(("dp", "blk"), None),
            P(),
            P(),
            P(),
            P(),
            P(),
            P(),
            P(),
            P(),
        ),
        out_specs=(
            P(("dp", "blk"), None),
            P(("dp", "blk"), None),
            P(),
            P(),
            P(),
            P(),
            P(),
            P(),
            P(),
            P(),
        ),
        check_vma=False,
    )
```

```python
import functools
import math

import jax
import jax.numpy as jnp
import numpy as np
from jax import lax
from jax.experimental import pallas as pl
from jax.experimental.pallas import tpu as pltpu
from jax.sharding import PartitionSpec as P

HEADS = 8
HEAD_DIM = 64
EPSILON = 1e-05
ROTARY_BASE = 10000.0
NEGATIVE = -1e30
LOG2E = math.log2(math.e)

MESH = pl.DeviceIdType.MESH
F32 = jnp.float32
BF16 = jnp.bfloat16
NN = (((1,), (0,)), ((), ()))
NT = (((1,), (1,)), ((), ()))
TN = (((0,), (0,)), ((), ()))


def mm(a, b, dims):
    return lax.dot_general(a, b, dims, preferred_element_type=F32)


def iota(shape, dim):
    return lax.broadcasted_iota(jnp.int32, shape, dim)


class Copy:
    def __init__(self, src, dst, send_sem, recv_sem, device, cond=None):
        self.parts = (src, dst, send_sem, recv_sem)
        self.device = device
        self.cond = cond

    def _do(self, act):
        def run():
            src, dst, send_sem, recv_sem = self.parts
            act(
                pltpu.make_async_remote_copy(
                    src_ref=src,
                    dst_ref=dst,
                    send_sem=send_sem,
                    recv_sem=recv_sem,
                    device_id=self.device,
                    device_id_type=MESH,
                )
            )

        if self.cond is None:
            run()
        else:
            pl.when(self.cond)(run)

    def start(self):
        self._do(lambda d: d.start())

    def wait_send(self):
        self._do(lambda d: d.wait_send())

    def wait_recv(self):
        self._do(lambda d: d.wait_recv())


CHUNKS = (
    (0, 2, "F0"),
    (2, 4, "F1"),
    (4, 6, "F2"),
    (6, 9, "post"),
    (9, 10, "W"),
    (10, 12, "W"),
)
SEMS_AR = 18
EARLY = 4
SCHEDULE = {
    "F2": ((0, 1), (1, 1)),
    "F3": ((2, 1),),
    "K0": ((3, 1),),
    "K1": ((0, 2), (1, 2)),
    "K2": ((2, 2),),
    "K3": ((0, 3), (1, 3)),
    "K4": ((2, 3), (3, 2)),
    "K5": ((0, 4), (1, 4), (3, 3)),
    "K6": ((2, 4),),
    "K7": ((0, 5), (3, 4), "deliver0", (2, 5)),
    "R4": ((1, 5),),
    "R6": ((4, 1), (5, 1)),
    "end": ("gain0", (0, 6), "deliver1", "out", (1, 6), "deliver3", "gain1", (2, 6), (3, 5), (4, 2), "gain2", (5, 2), (4, 3), (0, 7), "gain3", (1, 7), (2, 7), (4, 4), (5, 3), "gain4", (0, 8), "deliver2", (3, 6), (1, 8), (5, 4), (2, 8), (4, 5), (3, 7), "sums", (4, 6), (5, 5), (0, 9), "came", (0, 10), (4, 7), (5, 6), (1, 9), (3, 8), (2, 9), (4, 8), (1, 10), (5, 7), (2, 10), (4, 9), (5, 8), (4, 10), (3, 9), (3, 10), (5, 9), (5, 10)),
}


def layer_kernel(
    bytes_hbm,
    flags_ref,
    lengths_ref,
    cot_hbm,
    wq_hbm,
    wk_hbm,
    wv_hbm,
    wo_hbm,
    wup_hbm,
    wdn_hbm,
    gain_attn_ref,
    gain_ffn_ref,
    freq_ref,
    out_ref,
    gs_ref,
    came_ref,
    slots_ref,
    wgrad_hbm,
    ggain_ref,
    bytes_v,
    weights,
    wup,
    wdn,
    meta,
    tail,
    p_own,
    relay,
    p_all,
    n1,
    k_t,
    v_t,
    q_t,
    tab_c,
    tab_s,
    pos,
    gcol,
    cot_own,
    cot_w,
    o_acc,
    m_sc,
    l_sc,
    att,
    gb,
    hat2,
    d_o,
    d_sc,
    gmid,
    dk,
    dv,
    dq,
    gwqkv,
    big,
    wg,
    r1,
    r2,
    r3,
    r4,
    r5,
    ppart,
    rc,
    rz,
    gfin,
    out_s,
    out_r,
    rdiv,
    last_s,
    last_r,
    gain_acc,
    gain_s,
    gain_r,
    ss,
    rs,
    ls,
):
    cot_v, acc = hat2, big.at[0]
    dp = lax.axis_index("dp")
    z = lax.axis_index("blk")
    feat = 512
    half = 256
    nblk = 4
    c = lax.rem(dp, 2)
    x = lax.rem(lax.div(dp, 2), 2)
    y = lax.div(dp, 4)
    sib = (dp + 1 - 2 * c, z)
    xnb = (dp + 2 - 4 * x, z)
    ynb = (dp + 4 - 8 * y, z)
    g = lax.div(z, 2)
    zl = lax.rem(z, 2)
    w = 2 * (1 - zl) + c
    zo = 4 * g + 1 - z
    near = 1 + g
    is_near = z == near
    own_worker = g == c

    def dev(core, zz):
        return (dp - c + core, zz)

    counter = {"s": 0, "r": 0, "l": 0}

    def ids(kind, n):
        first = counter[kind]
        counter[kind] = first + n
        return first

    sends = []

    def go(copy):
        copy.start()
        sends.append(copy)

    l_bytes = ids("l", 8)
    rows_chunk = bytes_v.shape[1]
    l_cot = ids("l", 1)
    load_cot = pltpu.make_async_copy(cot_hbm, cot_v, ls.at[l_cot])
    load_cot.start()
    loads_bytes = [
        pltpu.make_async_copy(
            bytes_hbm.at[pl.ds(i * rows_chunk, rows_chunk)], bytes_v.at[i], ls.at[l_bytes + i]
        )
        for i in range(8)
    ]
    for d in loads_bytes:
        d.start()
    l_w = ids("l", 4)
    loads_w = [
        pltpu.make_async_copy(src, weights.at[i], ls.at[l_w + i])
        for i, src in enumerate((wq_hbm, wk_hbm, wv_hbm, wo_hbm))
    ]
    l_f = ids("l", 8)
    loads_f = []
    for j in range(4):
        loads_f.append(
            pltpu.make_async_copy(
                wup_hbm.at[:, pl.ds(j * feat, feat)], wup.at[j], ls.at[l_f + 2 * j]
            )
        )
        loads_f.append(
            pltpu.make_async_copy(
                wdn_hbm.at[pl.ds(j * feat, feat)], wdn.at[j], ls.at[l_f + 2 * j + 1]
            )
        )

    barrier = pltpu.get_barrier_semaphore()
    me_line = c * nblk + z
    line = []
    for k in range(1, 8):
        t = lax.rem(me_line + k, 8)
        line.append((lax.div(t, nblk), lax.rem(t, nblk)))
    for core, zz in line:
        pl.semaphore_signal(barrier, inc=1, device_id=dev(core, zz), device_id_type=MESH)
    for d in (xnb, ynb):
        pl.semaphore_signal(barrier, inc=1, device_id=d, device_id_type=MESH)

    cnt = jnp.sum(flags_ref[...].astype(F32))
    lane_row = iota((1, feat), 1).astype(F32)
    live_row = jnp.where(lane_row < cnt, 1.0, 0.0)
    for d in loads_w:
        d.start()
    for d in loads_f:
        d.start()

    s_meta, r_meta = ids("s", 7), ids("r", 8)
    s_tail, r_tail = ids("s", 1), ids("r", 1)
    copies_meta = [
        Copy(
            meta.at[c, z],
            meta.at[c, z],
            ss.at[s_meta + k],
            rs.at[r_meta + me_line],
            dev(core, zz),
        )
        for k, (core, zz) in enumerate(line)
    ]
    copy_tail = Copy(
        bytes_hbm.at[pl.ds(0, 16)],
        tail,
        ss.at[s_tail],
        rs.at[r_tail],
        (dp, lax.rem(z + nblk - 1, nblk)),
        z > 0,
    )

    def enter():
        pl.semaphore_wait(barrier, 9)
        meta[c, z, 0:32, :] = flags_ref[...]
        meta[c, z, 32:40, :] = jnp.zeros((8, 128), jnp.int32)
        meta[c, z, 32:33, 0:4] = lengths_ref[...]
        for one in copies_meta:
            go(one)
        go(copy_tail)

        @pl.when(z == nblk - 1)
        def _():
            tail[...] = jnp.zeros_like(tail)

    upper = (iota((128, 128), 0) <= iota((128, 128), 1)).astype(F32).astype(BF16)
    ones_sq = jnp.ones((128, 128), BF16)
    below = (iota((32, 32), 1) < iota((32, 32), 0)).astype(F32).astype(BF16)
    own_flags = flags_ref[...].astype(F32)
    flags_low = own_flags.astype(BF16)
    within = mm(flags_low, upper, NN)
    row_sums = mm(flags_low, ones_sq, NN)
    row_base = mm(below, row_sums.astype(BF16), NN)
    slot_of = within + row_base - 1.0
    slots_ref[...] = slot_of

    acc[...] = jnp.zeros_like(acc)
    rdiv[...] = jnp.zeros_like(rdiv)
    slot_iota = iota((feat, 128), 0).astype(F32)
    ones_rows = jnp.ones((16, feat), BF16)

    enter()

    cells = rows_chunk // 8
    for k in range(8):
        loads_bytes[k].wait()
        reach = cells * (k + 1)
        member = jnp.concatenate(
            [
                (slot_iota[0:reach] == slot_of[r : r + 1, :]).astype(F32).astype(BF16)
                for r in range(4 * k, 4 * k + 4)
            ],
            axis=1,
        )
        acc[0:reach, :] += mm(member, bytes_v[k], NN)
        rdiv[:, 0:feat] += mm(
            ones_rows,
            jnp.concatenate([member, jnp.zeros((feat - reach, rows_chunk), BF16)], axis=0)
            if reach < feat
            else member,
            NT,
        )

    for i, gain in enumerate((gain_attn_ref, gain_ffn_ref)):
        row = jnp.broadcast_to(gain[...], (128, feat))
        col = row.T
        gcol[i] = jnp.concatenate([col, col], axis=1)

    for core, zz in line:
        Copy(
            meta.at[core, zz],
            meta.at[core, zz],
            ss.at[0],
            rs.at[r_meta + core * nblk + zz],
            sib,
        ).wait_recv()
    Copy(tail, tail, ss.at[0], rs.at[r_tail], sib, z < nblk - 1).wait_recv()
    zn = jnp.minimum(z + 1, nblk - 1)
    next_flags = meta[c, zn, 0:16, :].astype(F32).astype(BF16)
    next_within = mm(next_flags, upper, NN)
    has_next = (z < nblk - 1).astype(F32)
    lead = jnp.where(next_within[0:1, :] < 0.5, 1.0, 0.0) * has_next
    is_last16 = iota((feat, 16), 0).astype(F32) == cnt - 1.0
    member_tail = jnp.where(is_last16, lead[:, 0:16], 0.0).astype(BF16)
    sums = acc[...] + mm(member_tail, tail[...], NN)
    tally = rdiv[0:1, :] + jnp.where(lane_row == cnt - 1.0, jnp.sum(lead), 0.0)
    inverse_tally = 1.0 / jnp.maximum(tally, 1.0)
    rdiv[0:1, :] = inverse_tally
    rdiv[1:2, :] = live_row
    pooled_t = (sums.T * inverse_tally).astype(BF16)
    p_own[0] = pooled_t[:, 0:half]
    p_own[1] = pooled_t[:, half:]

    s_p, r_p, r_relay = ids("s", 22), ids("r", 16), ids("r", 1)
    near_c = 1 + c
    pieces = (pl.ds(0, half), pl.ds(half, half))

    def p_piece(src, hb, piece, slot, device, cond=None):
        at = pieces[piece]
        return Copy(
            src.at[at],
            p_all.at[hb, at],
            ss.at[s_p + slot],
            rs.at[r_p + 2 * hb + piece],
            device,
            cond,
        )

    def p_whole(src, hb, slot, device, cond=None):
        return Copy(src, p_all.at[hb], ss.at[s_p + slot], rs.at[r_p + 2 * hb], device, cond)

    other_worker = jnp.logical_not(own_worker)
    to_pair = z != nblk - 1
    inner = jnp.logical_or(z == 1, z == 2)

    outer = jnp.logical_not(inner)

    def outside_copies(cond):
        own_out = jnp.logical_and(other_worker, cond)
        relayed = jnp.logical_and(own_worker, cond)
        return [
            p_piece(p_own.at[c], 2 * z + c, i, 4 + i, dev(c, near_c), own_out) for i in range(2)
        ] + [p_piece(relay, 2 * z + c, i, 4 + i, dev(c, 2 - c), relayed) for i in range(2)]

    outside_late = outside_copies(outer)

    go(Copy(p_own.at[1 - c], relay, ss.at[s_p + 3], rs.at[r_relay], sib, other_worker))
    for i in range(2):
        own_pair = jnp.logical_and(own_worker, to_pair)
        go(p_piece(p_own.at[c], 2 * z + c, i, i, dev(c, zo), own_pair))
    go(p_whole(p_own.at[1 - c], 2 * z + 1 - c, 3, sib, own_worker))
    go(p_whole(p_own.at[c], 2 * z + c, 2, sib, own_worker))

    @pl.when(own_worker)
    def _():
        p_all[2 * z] = p_own[0]
        p_all[2 * z + 1] = p_own[1]

    def p_wait(hb, cond=None):
        Copy(p_all.at[hb], p_all.at[hb], ss.at[0], rs.at[r_p + 2 * hb], sib, cond).wait_recv()

    Copy(relay, relay, ss.at[0], rs.at[r_relay], sib, own_worker).wait_recv()
    for one in outside_copies(inner):
        go(one)
    p_wait(2 * z + c, other_worker)
    for i in range(2):
        passed = jnp.logical_and(other_worker, to_pair)
        go(p_piece(p_all.at[2 * z + c], 2 * z + c, i, i, dev(c, zo), passed))
    p_wait(2 * z + 1 - c, other_worker)

    load_cot.wait()
    cot_t = (cot_v[...].T * live_row).astype(BF16)
    cot_own[0] = cot_t[:, 0:half]
    cot_own[1] = cot_t[:, half:]
    lo_here = False
    hi_here = jnp.logical_and(g == c, z >= 2)

    counts = []
    for b in range(nblk):
        counts.append(jnp.sum(meta[g, b, 0:32, :].astype(F32)))
    offsets = [jnp.float32(0.0)]
    for b in range(nblk):
        offsets.append(offsets[-1] + counts[b])
    lens = meta[g, z, 32:40, :].astype(F32)
    first_row = iota((8, 128), 0) == 0
    lane8 = iota((8, 128), 1)
    byte_at = (iota((32, 128), 0) * 128 + iota((32, 128), 1)).astype(F32)
    seq_first = [jnp.float32(0.0)]
    for s in range(1, 4):
        start = jnp.sum(jnp.where(jnp.logical_and(first_row, lane8 < s), lens, 0.0))
        prior = jnp.zeros((32, 128), F32)
        for b in range(nblk):
            prior = prior + jnp.where(
                byte_at + float(b * 4096) < start, meta[g, b, 0:32, :].astype(F32), 0.0
            )
        seq_first.append(jnp.sum(prior))

    freq = jnp.concatenate([freq_ref[...], freq_ref[...]], axis=1)
    lane_half = iota((1, half), 1).astype(F32)
    for hb in range(8):
        b = hb // 2
        j = lane_half + float((hb % 2) * half)
        p = offsets[b] + jnp.minimum(j, counts[b] - 1.0)
        first = jnp.zeros_like(p)
        for s in range(1, 4):
            first = jnp.maximum(first, jnp.where(p >= seq_first[s], seq_first[s], 0.0))
        pos[hb, 0:1, :] = p
        pos[hb, 1:2, :] = first
        angle = freq * p
        tab_c[hb] = jnp.cos(angle)
        tab_s[hb] = jnp.sin(angle)

    def pick(values, b):
        total = jnp.float32(0.0)
        for i, v in enumerate(values):
            total = total + jnp.where(b == i, v, 0.0)
        return total

    gain_col = gcol[0]

    def norm_parts(values):
        mean = jnp.mean(values, axis=0, keepdims=True)
        center = values - mean
        inverse = lax.rsqrt(jnp.mean(center * center, axis=0, keepdims=True) + EPSILON)
        return center * inverse, inverse

    def turned(values, hb, direction):
        cos = tab_c[hb]
        sin = tab_s[hb] * direction
        parts = []
        for h in range(HEADS):
            a = values[64 * h : 64 * h + 32, :]
            b = values[64 * h + 32 : 64 * h + 64, :]
            parts.append(a * cos - b * sin)
            parts.append(b * cos + a * sin)
        return jnp.concatenate(parts, axis=0).astype(BF16)

    for d in loads_w:
        d.wait()

    def keys_values(hb):
        unit, _ = norm_parts(p_all[hb].astype(F32))
        normed = (unit * gcol[0]).astype(BF16)
        n1[hb] = normed
        k_t[hb] = turned(mm(weights[1], normed, TN), hb, 1.0)
        v_t[hb] = mm(weights[2], normed, TN).astype(BF16)

    s_cot, r_cot = ids("s", 2), ids("r", 2)
    early = z < 2
    slot_to = jnp.where(early, 0, 1)
    chip_to = 2 * c + 1 - jnp.where(early, z, 3 - z)

    def cot_copy(i):
        core_to = jnp.where(early, i, 1 - i)
        here = jnp.logical_and(core_to == c, chip_to == z)
        return here, Copy(
            cot_own.at[i],
            cot_w.at[slot_to],
            ss.at[s_cot + i],
            rs.at[r_cot + slot_to],
            dev(core_to, chip_to),
            jnp.logical_not(here),
        )

    def send_cot():
        for i in range(2):
            here, copy = cot_copy(i)
            copy.start()

            @pl.when(here)
            def _():
                cot_w[slot_to] = cot_own[i]

    hq_of = (w, 7 - w)
    first_far, second_far = 2 - g, 3 - 3 * g
    score_scale = HEAD_DIM ** (-0.5) * LOG2E

    def hq_at(slot):
        return jnp.where(slot == 0, w, 7 - w)

    def bias_of(hq, kb):
        b = lax.div(kb, 2)
        j = (iota((half, half), 0) + lax.rem(kb, 2) * half).astype(F32)
        kpos = j + pick(offsets[:nblk], b)
        alive = j < pick(counts, b)
        qpos = pos[hq, 0:1, :]
        qfirst = pos[hq, 1:2, :]
        allowed = jnp.logical_and(alive, jnp.logical_and(kpos <= qpos, kpos >= qfirst))
        return jnp.where(allowed, 0.0, NEGATIVE)

    o_acc[...] = jnp.zeros_like(o_acc)
    l_sc[...] = jnp.zeros_like(l_sc)
    m_sc[...] = jnp.full(m_sc.shape, NEGATIVE, F32)

    def s_at(h):
        return gwqkv.at[h // 4, pl.ds(half * ((h // 2) % 2), half), pl.ds(half * (h % 2), half)]

    o_new = big.at[1, :, pl.ds(0, half)]

    def forward_step(slot, kb):
        hq = hq_at(slot)
        bias = bias_of(hq, kb)
        old = m_sc[slot]
        old_sum = l_sc[slot]
        for h in range(HEADS):
            part = slice(64 * h, 64 * h + 64)
            s_at(h)[...] = mm(k_t[kb, part, :], q_t[slot, part, :], TN)
        tops, sums = [], []
        for h in range(HEADS):
            part = slice(64 * h, 64 * h + 64)
            s = s_at(h)[...] * score_scale + bias
            top = jnp.maximum(old[h : h + 1, :], jnp.max(s, axis=0, keepdims=True))
            prob = jnp.exp2(s - top)
            tops.append(top)
            sums.append(jnp.sum(prob, axis=0, keepdims=True))
            o_new[part, :] = mm(v_t[kb, part, :], prob.astype(BF16), NN)
        new = jnp.concatenate(tops, axis=0)
        shrink = jnp.exp2(old - new)
        m_sc[slot] = new
        l_sc[slot] = old_sum * shrink + jnp.concatenate(sums, axis=0)
        for h in range(HEADS):
            part = slice(64 * h, 64 * h + 64)
            o_acc[slot, part, :] = o_acc[slot, part, :] * shrink[h : h + 1, :] + o_new[part, :]

    def block_nth(n):
        swapped = jnp.where(n < 2, 1 - n, n)
        return jnp.where(z == 0, n, jnp.where(z == 1, swapped, z - n))

    def pass_on(block, slot, cond, onward=None):
        hb = 2 * block + c

        @pl.when(cond)
        def _():
            for i in range(2):
                there = p_all.at[hb, pieces[i]]
                Copy(there, there, ss.at[0], rs.at[r_p + 2 * hb + i], sib).wait_recv()
                if onward is not None:
                    p_piece(p_all.at[hb], hb, i, slot + 2 + i, dev(c, zo), onward).start()
                p_piece(p_all.at[hb], hb, i, slot + i, sib).start()

    def pass_on_sent():
        for block, slot, cond, onward in passes:
            hb = 2 * block + c

            @pl.when(cond)
            def _(hb=hb, slot=slot, onward=onward):
                for i in range(2):
                    if onward is not None:
                        p_piece(p_all.at[hb], hb, i, slot + 2 + i, dev(c, zo), onward).wait_send()
                    p_piece(p_all.at[hb], hb, i, slot + i, sib).wait_send()

    second_near = z == 2
    passes = (
        (zo, 6, z != 2),
        (first_far, 8, is_near, is_near),
        (first_far, 12, jnp.logical_not(is_near)),
        (second_far, 14, second_near, second_near),
        (second_far, 18, zl == 1),
    )
    passes = tuple(p if len(p) == 4 else p + (None,) for p in passes)

    def arrival(n, carry):
        block = block_nth(n)

        @pl.when(n == 1)
        def _():
            for one in outside_late:
                one.start()
            pass_on(*passes[0])
            pass_on(*passes[1])

        @pl.when(n == 2)
        def _():
            pass_on(*passes[2])
            pass_on(*passes[3])

        @pl.when(n == 3)
        def _():
            pass_on(*passes[4])
            send_cot()

        @pl.when(jnp.logical_and(n > 0, n < 3 + zl))
        def _():
            for i in range(2):
                there = p_all.at[2 * block + 1 - c, pieces[i]]
                Copy(
                    there, there, ss.at[0], rs.at[r_p + 2 * (2 * block + 1 - c) + i], sib
                ).wait_recv()

        @pl.when(n < 3 + zl)
        def _():
            def one(i, carry):
                keys_values(2 * block + i)
                return carry

            lax.fori_loop(0, 2, one, 0)

            def query(slot, carry):
                hq = hq_at(slot)

                @pl.when(lax.div(hq, 2) == block)
                def _():
                    q_t[slot] = turned(mm(weights[0], n1[hq], TN), hq, 1.0)

                return carry

            lax.fori_loop(0, 2, query, 0)

            def pair(i, carry):
                slot, kb = lax.div(i, 8), lax.rem(i, 8)
                hq = hq_at(slot)
                q_block, k_block = lax.div(hq, 2), lax.div(kb, 2)

                def came_by(b, m):
                    found = block_nth(0) == b
                    for k in range(1, 4):
                        found = jnp.logical_or(
                            found, jnp.logical_and(block_nth(k) == b, k <= m)
                        )
                    return found

                new_query = jnp.logical_and(q_block == block, came_by(k_block, n))
                new_keys = jnp.logical_and(k_block == block, came_by(q_block, n))
                new = jnp.logical_or(new_query, new_keys)

                @pl.when(jnp.logical_and(kb <= hq, new))
                def _():
                    forward_step(slot, kb)

                return carry

            lax.fori_loop(0, 16, pair, 0)

        return carry

    lax.fori_loop(0, 4, arrival, 0)

    for slot in range(2):
        total = l_sc[slot]
        for h in range(HEADS):
            part = slice(64 * h, 64 * h + 64)
            o_acc[slot, part, :] = o_acc[slot, part, :] * (1.0 / total[h : h + 1, :])
        att[:, slot * half : (slot + 1) * half] = o_acc[slot].astype(BF16)
        m_sc[slot] = m_sc[slot] + jnp.log2(total)

    own_pooled = jnp.concatenate([p_all[hq_of[0]], p_all[hq_of[1]]], axis=1).astype(F32)
    middle = own_pooled + mm(weights[3], att[...], TN)
    unit2, inverse2 = norm_parts(middle)
    hat2[...] = unit2
    gain_col2 = jnp.concatenate([gcol[1], gcol[1]], axis=1)
    n2 = (unit2 * gain_col2).astype(BF16)
    big[0] = middle
    big[1] = jnp.zeros((feat, feat), F32)
    n2_ref = d_o
    n2_ref[...] = n2

    base1 = c * 256
    keep2x, give2x = base1 + x * 128, base1 + (1 - x) * 128
    keep2y, give2y = base1 + y * 128, base1 + (1 - y) * 128
    keep3x, give3x = keep2x + y * 64, keep2x + (1 - y) * 64
    keep3y, give3y = keep2y + x * 64, keep2y + (1 - x) * 64
    keep4x, give4x = keep3x + 32 * zl, keep3x + 32 * (1 - zl)
    keep4y, give4y = keep3y + 32 * zl, keep3y + 32 * (1 - zl)
    keep5x, give5x = keep4x + 16 * g, keep4x + 16 * (1 - g)
    keep5y, give5y = keep4y + 16 * g, keep4y + 16 * (1 - g)
    znb, zfar = (dp, z + 1 - 2 * zl), (dp, lax.rem(z + 2, nblk))
    lanes_x, lanes_y = pl.ds(0, 256), pl.ds(256, 256)

    def rows_of(first, n):
        return pl.ds(pl.multiple_of(first, 16), n)

    class Reduce:
        def __init__(self, chunk):
            self.b0, self.b1 = CHUNKS[chunk][:2]
            self.nb = self.b1 - self.b0
            self.s0, self.r0 = ids("s", SEMS_AR), ids("r", SEMS_AR)
            self.blocks = pl.ds(self.b0, self.nb)
            self.phases = {}

        def _w(self, first, n, lanes):
            return wg.at[self.blocks, rows_of(first, n), lanes]

        def _list(self, phase):
            every = pl.ds(0, 512)
            b, s0, r0 = self.blocks, self.s0, self.r0

            def copy(i, src, dst, device):
                return Copy(src, dst, ss.at[s0 + i], rs.at[r0 + i], device)

            if phase == 1:
                return [copy(0, self._w((1 - c) * 256, 256, every), r1.at[b], sib)]
            if phase == 2:
                return [
                    copy(1, self._w(give2x, 128, lanes_x), r2.at[b, :, lanes_x], xnb),
                    copy(2, self._w(give2y, 128, lanes_y), r2.at[b, :, lanes_y], ynb),
                ]
            if phase == 3:
                return [
                    copy(3, self._w(give3x, 64, lanes_x), r3.at[b, :, lanes_x], ynb),
                    copy(4, self._w(give3y, 64, lanes_y), r3.at[b, :, lanes_y], xnb),
                ]
            if phase == 4:
                return [
                    copy(5, self._w(give4x, 32, lanes_x), r4.at[b, :, lanes_x], znb),
                    copy(6, self._w(give4y, 32, lanes_y), r4.at[b, :, lanes_y], znb),
                ]
            if phase == 5:
                return [
                    copy(7, self._w(give5x, 16, lanes_x), r5.at[b, :, lanes_x], zfar),
                    copy(8, self._w(give5y, 16, lanes_y), r5.at[b, :, lanes_y], zfar),
                ]
            if phase < 10:
                keep_x, keep_y, n, to_x, to_y = (
                    (keep5x, keep5y, 16, zfar, zfar),
                    (keep4x, keep4y, 32, znb, znb),
                    (keep3x, keep3y, 64, ynb, xnb),
                    (keep2x, keep2y, 128, xnb, ynb),
                )[phase - 6]
                mine_x, mine_y = self._f(keep_x, n, lanes_x), self._f(keep_y, n, lanes_y)
                first = 2 * phase - 3
                return [copy(first, mine_x, mine_x, to_x), copy(first + 1, mine_y, mine_y, to_y)]
            return [copy(17, r1.at[b], self._out(base1), sib)]

        def _f(self, first, n, lanes):
            return r1.at[self.blocks, rows_of(first - base1, n), lanes]

        def _out(self, first):
            return wgrad_hbm.at[self.blocks, rows_of(first, 256), pl.ds(0, 512)]

        def start(self, phase):
            for one in self._list(phase):
                one.start()

        def finish(self, phase):
            if phase == 10:
                other = self._out((1 - c) * 256)
                Copy(other, other, ss.at[0], rs.at[self.r0 + 17], sib).wait_recv()
                return
            for one in self._list(phase):
                one.wait_recv()
            if phase > 5:
                return

            def add(i, carry):
                b = self.b0 + i
                if phase == 1:
                    here = (b, rows_of(base1, 256), slice(None))
                    wg[here] = wg[here] + r1[b]
                if phase == 2:
                    for keep, lo in ((keep2x, 0), (keep2y, 256)):
                        here = (b, rows_of(keep, 128), slice(lo, lo + 256))
                        wg[here] = wg[here] + r2[b, :, lo : lo + 256]
                if phase == 3:
                    for keep, lo in ((keep3x, 0), (keep3y, 256)):
                        here = (b, rows_of(keep, 64), slice(lo, lo + 256))
                        wg[here] = wg[here] + r3[b, :, lo : lo + 256]
                if phase == 4:
                    for keep, lo in ((keep4x, 0), (keep4y, 256)):
                        here = (b, rows_of(keep, 32), slice(lo, lo + 256))
                        wg[here] = wg[here] + r4[b, :, lo : lo + 256]
                if phase == 5:
                    for keep, lo in ((keep5x, 0), (keep5y, 256)):
                        total = wg[b, rows_of(keep, 16), lo : lo + 256] + r5[b, :, lo : lo + 256]
                        r1[b, rows_of(keep - base1, 16), lo : lo + 256] = total
                return carry

            lax.fori_loop(0, self.nb, add, 0)

        def step(self, phase):
            self.finish(phase)
            if phase < 10:
                self.begin(phase + 1)

        def begin(self, phase):
            self.start(phase)
            if phase == 10:
                self.store().start()

        def store(self):
            return pltpu.make_async_copy(r1.at[self.blocks], self._out(base1), ls.at[self.store_sem])

        def wait_sends(self):
            for phase in range(1, 11):
                for one in self._list(phase):
                    one.wait_send()

    red = [Reduce(i) for i in range(len(CHUNKS))]
    for one in red:
        one.store_sem = ids("l", 1)

    for d in loads_f:
        d.wait()

    def do(item):
        if not isinstance(item, str):
            if item[0] == "f":
                red[item[1]].finish(item[2])
            elif item[0] == "s":
                red[item[1]].begin(item[2])
            else:
                red[item[0]].step(item[1])
        elif item == "gain0":
            gains_start()
        elif item.startswith("gain"):
            gain_finish(int(item[4:]))
        elif item.startswith("deliver"):
            deliver(int(item[7:]))
        else:
            {"out": finish_output, "sums": finish_sums, "came": finish_came}[item]()

    def run_after(name, index=None):
        if index is None:
            for (_, _, when), one in zip(CHUNKS, red):
                if when == name:
                    one.start(1)
            for item in SCHEDULE.get(name, ()):
                do(item)
            return
        for i in range(9):
            full = name + str(i)
            if full in SCHEDULE or any(when == full for _, _, when in CHUNKS):

                @pl.when(index == i)
                def _():
                    run_after(full)

    def ffn_forward(j, carry):
        up = mm(wup[j], n2_ref[...], TN)
        size = jnp.abs(up) * (0.5**0.5)
        t = 1.0 / (1.0 + 0.3275911 * size)
        poly = t * (
            0.254829592
            + t * (-0.284496736 + t * (1.421413741 + t * (-1.453152027 + t * 1.061405429)))
        )
        decay = jnp.exp(-0.5 * up * up)
        far = 0.5 * poly * decay
        phi = jnp.where(up < 0.0, far, 1.0 - far)
        slope = phi + up * decay * (1.0 / math.sqrt(2.0 * math.pi))
        act = (up * phi).astype(BF16)
        bytes_v[j] = act
        bytes_v[4 + j] = slope.astype(BF16)
        big[0] += mm(wdn[j], act, TN)
        return carry

    lax.fori_loop(0, 4, ffn_forward, 0)

    Copy(cot_w.at[0], cot_w.at[0], ss.at[0], rs.at[r_cot], sib).wait_recv()
    Copy(cot_w.at[1], cot_w.at[1], ss.at[0], rs.at[r_cot + 1], sib, jnp.logical_not(hi_here)).wait_recv()
    gb[...] = jnp.concatenate([cot_w[0], cot_w[1]], axis=1)

    def ffn_backward(j, carry):
        wg[2 * j] = mm(bytes_v[j], gb[...], NT).astype(BF16)
        grad_up = (mm(wdn[j], gb[...], NN) * bytes_v[4 + j].astype(F32)).astype(BF16)
        wg[2 * j + 1] = mm(n2_ref[...], grad_up, NT).astype(BF16)
        big[1] += mm(wup[j], grad_up, NN)
        run_after("F", j)
        return carry

    lax.fori_loop(0, 4, ffn_backward, 0)

    s_out, r_out = ids("s", 2), ids("r", 2)
    res = big[0].astype(BF16)
    owners = ((1 - zl, c, lo_here), (2 + zl, 1 - c, hi_here))
    for slot, (chip, i, here) in enumerate(owners):
        out_s[slot] = res[:, slot * half : (slot + 1) * half]
        go(
            Copy(
                out_s.at[slot],
                out_r.at[i],
                ss.at[s_out + slot],
                rs.at[r_out + i],
                dev(g, chip),
                None if here is False else jnp.logical_not(here),
            )
        )
        if here is not False:

            @pl.when(here)
            def _():
                out_r[i] = out_s[slot]

    grad_n2 = big[1]
    unit2 = hat2[...]
    product = grad_n2 * unit2

    def lane_fold(values):
        total = values[:, 0:128]
        for k in range(1, values.shape[1] // 128):
            total = total + values[:, 128 * k : 128 * (k + 1)]
        return total

    gain_acc[1] = lane_fold(product)
    e = grad_n2 * gain_col2
    grad_mid = gb[...].astype(F32) + inverse2 * (
        e
        - jnp.mean(e, axis=0, keepdims=True)
        - unit2 * jnp.mean(e * unit2, axis=0, keepdims=True)
    )
    gmid[0] = grad_mid[:, 0:half]
    gmid[1] = grad_mid[:, half:]
    branch = grad_mid.astype(BF16)
    wg[8] = mm(att[...], branch, NT).astype(BF16)
    run_after("post")
    grad_att = mm(weights[3], branch, NN)
    d_o[...] = grad_att.astype(BF16)
    for slot in range(2):
        lanes = slice(slot * half, (slot + 1) * half)
        both = d_o[:, lanes].astype(F32) * o_acc[slot]
        for h in range(HEADS):
            d_sc[slot, h : h + 1, :] = jnp.sum(
                both[64 * h : 64 * h + 64, :], axis=0, keepdims=True
            )

    dq[...] = jnp.zeros_like(dq)
    gwqkv[...] = jnp.zeros_like(gwqkv)
    gain_acc[0] = jnp.zeros((feat, 128), F32)
    s_rc, r_rc = ids("s", 4), ids("r", 4)
    s_rz, r_rz = ids("s", 4), ids("r", 4)
    s_fin, r_fin = ids("s", 4), ids("r", 2)

    def sd_at(which, h):
        return big.at[which, pl.ds(half * ((h // 2) % 2), half), pl.ds(half * (h % 2), half)]

    def backward_step(slot, kb):
        hq = hq_at(slot)
        bias = bias_of(hq, kb)
        lanes = pl.ds(pl.multiple_of(slot * half, half), half)
        lse = m_sc[slot]
        dots = d_sc[slot]
        for first in (0, 4):
            for h in range(first, first + 4):
                part = slice(64 * h, 64 * h + 64)
                grad_o = d_o[part, lanes]
                sd_at(0, h)[...] = mm(k_t[kb, part, :], q_t[slot, part, :], TN)
                sd_at(1, h)[...] = mm(v_t[kb, part, :], grad_o, TN)
            for h in range(first, first + 4):
                part = slice(64 * h, 64 * h + 64)
                prob = jnp.exp2(sd_at(0, h)[...] * score_scale + bias - lse[h : h + 1, :])
                grad_s = (prob * (sd_at(1, h)[...] - dots[h : h + 1, :])).astype(BF16)
                dv[part, :] += mm(d_o[part, lanes], prob.astype(BF16), NT)
                dk[part, :] += mm(q_t[slot, part, :], grad_s, NT)
                dq[slot, part, :] += mm(k_t[kb, part, :], grad_s, NN)

    att_scale = HEAD_DIM ** (-0.5)

    def rc_copy(kb):
        zb = lax.div(kb, 2)
        return Copy(
            ppart.at[kb],
            rc.at[zb],
            ss.at[s_rc + zb],
            rs.at[r_rc + zb],
            sib,
            lax.rem(kb, 2) != c,
        )

    def is_final(zb):
        return jnp.where(lax.div(zb, 2) == g, z == zb, is_near)

    def rz_copy(zb):
        return Copy(
            ppart.at[2 * zb + c],
            rz.at[zb],
            ss.at[s_rz + zb],
            rs.at[r_rz + zb],
            dev(c, zo),
            jnp.logical_and(jnp.logical_not(is_final(zb)), zb < nblk - 1),
        )

    def fin_copy(zb):
        here = jnp.logical_and(zb == z, g == c)
        return Copy(
            ppart.at[2 * zb + c],
            gfin.at[c],
            ss.at[s_fin + zb],
            rs.at[r_fin + c],
            dev(g, zb),
            jnp.logical_and(is_final(zb), jnp.logical_not(here)),
        )

    def combine(zb):
        kb = 2 * zb + c
        Copy(rc.at[zb], rc.at[zb], ss.at[0], rs.at[r_rc + zb], sib).wait_recv()
        ppart[kb] = ppart[kb] + rc[zb]
        rz_copy(zb).start()

    def deliver(zb):
        kb = 2 * zb + c
        final = jnp.logical_and(is_final(zb), zb < nblk - 1)
        Copy(rz.at[zb], rz.at[zb], ss.at[0], rs.at[r_rz + zb], sib, final).wait_recv()

        @pl.when(final)
        def _():
            ppart[kb] = ppart[kb] + rz[zb]

        @pl.when(jnp.logical_and(zb == z, g == c))
        def _():
            gfin[c] = ppart[kb]

        fin_copy(zb).start()

    s_gain, r_gain = ids("s", 6), ids("r", 6)

    def gain_list(phase):
        if phase < 4:
            device = (sib, xnb, ynb)[phase - 1]
            k = phase - 1
            return [
                Copy(gain_s.at[k], gain_r.at[k], ss.at[s_gain + k], rs.at[r_gain + k], device)
            ]
        return [
            Copy(
                gain_s.at[3],
                gain_r.at[2 + k],
                ss.at[s_gain + 2 + k],
                rs.at[r_gain + 2 + k],
                (dp, lax.rem(z + k, nblk)),
            )
            for k in range(1, 4)
        ]

    def gain_finish(phase):
        for one in gain_list(phase):
            one.wait_recv()
        if phase < 4:
            gain_s[phase] = gain_s[phase - 1] + gain_r[phase - 1]
            for one in gain_list(phase + 1):
                one.start()
        else:
            total = jnp.zeros((8, feat), F32)
            for zz in range(nblk):
                k = lax.rem(z - zz + nblk, nblk)
                part = gain_s[3]
                for i in range(1, 4):
                    part = jnp.where(k == i, gain_r[2 + i], part)
                total = total + part
            ggain_ref[...] = total

    def gains_start():
        for i in range(2):
            gain_s[0, i : i + 1, :] = jnp.sum(gain_acc[i].T, axis=0, keepdims=True)
        gain_s[0, 2:8, :] = jnp.zeros((6, feat), F32)
        gain_list(1)[0].start()

    s_last, r_last = ids("s", 1), ids("r", 1)
    copy_last = Copy(
        last_s,
        last_r,
        ss.at[s_last],
        rs.at[r_last],
        (dp, lax.rem(z + 1, nblk)),
        z < nblk - 1,
    )

    def finish_output():
        for i in range(2):
            mine = out_from_self(i, c, z)
            Copy(
                out_r.at[i], out_r.at[i], ss.at[0], rs.at[r_out + i], sib, jnp.logical_not(mine)
            ).wait_recv()
            live = rdiv[1:2, i * half : (i + 1) * half]
            out_ref[i * half : (i + 1) * half, :] = (out_r[i].astype(F32) * live).T.astype(BF16)

    def finish_sums():
        for i in range(2):
            mine = jnp.logical_and(own_worker, c == i)
            Copy(
                gfin.at[i], gfin.at[i], ss.at[0], rs.at[r_fin + i], sib, jnp.logical_not(mine)
            ).wait_recv()
            grad_sums = gfin[i].astype(F32) * rdiv[0:1, i * half : (i + 1) * half]
            gs_ref[i * half : (i + 1) * half, :] = grad_sums.T.astype(BF16)

        is_last = jnp.where(iota((16, feat), 1).astype(F32) == cnt - 1.0, 1.0, 0.0).astype(BF16)
        last_s[...] = mm(is_last, gs_ref[...], NN).astype(BF16)
        copy_last.start()

    def finish_came():
        Copy(last_r, last_r, ss.at[0], rs.at[r_last], sib, z > 0).wait_recv()

        @pl.when(z == 0)
        def _():
            last_r[...] = jnp.zeros_like(last_r)

        came_ref[...] = last_r[...]

    def key_step(t, carry):
        both = t < 2 * w + 2
        kb = jnp.where(both, lax.div(t, 2), t - w - 1)
        slot = jnp.where(both, 1 - lax.rem(t, 2), 1)
        first = jnp.logical_or(jnp.logical_not(both), lax.rem(t, 2) == 0)
        last = jnp.logical_or(jnp.logical_not(both), lax.rem(t, 2) == 1)

        @pl.when(first)
        def _():
            dk[...] = jnp.zeros_like(dk)
            dv[...] = jnp.zeros_like(dv)

        backward_step(slot, kb)

        @pl.when(last)
        def _():
            grad_key = turned(dk[...] * att_scale, kb, -1.0)
            grad_value = dv[...].astype(BF16)
            normed = n1[kb]
            k_t[kb] = grad_key
            v_t[kb] = grad_value
            gwqkv[1] += mm(normed, grad_key, NT)
            gwqkv[2] += mm(normed, grad_value, NT)

            @pl.when(jnp.logical_or(kb == w, kb == 7 - w))
            def _():
                slot = jnp.where(kb == w, 0, 1)
                grad_query = turned(dq[slot] * att_scale, kb, -1.0)
                q_t[slot] = grad_query
                gwqkv[0] += mm(normed, grad_query, NT)


        @pl.when(jnp.logical_and(lax.rem(t, 2) == 1, t < 2 * EARLY))
        def _():
            row_block(lax.div(t, 2))

        run_after("K", t)
        return carry

    def row_block(kb):
        @pl.when(kb <= 7 - w)
        def _():
            big[0, :, 0:half] = mm(weights[1], k_t[kb], NN) + mm(weights[2], v_t[kb], NN)
            own = jnp.logical_or(kb == w, kb == 7 - w)
            slot = jnp.where(kb == w, 0, 1)

            @pl.when(own)
            def _():
                big[0, :, 0:half] += mm(weights[0], q_t[slot], NN)

            grad_n1 = big[0, :, 0:half]
            unit, inverse = norm_parts(p_all[kb].astype(F32))
            gain_acc[0] += lane_fold(grad_n1 * unit)
            e = grad_n1 * gcol[0]
            total = inverse * (
                e
                - jnp.mean(e, axis=0, keepdims=True)
                - unit * jnp.mean(e * unit, axis=0, keepdims=True)
            )
            ppart[kb] = (total + jnp.where(own, 1.0, 0.0) * gmid[slot]).astype(BF16)

        @pl.when(kb > 7 - w)
        def _():
            ppart[kb] = jnp.zeros(ppart.shape[1:], BF16)

        rc_copy(kb).start()

        @pl.when(lax.rem(kb, 2) == 1)
        def _():
            combine(lax.div(kb, 2))

    def late_row_block(kb, carry):
        row_block(kb)
        run_after("R", kb)
        return carry

    lax.fori_loop(0, 9, key_step, 0)
    for i in range(3):
        wg[9 + i] = gwqkv[i].astype(BF16)
    run_after("W")
    lax.fori_loop(EARLY, 8, late_row_block, 0)

    run_after("end")

    for one in sends:
        one.wait_send()
    pass_on_sent()
    copy_last.wait_send()
    for one in outside_late:
        one.wait_send()
    for i in range(2):
        cot_copy(i)[1].wait_send()

    def close_key(kb, carry):
        rc_copy(kb).wait_send()
        return carry

    lax.fori_loop(0, 8, close_key, 0)

    def close_block(zb, carry):
        rz_copy(zb).wait_send()
        fin_copy(zb).wait_send()
        return carry

    lax.fori_loop(0, 4, close_block, 0)
    for phase in range(1, 5):
        for one in gain_list(phase):
            one.wait_send()
    for one in red:
        one.wait_sends()
        one.store().wait()


def out_from_self(i, c, z):
    chip = 2 * c + 1 - jnp.where(z < 2, z, 3 - z)
    core = jnp.where(z < 2, i, 1 - i)
    return jnp.logical_and(core == c, chip == z)


def expand_kernel(
    slots_ref, gs_ref, came_ref, out_ref, ggain_ref, w_hbm,
    bytes_out, out_out, ga_out, gf_out, dn_out, up_out, wo_out, wq_out, wk_out, wv_out,
    w_v, bytes_v, out_v, dn_v, up_v, rest_v, sem_in, sem_out,
):
    loads = [pltpu.make_async_copy(w_hbm.at[i], w_v.at[i], sem_in.at[i]) for i in range(12)]
    for one in loads:
        one.start()
    stores = []

    def store(src, dst):
        copy = pltpu.make_async_copy(src, dst, sem_out.at[len(stores)])
        copy.start()
        stores.append(copy)

    out_v[...] = out_ref[...].astype(F32)
    store(out_v, out_out)
    ga_out[...] = ggain_ref[0:1, :]
    gf_out[...] = ggain_ref[1:2, :]
    slot_iota = iota((512, 128), 0).astype(F32)
    first = iota((16, 128), 0) == 0

    def weights(j):
        loads[2 * j].wait()
        dn_v[j] = w_v[2 * j].astype(F32)
        store(dn_v.at[j], dn_out.at[pl.ds(512 * j, 512)])
        loads[2 * j + 1].wait()
        up_v[j] = w_v[2 * j + 1].astype(F32)
        store(up_v.at[j], up_out.at[:, pl.ds(512 * j, 512)])

    for k in range(8):
        rows = [slots_ref[4 * k + r : 4 * k + r + 1, :] for r in range(4)]
        member = jnp.concatenate(
            [(slot_iota == row).astype(F32).astype(BF16) for row in rows], axis=1
        )
        spread = mm(member, gs_ref[...], TN)
        if k == 0:
            lead = jnp.concatenate(
                [
                    jnp.where(jnp.logical_and(first, row < -0.5), 1.0, 0.0).astype(BF16)
                    for row in rows
                ],
                axis=1,
            )
            spread = spread + mm(lead, came_ref[...], TN)
        bytes_v[k] = spread
        store(bytes_v.at[k], bytes_out.at[pl.ds(512 * k, 512)])
        if k % 2 == 1:
            weights(k // 2)
    for i, dst in enumerate((wo_out, wq_out, wk_out, wv_out)):
        loads[8 + i].wait()
        rest_v[i] = w_v[8 + i].astype(F32)
        store(rest_v.at[i], dst)
    for one in stores:
        one.wait()


def fast_local(
    bytes_in, flags, lengths, cotangent, w_query, w_key, w_value, w_out, w_up, w_down, gain_attn, gain_ffn
):
    meta_flags = flags.reshape(32, 128)
    freqs = np.float32(ROTARY_BASE) ** (-2.0 * np.arange(32, dtype=np.float32) / np.float32(64))
    freq = np.ascontiguousarray(np.broadcast_to(freqs.astype(np.float32)[:, None], (32, 128)))
    vm = pl.BlockSpec(memory_space=pltpu.VMEM)
    hbm = pl.BlockSpec(memory_space=pl.ANY)
    hb = lambda n: pltpu.VMEM((n, 512, 256), BF16)
    hbf = lambda n: pltpu.VMEM((n, 512, 256), F32)
    sq = lambda n, t: pltpu.VMEM((n, 512, 512), t)
    scratch = dict(
        bytes_v=sq(8, BF16),
        weights=sq(4, BF16),
        wup=sq(4, BF16),
        wdn=sq(4, BF16),
        meta=pltpu.VMEM((2, 4, 40, 128), jnp.int32),
        tail=pltpu.VMEM((16, 512), BF16),
        p_own=hb(2),
        relay=pltpu.VMEM((512, 256), BF16),
        p_all=hb(8),
        n1=hb(8),
        k_t=hb(8),
        v_t=hb(8),
        q_t=hb(2),
        tab_c=pltpu.VMEM((8, 32, 256), F32),
        tab_s=pltpu.VMEM((8, 32, 256), F32),
        pos=pltpu.VMEM((8, 8, 256), F32),
        gcol=hbf(2),
        cot_own=hb(2),
        cot_w=hb(2),
        o_acc=hbf(2),
        m_sc=pltpu.VMEM((2, 8, 256), F32),
        l_sc=pltpu.VMEM((2, 8, 256), F32),
        att=pltpu.VMEM((512, 512), BF16),
        gb=pltpu.VMEM((512, 512), BF16),
        hat2=pltpu.VMEM((512, 512), F32),
        d_o=pltpu.VMEM((512, 512), BF16),
        d_sc=pltpu.VMEM((2, 8, 256), F32),
        gmid=hbf(2),
        dk=pltpu.VMEM((512, 256), F32),
        dv=pltpu.VMEM((512, 256), F32),
        dq=hbf(2),
        gwqkv=sq(3, F32),
        big=sq(2, F32),
        wg=sq(12, BF16),
        r1=pltpu.VMEM((12, 256, 512), BF16),
        r2=pltpu.VMEM((12, 128, 512), BF16),
        r3=pltpu.VMEM((12, 64, 512), BF16),
        r4=pltpu.VMEM((12, 32, 512), BF16),
        r5=pltpu.VMEM((12, 16, 512), BF16),
        ppart=hb(8),
        rc=hb(4),
        rz=hb(4),
        gfin=hb(2),
        out_s=hb(2),
        out_r=hb(2),
        rdiv=pltpu.VMEM((16, 512), F32),
        last_s=pltpu.VMEM((16, 512), BF16),
        last_r=pltpu.VMEM((16, 512), BF16),
        gain_acc=pltpu.VMEM((2, 512, 128), F32),
        gain_s=pltpu.VMEM((4, 8, 512), F32),
        gain_r=pltpu.VMEM((6, 8, 512), F32),
        ss=pltpu.SemaphoreType.DMA((224,)),
        rs=pltpu.SemaphoreType.DMA((224,)),
        ls=pltpu.SemaphoreType.DMA((32,)),
    )
    out, gs, came, slots, wgrad, ggain = pl.pallas_call(
        layer_kernel,
        out_shape=(
            jax.ShapeDtypeStruct((512, 512), BF16),
            jax.ShapeDtypeStruct((512, 512), BF16),
            jax.ShapeDtypeStruct((16, 512), BF16),
            jax.ShapeDtypeStruct((32, 128), F32),
            jax.ShapeDtypeStruct((12, 512, 512), BF16),
            jax.ShapeDtypeStruct((8, 512), F32),
        ),
        in_specs=[hbm, vm, vm, hbm, hbm, hbm, hbm, hbm, hbm, hbm, vm, vm, vm],
        out_specs=(vm, vm, vm, vm, hbm, vm),
        scratch_shapes=list(scratch.values()),
        compiler_params=pltpu.CompilerParams(
            collective_id=0, has_side_effects=True, vmem_limit_bytes=60 * 2**20
        ),
        name="layer",
    )(
        bytes_in, meta_flags, lengths, cotangent, w_query, w_key, w_value, w_out, w_up, w_down,
        gain_attn.reshape(1, 512), gain_ffn.reshape(1, 512), freq,
    )
    grad_bytes, out, g_attn, g_ffn, dn, up, wo, wq, wk, wv = pl.pallas_call(
        expand_kernel,
        out_shape=(
            jax.ShapeDtypeStruct((4096, 512), F32),
            jax.ShapeDtypeStruct((512, 512), F32),
            jax.ShapeDtypeStruct((1, 512), F32),
            jax.ShapeDtypeStruct((1, 512), F32),
            jax.ShapeDtypeStruct((2048, 512), F32),
            jax.ShapeDtypeStruct((512, 2048), F32),
        )
        + (jax.ShapeDtypeStruct((512, 512), F32),) * 4,
        in_specs=[vm, vm, vm, vm, vm, hbm],
        out_specs=(hbm, hbm, vm, vm) + (hbm,) * 6,
        scratch_shapes=[
            sq(12, BF16),
            sq(8, F32),
            pltpu.VMEM((512, 512), F32),
            sq(4, F32),
            sq(4, F32),
            sq(4, F32),
            pltpu.SemaphoreType.DMA((12,)),
            pltpu.SemaphoreType.DMA((24,)),
        ],
        compiler_params=pltpu.CompilerParams(vmem_limit_bytes=60 * 2**20),
        name="expand",
    )(slots, gs, came, out, ggain, wgrad)
    return out, grad_bytes, wq, wk, wv, wo, up, dn, g_attn.reshape(512), g_ffn.reshape(512)


def passed_along(block, axis, distance):
    devices = range(lax.axis_size(axis))
    route = [((i - distance) % len(devices), i) for i in devices]
    return lax.ppermute(block, axis, route)


def from_behind(value, axis, by):
    count = lax.axis_size(axis)
    pairs = [(i, i + by) for i in range(count) if 0 <= i + by < count]
    return lax.ppermute(value, axis, pairs)


def rotate(vectors, positions, direction):
    half_dim = vectors.shape[-1] // 2
    freqs = ROTARY_BASE ** (-2.0 * jnp.arange(half_dim, dtype=jnp.float32) / vectors.shape[-1])
    angles = positions.astype(jnp.float32)[:, None] * freqs[None, :]
    cosine = jnp.cos(angles)[:, None, :]
    sine = direction * jnp.sin(angles)[:, None, :]
    first_half = vectors[..., :half_dim]
    second_half = vectors[..., half_dim:]
    return jnp.concatenate(
        [first_half * cosine - second_half * sine, second_half * cosine + first_half * sine],
        axis=-1,
    )


def layer_norm_parts(values, gain):
    center = values - jnp.mean(values, axis=-1, keepdims=True)
    spread = jnp.mean(center * center, axis=-1, keepdims=True)
    inverse = lax.rsqrt(spread + EPSILON)
    normed = center * inverse
    return (normed * gain, normed, inverse)


def layer_norm_back(grad_in, normed, inverse, gain):
    scaled = grad_in * gain
    grad_values = inverse * (
        scaled
        - jnp.mean(scaled, axis=-1, keepdims=True)
        - normed * jnp.mean(scaled * normed, axis=-1, keepdims=True)
    )
    grad_gain = jnp.sum(grad_in * normed, axis=0)
    return (grad_values, grad_gain)


def pass_grads(grad_key, grad_value):
    return (
        passed_along(grad_key.astype(jnp.bfloat16), "blk", 1).astype(grad_key.dtype),
        passed_along(grad_value.astype(jnp.bfloat16), "blk", 1).astype(grad_value.dtype),
    )


def local(
    bytes_in,
    flags,
    lengths,
    cotangent,
    w_query,
    w_key,
    w_value,
    w_out,
    w_up,
    w_down,
    gain_attn,
    gain_ffn,
):
    blocks = lax.axis_size("blk")
    own_index = lax.axis_index("blk")
    seg_rows = cotangent.shape[0]
    byte_rows = bytes_in.shape[0]
    features = bytes_in.shape[1]
    scale = HEAD_DIM ** (-0.5)
    running = jnp.cumsum(flags)
    slot_of = running - 1
    seg_count = running[-1]
    slot_ids = jnp.arange(seg_rows, dtype=jnp.int32)
    member = (slot_of[None, :] == slot_ids[:, None]).astype(jnp.bfloat16)
    seg_sums = jnp.dot(member, bytes_in, preferred_element_type=jnp.float32)
    seg_tally = jnp.sum(member, axis=1, dtype=jnp.float32)
    leading = slot_of < 0
    tail_sum = jnp.dot(
        leading.astype(jnp.bfloat16)[None, :], bytes_in, preferred_element_type=jnp.float32
    )
    tail_count = jnp.sum(leading.astype(jnp.float32), keepdims=True)
    got_sum, got_count = from_behind((tail_sum, tail_count), "blk", -1)
    last_slot = slot_ids == seg_count - 1
    seg_sums = seg_sums + jnp.where(last_slot[:, None], got_sum, 0.0)
    seg_tally = seg_tally + jnp.where(last_slot, got_count[0], 0.0)
    divisor = jnp.maximum(seg_tally, 1.0)
    pooled = seg_sums / divisor[:, None]
    starts = jnp.cumsum(lengths[0]) - lengths[0]
    byte_at = own_index * byte_rows + jnp.arange(byte_rows, dtype=jnp.int32)
    prior_flags = jnp.sum(
        flags[None, :] * (byte_at[None, :] < starts[:, None]).astype(jnp.int32), axis=1
    )
    all_counts, all_prior = (
        lax.all_gather(seg_count[None], "blk", axis=0, tiled=True),
        lax.all_gather(prior_flags[None, :], "blk", axis=0, tiled=True),
    )
    offsets = jnp.cumsum(all_counts) - all_counts
    seq_first = jnp.sum(all_prior, axis=0)
    dev_ids = jnp.arange(blocks, dtype=jnp.int32)

    def layout(first_row, row_count):
        row_index = first_row + jnp.arange(row_count, dtype=jnp.int32)
        owner_dev = row_index // seg_rows
        within = row_index % seg_rows
        dev_pick = owner_dev[:, None] == dev_ids[None, :]
        dev_base = jnp.sum(jnp.where(dev_pick, offsets[None, :], 0), axis=1)
        dev_have = jnp.sum(jnp.where(dev_pick, all_counts[None, :], 0), axis=1)
        return (dev_base + jnp.minimum(within, dev_have - 1), within < dev_have)

    query_pos, query_live = layout(own_index * seg_rows, seg_rows)
    query_first = jnp.max(
        jnp.where(seq_first[None, :] <= query_pos[:, None], seq_first[None, :], 0), axis=1
    )

    def visible(first_row, row_count):
        key_pos, key_live = layout(first_row, row_count)
        return (
            (key_pos[None, :] <= query_pos[:, None])
            & (key_pos[None, :] >= query_first[:, None])
            & key_live[None, :]
        )

    normed_attn, unit_attn, scale_attn = layer_norm_parts(pooled, gain_attn)
    n_one = normed_attn.astype(jnp.bfloat16)
    query_pre = jnp.dot(n_one, w_query, preferred_element_type=jnp.float32)
    query_rot = rotate(query_pre.reshape(seg_rows, HEADS, HEAD_DIM), query_pos, 1.0).astype(
        jnp.bfloat16
    )
    key_pre = jnp.dot(n_one, w_key, preferred_element_type=jnp.float32)
    key_rot = (
        rotate(key_pre.reshape(seg_rows, HEADS, HEAD_DIM), query_pos, 1.0)
        .reshape(seg_rows, features)
        .astype(jnp.bfloat16)
    )
    value_low = jnp.dot(n_one, w_value, preferred_element_type=jnp.float32).astype(jnp.bfloat16)
    start_state = (
        jnp.full((HEADS, seg_rows), NEGATIVE, jnp.float32),
        jnp.zeros((HEADS, seg_rows), jnp.float32),
        jnp.zeros((seg_rows, HEADS, HEAD_DIM), jnp.float32),
    )
    key_piece = lax.all_gather(key_rot, "blk", axis=0, tiled=True)
    value_piece = lax.all_gather(value_low, "blk", axis=0, tiled=True)
    row_count = key_piece.shape[0]
    allowed = visible(jnp.int32(0), row_count)

    def absorb_update(running_state):
        row_max, row_sum, weighted = running_state
        scores = (
            jnp.einsum(
                "qhe,khe->hqk",
                query_rot,
                key_piece.reshape(row_count, HEADS, HEAD_DIM),
                preferred_element_type=jnp.float32,
            )
            * scale
        )
        scores = jnp.where(allowed[None], scores, NEGATIVE)
        new_max = jnp.maximum(row_max, jnp.max(scores, axis=-1))
        weights = jnp.where(allowed[None], jnp.exp(scores - new_max[:, :, None]), 0.0)
        shrink = jnp.exp(row_max - new_max)
        row_sum = jnp.sum(weights, axis=-1)
        weighted = weighted * shrink.T[:, :, None] + jnp.einsum(
            "hqk,khe->qhe",
            weights.astype(jnp.bfloat16),
            value_piece.reshape(row_count, HEADS, HEAD_DIM),
            preferred_element_type=jnp.float32,
        )
        return (new_max, row_sum, weighted)

    row_max, row_sum, weighted = lax.cond(
        jnp.any(allowed), absorb_update, lambda unchanged: unchanged, start_state
    )
    log_total = row_max + jnp.log(row_sum)
    attended_full = weighted / row_sum.T[:, :, None]
    attended = attended_full.reshape(seg_rows, features).astype(jnp.bfloat16)
    middle = pooled + jnp.dot(attended, w_out, preferred_element_type=jnp.float32)
    normed_ffn, unit_ffn, scale_ffn = layer_norm_parts(middle, gain_ffn)
    n_two = normed_ffn.astype(jnp.bfloat16)
    up_proj = jnp.dot(n_two, w_up, preferred_element_type=jnp.float32)
    act_full, gelu_back = jax.vjp(lambda inner: jax.nn.gelu(inner, approximate=False), up_proj)
    act_low = act_full.astype(jnp.bfloat16)
    result = middle + jnp.dot(act_low, w_down, preferred_element_type=jnp.float32)
    live_rows = query_live.astype(jnp.float32)[:, None]
    output = result * live_rows
    grad_out = cotangent * live_rows
    grad_branch = grad_out.astype(jnp.bfloat16)
    grad_w_down = jnp.einsum("sf,sd->fd", act_low, grad_branch, preferred_element_type=jnp.float32)
    grad_act = jnp.einsum("sd,fd->sf", grad_branch, w_down, preferred_element_type=jnp.float32)
    grad_up = gelu_back(grad_act)[0].astype(jnp.bfloat16)
    grad_w_up = jnp.einsum("sd,sf->df", n_two, grad_up, preferred_element_type=jnp.float32)
    grad_n_two = jnp.einsum("sf,df->sd", grad_up, w_up, preferred_element_type=jnp.float32)
    grad_mid_norm, grad_gain_ffn = layer_norm_back(grad_n_two, unit_ffn, scale_ffn, gain_ffn)
    grad_middle = grad_out + grad_mid_norm
    grad_attn_branch = grad_middle.astype(jnp.bfloat16)
    grad_w_out = jnp.einsum(
        "sd,se->de", attended, grad_attn_branch, preferred_element_type=jnp.float32
    )
    grad_attended = jnp.einsum(
        "se,de->sd", grad_attn_branch, w_out, preferred_element_type=jnp.float32
    ).astype(jnp.bfloat16)
    grad_att_three = grad_attended.reshape(seg_rows, HEADS, HEAD_DIM)
    row_dot = jnp.sum(grad_att_three.astype(jnp.float32) * attended_full, axis=-1).T

    def block_grads(key_piece, value_piece, source, grad_parts):
        allowed = visible(source * seg_rows, seg_rows)

        def block_update(grad_parts):
            grad_key, grad_value, grad_query = grad_parts
            key_three = key_piece.reshape(seg_rows, HEADS, HEAD_DIM)
            value_three = value_piece.reshape(seg_rows, HEADS, HEAD_DIM)
            scores = (
                jnp.einsum("qhe,khe->hqk", query_rot, key_three, preferred_element_type=jnp.float32)
                * scale
            )
            prob_full = jnp.where(allowed[None], jnp.exp(scores - log_total[:, :, None]), 0.0)
            grad_value = grad_value + jnp.einsum(
                "hqk,qhe->khe",
                prob_full.astype(jnp.bfloat16),
                grad_att_three,
                preferred_element_type=jnp.float32,
            ).reshape(seg_rows, features)
            grad_prob = jnp.einsum(
                "qhe,khe->hqk", grad_att_three, value_three, preferred_element_type=jnp.float32
            )
            grad_scores = (prob_full * (grad_prob - row_dot[:, :, None])).astype(jnp.bfloat16)
            grad_query = (
                grad_query
                + jnp.einsum(
                    "hqk,khe->qhe", grad_scores, key_three, preferred_element_type=jnp.float32
                )
                * scale
            )
            grad_key = grad_key + (
                jnp.einsum(
                    "hqk,qhe->khe", grad_scores, query_rot, preferred_element_type=jnp.float32
                )
                * scale
            ).reshape(seg_rows, features)
            return (grad_key, grad_value, grad_query)

        return lax.cond(jnp.any(allowed), block_update, lambda unchanged: unchanged, grad_parts)

    zero_rows = jnp.zeros((seg_rows, features), jnp.float32)
    zero_query = jnp.zeros((seg_rows, HEADS, HEAD_DIM), jnp.float32)

    def visit(visit_no, loop_state):
        key_piece, value_piece, grad_key, grad_value, grad_query = loop_state
        source = (own_index - visit_no) % blocks
        grad_key, grad_value, grad_query = block_grads(
            key_piece, value_piece, source, (grad_key, grad_value, grad_query)
        )
        key_piece, value_piece = from_behind((key_piece, value_piece), "blk", 1)
        grad_key, grad_value = pass_grads(grad_key, grad_value)
        return (key_piece, value_piece, grad_key, grad_value, grad_query)

    loop_out = lax.fori_loop(
        0, blocks, visit, (key_rot, value_low, zero_rows, zero_rows, zero_query)
    )
    grad_key_sum, grad_value_sum, grad_query_rot = (loop_out[2], loop_out[3], loop_out[4])
    grad_query = (
        rotate(grad_query_rot, query_pos, -1.0).reshape(seg_rows, features).astype(jnp.bfloat16)
    )
    grad_key = (
        rotate(grad_key_sum.reshape(seg_rows, HEADS, HEAD_DIM), query_pos, -1.0)
        .reshape(seg_rows, features)
        .astype(jnp.bfloat16)
    )
    grad_value_low = grad_value_sum.astype(jnp.bfloat16)
    grad_w_query = jnp.einsum("sd,se->de", n_one, grad_query, preferred_element_type=jnp.float32)
    grad_w_key = jnp.einsum("sd,se->de", n_one, grad_key, preferred_element_type=jnp.float32)
    grad_w_value = jnp.einsum(
        "sd,se->de", n_one, grad_value_low, preferred_element_type=jnp.float32
    )
    grad_n_one = jnp.einsum("se,de->sd", grad_query, w_query, preferred_element_type=jnp.float32)
    grad_n_one = grad_n_one + jnp.einsum(
        "se,de->sd", grad_key, w_key, preferred_element_type=jnp.float32
    )
    grad_n_one = grad_n_one + jnp.einsum(
        "se,de->sd", grad_value_low, w_value, preferred_element_type=jnp.float32
    )
    grad_pool_norm, grad_gain_attn = layer_norm_back(grad_n_one, unit_attn, scale_attn, gain_attn)
    grad_pooled = grad_middle + grad_pool_norm
    grad_sums = (grad_pooled / divisor[:, None]).astype(jnp.bfloat16)
    last_grad = jnp.dot(
        last_slot.astype(jnp.bfloat16)[None, :], grad_sums, preferred_element_type=jnp.float32
    ).astype(jnp.bfloat16)
    came_grad = from_behind(last_grad, "blk", 1)
    spread_rows = jnp.take(grad_sums, jnp.maximum(slot_of, 0), axis=0)
    grad_bytes = jnp.where(leading[:, None], came_grad, spread_rows).astype(jnp.float32)
    (
        grad_w_query,
        grad_w_key,
        grad_w_value,
        grad_w_out,
        grad_w_up,
        grad_w_down,
        grad_gain_attn,
        grad_gain_ffn,
    ) = lax.psum(
        (
            grad_w_query,
            grad_w_key,
            grad_w_value,
            grad_w_out,
            grad_w_up,
            grad_w_down,
            grad_gain_attn,
            grad_gain_ffn,
        ),
        ("dp", "blk"),
    )
    return (
        output,
        grad_bytes,
        grad_w_query,
        grad_w_key,
        grad_w_value,
        grad_w_out,
        grad_w_up,
        grad_w_down,
        grad_gain_attn,
        grad_gain_ffn,
    )


def solution(mesh):
    fits = mesh.shape["blk"] == 4 and mesh.shape["dp"] == 8
    return jax.shard_map(
        fast_local if fits else local,
        mesh=mesh,
        in_specs=(
            P(("dp", "blk"), None),
            P(("dp", "blk")),
            P("dp", None),
            P(("dp", "blk"), None),
            P(),
            P(),
            P(),
            P(),
            P(),
            P(),
            P(),
            P(),
        ),
        out_specs=(
            P(("dp", "blk"), None),
            P(("dp", "blk"), None),
            P(),
            P(),
            P(),
            P(),
            P(),
            P(),
            P(),
            P(),
        ),
        check_vma=False,
    )
```

```python
import functools
import math

import jax
import jax.numpy as jnp
import numpy as np
from jax import lax
from jax.experimental import pallas as pl
from jax.experimental.pallas import tpu as pltpu
from jax.sharding import PartitionSpec as P

HEADS = 8
HEAD_DIM = 64
EPSILON = 1e-05
ROTARY_BASE = 10000.0
NEGATIVE = -1e30
LOG2E = math.log2(math.e)

MESH = pl.DeviceIdType.MESH
F32 = jnp.float32
BF16 = jnp.bfloat16
NN = (((1,), (0,)), ((), ()))
NT = (((1,), (1,)), ((), ()))
TN = (((0,), (0,)), ((), ()))


def mm(a, b, dims):
    return lax.dot_general(a, b, dims, preferred_element_type=F32)


def iota(shape, dim):
    return lax.broadcasted_iota(jnp.int32, shape, dim)


class Copy:
    def __init__(self, src, dst, send_sem, recv_sem, device, cond=None):
        self.parts = (src, dst, send_sem, recv_sem)
        self.device = device
        self.cond = cond

    def _do(self, act):
        def run():
            src, dst, send_sem, recv_sem = self.parts
            act(
                pltpu.make_async_remote_copy(
                    src_ref=src,
                    dst_ref=dst,
                    send_sem=send_sem,
                    recv_sem=recv_sem,
                    device_id=self.device,
                    device_id_type=MESH,
                )
            )

        if self.cond is None:
            run()
        else:
            pl.when(self.cond)(run)

    def start(self):
        self._do(lambda d: d.start())

    def wait_send(self):
        self._do(lambda d: d.wait_send())

    def wait_recv(self):
        self._do(lambda d: d.wait_recv())


CHUNKS = (
    (0, 2, "F0"),
    (2, 4, "F1"),
    (4, 6, "F2"),
    (6, 9, "post"),
    (9, 10, "W"),
    (10, 12, "W"),
)
SEMS_AR = 18
EARLY = 4
SCHEDULE = {
    "F2": ((0, 1), (1, 1)),
    "F3": ((2, 1),),
    "K0": ((3, 1),),
    "K1": ((0, 2), (1, 2)),
    "K2": ((2, 2),),
    "K3": ((0, 3), (1, 3)),
    "K4": ((2, 3), (3, 2)),
    "K5": ((0, 4), (1, 4), (3, 3)),
    "K6": ((2, 4),),
    "K7": ((0, 5), (3, 4), "deliver0", (2, 5)),
    "R4": ((1, 5),),
    "R6": ((4, 1), (5, 1)),
    "end": ("gain0", (0, 6), "deliver1", "out", (1, 6), "deliver3", "gain1", (2, 6), (3, 5), (4, 2), "gain2", (5, 2), (4, 3), (0, 7), "gain3", (1, 7), (2, 7), (4, 4), (5, 3), "gain4", (0, 8), "deliver2", (3, 6), (1, 8), (5, 4), (2, 8), (4, 5), (3, 7), "sums", (4, 6), (5, 5), (0, 9), "came", (0, 10), (4, 7), (5, 6), (1, 9), (3, 8), (2, 9), (4, 8), (1, 10), (5, 7), (2, 10), (4, 9), (5, 8), (4, 10), (3, 9), (3, 10), (5, 9), (5, 10)),
}


def layer_kernel(
    bytes_hbm,
    flags_ref,
    lengths_ref,
    cot_hbm,
    wq_hbm,
    wk_hbm,
    wv_hbm,
    wo_hbm,
    wup_hbm,
    wdn_hbm,
    gain_attn_ref,
    gain_ffn_ref,
    freq_ref,
    out_ref,
    gs_ref,
    came_ref,
    slots_ref,
    wgrad_hbm,
    ggain_ref,
    bytes_v,
    weights,
    wup,
    wdn,
    meta,
    tail,
    p_own,
    relay,
    p_all,
    n1,
    k_t,
    v_t,
    q_t,
    tab_c,
    tab_s,
    pos,
    gcol,
    cot_own,
    cot_w,
    o_acc,
    m_sc,
    l_sc,
    att,
    gb,
    hat2,
    d_o,
    d_sc,
    gmid,
    dk,
    dv,
    dq,
    gwqkv,
    big,
    wg,
    r1,
    r2,
    r3,
    r4,
    r5,
    ppart,
    rc,
    rz,
    gfin,
    out_s,
    out_r,
    rdiv,
    last_s,
    last_r,
    gain_acc,
    gain_s,
    gain_r,
    ss,
    rs,
    ls,
):
    cot_v, acc = hat2, big.at[0]
    dp = lax.axis_index("dp")
    z = lax.axis_index("blk")
    feat = 512
    half = 256
    nblk = 4
    c = lax.rem(dp, 2)
    x = lax.rem(lax.div(dp, 2), 2)
    y = lax.div(dp, 4)
    sib = (dp + 1 - 2 * c, z)
    xnb = (dp + 2 - 4 * x, z)
    ynb = (dp + 4 - 8 * y, z)
    g = lax.div(z, 2)
    zl = lax.rem(z, 2)
    w = 2 * (1 - zl) + c
    zo = 4 * g + 1 - z
    near = 1 + g
    is_near = z == near
    own_worker = g == c

    def dev(core, zz):
        return (dp - c + core, zz)

    counter = {"s": 0, "r": 0, "l": 0}

    def ids(kind, n):
        first = counter[kind]
        counter[kind] = first + n
        return first

    sends = []

    def go(copy):
        copy.start()
        sends.append(copy)

    l_bytes = ids("l", 8)
    rows_chunk = bytes_v.shape[1]
    l_cot = ids("l", 1)
    load_cot = pltpu.make_async_copy(cot_hbm, cot_v, ls.at[l_cot])
    load_cot.start()
    loads_bytes = [
        pltpu.make_async_copy(
            bytes_hbm.at[pl.ds(i * rows_chunk, rows_chunk)], bytes_v.at[i], ls.at[l_bytes + i]
        )
        for i in range(8)
    ]
    for d in loads_bytes:
        d.start()
    l_w = ids("l", 4)
    loads_w = [
        pltpu.make_async_copy(src, weights.at[i], ls.at[l_w + i])
        for i, src in enumerate((wq_hbm, wk_hbm, wv_hbm, wo_hbm))
    ]
    l_f = ids("l", 8)
    loads_f = []
    for j in range(4):
        loads_f.append(
            pltpu.make_async_copy(
                wup_hbm.at[:, pl.ds(j * feat, feat)], wup.at[j], ls.at[l_f + 2 * j]
            )
        )
        loads_f.append(
            pltpu.make_async_copy(
                wdn_hbm.at[pl.ds(j * feat, feat)], wdn.at[j], ls.at[l_f + 2 * j + 1]
            )
        )

    barrier = pltpu.get_barrier_semaphore()
    me_line = c * nblk + z
    line = []
    for k in range(1, 8):
        t = lax.rem(me_line + k, 8)
        line.append((lax.div(t, nblk), lax.rem(t, nblk)))
    for core, zz in line:
        pl.semaphore_signal(barrier, inc=1, device_id=dev(core, zz), device_id_type=MESH)
    for d in (xnb, ynb):
        pl.semaphore_signal(barrier, inc=1, device_id=d, device_id_type=MESH)

    cnt = jnp.sum(flags_ref[...].astype(F32))
    lane_row = iota((1, feat), 1).astype(F32)
    live_row = jnp.where(lane_row < cnt, 1.0, 0.0)
    for d in loads_w:
        d.start()
    for d in loads_f:
        d.start()

    s_meta, r_meta = ids("s", 7), ids("r", 8)
    s_tail, r_tail = ids("s", 1), ids("r", 1)
    copies_meta = [
        Copy(
            meta.at[c, z],
            meta.at[c, z],
            ss.at[s_meta + k],
            rs.at[r_meta + me_line],
            dev(core, zz),
        )
        for k, (core, zz) in enumerate(line)
    ]
    copy_tail = Copy(
        bytes_hbm.at[pl.ds(0, 16)],
        tail,
        ss.at[s_tail],
        rs.at[r_tail],
        (dp, lax.rem(z + nblk - 1, nblk)),
        z > 0,
    )

    def enter():
        pl.semaphore_wait(barrier, 9)
        meta[c, z, 0:32, :] = flags_ref[...]
        meta[c, z, 32:40, :] = jnp.zeros((8, 128), jnp.int32)
        meta[c, z, 32:33, 0:4] = lengths_ref[...]
        for one in copies_meta:
            go(one)
        go(copy_tail)

        @pl.when(z == nblk - 1)
        def _():
            tail[...] = jnp.zeros_like(tail)

    upper = (iota((128, 128), 0) <= iota((128, 128), 1)).astype(F32).astype(BF16)
    ones_sq = jnp.ones((128, 128), BF16)
    below = (iota((32, 32), 1) < iota((32, 32), 0)).astype(F32).astype(BF16)
    own_flags = flags_ref[...].astype(F32)
    flags_low = own_flags.astype(BF16)
    within = mm(flags_low, upper, NN)
    row_sums = mm(flags_low, ones_sq, NN)
    row_base = mm(below, row_sums.astype(BF16), NN)
    slot_of = within + row_base - 1.0
    slots_ref[...] = slot_of

    acc[...] = jnp.zeros_like(acc)
    rdiv[...] = jnp.zeros_like(rdiv)
    slot_iota = iota((feat, 128), 0).astype(F32)
    ones_rows = jnp.ones((16, feat), BF16)

    enter()

    cells = rows_chunk // 8
    for k in range(8):
        loads_bytes[k].wait()
        reach = cells * (k + 1)
        member = jnp.concatenate(
            [
                (slot_iota[0:reach] == slot_of[r : r + 1, :]).astype(F32).astype(BF16)
                for r in range(4 * k, 4 * k + 4)
            ],
            axis=1,
        )
        acc[0:reach, :] += mm(member, bytes_v[k], NN)
        rdiv[:, 0:feat] += mm(
            ones_rows,
            jnp.concatenate([member, jnp.zeros((feat - reach, rows_chunk), BF16)], axis=0)
            if reach < feat
            else member,
            NT,
        )

    for i, gain in enumerate((gain_attn_ref, gain_ffn_ref)):
        row = jnp.broadcast_to(gain[...], (128, feat))
        col = row.T
        gcol[i] = jnp.concatenate([col, col], axis=1)

    for core, zz in line:
        Copy(
            meta.at[core, zz],
            meta.at[core, zz],
            ss.at[0],
            rs.at[r_meta + core * nblk + zz],
            sib,
        ).wait_recv()
    Copy(tail, tail, ss.at[0], rs.at[r_tail], sib, z < nblk - 1).wait_recv()
    zn = jnp.minimum(z + 1, nblk - 1)
    next_flags = meta[c, zn, 0:16, :].astype(F32).astype(BF16)
    next_within = mm(next_flags, upper, NN)
    has_next = (z < nblk - 1).astype(F32)
    lead = jnp.where(next_within[0:1, :] < 0.5, 1.0, 0.0) * has_next
    is_last16 = iota((feat, 16), 0).astype(F32) == cnt - 1.0
    member_tail = jnp.where(is_last16, lead[:, 0:16], 0.0).astype(BF16)
    sums = acc[...] + mm(member_tail, tail[...], NN)
    tally = rdiv[0:1, :] + jnp.where(lane_row == cnt - 1.0, jnp.sum(lead), 0.0)
    inverse_tally = 1.0 / jnp.maximum(tally, 1.0)
    rdiv[0:1, :] = inverse_tally
    rdiv[1:2, :] = live_row
    pooled_t = (sums.T * inverse_tally).astype(BF16)
    p_own[0] = pooled_t[:, 0:half]
    p_own[1] = pooled_t[:, half:]

    s_p, r_p, r_relay = ids("s", 22), ids("r", 16), ids("r", 1)
    near_c = 1 + c
    pieces = (pl.ds(0, half), pl.ds(half, half))

    def p_piece(src, hb, piece, slot, device, cond=None):
        at = pieces[piece]
        return Copy(
            src.at[at],
            p_all.at[hb, at],
            ss.at[s_p + slot],
            rs.at[r_p + 2 * hb + piece],
            device,
            cond,
        )

    def p_whole(src, hb, slot, device, cond=None):
        return Copy(src, p_all.at[hb], ss.at[s_p + slot], rs.at[r_p + 2 * hb], device, cond)

    other_worker = jnp.logical_not(own_worker)
    to_pair = z != nblk - 1
    inner = jnp.logical_or(z == 1, z == 2)

    outer = jnp.logical_not(inner)

    def outside_copies(cond):
        own_out = jnp.logical_and(other_worker, cond)
        relayed = jnp.logical_and(own_worker, cond)
        return [
            p_piece(p_own.at[c], 2 * z + c, i, 4 + i, dev(c, near_c), own_out) for i in range(2)
        ] + [p_piece(relay, 2 * z + c, i, 4 + i, dev(c, 2 - c), relayed) for i in range(2)]

    outside_late = outside_copies(outer)

    go(Copy(p_own.at[1 - c], relay, ss.at[s_p + 3], rs.at[r_relay], sib, other_worker))
    for i in range(2):
        own_pair = jnp.logical_and(own_worker, to_pair)
        go(p_piece(p_own.at[c], 2 * z + c, i, i, dev(c, zo), own_pair))
    go(p_whole(p_own.at[1 - c], 2 * z + 1 - c, 3, sib, own_worker))
    go(p_whole(p_own.at[c], 2 * z + c, 2, sib, own_worker))

    @pl.when(own_worker)
    def _():
        p_all[2 * z] = p_own[0]
        p_all[2 * z + 1] = p_own[1]

    def p_wait(hb, cond=None):
        Copy(p_all.at[hb], p_all.at[hb], ss.at[0], rs.at[r_p + 2 * hb], sib, cond).wait_recv()

    Copy(relay, relay, ss.at[0], rs.at[r_relay], sib, own_worker).wait_recv()
    for one in outside_copies(inner):
        go(one)
    p_wait(2 * z + c, other_worker)
    for i in range(2):
        passed = jnp.logical_and(other_worker, to_pair)
        go(p_piece(p_all.at[2 * z + c], 2 * z + c, i, i, dev(c, zo), passed))
    p_wait(2 * z + 1 - c, other_worker)

    load_cot.wait()
    cot_t = (cot_v[...].T * live_row).astype(BF16)
    cot_own[0] = cot_t[:, 0:half]
    cot_own[1] = cot_t[:, half:]
    lo_here = False
    hi_here = jnp.logical_and(g == c, z >= 2)

    counts = []
    for b in range(nblk):
        counts.append(jnp.sum(meta[g, b, 0:32, :].astype(F32)))
    offsets = [jnp.float32(0.0)]
    for b in range(nblk):
        offsets.append(offsets[-1] + counts[b])
    lens = meta[g, z, 32:40, :].astype(F32)
    first_row = iota((8, 128), 0) == 0
    lane8 = iota((8, 128), 1)
    byte_at = (iota((32, 128), 0) * 128 + iota((32, 128), 1)).astype(F32)
    seq_first = [jnp.float32(0.0)]
    for s in range(1, 4):
        start = jnp.sum(jnp.where(jnp.logical_and(first_row, lane8 < s), lens, 0.0))
        prior = jnp.zeros((32, 128), F32)
        for b in range(nblk):
            prior = prior + jnp.where(
                byte_at + float(b * 4096) < start, meta[g, b, 0:32, :].astype(F32), 0.0
            )
        seq_first.append(jnp.sum(prior))

    freq = jnp.concatenate([freq_ref[...], freq_ref[...]], axis=1)
    lane_half = iota((1, half), 1).astype(F32)
    for hb in range(8):
        b = hb // 2
        j = lane_half + float((hb % 2) * half)
        p = offsets[b] + jnp.minimum(j, counts[b] - 1.0)
        first = jnp.zeros_like(p)
        for s in range(1, 4):
            first = jnp.maximum(first, jnp.where(p >= seq_first[s], seq_first[s], 0.0))
        pos[hb, 0:1, :] = p
        pos[hb, 1:2, :] = first
        angle = freq * p
        tab_c[hb] = jnp.cos(angle)
        tab_s[hb] = jnp.sin(angle)

    def pick(values, b):
        total = jnp.float32(0.0)
        for i, v in enumerate(values):
            total = total + jnp.where(b == i, v, 0.0)
        return total

    gain_col = gcol[0]

    def norm_parts(values):
        mean = jnp.mean(values, axis=0, keepdims=True)
        center = values - mean
        inverse = lax.rsqrt(jnp.mean(center * center, axis=0, keepdims=True) + EPSILON)
        return center * inverse, inverse

    def turned(values, hb, direction):
        cos = tab_c[hb]
        sin = tab_s[hb] * direction
        parts = []
        for h in range(HEADS):
            a = values[64 * h : 64 * h + 32, :]
            b = values[64 * h + 32 : 64 * h + 64, :]
            parts.append(a * cos - b * sin)
            parts.append(b * cos + a * sin)
        return jnp.concatenate(parts, axis=0).astype(BF16)

    for d in loads_w:
        d.wait()

    def keys_values(hb):
        unit, _ = norm_parts(p_all[hb].astype(F32))
        normed = (unit * gcol[0]).astype(BF16)
        n1[hb] = normed
        k_t[hb] = turned(mm(weights[1], normed, TN), hb, 1.0)
        v_t[hb] = mm(weights[2], normed, TN).astype(BF16)

    s_cot, r_cot = ids("s", 2), ids("r", 2)
    early = z < 2
    slot_to = jnp.where(early, 0, 1)
    chip_to = 2 * c + 1 - jnp.where(early, z, 3 - z)

    def cot_copy(i):
        core_to = jnp.where(early, i, 1 - i)
        here = jnp.logical_and(core_to == c, chip_to == z)
        return here, Copy(
            cot_own.at[i],
            cot_w.at[slot_to],
            ss.at[s_cot + i],
            rs.at[r_cot + slot_to],
            dev(core_to, chip_to),
            jnp.logical_not(here),
        )

    def send_cot():
        for i in range(2):
            here, copy = cot_copy(i)
            copy.start()

            @pl.when(here)
            def _():
                cot_w[slot_to] = cot_own[i]

    hq_of = (w, 7 - w)
    first_far, second_far = 2 - g, 3 - 3 * g
    score_scale = HEAD_DIM ** (-0.5) * LOG2E

    def hq_at(slot):
        return jnp.where(slot == 0, w, 7 - w)

    def bias_of(hq, kb):
        b = lax.div(kb, 2)
        j = (iota((half, half), 0) + lax.rem(kb, 2) * half).astype(F32)
        kpos = j + pick(offsets[:nblk], b)
        alive = j < pick(counts, b)
        qpos = pos[hq, 0:1, :]
        qfirst = pos[hq, 1:2, :]
        allowed = jnp.logical_and(alive, jnp.logical_and(kpos <= qpos, kpos >= qfirst))
        return jnp.where(allowed, 0.0, NEGATIVE)

    o_acc[...] = jnp.zeros_like(o_acc)
    l_sc[...] = jnp.zeros_like(l_sc)
    m_sc[...] = jnp.full(m_sc.shape, NEGATIVE, F32)

    def s_at(h):
        return gwqkv.at[h // 4, pl.ds(half * ((h // 2) % 2), half), pl.ds(half * (h % 2), half)]

    o_new = big.at[1, :, pl.ds(0, half)]

    def forward_step(slot, kb):
        hq = hq_at(slot)
        bias = bias_of(hq, kb)
        old = m_sc[slot]
        old_sum = l_sc[slot]
        for h in range(HEADS):
            part = slice(64 * h, 64 * h + 64)
            s_at(h)[...] = mm(k_t[kb, part, :], q_t[slot, part, :], TN)
        tops, sums = [], []
        for h in range(HEADS):
            part = slice(64 * h, 64 * h + 64)
            s = s_at(h)[...] * score_scale + bias
            top = jnp.maximum(old[h : h + 1, :], jnp.max(s, axis=0, keepdims=True))
            prob = jnp.exp2(s - top)
            tops.append(top)
            sums.append(jnp.sum(prob, axis=0, keepdims=True))
            o_new[part, :] = mm(v_t[kb, part, :], prob.astype(BF16), NN)
        new = jnp.concatenate(tops, axis=0)
        shrink = jnp.exp2(old - new)
        m_sc[slot] = new
        l_sc[slot] = old_sum * shrink + jnp.concatenate(sums, axis=0)
        for h in range(HEADS):
            part = slice(64 * h, 64 * h + 64)
            o_acc[slot, part, :] = o_acc[slot, part, :] * shrink[h : h + 1, :] + o_new[part, :]

    def block_nth(n):
        swapped = jnp.where(n < 2, 1 - n, n)
        return jnp.where(z == 0, n, jnp.where(z == 1, swapped, z - n))

    def pass_on(block, slot, cond, onward=None):
        hb = 2 * block + c

        @pl.when(cond)
        def _():
            for i in range(2):
                there = p_all.at[hb, pieces[i]]
                Copy(there, there, ss.at[0], rs.at[r_p + 2 * hb + i], sib).wait_recv()
                if onward is not None:
                    p_piece(p_all.at[hb], hb, i, slot + 2 + i, dev(c, zo), onward).start()
                p_piece(p_all.at[hb], hb, i, slot + i, sib).start()

    def pass_on_sent():
        for block, slot, cond, onward in passes:
            hb = 2 * block + c

            @pl.when(cond)
            def _(hb=hb, slot=slot, onward=onward):
                for i in range(2):
                    if onward is not None:
                        p_piece(p_all.at[hb], hb, i, slot + 2 + i, dev(c, zo), onward).wait_send()
                    p_piece(p_all.at[hb], hb, i, slot + i, sib).wait_send()

    second_near = z == 2
    passes = (
        (zo, 6, z != 2),
        (first_far, 8, is_near, is_near),
        (first_far, 12, jnp.logical_not(is_near)),
        (second_far, 14, second_near, second_near),
        (second_far, 18, zl == 1),
    )
    passes = tuple(p if len(p) == 4 else p + (None,) for p in passes)

    def arrival(n, carry):
        block = block_nth(n)

        @pl.when(n == 1)
        def _():
            for one in outside_late:
                one.start()
            pass_on(*passes[0])
            pass_on(*passes[1])

        @pl.when(n == 2)
        def _():
            pass_on(*passes[2])
            pass_on(*passes[3])

        @pl.when(n == 3)
        def _():
            pass_on(*passes[4])
            send_cot()

        @pl.when(jnp.logical_and(n > 0, n < 3 + zl))
        def _():
            for i in range(2):
                there = p_all.at[2 * block + 1 - c, pieces[i]]
                Copy(
                    there, there, ss.at[0], rs.at[r_p + 2 * (2 * block + 1 - c) + i], sib
                ).wait_recv()

        @pl.when(n < 3 + zl)
        def _():
            def one(i, carry):
                keys_values(2 * block + i)
                return carry

            lax.fori_loop(0, 2, one, 0)

            def query(slot, carry):
                hq = hq_at(slot)

                @pl.when(lax.div(hq, 2) == block)
                def _():
                    q_t[slot] = turned(mm(weights[0], n1[hq], TN), hq, 1.0)

                return carry

            lax.fori_loop(0, 2, query, 0)

            def pair(i, carry):
                slot, kb = lax.div(i, 8), lax.rem(i, 8)
                hq = hq_at(slot)
                q_block, k_block = lax.div(hq, 2), lax.div(kb, 2)

                def came_by(b, m):
                    found = block_nth(0) == b
                    for k in range(1, 4):
                        found = jnp.logical_or(
                            found, jnp.logical_and(block_nth(k) == b, k <= m)
                        )
                    return found

                new_query = jnp.logical_and(q_block == block, came_by(k_block, n))
                new_keys = jnp.logical_and(k_block == block, came_by(q_block, n))
                new = jnp.logical_or(new_query, new_keys)

                @pl.when(jnp.logical_and(kb <= hq, new))
                def _():
                    forward_step(slot, kb)

                return carry

            lax.fori_loop(0, 16, pair, 0)

        return carry

    lax.fori_loop(0, 4, arrival, 0)

    for slot in range(2):
        total = l_sc[slot]
        for h in range(HEADS):
            part = slice(64 * h, 64 * h + 64)
            o_acc[slot, part, :] = o_acc[slot, part, :] * (1.0 / total[h : h + 1, :])
        att[:, slot * half : (slot + 1) * half] = o_acc[slot].astype(BF16)
        m_sc[slot] = m_sc[slot] + jnp.log2(total)

    own_pooled = jnp.concatenate([p_all[hq_of[0]], p_all[hq_of[1]]], axis=1).astype(F32)
    middle = own_pooled + mm(weights[3], att[...], TN)
    unit2, inverse2 = norm_parts(middle)
    hat2[...] = unit2
    gain_col2 = jnp.concatenate([gcol[1], gcol[1]], axis=1)
    n2 = (unit2 * gain_col2).astype(BF16)
    big[0] = middle
    big[1] = jnp.zeros((feat, feat), F32)
    n2_ref = d_o
    n2_ref[...] = n2

    base1 = c * 256
    keep2x, give2x = base1 + x * 128, base1 + (1 - x) * 128
    keep2y, give2y = base1 + y * 128, base1 + (1 - y) * 128
    keep3x, give3x = keep2x + y * 64, keep2x + (1 - y) * 64
    keep3y, give3y = keep2y + x * 64, keep2y + (1 - x) * 64
    keep4x, give4x = keep3x + 32 * zl, keep3x + 32 * (1 - zl)
    keep4y, give4y = keep3y + 32 * zl, keep3y + 32 * (1 - zl)
    keep5x, give5x = keep4x + 16 * g, keep4x + 16 * (1 - g)
    keep5y, give5y = keep4y + 16 * g, keep4y + 16 * (1 - g)
    znb, zfar = (dp, z + 1 - 2 * zl), (dp, lax.rem(z + 2, nblk))
    lanes_x, lanes_y = pl.ds(0, 256), pl.ds(256, 256)

    def rows_of(first, n):
        return pl.ds(pl.multiple_of(first, 16), n)

    class Reduce:
        def __init__(self, chunk):
            self.b0, self.b1 = CHUNKS[chunk][:2]
            self.nb = self.b1 - self.b0
            self.s0, self.r0 = ids("s", SEMS_AR), ids("r", SEMS_AR)
            self.blocks = pl.ds(self.b0, self.nb)
            self.phases = {}

        def _w(self, first, n, lanes):
            return wg.at[self.blocks, rows_of(first, n), lanes]

        def _list(self, phase):
            every = pl.ds(0, 512)
            b, s0, r0 = self.blocks, self.s0, self.r0

            def copy(i, src, dst, device):
                return Copy(src, dst, ss.at[s0 + i], rs.at[r0 + i], device)

            if phase == 1:
                return [copy(0, self._w((1 - c) * 256, 256, every), r1.at[b], sib)]
            if phase == 2:
                return [
                    copy(1, self._w(give2x, 128, lanes_x), r2.at[b, :, lanes_x], xnb),
                    copy(2, self._w(give2y, 128, lanes_y), r2.at[b, :, lanes_y], ynb),
                ]
            if phase == 3:
                return [
                    copy(3, self._w(give3x, 64, lanes_x), r3.at[b, :, lanes_x], ynb),
                    copy(4, self._w(give3y, 64, lanes_y), r3.at[b, :, lanes_y], xnb),
                ]
            if phase == 4:
                return [
                    copy(5, self._w(give4x, 32, lanes_x), r4.at[b, :, lanes_x], znb),
                    copy(6, self._w(give4y, 32, lanes_y), r4.at[b, :, lanes_y], znb),
                ]
            if phase == 5:
                return [
                    copy(7, self._w(give5x, 16, lanes_x), r5.at[b, :, lanes_x], zfar),
                    copy(8, self._w(give5y, 16, lanes_y), r5.at[b, :, lanes_y], zfar),
                ]
            if phase < 10:
                keep_x, keep_y, n, to_x, to_y = (
                    (keep5x, keep5y, 16, zfar, zfar),
                    (keep4x, keep4y, 32, znb, znb),
                    (keep3x, keep3y, 64, ynb, xnb),
                    (keep2x, keep2y, 128, xnb, ynb),
                )[phase - 6]
                mine_x, mine_y = self._f(keep_x, n, lanes_x), self._f(keep_y, n, lanes_y)
                first = 2 * phase - 3
                return [copy(first, mine_x, mine_x, to_x), copy(first + 1, mine_y, mine_y, to_y)]
            return [copy(17, r1.at[b], self._out(base1), sib)]

        def _f(self, first, n, lanes):
            return r1.at[self.blocks, rows_of(first - base1, n), lanes]

        def _out(self, first):
            return wgrad_hbm.at[self.blocks, rows_of(first, 256), pl.ds(0, 512)]

        def start(self, phase):
            for one in self._list(phase):
                one.start()

        def finish(self, phase):
            if phase == 10:
                other = self._out((1 - c) * 256)
                Copy(other, other, ss.at[0], rs.at[self.r0 + 17], sib).wait_recv()
                return
            for one in self._list(phase):
                one.wait_recv()
            if phase > 5:
                return

            def add(i, carry):
                b = self.b0 + i
                if phase == 1:
                    here = (b, rows_of(base1, 256), slice(None))
                    wg[here] = wg[here] + r1[b]
                if phase == 2:
                    for keep, lo in ((keep2x, 0), (keep2y, 256)):
                        here = (b, rows_of(keep, 128), slice(lo, lo + 256))
                        wg[here] = wg[here] + r2[b, :, lo : lo + 256]
                if phase == 3:
                    for keep, lo in ((keep3x, 0), (keep3y, 256)):
                        here = (b, rows_of(keep, 64), slice(lo, lo + 256))
                        wg[here] = wg[here] + r3[b, :, lo : lo + 256]
                if phase == 4:
                    for keep, lo in ((keep4x, 0), (keep4y, 256)):
                        here = (b, rows_of(keep, 32), slice(lo, lo + 256))
                        wg[here] = wg[here] + r4[b, :, lo : lo + 256]
                if phase == 5:
                    for keep, lo in ((keep5x, 0), (keep5y, 256)):
                        total = wg[b, rows_of(keep, 16), lo : lo + 256] + r5[b, :, lo : lo + 256]
                        r1[b, rows_of(keep - base1, 16), lo : lo + 256] = total
                return carry

            lax.fori_loop(0, self.nb, add, 0)

        def step(self, phase):
            self.finish(phase)
            if phase < 10:
                self.begin(phase + 1)

        def begin(self, phase):
            self.start(phase)
            if phase == 10:
                self.store().start()

        def store(self):
            return pltpu.make_async_copy(r1.at[self.blocks], self._out(base1), ls.at[self.store_sem])

        def wait_sends(self):
            for phase in range(1, 11):
                for one in self._list(phase):
                    one.wait_send()

    red = [Reduce(i) for i in range(len(CHUNKS))]
    for one in red:
        one.store_sem = ids("l", 1)

    for d in loads_f:
        d.wait()

    def do(item):
        if not isinstance(item, str):
            if item[0] == "f":
                red[item[1]].finish(item[2])
            elif item[0] == "s":
                red[item[1]].begin(item[2])
            else:
                red[item[0]].step(item[1])
        elif item == "gain0":
            gains_start()
        elif item.startswith("gain"):
            gain_finish(int(item[4:]))
        elif item.startswith("deliver"):
            deliver(int(item[7:]))
        else:
            {"out": finish_output, "sums": finish_sums, "came": finish_came}[item]()

    def run_after(name, index=None):
        if index is None:
            for (_, _, when), one in zip(CHUNKS, red):
                if when == name:
                    one.start(1)
            for item in SCHEDULE.get(name, ()):
                do(item)
            return
        for i in range(9):
            full = name + str(i)
            if full in SCHEDULE or any(when == full for _, _, when in CHUNKS):

                @pl.when(index == i)
                def _():
                    run_after(full)

    def ffn_forward(j, carry):
        up = mm(wup[j], n2_ref[...], TN)
        size = jnp.abs(up) * (0.5**0.5)
        t = 1.0 / (1.0 + 0.3275911 * size)
        poly = t * (
            0.254829592
            + t * (-0.284496736 + t * (1.421413741 + t * (-1.453152027 + t * 1.061405429)))
        )
        decay = jnp.exp(-0.5 * up * up)
        far = 0.5 * poly * decay
        phi = jnp.where(up < 0.0, far, 1.0 - far)
        slope = phi + up * decay * (1.0 / math.sqrt(2.0 * math.pi))
        act = (up * phi).astype(BF16)
        bytes_v[j] = act
        bytes_v[4 + j] = slope.astype(BF16)
        big[0] += mm(wdn[j], act, TN)
        return carry

    lax.fori_loop(0, 4, ffn_forward, 0)

    Copy(cot_w.at[0], cot_w.at[0], ss.at[0], rs.at[r_cot], sib).wait_recv()
    Copy(cot_w.at[1], cot_w.at[1], ss.at[0], rs.at[r_cot + 1], sib, jnp.logical_not(hi_here)).wait_recv()
    gb[...] = jnp.concatenate([cot_w[0], cot_w[1]], axis=1)

    def ffn_backward(j, carry):
        wg[2 * j] = mm(bytes_v[j], gb[...], NT).astype(BF16)
        grad_up = (mm(wdn[j], gb[...], NN) * bytes_v[4 + j].astype(F32)).astype(BF16)
        wg[2 * j + 1] = mm(n2_ref[...], grad_up, NT).astype(BF16)
        big[1] += mm(wup[j], grad_up, NN)
        run_after("F", j)
        return carry

    lax.fori_loop(0, 4, ffn_backward, 0)

    s_out, r_out = ids("s", 2), ids("r", 2)
    res = big[0].astype(BF16)
    owners = ((1 - zl, c, lo_here), (2 + zl, 1 - c, hi_here))
    for slot, (chip, i, here) in enumerate(owners):
        out_s[slot] = res[:, slot * half : (slot + 1) * half]
        go(
            Copy(
                out_s.at[slot],
                out_r.at[i],
                ss.at[s_out + slot],
                rs.at[r_out + i],
                dev(g, chip),
                None if here is False else jnp.logical_not(here),
            )
        )
        if here is not False:

            @pl.when(here)
            def _():
                out_r[i] = out_s[slot]

    grad_n2 = big[1]
    unit2 = hat2[...]
    product = grad_n2 * unit2

    def lane_fold(values):
        total = values[:, 0:128]
        for k in range(1, values.shape[1] // 128):
            total = total + values[:, 128 * k : 128 * (k + 1)]
        return total

    gain_acc[1] = lane_fold(product)
    e = grad_n2 * gain_col2
    grad_mid = gb[...].astype(F32) + inverse2 * (
        e
        - jnp.mean(e, axis=0, keepdims=True)
        - unit2 * jnp.mean(e * unit2, axis=0, keepdims=True)
    )
    gmid[0] = grad_mid[:, 0:half]
    gmid[1] = grad_mid[:, half:]
    branch = grad_mid.astype(BF16)
    wg[8] = mm(att[...], branch, NT).astype(BF16)
    run_after("post")
    grad_att = mm(weights[3], branch, NN)
    d_o[...] = grad_att.astype(BF16)
    for slot in range(2):
        lanes = slice(slot * half, (slot + 1) * half)
        both = d_o[:, lanes].astype(F32) * o_acc[slot]
        for h in range(HEADS):
            d_sc[slot, h : h + 1, :] = jnp.sum(
                both[64 * h : 64 * h + 64, :], axis=0, keepdims=True
            )

    dq[...] = jnp.zeros_like(dq)
    gwqkv[...] = jnp.zeros_like(gwqkv)
    gain_acc[0] = jnp.zeros((feat, 128), F32)
    s_rc, r_rc = ids("s", 4), ids("r", 4)
    s_rz, r_rz = ids("s", 4), ids("r", 4)
    s_fin, r_fin = ids("s", 4), ids("r", 2)

    def sd_at(which, h):
        return big.at[which, pl.ds(half * ((h // 2) % 2), half), pl.ds(half * (h % 2), half)]

    def backward_step(slot, kb):
        hq = hq_at(slot)
        bias = bias_of(hq, kb)
        lanes = pl.ds(pl.multiple_of(slot * half, half), half)
        lse = m_sc[slot]
        dots = d_sc[slot]
        for first in (0, 4):
            for h in range(first, first + 4):
                part = slice(64 * h, 64 * h + 64)
                grad_o = d_o[part, lanes]
                sd_at(0, h)[...] = mm(k_t[kb, part, :], q_t[slot, part, :], TN)
                sd_at(1, h)[...] = mm(v_t[kb, part, :], grad_o, TN)
            for h in range(first, first + 4):
                part = slice(64 * h, 64 * h + 64)
                prob = jnp.exp2(sd_at(0, h)[...] * score_scale + bias - lse[h : h + 1, :])
                grad_s = (prob * (sd_at(1, h)[...] - dots[h : h + 1, :])).astype(BF16)
                dv[part, :] += mm(d_o[part, lanes], prob.astype(BF16), NT)
                dk[part, :] += mm(q_t[slot, part, :], grad_s, NT)
                dq[slot, part, :] += mm(k_t[kb, part, :], grad_s, NN)

    att_scale = HEAD_DIM ** (-0.5)

    def rc_copy(kb):
        zb = lax.div(kb, 2)
        return Copy(
            ppart.at[kb],
            rc.at[zb],
            ss.at[s_rc + zb],
            rs.at[r_rc + zb],
            sib,
            lax.rem(kb, 2) != c,
        )

    def is_final(zb):
        return jnp.where(lax.div(zb, 2) == g, z == zb, is_near)

    def rz_copy(zb):
        return Copy(
            ppart.at[2 * zb + c],
            rz.at[zb],
            ss.at[s_rz + zb],
            rs.at[r_rz + zb],
            dev(c, zo),
            jnp.logical_and(jnp.logical_not(is_final(zb)), zb < nblk - 1),
        )

    def fin_copy(zb):
        here = jnp.logical_and(zb == z, g == c)
        return Copy(
            ppart.at[2 * zb + c],
            gfin.at[c],
            ss.at[s_fin + zb],
            rs.at[r_fin + c],
            dev(g, zb),
            jnp.logical_and(is_final(zb), jnp.logical_not(here)),
        )

    def combine(zb):
        kb = 2 * zb + c
        Copy(rc.at[zb], rc.at[zb], ss.at[0], rs.at[r_rc + zb], sib).wait_recv()
        ppart[kb] = ppart[kb] + rc[zb]
        rz_copy(zb).start()

    def deliver(zb):
        kb = 2 * zb + c
        final = jnp.logical_and(is_final(zb), zb < nblk - 1)
        Copy(rz.at[zb], rz.at[zb], ss.at[0], rs.at[r_rz + zb], sib, final).wait_recv()

        @pl.when(final)
        def _():
            ppart[kb] = ppart[kb] + rz[zb]

        @pl.when(jnp.logical_and(zb == z, g == c))
        def _():
            gfin[c] = ppart[kb]

        fin_copy(zb).start()

    s_gain, r_gain = ids("s", 6), ids("r", 6)

    def gain_list(phase):
        if phase < 4:
            device = (sib, xnb, ynb)[phase - 1]
            k = phase - 1
            return [
                Copy(gain_s.at[k], gain_r.at[k], ss.at[s_gain + k], rs.at[r_gain + k], device)
            ]
        return [
            Copy(
                gain_s.at[3],
                gain_r.at[2 + k],
                ss.at[s_gain + 2 + k],
                rs.at[r_gain + 2 + k],
                (dp, lax.rem(z + k, nblk)),
            )
            for k in range(1, 4)
        ]

    def gain_finish(phase):
        for one in gain_list(phase):
            one.wait_recv()
        if phase < 4:
            gain_s[phase] = gain_s[phase - 1] + gain_r[phase - 1]
            for one in gain_list(phase + 1):
                one.start()
        else:
            total = jnp.zeros((8, feat), F32)
            for zz in range(nblk):
                k = lax.rem(z - zz + nblk, nblk)
                part = gain_s[3]
                for i in range(1, 4):
                    part = jnp.where(k == i, gain_r[2 + i], part)
                total = total + part
            ggain_ref[...] = total

    def gains_start():
        for i in range(2):
            gain_s[0, i : i + 1, :] = jnp.sum(gain_acc[i].T, axis=0, keepdims=True)
        gain_s[0, 2:8, :] = jnp.zeros((6, feat), F32)
        gain_list(1)[0].start()

    s_last, r_last = ids("s", 1), ids("r", 1)
    copy_last = Copy(
        last_s,
        last_r,
        ss.at[s_last],
        rs.at[r_last],
        (dp, lax.rem(z + 1, nblk)),
        z < nblk - 1,
    )

    def finish_output():
        for i in range(2):
            mine = out_from_self(i, c, z)
            Copy(
                out_r.at[i], out_r.at[i], ss.at[0], rs.at[r_out + i], sib, jnp.logical_not(mine)
            ).wait_recv()
            live = rdiv[1:2, i * half : (i + 1) * half]
            out_ref[i * half : (i + 1) * half, :] = (out_r[i].astype(F32) * live).T.astype(BF16)

    def finish_sums():
        for i in range(2):
            mine = jnp.logical_and(own_worker, c == i)
            Copy(
                gfin.at[i], gfin.at[i], ss.at[0], rs.at[r_fin + i], sib, jnp.logical_not(mine)
            ).wait_recv()
            grad_sums = gfin[i].astype(F32) * rdiv[0:1, i * half : (i + 1) * half]
            gs_ref[i * half : (i + 1) * half, :] = grad_sums.T.astype(BF16)

        is_last = jnp.where(iota((16, feat), 1).astype(F32) == cnt - 1.0, 1.0, 0.0).astype(BF16)
        last_s[...] = mm(is_last, gs_ref[...], NN).astype(BF16)
        copy_last.start()

    def finish_came():
        Copy(last_r, last_r, ss.at[0], rs.at[r_last], sib, z > 0).wait_recv()

        @pl.when(z == 0)
        def _():
            last_r[...] = jnp.zeros_like(last_r)

        came_ref[...] = last_r[...]

    def key_step(t, carry):
        both = t < 2 * w + 2
        kb = jnp.where(both, lax.div(t, 2), t - w - 1)
        slot = jnp.where(both, 1 - lax.rem(t, 2), 1)
        first = jnp.logical_or(jnp.logical_not(both), lax.rem(t, 2) == 0)
        last = jnp.logical_or(jnp.logical_not(both), lax.rem(t, 2) == 1)

        @pl.when(first)
        def _():
            dk[...] = jnp.zeros_like(dk)
            dv[...] = jnp.zeros_like(dv)

        backward_step(slot, kb)

        @pl.when(last)
        def _():
            grad_key = turned(dk[...] * att_scale, kb, -1.0)
            grad_value = dv[...].astype(BF16)
            normed = n1[kb]
            k_t[kb] = grad_key
            v_t[kb] = grad_value
            gwqkv[1] += mm(normed, grad_key, NT)
            gwqkv[2] += mm(normed, grad_value, NT)

            @pl.when(jnp.logical_or(kb == w, kb == 7 - w))
            def _():
                slot = jnp.where(kb == w, 0, 1)
                grad_query = turned(dq[slot] * att_scale, kb, -1.0)
                q_t[slot] = grad_query
                gwqkv[0] += mm(normed, grad_query, NT)


        @pl.when(jnp.logical_and(lax.rem(t, 2) == 1, t < 2 * EARLY))
        def _():
            row_block(lax.div(t, 2))

        run_after("K", t)
        return carry

    def row_block(kb):
        @pl.when(kb <= 7 - w)
        def _():
            big[0, :, 0:half] = mm(weights[1], k_t[kb], NN) + mm(weights[2], v_t[kb], NN)
            own = jnp.logical_or(kb == w, kb == 7 - w)
            slot = jnp.where(kb == w, 0, 1)

            @pl.when(own)
            def _():
                big[0, :, 0:half] += mm(weights[0], q_t[slot], NN)

            grad_n1 = big[0, :, 0:half]
            unit, inverse = norm_parts(p_all[kb].astype(F32))
            gain_acc[0] += lane_fold(grad_n1 * unit)
            e = grad_n1 * gcol[0]
            total = inverse * (
                e
                - jnp.mean(e, axis=0, keepdims=True)
                - unit * jnp.mean(e * unit, axis=0, keepdims=True)
            )
            ppart[kb] = (total + jnp.where(own, 1.0, 0.0) * gmid[slot]).astype(BF16)

        @pl.when(kb > 7 - w)
        def _():
            ppart[kb] = jnp.zeros(ppart.shape[1:], BF16)

        rc_copy(kb).start()

        @pl.when(lax.rem(kb, 2) == 1)
        def _():
            combine(lax.div(kb, 2))

    def late_row_block(kb, carry):
        row_block(kb)
        run_after("R", kb)
        return carry

    lax.fori_loop(0, 9, key_step, 0)
    for i in range(3):
        wg[9 + i] = gwqkv[i].astype(BF16)
    run_after("W")
    lax.fori_loop(EARLY, 8, late_row_block, 0)

    run_after("end")

    for one in sends:
        one.wait_send()
    pass_on_sent()
    copy_last.wait_send()
    for one in outside_late:
        one.wait_send()
    for i in range(2):
        cot_copy(i)[1].wait_send()

    def close_key(kb, carry):
        rc_copy(kb).wait_send()
        return carry

    lax.fori_loop(0, 8, close_key, 0)

    def close_block(zb, carry):
        rz_copy(zb).wait_send()
        fin_copy(zb).wait_send()
        return carry

    lax.fori_loop(0, 4, close_block, 0)
    for phase in range(1, 5):
        for one in gain_list(phase):
            one.wait_send()
    for one in red:
        one.wait_sends()
        one.store().wait()


def out_from_self(i, c, z):
    chip = 2 * c + 1 - jnp.where(z < 2, z, 3 - z)
    core = jnp.where(z < 2, i, 1 - i)
    return jnp.logical_and(core == c, chip == z)


def expand_kernel(
    slots_ref, gs_ref, came_ref, out_ref, ggain_ref, w_hbm,
    bytes_out, out_out, ga_out, gf_out, dn_out, up_out, wo_out, wq_out, wk_out, wv_out,
    w_v, bytes_v, out_v, dn_v, up_v, rest_v, sem_in, sem_out,
):
    loads = [pltpu.make_async_copy(w_hbm.at[i], w_v.at[i], sem_in.at[i]) for i in range(12)]
    for one in loads:
        one.start()
    stores = []

    def store(src, dst):
        copy = pltpu.make_async_copy(src, dst, sem_out.at[len(stores)])
        copy.start()
        stores.append(copy)

    out_v[...] = out_ref[...].astype(F32)
    store(out_v, out_out)
    ga_out[...] = ggain_ref[0:1, :]
    gf_out[...] = ggain_ref[1:2, :]
    slot_iota = iota((512, 128), 0).astype(F32)
    first = iota((16, 128), 0) == 0

    def weights(j):
        loads[2 * j].wait()
        dn_v[j] = w_v[2 * j].astype(F32)
        store(dn_v.at[j], dn_out.at[pl.ds(512 * j, 512)])
        loads[2 * j + 1].wait()
        up_v[j] = w_v[2 * j + 1].astype(F32)
        store(up_v.at[j], up_out.at[:, pl.ds(512 * j, 512)])

    for k in range(8):
        rows = [slots_ref[4 * k + r : 4 * k + r + 1, :] for r in range(4)]
        reach = 64 * (k + 1)
        member = jnp.concatenate(
            [(slot_iota[0:reach] == row).astype(F32).astype(BF16) for row in rows], axis=1
        )
        spread = mm(member, gs_ref[0:reach, :], TN)
        if k == 0:
            lead = jnp.concatenate(
                [
                    jnp.where(jnp.logical_and(first, row < -0.5), 1.0, 0.0).astype(BF16)
                    for row in rows
                ],
                axis=1,
            )
            spread = spread + mm(lead, came_ref[...], TN)
        bytes_v[k] = spread
        store(bytes_v.at[k], bytes_out.at[pl.ds(512 * k, 512)])
        if k % 2 == 1:
            weights(k // 2)
    for i, dst in enumerate((wo_out, wq_out, wk_out, wv_out)):
        loads[8 + i].wait()
        rest_v[i] = w_v[8 + i].astype(F32)
        store(rest_v.at[i], dst)
    for one in stores:
        one.wait()


def fast_local(
    bytes_in, flags, lengths, cotangent, w_query, w_key, w_value, w_out, w_up, w_down, gain_attn, gain_ffn
):
    meta_flags = flags.reshape(32, 128)
    freqs = np.float32(ROTARY_BASE) ** (-2.0 * np.arange(32, dtype=np.float32) / np.float32(64))
    freq = np.ascontiguousarray(np.broadcast_to(freqs.astype(np.float32)[:, None], (32, 128)))
    vm = pl.BlockSpec(memory_space=pltpu.VMEM)
    hbm = pl.BlockSpec(memory_space=pl.ANY)
    hb = lambda n: pltpu.VMEM((n, 512, 256), BF16)
    hbf = lambda n: pltpu.VMEM((n, 512, 256), F32)
    sq = lambda n, t: pltpu.VMEM((n, 512, 512), t)
    scratch = dict(
        bytes_v=sq(8, BF16),
        weights=sq(4, BF16),
        wup=sq(4, BF16),
        wdn=sq(4, BF16),
        meta=pltpu.VMEM((2, 4, 40, 128), jnp.int32),
        tail=pltpu.VMEM((16, 512), BF16),
        p_own=hb(2),
        relay=pltpu.VMEM((512, 256), BF16),
        p_all=hb(8),
        n1=hb(8),
        k_t=hb(8),
        v_t=hb(8),
        q_t=hb(2),
        tab_c=pltpu.VMEM((8, 32, 256), F32),
        tab_s=pltpu.VMEM((8, 32, 256), F32),
        pos=pltpu.VMEM((8, 8, 256), F32),
        gcol=hbf(2),
        cot_own=hb(2),
        cot_w=hb(2),
        o_acc=hbf(2),
        m_sc=pltpu.VMEM((2, 8, 256), F32),
        l_sc=pltpu.VMEM((2, 8, 256), F32),
        att=pltpu.VMEM((512, 512), BF16),
        gb=pltpu.VMEM((512, 512), BF16),
        hat2=pltpu.VMEM((512, 512), F32),
        d_o=pltpu.VMEM((512, 512), BF16),
        d_sc=pltpu.VMEM((2, 8, 256), F32),
        gmid=hbf(2),
        dk=pltpu.VMEM((512, 256), F32),
        dv=pltpu.VMEM((512, 256), F32),
        dq=hbf(2),
        gwqkv=sq(3, F32),
        big=sq(2, F32),
        wg=sq(12, BF16),
        r1=pltpu.VMEM((12, 256, 512), BF16),
        r2=pltpu.VMEM((12, 128, 512), BF16),
        r3=pltpu.VMEM((12, 64, 512), BF16),
        r4=pltpu.VMEM((12, 32, 512), BF16),
        r5=pltpu.VMEM((12, 16, 512), BF16),
        ppart=hb(8),
        rc=hb(4),
        rz=hb(4),
        gfin=hb(2),
        out_s=hb(2),
        out_r=hb(2),
        rdiv=pltpu.VMEM((16, 512), F32),
        last_s=pltpu.VMEM((16, 512), BF16),
        last_r=pltpu.VMEM((16, 512), BF16),
        gain_acc=pltpu.VMEM((2, 512, 128), F32),
        gain_s=pltpu.VMEM((4, 8, 512), F32),
        gain_r=pltpu.VMEM((6, 8, 512), F32),
        ss=pltpu.SemaphoreType.DMA((224,)),
        rs=pltpu.SemaphoreType.DMA((224,)),
        ls=pltpu.SemaphoreType.DMA((32,)),
    )
    out, gs, came, slots, wgrad, ggain = pl.pallas_call(
        layer_kernel,
        out_shape=(
            jax.ShapeDtypeStruct((512, 512), BF16),
            jax.ShapeDtypeStruct((512, 512), BF16),
            jax.ShapeDtypeStruct((16, 512), BF16),
            jax.ShapeDtypeStruct((32, 128), F32),
            jax.ShapeDtypeStruct((12, 512, 512), BF16),
            jax.ShapeDtypeStruct((8, 512), F32),
        ),
        in_specs=[hbm, vm, vm, hbm, hbm, hbm, hbm, hbm, hbm, hbm, vm, vm, vm],
        out_specs=(vm, vm, vm, vm, hbm, vm),
        scratch_shapes=list(scratch.values()),
        compiler_params=pltpu.CompilerParams(
            collective_id=0, has_side_effects=True, vmem_limit_bytes=60 * 2**20
        ),
        name="layer",
    )(
        bytes_in, meta_flags, lengths, cotangent, w_query, w_key, w_value, w_out, w_up, w_down,
        gain_attn.reshape(1, 512), gain_ffn.reshape(1, 512), freq,
    )
    grad_bytes, out, g_attn, g_ffn, dn, up, wo, wq, wk, wv = pl.pallas_call(
        expand_kernel,
        out_shape=(
            jax.ShapeDtypeStruct((4096, 512), F32),
            jax.ShapeDtypeStruct((512, 512), F32),
            jax.ShapeDtypeStruct((1, 512), F32),
            jax.ShapeDtypeStruct((1, 512), F32),
            jax.ShapeDtypeStruct((2048, 512), F32),
            jax.ShapeDtypeStruct((512, 2048), F32),
        )
        + (jax.ShapeDtypeStruct((512, 512), F32),) * 4,
        in_specs=[vm, vm, vm, vm, vm, hbm],
        out_specs=(hbm, hbm, vm, vm) + (hbm,) * 6,
        scratch_shapes=[
            sq(12, BF16),
            sq(8, F32),
            pltpu.VMEM((512, 512), F32),
            sq(4, F32),
            sq(4, F32),
            sq(4, F32),
            pltpu.SemaphoreType.DMA((12,)),
            pltpu.SemaphoreType.DMA((24,)),
        ],
        compiler_params=pltpu.CompilerParams(vmem_limit_bytes=60 * 2**20),
        name="expand",
    )(slots, gs, came, out, ggain, wgrad)
    return out, grad_bytes, wq, wk, wv, wo, up, dn, g_attn.reshape(512), g_ffn.reshape(512)


def passed_along(block, axis, distance):
    devices = range(lax.axis_size(axis))
    route = [((i - distance) % len(devices), i) for i in devices]
    return lax.ppermute(block, axis, route)


def from_behind(value, axis, by):
    count = lax.axis_size(axis)
    pairs = [(i, i + by) for i in range(count) if 0 <= i + by < count]
    return lax.ppermute(value, axis, pairs)


def rotate(vectors, positions, direction):
    half_dim = vectors.shape[-1] // 2
    freqs = ROTARY_BASE ** (-2.0 * jnp.arange(half_dim, dtype=jnp.float32) / vectors.shape[-1])
    angles = positions.astype(jnp.float32)[:, None] * freqs[None, :]
    cosine = jnp.cos(angles)[:, None, :]
    sine = direction * jnp.sin(angles)[:, None, :]
    first_half = vectors[..., :half_dim]
    second_half = vectors[..., half_dim:]
    return jnp.concatenate(
        [first_half * cosine - second_half * sine, second_half * cosine + first_half * sine],
        axis=-1,
    )


def layer_norm_parts(values, gain):
    center = values - jnp.mean(values, axis=-1, keepdims=True)
    spread = jnp.mean(center * center, axis=-1, keepdims=True)
    inverse = lax.rsqrt(spread + EPSILON)
    normed = center * inverse
    return (normed * gain, normed, inverse)


def layer_norm_back(grad_in, normed, inverse, gain):
    scaled = grad_in * gain
    grad_values = inverse * (
        scaled
        - jnp.mean(scaled, axis=-1, keepdims=True)
        - normed * jnp.mean(scaled * normed, axis=-1, keepdims=True)
    )
    grad_gain = jnp.sum(grad_in * normed, axis=0)
    return (grad_values, grad_gain)


def pass_grads(grad_key, grad_value):
    return (
        passed_along(grad_key.astype(jnp.bfloat16), "blk", 1).astype(grad_key.dtype),
        passed_along(grad_value.astype(jnp.bfloat16), "blk", 1).astype(grad_value.dtype),
    )


def local(
    bytes_in,
    flags,
    lengths,
    cotangent,
    w_query,
    w_key,
    w_value,
    w_out,
    w_up,
    w_down,
    gain_attn,
    gain_ffn,
):
    blocks = lax.axis_size("blk")
    own_index = lax.axis_index("blk")
    seg_rows = cotangent.shape[0]
    byte_rows = bytes_in.shape[0]
    features = bytes_in.shape[1]
    scale = HEAD_DIM ** (-0.5)
    running = jnp.cumsum(flags)
    slot_of = running - 1
    seg_count = running[-1]
    slot_ids = jnp.arange(seg_rows, dtype=jnp.int32)
    member = (slot_of[None, :] == slot_ids[:, None]).astype(jnp.bfloat16)
    seg_sums = jnp.dot(member, bytes_in, preferred_element_type=jnp.float32)
    seg_tally = jnp.sum(member, axis=1, dtype=jnp.float32)
    leading = slot_of < 0
    tail_sum = jnp.dot(
        leading.astype(jnp.bfloat16)[None, :], bytes_in, preferred_element_type=jnp.float32
    )
    tail_count = jnp.sum(leading.astype(jnp.float32), keepdims=True)
    got_sum, got_count = from_behind((tail_sum, tail_count), "blk", -1)
    last_slot = slot_ids == seg_count - 1
    seg_sums = seg_sums + jnp.where(last_slot[:, None], got_sum, 0.0)
    seg_tally = seg_tally + jnp.where(last_slot, got_count[0], 0.0)
    divisor = jnp.maximum(seg_tally, 1.0)
    pooled = seg_sums / divisor[:, None]
    starts = jnp.cumsum(lengths[0]) - lengths[0]
    byte_at = own_index * byte_rows + jnp.arange(byte_rows, dtype=jnp.int32)
    prior_flags = jnp.sum(
        flags[None, :] * (byte_at[None, :] < starts[:, None]).astype(jnp.int32), axis=1
    )
    all_counts, all_prior = (
        lax.all_gather(seg_count[None], "blk", axis=0, tiled=True),
        lax.all_gather(prior_flags[None, :], "blk", axis=0, tiled=True),
    )
    offsets = jnp.cumsum(all_counts) - all_counts
    seq_first = jnp.sum(all_prior, axis=0)
    dev_ids = jnp.arange(blocks, dtype=jnp.int32)

    def layout(first_row, row_count):
        row_index = first_row + jnp.arange(row_count, dtype=jnp.int32)
        owner_dev = row_index // seg_rows
        within = row_index % seg_rows
        dev_pick = owner_dev[:, None] == dev_ids[None, :]
        dev_base = jnp.sum(jnp.where(dev_pick, offsets[None, :], 0), axis=1)
        dev_have = jnp.sum(jnp.where(dev_pick, all_counts[None, :], 0), axis=1)
        return (dev_base + jnp.minimum(within, dev_have - 1), within < dev_have)

    query_pos, query_live = layout(own_index * seg_rows, seg_rows)
    query_first = jnp.max(
        jnp.where(seq_first[None, :] <= query_pos[:, None], seq_first[None, :], 0), axis=1
    )

    def visible(first_row, row_count):
        key_pos, key_live = layout(first_row, row_count)
        return (
            (key_pos[None, :] <= query_pos[:, None])
            & (key_pos[None, :] >= query_first[:, None])
            & key_live[None, :]
        )

    normed_attn, unit_attn, scale_attn = layer_norm_parts(pooled, gain_attn)
    n_one = normed_attn.astype(jnp.bfloat16)
    query_pre = jnp.dot(n_one, w_query, preferred_element_type=jnp.float32)
    query_rot = rotate(query_pre.reshape(seg_rows, HEADS, HEAD_DIM), query_pos, 1.0).astype(
        jnp.bfloat16
    )
    key_pre = jnp.dot(n_one, w_key, preferred_element_type=jnp.float32)
    key_rot = (
        rotate(key_pre.reshape(seg_rows, HEADS, HEAD_DIM), query_pos, 1.0)
        .reshape(seg_rows, features)
        .astype(jnp.bfloat16)
    )
    value_low = jnp.dot(n_one, w_value, preferred_element_type=jnp.float32).astype(jnp.bfloat16)
    start_state = (
        jnp.full((HEADS, seg_rows), NEGATIVE, jnp.float32),
        jnp.zeros((HEADS, seg_rows), jnp.float32),
        jnp.zeros((seg_rows, HEADS, HEAD_DIM), jnp.float32),
    )
    key_piece = lax.all_gather(key_rot, "blk", axis=0, tiled=True)
    value_piece = lax.all_gather(value_low, "blk", axis=0, tiled=True)
    row_count = key_piece.shape[0]
    allowed = visible(jnp.int32(0), row_count)

    def absorb_update(running_state):
        row_max, row_sum, weighted = running_state
        scores = (
            jnp.einsum(
                "qhe,khe->hqk",
                query_rot,
                key_piece.reshape(row_count, HEADS, HEAD_DIM),
                preferred_element_type=jnp.float32,
            )
            * scale
        )
        scores = jnp.where(allowed[None], scores, NEGATIVE)
        new_max = jnp.maximum(row_max, jnp.max(scores, axis=-1))
        weights = jnp.where(allowed[None], jnp.exp(scores - new_max[:, :, None]), 0.0)
        shrink = jnp.exp(row_max - new_max)
        row_sum = jnp.sum(weights, axis=-1)
        weighted = weighted * shrink.T[:, :, None] + jnp.einsum(
            "hqk,khe->qhe",
            weights.astype(jnp.bfloat16),
            value_piece.reshape(row_count, HEADS, HEAD_DIM),
            preferred_element_type=jnp.float32,
        )
        return (new_max, row_sum, weighted)

    row_max, row_sum, weighted = lax.cond(
        jnp.any(allowed), absorb_update, lambda unchanged: unchanged, start_state
    )
    log_total = row_max + jnp.log(row_sum)
    attended_full = weighted / row_sum.T[:, :, None]
    attended = attended_full.reshape(seg_rows, features).astype(jnp.bfloat16)
    middle = pooled + jnp.dot(attended, w_out, preferred_element_type=jnp.float32)
    normed_ffn, unit_ffn, scale_ffn = layer_norm_parts(middle, gain_ffn)
    n_two = normed_ffn.astype(jnp.bfloat16)
    up_proj = jnp.dot(n_two, w_up, preferred_element_type=jnp.float32)
    act_full, gelu_back = jax.vjp(lambda inner: jax.nn.gelu(inner, approximate=False), up_proj)
    act_low = act_full.astype(jnp.bfloat16)
    result = middle + jnp.dot(act_low, w_down, preferred_element_type=jnp.float32)
    live_rows = query_live.astype(jnp.float32)[:, None]
    output = result * live_rows
    grad_out = cotangent * live_rows
    grad_branch = grad_out.astype(jnp.bfloat16)
    grad_w_down = jnp.einsum("sf,sd->fd", act_low, grad_branch, preferred_element_type=jnp.float32)
    grad_act = jnp.einsum("sd,fd->sf", grad_branch, w_down, preferred_element_type=jnp.float32)
    grad_up = gelu_back(grad_act)[0].astype(jnp.bfloat16)
    grad_w_up = jnp.einsum("sd,sf->df", n_two, grad_up, preferred_element_type=jnp.float32)
    grad_n_two = jnp.einsum("sf,df->sd", grad_up, w_up, preferred_element_type=jnp.float32)
    grad_mid_norm, grad_gain_ffn = layer_norm_back(grad_n_two, unit_ffn, scale_ffn, gain_ffn)
    grad_middle = grad_out + grad_mid_norm
    grad_attn_branch = grad_middle.astype(jnp.bfloat16)
    grad_w_out = jnp.einsum(
        "sd,se->de", attended, grad_attn_branch, preferred_element_type=jnp.float32
    )
    grad_attended = jnp.einsum(
        "se,de->sd", grad_attn_branch, w_out, preferred_element_type=jnp.float32
    ).astype(jnp.bfloat16)
    grad_att_three = grad_attended.reshape(seg_rows, HEADS, HEAD_DIM)
    row_dot = jnp.sum(grad_att_three.astype(jnp.float32) * attended_full, axis=-1).T

    def block_grads(key_piece, value_piece, source, grad_parts):
        allowed = visible(source * seg_rows, seg_rows)

        def block_update(grad_parts):
            grad_key, grad_value, grad_query = grad_parts
            key_three = key_piece.reshape(seg_rows, HEADS, HEAD_DIM)
            value_three = value_piece.reshape(seg_rows, HEADS, HEAD_DIM)
            scores = (
                jnp.einsum("qhe,khe->hqk", query_rot, key_three, preferred_element_type=jnp.float32)
                * scale
            )
            prob_full = jnp.where(allowed[None], jnp.exp(scores - log_total[:, :, None]), 0.0)
            grad_value = grad_value + jnp.einsum(
                "hqk,qhe->khe",
                prob_full.astype(jnp.bfloat16),
                grad_att_three,
                preferred_element_type=jnp.float32,
            ).reshape(seg_rows, features)
            grad_prob = jnp.einsum(
                "qhe,khe->hqk", grad_att_three, value_three, preferred_element_type=jnp.float32
            )
            grad_scores = (prob_full * (grad_prob - row_dot[:, :, None])).astype(jnp.bfloat16)
            grad_query = (
                grad_query
                + jnp.einsum(
                    "hqk,khe->qhe", grad_scores, key_three, preferred_element_type=jnp.float32
                )
                * scale
            )
            grad_key = grad_key + (
                jnp.einsum(
                    "hqk,qhe->khe", grad_scores, query_rot, preferred_element_type=jnp.float32
                )
                * scale
            ).reshape(seg_rows, features)
            return (grad_key, grad_value, grad_query)

        return lax.cond(jnp.any(allowed), block_update, lambda unchanged: unchanged, grad_parts)

    zero_rows = jnp.zeros((seg_rows, features), jnp.float32)
    zero_query = jnp.zeros((seg_rows, HEADS, HEAD_DIM), jnp.float32)

    def visit(visit_no, loop_state):
        key_piece, value_piece, grad_key, grad_value, grad_query = loop_state
        source = (own_index - visit_no) % blocks
        grad_key, grad_value, grad_query = block_grads(
            key_piece, value_piece, source, (grad_key, grad_value, grad_query)
        )
        key_piece, value_piece = from_behind((key_piece, value_piece), "blk", 1)
        grad_key, grad_value = pass_grads(grad_key, grad_value)
        return (key_piece, value_piece, grad_key, grad_value, grad_query)

    loop_out = lax.fori_loop(
        0, blocks, visit, (key_rot, value_low, zero_rows, zero_rows, zero_query)
    )
    grad_key_sum, grad_value_sum, grad_query_rot = (loop_out[2], loop_out[3], loop_out[4])
    grad_query = (
        rotate(grad_query_rot, query_pos, -1.0).reshape(seg_rows, features).astype(jnp.bfloat16)
    )
    grad_key = (
        rotate(grad_key_sum.reshape(seg_rows, HEADS, HEAD_DIM), query_pos, -1.0)
        .reshape(seg_rows, features)
        .astype(jnp.bfloat16)
    )
    grad_value_low = grad_value_sum.astype(jnp.bfloat16)
    grad_w_query = jnp.einsum("sd,se->de", n_one, grad_query, preferred_element_type=jnp.float32)
    grad_w_key = jnp.einsum("sd,se->de", n_one, grad_key, preferred_element_type=jnp.float32)
    grad_w_value = jnp.einsum(
        "sd,se->de", n_one, grad_value_low, preferred_element_type=jnp.float32
    )
    grad_n_one = jnp.einsum("se,de->sd", grad_query, w_query, preferred_element_type=jnp.float32)
    grad_n_one = grad_n_one + jnp.einsum(
        "se,de->sd", grad_key, w_key, preferred_element_type=jnp.float32
    )
    grad_n_one = grad_n_one + jnp.einsum(
        "se,de->sd", grad_value_low, w_value, preferred_element_type=jnp.float32
    )
    grad_pool_norm, grad_gain_attn = layer_norm_back(grad_n_one, unit_attn, scale_attn, gain_attn)
    grad_pooled = grad_middle + grad_pool_norm
    grad_sums = (grad_pooled / divisor[:, None]).astype(jnp.bfloat16)
    last_grad = jnp.dot(
        last_slot.astype(jnp.bfloat16)[None, :], grad_sums, preferred_element_type=jnp.float32
    ).astype(jnp.bfloat16)
    came_grad = from_behind(last_grad, "blk", 1)
    spread_rows = jnp.take(grad_sums, jnp.maximum(slot_of, 0), axis=0)
    grad_bytes = jnp.where(leading[:, None], came_grad, spread_rows).astype(jnp.float32)
    (
        grad_w_query,
        grad_w_key,
        grad_w_value,
        grad_w_out,
        grad_w_up,
        grad_w_down,
        grad_gain_attn,
        grad_gain_ffn,
    ) = lax.psum(
        (
            grad_w_query,
            grad_w_key,
            grad_w_value,
            grad_w_out,
            grad_w_up,
            grad_w_down,
            grad_gain_attn,
            grad_gain_ffn,
        ),
        ("dp", "blk"),
    )
    return (
        output,
        grad_bytes,
        grad_w_query,
        grad_w_key,
        grad_w_value,
        grad_w_out,
        grad_w_up,
        grad_w_down,
        grad_gain_attn,
        grad_gain_ffn,
    )


def solution(mesh):
    fits = mesh.shape["blk"] == 4 and mesh.shape["dp"] == 8
    return jax.shard_map(
        fast_local if fits else local,
        mesh=mesh,
        in_specs=(
            P(("dp", "blk"), None),
            P(("dp", "blk")),
            P("dp", None),
            P(("dp", "blk"), None),
            P(),
            P(),
            P(),
            P(),
            P(),
            P(),
            P(),
            P(),
        ),
        out_specs=(
            P(("dp", "blk"), None),
            P(("dp", "blk"), None),
            P(),
            P(),
            P(),
            P(),
            P(),
            P(),
            P(),
            P(),
        ),
        check_vma=False,
    )
```
